32 devices in a mesh: groups: 2 (over x), dom: 16 (over z, y, core).
Axes of the slice: x: 2, y: 2, z: 4, core: 2. Of those that a mesh axis runs over, the one named last changes fastest.
Arguments:
- grid: bfloat16 [32768, 1024], P(('groups', 'dom')), parts along dimension 0, may hold values from -6 to 6
- latent_in: bfloat16 [512, 1024], P(('groups', 'dom')), parts along dimension 0, may hold values from -3 to 3
- grid_gain: float32 [1024], replicated, may hold values from 0.5 to 1.5
- node_gain: float32 [1024], replicated, may hold values from 0.5 to 1.5
- dec_gain: float32 [1024], replicated, may hold values from 0.5 to 1.5
- w_q_enc: bfloat16 [1024, 512], replicated
- w_kv_enc: bfloat16 [1024, 1024], replicated, may hold values from -0.1875 to 0.1875
- w_o_enc: bfloat16 [512, 1024], replicated, may hold values from -0.25 to 0.25
- w_q_dec: bfloat16 [1024, 512], replicated
- w_kv_dec: bfloat16 [1024, 1024], replicated, may hold values from -0.1875 to 0.1875
- w_o_dec: bfloat16 [512, 1024], replicated, may hold values from -0.25 to 0.25
- enc_need: int32 [16, 512], P('dom'), may hold values from 0 to 1023
- enc_slot: int32 [32, 256], P(None, 'dom'), may hold values from 0 to 511
- enc_count: int32 [256], P('dom'), may hold values from 1 to 32
- dec_need: int32 [16, 4096], P('dom'), may hold values from 0 to 15
- dec_slot: int32 [4, 16384], P(None, 'dom'), may hold values from 0 to 4095
Outputs:
- latent_out: bfloat16 [512, 1024], P(('groups', 'dom')), parts along dimension 0
- grid_out: bfloat16 [32768, 1024], P(('groups', 'dom')), parts along dimension 0
The draws below stay inside these ranges and needn't reach their ends.
There are 2 independent parts, one for each index of `groups`. The reference program is written for one: setup_inputs(seed, part) draws one part's arguments, and reference() takes and returns one part's arrays. A program takes and returns all parts, laid end to end along the dimension named above; an argument that names none is the same for every part. Nothing has to cross between parts.
Inputs may be any that keep to these rules, and one draw needn't show every extreme that they name: `enc_need`: a grid point's index within its band; entries may repeat. Edges of node n are enc_slot[0..enc_count[n]-1, n]; entries may repeat. `dec_need`: a latent node's index within its window; entries may repeat. `dec_slot`: entries may repeat.
All inputs are finite; a program needn't handle non-finite values.
Results may differ from the reference program's by a relative error of at most 0.02.
The reference program's roundings to bfloat16 on the way count: a program that leaves them out, or rounds other values in their place, can miss the bound.
Values may be sent and summed in bfloat16 or wider, within the bound.
No kernel may reach another device: no remote copies, remote signals or barrier semaphores. Data moves between devices by JAX's collectives and lax.ppermute only.
A program may use at most 128 MiB of HBM per device.

```python
import math
import jax
import jax.numpy as jnp
from jax import lax

D = 1024
HEADS = 8
KE = 32
KD = 4
GP_DEV = 1024
NODE_DEV = 16
HH = 512
GRID = 16384
NODES = 256
N_DOM = 16


def query_weight(key):
    values = jax.random.normal(key, (D, HH), jnp.float32) * D ** (-0.5)
    values = values * 1.5
    return values.astype(jnp.bfloat16)


def draw_w_q_enc(key, part):
    return query_weight(jax.random.fold_in(key, 11))


def draw_w_q_dec(key, part):
    return query_weight(jax.random.fold_in(key, 23))


def with_ends(entries, own_key, smallest, largest):
    dims = entries.shape
    place = [jax.random.randint(jax.random.fold_in(own_key, axis), (), 0, dims[axis]) for axis in range(len(dims))]
    entries = entries.at[tuple(place)].set(smallest)
    longest = dims.index(max(dims))
    place[longest] = (place[longest] + 1) % dims[longest]
    return entries.at[tuple(place)].set(largest)


def levels(key, shape, cuts, least, top_value):
    factor_of, own = 1.0, jax.random.fold_in(key, 6)
    for dim, blocks in cuts:
        heights = jnp.exp(jax.random.uniform(jax.random.fold_in(own, dim), (blocks,), jnp.float32, least / len(cuts), top_value / len(cuts)))
        factor_of = factor_of * jnp.repeat(heights, shape[dim] // blocks).reshape([-1 if axis == dim else 1 for axis in range(len(shape))])
    return factor_of


def noise(own_key, shape, scale, reach, pieces=(), kind=jnp.bfloat16):
    array = scale * jax.random.normal(own_key, shape, jnp.float32)
    if pieces:
        array = array * levels(own_key, shape, pieces, -0.22, 0.18)
    return jnp.clip(array, -reach, reach).astype(kind)


def setup_inputs(seed: int = 0, part: int = 0) -> dict:
    keys = jax.random.split(jax.random.key(seed), 17)
    part_splits = jax.random.split(jax.random.fold_in(keys[16], part), 17)
    return {
        "grid": noise(part_splits[0], (GRID, D), 1.0, 6.0, ((0, 16),)),
        "latent_in": noise(part_splits[1], (NODES, D), 0.5, 3.0, ((0, 16),)),
        "grid_gain": jnp.clip(1.0 + 0.1 * jax.random.normal(keys[2], (D,), jnp.float32), 0.5, 1.5),
        "node_gain": jnp.clip(1.0 + 0.1 * jax.random.normal(keys[3], (D,), jnp.float32), 0.5, 1.5),
        "dec_gain": jnp.clip(1.0 + 0.1 * jax.random.normal(keys[4], (D,), jnp.float32), 0.5, 1.5),
        "w_q_enc": draw_w_q_enc(jax.random.fold_in(keys[16], 71), part),
        "w_kv_enc": noise(keys[6], (D, 2 * HH), D ** -0.5, 0.1875),
        "w_o_enc": noise(keys[7], (HH, D), HH ** -0.5, 0.25),
        "w_q_dec": draw_w_q_dec(jax.random.fold_in(keys[16], 71), part),
        "w_kv_dec": noise(keys[9], (D, 2 * HH), D ** -0.5, 0.1875),
        "w_o_dec": noise(keys[10], (HH, D), HH ** -0.5, 0.25),
        "enc_need": with_ends(jax.random.randint(keys[11], (N_DOM, NODE_DEV * KE), 0, GP_DEV), jax.random.fold_in(keys[11], 1), 0, GP_DEV - 1).astype(jnp.int32),
        "enc_slot": with_ends(jax.random.randint(keys[12], (KE, NODES), 0, NODE_DEV * KE), jax.random.fold_in(keys[12], 1), 0, (NODE_DEV * KE) - 1).astype(jnp.int32),
        "enc_count": with_ends(jax.random.randint(keys[13], (NODES,), 1, KE + 1), jax.random.fold_in(keys[13], 1), 1, KE).astype(jnp.int32),
        "dec_need": with_ends(jax.random.randint(keys[14], (N_DOM, GP_DEV * KD), 0, NODE_DEV), jax.random.fold_in(keys[14], 1), 0, NODE_DEV - 1).astype(jnp.int32),
        "dec_slot": with_ends(jax.random.randint(keys[15], (KD, GRID), 0, GP_DEV * KD), jax.random.fold_in(keys[15], 1), 0, (GP_DEV * KD) - 1).astype(jnp.int32),
    }


norm_eps = 1e-06

def rms_norm(values, weight_gain):
    widened = values.astype(jnp.float32)
    spread = lax.optimization_barrier(jnp.mean(widened * widened, axis=-1, keepdims=True))
    return (widened * lax.rsqrt(spread + norm_eps) * weight_gain).astype(jnp.bfloat16)

def attend_keys(queries, key_rows, keep_mask):
    rows_here = queries.shape[0]
    inner_width = queries.shape[1]
    head_size = inner_width // HEADS
    edge_count = key_rows.shape[0]
    query_heads = queries.reshape(rows_here, HEADS, head_size).astype(jnp.float32)
    key_heads = key_rows[..., :inner_width].reshape(edge_count, rows_here, HEADS, head_size).astype(jnp.float32)
    value_heads = key_rows[..., inner_width:].reshape(edge_count, rows_here, HEADS, head_size).astype(jnp.float32)
    scores = jnp.einsum('rhd,krhd->krh', query_heads, key_heads) * (1.0 / math.sqrt(head_size))
    if keep_mask is not None:
        scores = jnp.where(keep_mask[:, :, None], scores, -1e+30)
    highest = lax.optimization_barrier(jnp.max(scores, axis=0, keepdims=True))
    raised = jnp.exp(scores - highest)
    weights = (raised / lax.optimization_barrier(jnp.sum(raised, axis=0, keepdims=True))).astype(jnp.bfloat16)
    mixed = jnp.einsum('krh,krhd->rhd', weights.astype(jnp.float32), value_heads)
    return mixed.reshape(rows_here, inner_width).astype(jnp.bfloat16)

def reference(grid, latent_in, grid_gain, node_gain, dec_gain, w_q_enc, w_kv_enc, w_o_enc, w_q_dec, w_kv_dec, w_o_dec, enc_need, enc_slot, enc_count, dec_need, dec_slot):
    normed_grid = rms_norm(grid, grid_gain)
    grid_pairs = jnp.dot(normed_grid, w_kv_enc, preferred_element_type=jnp.float32).astype(jnp.bfloat16)
    enc_cap = NODE_DEV * KE // N_DOM
    enc_owner = jnp.arange(NODE_DEV * KE, dtype=jnp.int32) // enc_cap

    def encode_block(block):
        wanted = enc_owner * GP_DEV + enc_need[block]
        buffer = grid_pairs[wanted]
        start = (block * NODE_DEV).astype(jnp.int32)
        slots = lax.dynamic_slice_in_dim(enc_slot, start, NODE_DEV, 1)
        counts = lax.dynamic_slice_in_dim(enc_count, start, NODE_DEV, 0)
        own_rows = lax.dynamic_slice_in_dim(latent_in, start, NODE_DEV, 0)
        queries = jnp.dot(rms_norm(own_rows, node_gain), w_q_enc, preferred_element_type=jnp.float32).astype(jnp.bfloat16)
        keep_mask = jnp.arange(KE, dtype=jnp.int32)[:, None] < counts[None, :]
        mixed = attend_keys(queries, buffer[slots], keep_mask)
        update = jnp.dot(mixed, w_o_enc, preferred_element_type=jnp.float32)
        return (own_rows.astype(jnp.float32) + update).astype(jnp.bfloat16)
    latent_out = lax.map(encode_block, jnp.arange(N_DOM, dtype=jnp.int32)).reshape(NODES, D)
    latent_pairs = jnp.dot(rms_norm(latent_out, dec_gain), w_kv_dec, preferred_element_type=jnp.float32).astype(jnp.bfloat16)
    dec_cap = GP_DEV * KD // N_DOM
    dec_owner = jnp.arange(GP_DEV * KD, dtype=jnp.int32) // dec_cap

    def decode_block(block):
        wanted = dec_owner * NODE_DEV + dec_need[block]
        buffer = latent_pairs[wanted]
        start = (block * GP_DEV).astype(jnp.int32)
        slots = lax.dynamic_slice_in_dim(dec_slot, start, GP_DEV, 1)
        own_rows = lax.dynamic_slice_in_dim(grid, start, GP_DEV, 0)
        own_normed = lax.dynamic_slice_in_dim(normed_grid, start, GP_DEV, 0)
        queries = jnp.dot(own_normed, w_q_dec, preferred_element_type=jnp.float32).astype(jnp.bfloat16)
        mixed = attend_keys(queries, buffer[slots], None)
        update = jnp.dot(mixed, w_o_dec, preferred_element_type=jnp.float32)
        return (own_rows.astype(jnp.float32) + update).astype(jnp.bfloat16)
    grid_out = lax.map(decode_block, jnp.arange(N_DOM, dtype=jnp.int32)).reshape(GRID, D)
    return (latent_out, grid_out)
```

```python
import functools
import math

import jax
import jax.numpy as jnp
from jax import lax
from jax.experimental import pallas as pl
from jax.experimental.pallas import tpu as pltpu
from jax.sharding import PartitionSpec as P

HEADS = 8
LANES = 128
NEG = -1e30
norm_eps = 1e-06
f32 = jnp.float32
bf16 = jnp.bfloat16


def iota(shape, dim):
    return lax.broadcasted_iota(jnp.int32, shape, dim)


def div(values, by):
    if by & (by - 1) == 0:
        return values >> (by.bit_length() - 1)
    return values // by


def mod(values, by):
    if by & (by - 1) == 0:
        return values & (by - 1)
    return values % by


def dot(a, b):
    return jnp.dot(a, b, preferred_element_type=f32)


def dot_t(a, b):
    return lax.dot_general(a, b, (((1,), (1,)), ((), ())), preferred_element_type=f32)


def normed(values, gain):
    widened = values.astype(f32)
    spread = jnp.mean(widened * widened, axis=-1, keepdims=True)
    return (widened * lax.rsqrt(spread + norm_eps) * gain).astype(bf16)


def params(mib, grid_dims=0):
    return pltpu.CompilerParams(
        vmem_limit_bytes=mib * 2**20,
        dimension_semantics=("arbitrary",) * grid_dims if grid_dims else None,
    )


def cost(flops, read, exps=0):
    return pl.CostEstimate(flops=int(flops), bytes_accessed=int(read), transcendentals=int(exps))


def ask_kernel(cap, latent_ref, gain_ref, w_ref, slot_ref, count_ref, need_ref, out_ref):
    peers, rows, _ = out_ref.shape
    width = w_ref.shape[1]
    entries = need_ref.shape[1]
    edges = slot_ref.shape[1]
    queries = dot(normed(latent_ref[...], gain_ref[...]), w_ref[...]).astype(bf16)
    eye = iota((rows, rows), 0) == iota((rows, rows), 1)
    counts = jnp.sum(jnp.where(eye, count_ref[...], 0), axis=1, keepdims=True)
    slots = jnp.where(iota((rows, edges), 1) < counts, slot_ref[...], -1)
    place = iota((rows, entries), 1)
    uses = jnp.zeros((rows, entries), f32)
    for j in range(edges):
        uses += jnp.where(slots[:, j : j + 1] == place, 1.0, 0.0)
    need = need_ref[...]
    low = jnp.broadcast_to((need & 255).astype(f32), (rows, entries))
    high = jnp.broadcast_to((need >> 8).astype(f32), (rows, entries))
    lane = iota((rows, LANES), 1)
    for p in range(peers):
        at = p * cap
        block, start = at // LANES * LANES, at % LANES

        def moved(values, to):
            piece = values[:, block : block + LANES]
            shift = (to - start) % LANES
            return pltpu.roll(piece, shift, 1) if shift else piece

        extra = jnp.where(
            lane < cap,
            moved(uses, 0),
            jnp.where(
                lane < 2 * cap,
                moved(low, cap),
                jnp.where(lane < 3 * cap, moved(high, 2 * cap), 0.0),
            ),
        )
        out_ref[p, :, :width] = queries
        out_ref[p, :, width:] = extra.astype(bf16)


def front_kernel(x_ref, gain_ref, w_ref, normed_ref, pairs_ref):
    rows = normed(x_ref[...], gain_ref[...])
    normed_ref[...] = rows
    pairs_ref[...] = dot(rows, w_ref[...]).astype(bf16)


def head_scores(keys, queries, h, size, scale):
    per = LANES // size
    at = h // per * LANES
    key_part = keys[:, at : at + LANES]
    lane = iota(key_part.shape, 1)
    own = div(lane, size) == h % per
    key_part = jnp.where(own, key_part, jnp.zeros_like(key_part))
    return dot_t(key_part, queries[:, at : at + LANES]) * scale


def partial_kernel(cap, rows, asked_ref, pairs_ref, out_ref, mixed_ref):
    nodes = asked_ref.shape[0]
    points, both = pairs_ref.shape
    width = both // 2
    size = width // HEADS
    entries = nodes // rows * cap
    scale = math.log2(math.e) / math.sqrt(size)
    extra = asked_ref[:, width:]
    pick = iota((entries, nodes), 1) == div(iota((entries, nodes), 0), cap) * rows
    lists = dot(pick.astype(bf16), extra)
    lane = iota((entries, LANES), 1)
    within = mod(iota((entries, LANES), 0), cap)
    weights = jnp.where(lane == within + cap, 1.0, jnp.where(lane == within + 2 * cap, 256.0, 0.0))
    index = jnp.sum(lists * weights, axis=1, keepdims=True).astype(jnp.int32)
    chosen = (index == iota((entries, points), 1)).astype(bf16)
    keys = dot(chosen, pairs_ref[:, :width]).astype(bf16)
    values = dot(chosen, pairs_ref[:, width:]).astype(bf16)
    values_t = values.T
    uses = dot_t((lane == within).astype(bf16), extra)
    here = div(iota((entries, nodes), 0), cap) == div(iota((entries, nodes), 1), rows)
    live = here & (uses > 0.5)
    bias = jnp.where(live, jnp.log2(jnp.where(live, uses, 1.0)), NEG)
    queries = asked_ref[:, :width]
    tops, totals = [], []
    for h in range(HEADS):
        scores = head_scores(keys, queries, h, size, scale) + bias
        top = jnp.max(scores, axis=0, keepdims=True)
        raised = jnp.exp2(scores - top)
        tops.append(top)
        totals.append(jnp.sum(raised, axis=0, keepdims=True))
        mixed_ref[h * size : (h + 1) * size, :] = dot(
            values_t[h * size : (h + 1) * size, :], raised.astype(bf16)
        )
    top = jnp.concatenate(tops, axis=0)
    total = jnp.concatenate(totals, axis=0)
    top_1 = top.astype(bf16).astype(f32)
    top_2 = (top - top_1).astype(bf16).astype(f32)
    top_3 = top - top_1 - top_2
    total_1 = total.astype(bf16).astype(f32)
    for i, part in enumerate((top_1, top_2, top_3, total_1, total - total_1)):
        mixed_ref[width + i * HEADS : width + (i + 1) * HEADS, :] = part
    mixed_ref[width + 5 * HEADS :, :] = jnp.zeros_like(mixed_ref[width + 5 * HEADS :, :])
    out_ref[...] = mixed_ref[...].T.astype(bf16)


def combine_kernel(parts_ref, latent_ref, gain_ref, w_o_ref, w_kv_ref, latent_out_ref, out_ref):
    peers, rows, total_width = parts_ref.shape
    width = w_o_ref.shape[0]
    size = width // HEADS
    parts = parts_ref[...].reshape(peers * rows, total_width)
    stats = parts[:, width:]
    col, head = iota((LANES, LANES), 0), iota((LANES, LANES), 1)
    head_of = mod(col, HEADS) == head
    take_top = head_of & (col < 3 * HEADS)
    take_sum = head_of & (col >= 3 * HEADS) & (col < 5 * HEADS)
    top = dot(stats, take_top.astype(bf16)).reshape(peers, rows, LANES)
    total = dot(stats, take_sum.astype(bf16)).reshape(peers, rows, LANES)
    highest = jnp.max(top, axis=0, keepdims=True)
    factor = jnp.exp2(top - highest)
    whole = jnp.sum(total * factor, axis=0, keepdims=True)
    used = iota((1, rows, LANES), 2) < HEADS
    factor = factor * jnp.where(used, 1.0 / jnp.where(used, whole, 1.0), 0.0)
    factor = factor.reshape(peers * rows, LANES)
    spread = (div(iota((LANES, width), 1), size) == iota((LANES, width), 0)).astype(bf16)
    factor_1 = factor.astype(bf16)
    factor_2 = (factor - factor_1.astype(f32)).astype(bf16)
    wide = dot(factor_1, spread) + dot(factor_2, spread)
    mixed = jnp.sum((parts[:, :width].astype(f32) * wide).reshape(peers, rows, width), axis=0)
    update = dot(mixed.astype(bf16), w_o_ref[...])
    latent_out = (latent_ref[...].astype(f32) + update).astype(bf16)
    latent_out_ref[...] = latent_out
    pairs = dot(normed(latent_out, gain_ref[...]), w_kv_ref[...]).astype(bf16)
    for p in range(peers):
        out_ref[p] = pairs


def middle_kernel(cap, rows, x_ref, w_ref, need_ref, slot_ref, query_ref, bias_ref):
    query_ref[...] = dot(x_ref[...], w_ref[...]).astype(bf16)
    nodes, points = bias_ref.shape
    high_count = need_ref.shape[0]
    need = need_ref[...].astype(f32).astype(bf16)
    uses = jnp.zeros((nodes, points), f32)
    for j in range(slot_ref.shape[0]):
        slots = slot_ref[j : j + 1, :]
        row_of = (div(slots, LANES) == iota((high_count, points), 0)).astype(bf16)
        listed = lax.dot_general(need, row_of, (((0,), (0,)), ((), ())), preferred_element_type=f32)
        own = mod(slots, LANES) == iota((LANES, points), 0)
        found = jnp.sum(jnp.where(own, listed, 0.0), axis=0, keepdims=True).astype(jnp.int32)
        node = div(slots, cap) * rows + found
        uses += jnp.where(node == iota((nodes, points), 0), 1.0, 0.0)
    live = uses > 0.5
    bias_ref[...] = jnp.where(live, jnp.log2(jnp.where(live, uses, 1.0)), NEG)


def decode_kernel(x_ref, query_ref, bias_ref, pairs_ref, w_ref, out_ref, mixed_ref):
    width = w_ref.shape[0]
    size = width // HEADS
    scale = math.log2(math.e) / math.sqrt(size)
    keys = pairs_ref[:, :width]
    values_t = pairs_ref[:, width:].T
    queries = query_ref[...]
    bias = bias_ref[...]
    for h in range(HEADS):
        scores = head_scores(keys, queries, h, size, scale) + bias
        raised = jnp.exp2(scores - jnp.max(scores, axis=0, keepdims=True))
        total = jnp.sum(raised, axis=0, keepdims=True)
        mixed = dot(values_t[h * size : (h + 1) * size, :], raised.astype(bf16))
        mixed_ref[h * size : (h + 1) * size, :] = mixed * (1.0 / total)
    update = dot(mixed_ref[...].T.astype(bf16), w_ref[...])
    out_ref[...] = (x_ref[...].astype(f32) + update).astype(bf16)


def whole(*shape):
    return pl.BlockSpec(shape, lambda *_: (0,) * len(shape))


def on_device(
    grid,
    latent_in,
    grid_gain,
    node_gain,
    dec_gain,
    w_q_enc,
    w_kv_enc,
    w_o_enc,
    w_q_dec,
    w_kv_dec,
    w_o_dec,
    enc_need,
    enc_slot,
    enc_count,
    dec_need,
    dec_slot,
):
    peers = lax.axis_size("dom")
    points, depth = grid.shape
    rows = latent_in.shape[0]
    width = w_q_enc.shape[1]
    nodes = peers * rows
    entries = enc_need.shape[1]
    cap = entries // peers
    sent = width + LANES
    block = math.gcd(points, 256)

    asked = pl.pallas_call(
        functools.partial(ask_kernel, cap),
        out_shape=jax.ShapeDtypeStruct((peers, rows, sent), bf16),
        compiler_params=params(16),
        cost_estimate=cost(2 * rows * depth * width, 2 * depth * width),
        name="ask",
    )(
        latent_in,
        node_gain.reshape(1, -1),
        w_q_enc,
        enc_slot.T,
        enc_count.reshape(1, -1),
        enc_need,
    )
    asked = lax.all_to_all(asked, "dom", split_axis=0, concat_axis=0, tiled=True)

    normed_grid, pairs = pl.pallas_call(
        front_kernel,
        grid=(points // block,),
        in_specs=[
            pl.BlockSpec((block, depth), lambda i: (i, 0)),
            whole(1, depth),
            whole(depth, 2 * width),
        ],
        out_specs=[
            pl.BlockSpec((block, depth), lambda i: (i, 0)),
            pl.BlockSpec((block, 2 * width), lambda i: (i, 0)),
        ],
        out_shape=[
            jax.ShapeDtypeStruct((points, depth), bf16),
            jax.ShapeDtypeStruct((points, 2 * width), bf16),
        ],
        compiler_params=params(20, 1),
        cost_estimate=cost(4 * points * depth * width, 8 * points * depth),
        name="front",
    )(grid, grid_gain.reshape(1, -1), w_kv_enc)

    parts = pl.pallas_call(
        functools.partial(partial_kernel, cap, rows),
        out_shape=jax.ShapeDtypeStruct((nodes, sent), bf16),
        scratch_shapes=[pltpu.VMEM((sent, nodes), f32)],
        compiler_params=params(32),
        cost_estimate=cost(4 * entries * points * width, 4 * points * width),
        name="partial",
    )(asked.reshape(nodes, sent), pairs)
    parts = lax.all_to_all(
        parts.reshape(peers, rows, sent), "dom", split_axis=0, concat_axis=0, tiled=True
    )

    slot_total = dec_need.shape[1]
    queries, bias = pl.pallas_call(
        functools.partial(middle_kernel, slot_total // peers, rows),
        out_shape=[
            jax.ShapeDtypeStruct((points, width), bf16),
            jax.ShapeDtypeStruct((nodes, points), f32),
        ],
        compiler_params=params(32),
        cost_estimate=cost(2 * points * depth * width, 8 * points * depth),
        name="middle",
    )(normed_grid, w_q_dec, dec_need.reshape(slot_total // LANES, LANES), dec_slot)

    latent_out, everyone = pl.pallas_call(
        combine_kernel,
        out_shape=[
            jax.ShapeDtypeStruct((rows, depth), bf16),
            jax.ShapeDtypeStruct((peers, rows, 2 * width), bf16),
        ],
        compiler_params=params(24),
        cost_estimate=cost(6 * rows * depth * width, 6 * depth * width),
        name="combine",
    )(parts, latent_in, dec_gain.reshape(1, -1), w_o_enc, w_kv_dec)
    everyone = lax.all_to_all(everyone, "dom", split_axis=0, concat_axis=0, tiled=True)

    grid_out = pl.pallas_call(
        decode_kernel,
        grid=(points // block,),
        in_specs=[
            pl.BlockSpec((block, depth), lambda i: (i, 0)),
            pl.BlockSpec((block, width), lambda i: (i, 0)),
            pl.BlockSpec((nodes, block), lambda i: (0, i)),
            whole(nodes, 2 * width),
            whole(width, depth),
        ],
        out_specs=pl.BlockSpec((block, depth), lambda i: (i, 0)),
        out_shape=jax.ShapeDtypeStruct((points, depth), bf16),
        scratch_shapes=[pltpu.VMEM((width, block), f32)],
        compiler_params=params(32, 1),
        cost_estimate=cost(8 * points * depth * width, 8 * points * depth),
        name="decode",
    )(grid, queries, bias, everyone.reshape(nodes, 2 * width), w_o_dec)
    return (latent_out, grid_out)


def solution(mesh):
    return jax.shard_map(
        on_device,
        mesh=mesh,
        in_specs=(
            P(("groups", "dom"), None),
            P(("groups", "dom"), None),
            P(),
            P(),
            P(),
            P(),
            P(),
            P(),
            P(),
            P(),
            P(),
            P("dom", None),
            P(None, "dom"),
            P("dom"),
            P("dom", None),
            P(None, "dom"),
        ),
        out_specs=(P(("groups", "dom"), None), P(("groups", "dom"), None)),
        check_vma=False,
    )
```

```python
import functools
import math

import jax
import jax.numpy as jnp
from jax import lax
from jax.experimental import pallas as pl
from jax.experimental.pallas import tpu as pltpu
from jax.sharding import PartitionSpec as P

HEADS = 8
LANES = 128
NEG = -1e30
norm_eps = 1e-06
f32 = jnp.float32
bf16 = jnp.bfloat16


def iota(shape, dim):
    return lax.broadcasted_iota(jnp.int32, shape, dim)


def div(values, by):
    if by & (by - 1) == 0:
        return values >> (by.bit_length() - 1)
    return values // by


def mod(values, by):
    if by & (by - 1) == 0:
        return values & (by - 1)
    return values % by


def dot(a, b):
    return jnp.dot(a, b, preferred_element_type=f32)


def dot_t(a, b):
    return lax.dot_general(a, b, (((1,), (1,)), ((), ())), preferred_element_type=f32)


def normed(values, gain):
    widened = values.astype(f32)
    spread = jnp.mean(widened * widened, axis=-1, keepdims=True)
    return (widened * lax.rsqrt(spread + norm_eps) * gain).astype(bf16)


def params(mib, grid_dims=0):
    return pltpu.CompilerParams(
        vmem_limit_bytes=mib * 2**20,
        dimension_semantics=("arbitrary",) * grid_dims if grid_dims else None,
    )


def cost(flops, read, exps=0):
    return pl.CostEstimate(flops=int(flops), bytes_accessed=int(read), transcendentals=int(exps))


def digits(index):
    return div(index, 4), div(index, 2) & 1, index & 1


def place_of(index, me, far):
    there, here = digits(index), digits(me)
    step = mod(there[0] - here[0] + far, far)
    return ((there[2] ^ here[2]) * 2 + (there[1] ^ here[1])) * far + step


def far_perm(far, step):
    return [(i, (i // 4 + step) % far * 4 + i % 4) for i in range(4 * far)]


def flip_perm(count, bits):
    return [(i, i ^ bits) for i in range(count)]


def gather_half(block, far):
    blocks = [block] + [lax.ppermute(block, "dom", far_perm(far, -s)) for s in range(1, far)]
    column = jnp.concatenate(blocks, axis=0)
    other = lax.ppermute(column, "dom", flip_perm(4 * far, 2))
    half = jnp.concatenate([column, other], axis=0)
    return half, lax.ppermute(half, "dom", flip_perm(4 * far, 1))


def ask_kernel(latent_ref, gain_ref, w_ref, slot_ref, count_ref, need_ref, out_ref):
    rows = latent_ref.shape[0]
    width = w_ref.shape[1]
    entries = need_ref.shape[1]
    edges = slot_ref.shape[1]
    per = entries // rows
    out_ref[:, :width] = dot(normed(latent_ref[...], gain_ref[...]), w_ref[...]).astype(bf16)
    eye = iota((rows, rows), 0) == iota((rows, rows), 1)
    counts = jnp.sum(jnp.where(eye, count_ref[...], 0), axis=1, keepdims=True)
    slots = jnp.where(iota((rows, edges), 1) < counts, slot_ref[...], 65535)
    need = need_ref[...]
    own = div(iota((rows, entries), 1), per) == iota((rows, entries), 0)
    extra = jnp.zeros((rows, LANES), f32)
    for i, part in enumerate((slots & 255, slots >> 8)):
        to = iota((edges, LANES), 1) == iota((edges, LANES), 0) + i * edges
        extra += dot(part.astype(f32).astype(bf16), to.astype(bf16))
    for i, part in enumerate((need & 255, need >> 8)):
        to = iota((entries, LANES), 1) == mod(iota((entries, LANES), 0), per) + 2 * edges + i * per
        spread = jnp.where(own, part.astype(f32), 0.0).astype(bf16)
        extra += dot(spread, to.astype(bf16))
    out_ref[:, width:] = extra.astype(bf16)


def front_kernel(x_ref, gain_ref, w_ref, normed_ref, pairs_ref):
    rows = normed(x_ref[...], gain_ref[...])
    normed_ref[...] = rows
    pairs_ref[...] = dot(rows, w_ref[...]).astype(bf16)


def head_keys(keys, h, size):
    per = LANES // size
    part = keys[:, h // per * LANES : (h // per + 1) * LANES]
    return jnp.where(div(iota(part.shape, 1), size) == h % per, part, jnp.zeros_like(part))


def stat_parts(top, total):
    top_1 = top.astype(bf16).astype(f32)
    top_2 = (top - top_1).astype(bf16).astype(f32)
    total_1 = total.astype(bf16).astype(f32)
    return top_1, top_2, top - top_1 - top_2, total_1, total - total_1


def partial_kernel(cap, rows, edges, near_ref, far_ref, pairs_ref, *refs):
    out_refs, mixed_ref = refs[:-1], refs[-1]
    me = lax.axis_index("dom")
    points, both = pairs_ref.shape
    width = both // 2
    size = width // HEADS
    per = rows * edges // rows
    scale = math.log2(math.e) / math.sqrt(size)
    nodes = near_ref.shape[0]
    entries = nodes // rows * cap
    list_row, list_lane = div(me * cap, per), mod(me * cap, per)
    pick = iota((entries, nodes), 1) == div(iota((entries, nodes), 0), cap) * rows + list_row
    pick = pick.astype(bf16)
    lane = iota((entries, LANES), 1)
    within = mod(iota((entries, LANES), 0), cap)
    low_lane = within + (2 * edges + list_lane)
    weights = jnp.where(lane == low_lane, 1.0, jnp.where(lane == low_lane + per, 256.0, 0.0))
    here = div(iota((entries, nodes), 0), cap) == div(iota((entries, nodes), 1), rows)
    listed = -(-cap // 8) * 8
    repeat = iota((entries, listed), 1) == mod(iota((entries, listed), 0), cap)
    for half, asked_ref in enumerate((near_ref, far_ref)):
        extra = asked_ref[:, width:]
        index = jnp.sum(dot(pick, extra) * weights, axis=1, keepdims=True).astype(jnp.int32)
        chosen = (index == iota((entries, points), 1)).astype(bf16)
        keys = dot(chosen, pairs_ref[:, :width]).astype(bf16)
        values_t = dot(chosen, pairs_ref[:, width:]).T.astype(bf16)
        extra_t = extra.astype(f32).T
        slots = (extra_t[:edges] + 256.0 * extra_t[edges : 2 * edges]).astype(jnp.int32) - me * cap
        uses = jnp.zeros((listed, nodes), f32)
        for j in range(edges):
            uses += jnp.where(slots[j : j + 1] == iota((listed, nodes), 0), 1.0, 0.0)
        uses = dot(repeat.astype(bf16), uses.astype(bf16))
        live = here & (uses > 0.5)
        bias = jnp.where(live, jnp.log2(jnp.where(live, uses, 1.0)), NEG)
        tops, totals = [], []
        for h in range(HEADS):
            at = h * size // LANES * LANES
            queries = asked_ref[:, at : at + LANES]
            scores = dot_t(head_keys(keys, h, size), queries) * scale + bias
            top = jnp.max(scores, axis=0, keepdims=True)
            raised = jnp.exp2(scores - top)
            tops.append(top)
            totals.append(jnp.sum(raised, axis=0, keepdims=True))
            mixed_ref[h * size : (h + 1) * size, :] = dot(
                values_t[h * size : (h + 1) * size, :], raised.astype(bf16)
            )
        stats = stat_parts(jnp.concatenate(tops, axis=0), jnp.concatenate(totals, axis=0))
        for i, part in enumerate(stats):
            mixed_ref[width + i * HEADS : width + (i + 1) * HEADS, :] = part
        rest = mixed_ref.shape[0] - width - len(stats) * HEADS
        mixed_ref[width + len(stats) * HEADS :, :] = jnp.zeros((rest, nodes), f32)
        result = mixed_ref[...].T.astype(bf16)
        out_refs[2 * half][...] = result[: nodes // 2]
        out_refs[2 * half + 1][...] = result[nodes // 2 :]


def read_stats(stats):
    col, head = iota((LANES, LANES), 0), iota((LANES, LANES), 1)
    head_of = mod(col, HEADS) == head
    take_top = head_of & (col < 3 * HEADS)
    take_sum = head_of & (col >= 3 * HEADS) & (col < 5 * HEADS)
    return dot(stats, take_top.astype(bf16)), dot(stats, take_sum.astype(bf16))


def spread_heads(factor, width):
    size = width // HEADS
    spread = (div(iota((LANES, width), 1), size) == iota((LANES, width), 0)).astype(bf16)
    factor_1 = factor.astype(bf16)
    factor_2 = (factor - factor_1.astype(f32)).astype(bf16)
    return dot(factor_1, spread) + dot(factor_2, spread)


def merged(part_refs, width):
    tops, totals = zip(*[read_stats(ref[:, width:]) for ref in part_refs])
    highest = functools.reduce(jnp.maximum, tops)
    factors = [jnp.exp2(top - highest) for top in tops]
    total = sum(total * factor for total, factor in zip(totals, factors))
    return highest, total, factors


def merge_kernel(own_ref, *refs):
    part_refs, out_refs = (own_ref,) + refs[:3], refs[3:]
    width = own_ref.shape[1] - LANES
    highest, total, factors = merged(part_refs, width)
    mixed = sum(
        ref[:, :width].astype(f32) * spread_heads(factor, width)
        for ref, factor in zip(part_refs, factors)
    )
    used = iota(total.shape, 1) < HEADS
    stats = jnp.zeros_like(total)
    for i, part in enumerate(stat_parts(highest, total)):
        part = jnp.where(used, part, 0.0)
        stats += pltpu.roll(part, i * HEADS, 1) if i else part
    mixed, stats = mixed.astype(bf16), stats.astype(bf16)
    rows = out_refs[0].shape[0]
    for i, out_ref in enumerate(out_refs):
        out_ref[:, :width] = mixed[i * rows : (i + 1) * rows]
        out_ref[:, width:] = stats[i * rows : (i + 1) * rows]


def combine_kernel(part_count, *refs):
    part_refs, refs = refs[:part_count], refs[part_count:]
    latent_ref, gain_ref, w_o_ref, w_kv_ref, latent_out_ref, out_ref = refs
    width = w_o_ref.shape[0]
    _, total, factors = merged(part_refs, width)
    used = iota(total.shape, 1) < HEADS
    inverse = jnp.where(used, 1.0 / jnp.where(used, total, 1.0), 0.0)
    mixed = sum(
        ref[:, :width].astype(f32) * spread_heads(factor * inverse, width)
        for ref, factor in zip(part_refs, factors)
    )
    update = dot(mixed.astype(bf16), w_o_ref[...])
    latent_out = (latent_ref[...].astype(f32) + update).astype(bf16)
    latent_out_ref[...] = latent_out
    out_ref[...] = dot(normed(latent_out, gain_ref[...]), w_kv_ref[...]).astype(bf16)


def middle_kernel(cap, rows, far, x_ref, w_ref, need_ref, slot_ref, query_ref, pick_ref):
    query_ref[...] = dot(x_ref[...], w_ref[...]).T.astype(bf16)
    me = lax.axis_index("dom")
    edges, nodes, points = pick_ref.shape
    high_count = need_ref.shape[0]
    need = need_ref[...].astype(f32).astype(bf16)
    for j in range(edges):
        slots = slot_ref[j : j + 1, :]
        row_of = (div(slots, LANES) == iota((high_count, points), 0)).astype(bf16)
        listed = lax.dot_general(need, row_of, (((0,), (0,)), ((), ())), preferred_element_type=f32)
        own = mod(slots, LANES) == iota((LANES, points), 0)
        found = jnp.sum(jnp.where(own, listed, 0.0), axis=0, keepdims=True).astype(jnp.int32)
        node = place_of(div(slots, cap), me, far) * rows + found
        pick_ref[j] = (node == iota((nodes, points), 0)).astype(bf16)


def decode_kernel(x_ref, query_ref, pick_ref, near_ref, far_ref, w_ref, out_ref, pairs_ref):
    width, points = query_ref.shape
    edges = pick_ref.shape[0]
    size = width // HEADS
    half = width // 2

    @pl.when(pl.program_id(0) == 0)
    def _():
        nodes = near_ref.shape[0]
        pairs_ref[:, :nodes] = near_ref[...].T
        pairs_ref[:, nodes:] = far_ref[...].T

    scores = []
    for j in range(edges):
        parts = []
        for start in (0, half):
            keys = dot(pairs_ref[start : start + half, :], pick_ref[j])
            products = keys * query_ref[start : start + half, :].astype(f32)
            parts.append(jnp.sum(products.reshape(HEADS // 2, size, points), axis=1))
        scores.append(jnp.concatenate(parts, axis=0) * (1.0 / math.sqrt(size)))
    highest = functools.reduce(jnp.maximum, scores)
    raised = [jnp.exp(score - highest) for score in scores]
    inverse = 1.0 / sum(raised)
    weights = [(one * inverse).astype(bf16).astype(f32) for one in raised]
    mixed = []
    for start in (0, half):
        total = jnp.zeros((HEADS // 2, size, points), f32)
        for j in range(edges):
            values = dot(pairs_ref[width + start : width + start + half, :], pick_ref[j])
            first = start // size
            weight = weights[j][first : first + HEADS // 2].reshape(HEADS // 2, 1, points)
            total += values.reshape(HEADS // 2, size, points) * weight
        mixed.append(total.reshape(half, points).T.astype(bf16))
    update = dot(jnp.concatenate(mixed, axis=1), w_ref[...])
    out_ref[...] = (x_ref[...].astype(f32) + update).astype(bf16)


def whole(*shape):
    return pl.BlockSpec(shape, lambda *_: (0,) * len(shape))


def on_device(
    grid,
    latent_in,
    grid_gain,
    node_gain,
    dec_gain,
    w_q_enc,
    w_kv_enc,
    w_o_enc,
    w_q_dec,
    w_kv_dec,
    w_o_dec,
    enc_need,
    enc_slot,
    enc_count,
    dec_need,
    dec_slot,
):
    peers = lax.axis_size("dom")
    far = peers // 4
    points, depth = grid.shape
    rows = latent_in.shape[0]
    width = w_q_enc.shape[1]
    nodes = peers * rows
    entries = enc_need.shape[1]
    edges = enc_slot.shape[0]
    cap = entries // peers
    sent = width + LANES
    block = math.gcd(points, 256)

    asked = pl.pallas_call(
        ask_kernel,
        out_shape=jax.ShapeDtypeStruct((rows, sent), bf16),
        compiler_params=params(58),
        cost_estimate=cost(2 * rows * depth * width, 2 * depth * width),
        name="ask",
    )(
        latent_in,
        node_gain.reshape(1, -1),
        w_q_enc,
        enc_slot.T,
        enc_count.reshape(1, -1),
        enc_need,
    )
    asked = gather_half(asked, far)

    normed_grid, pairs = pl.pallas_call(
        front_kernel,
        grid=(points // block,),
        in_specs=[
            pl.BlockSpec((block, depth), lambda i: (i, 0)),
            whole(1, depth),
            whole(depth, 2 * width),
        ],
        out_specs=[
            pl.BlockSpec((block, depth), lambda i: (i, 0)),
            pl.BlockSpec((block, 2 * width), lambda i: (i, 0)),
        ],
        out_shape=[
            jax.ShapeDtypeStruct((points, depth), bf16),
            jax.ShapeDtypeStruct((points, 2 * width), bf16),
        ],
        compiler_params=params(58, 1),
        cost_estimate=cost(4 * points * depth * width, 8 * points * depth),
        name="front",
    )(grid, grid_gain.reshape(1, -1), w_kv_enc)

    parts = pl.pallas_call(
        functools.partial(partial_kernel, cap, rows, edges),
        out_shape=[jax.ShapeDtypeStruct((far * rows, sent), bf16)] * 4,
        scratch_shapes=[pltpu.VMEM((sent, nodes // 2), f32)],
        compiler_params=params(58),
        cost_estimate=cost(4 * entries * points * width, 4 * points * width),
        name="partial",
    )(*asked, pairs)
    parts = [parts[0]] + [
        lax.ppermute(parts[i], "dom", flip_perm(peers, (i & 1) * 2 + (i >> 1))) for i in (1, 2, 3)
    ]
    parts = pl.pallas_call(
        merge_kernel,
        out_shape=[jax.ShapeDtypeStruct((rows, sent), bf16)] * far,
        compiler_params=params(58),
        cost_estimate=cost(2 * nodes * LANES * width, 4 * nodes * width),
        name="merge",
    )(*parts)
    parts = [parts[0]] + [
        lax.ppermute(parts[s], "dom", far_perm(far, s)) for s in range(1, far)
    ]

    slot_total = dec_need.shape[1]
    queries, picks = pl.pallas_call(
        functools.partial(middle_kernel, slot_total // peers, rows, far),
        out_shape=[
            jax.ShapeDtypeStruct((width, points), bf16),
            jax.ShapeDtypeStruct((dec_slot.shape[0], nodes, points), bf16),
        ],
        compiler_params=params(58),
        cost_estimate=cost(2 * points * depth * width, 8 * points * depth),
        name="middle",
    )(normed_grid, w_q_dec, dec_need.reshape(slot_total // LANES, LANES), dec_slot)

    latent_out, own_pairs = pl.pallas_call(
        functools.partial(combine_kernel, far),
        out_shape=[
            jax.ShapeDtypeStruct((rows, depth), bf16),
            jax.ShapeDtypeStruct((rows, 2 * width), bf16),
        ],
        compiler_params=params(58),
        cost_estimate=cost(6 * rows * depth * width, 6 * depth * width),
        name="combine",
    )(*parts, latent_in, dec_gain.reshape(1, -1), w_o_enc, w_kv_dec)
    near, other = gather_half(own_pairs, far)

    grid_out = pl.pallas_call(
        decode_kernel,
        grid=(points // block,),
        in_specs=[
            pl.BlockSpec((block, depth), lambda i: (i, 0)),
            pl.BlockSpec((width, block), lambda i: (0, i)),
            pl.BlockSpec((dec_slot.shape[0], nodes, block), lambda i: (0, 0, i)),
            whole(nodes // 2, 2 * width),
            whole(nodes // 2, 2 * width),
            whole(width, depth),
        ],
        out_specs=pl.BlockSpec((block, depth), lambda i: (i, 0)),
        out_shape=jax.ShapeDtypeStruct((points, depth), bf16),
        scratch_shapes=[pltpu.VMEM((2 * width, nodes), bf16)],
        compiler_params=params(58, 1),
        cost_estimate=cost(8 * points * depth * width, 8 * points * depth),
        name="decode",
    )(grid, queries, picks, near, other, w_o_dec)
    return (latent_out, grid_out)


def solution(mesh):
    return jax.shard_map(
        on_device,
        mesh=mesh,
        in_specs=(
            P(("groups", "dom"), None),
            P(("groups", "dom"), None),
            P(),
            P(),
            P(),
            P(),
            P(),
            P(),
            P(),
            P(),
            P(),
            P("dom", None),
            P(None, "dom"),
            P("dom"),
            P("dom", None),
            P(None, "dom"),
        ),
        out_specs=(P(("groups", "dom"), None), P(("groups", "dom"), None)),
        check_vma=False,
    )
```

```python
import functools
import math

import jax
import jax.numpy as jnp
from jax import lax
from jax.experimental import pallas as pl
from jax.experimental.pallas import tpu as pltpu
from jax.sharding import PartitionSpec as P

HEADS = 8
LANES = 128
NEG = -1e30
norm_eps = 1e-06
f32 = jnp.float32
bf16 = jnp.bfloat16


def iota(shape, dim):
    return lax.broadcasted_iota(jnp.int32, shape, dim)


def div(values, by):
    if by & (by - 1) == 0:
        return values >> (by.bit_length() - 1)
    return values // by


def mod(values, by):
    if by & (by - 1) == 0:
        return values & (by - 1)
    return values % by


def dot(a, b):
    return jnp.dot(a, b, preferred_element_type=f32)


def dot_t(a, b):
    return lax.dot_general(a, b, (((1,), (1,)), ((), ())), preferred_element_type=f32)


def normed(values, gain):
    widened = values.astype(f32)
    spread = jnp.mean(widened * widened, axis=-1, keepdims=True)
    return (widened * lax.rsqrt(spread + norm_eps) * gain).astype(bf16)


def params(mib, grid_dims=0):
    return pltpu.CompilerParams(
        vmem_limit_bytes=mib * 2**20,
        dimension_semantics=("arbitrary",) * grid_dims if grid_dims else None,
    )


def cost(flops, read, exps=0):
    return pl.CostEstimate(flops=int(flops), bytes_accessed=int(read), transcendentals=int(exps))


def column_groups(far):
    return [[z * 4 + p for z in range(far)] for p in range(4)]


def plane_groups(far):
    return [[z * 4 + p for p in range(4)] for z in range(far)]


def ask_kernel(latent_ref, gain_ref, w_ref, slot_ref, count_ref, need_ref, out_ref):
    rows = latent_ref.shape[0]
    width = w_ref.shape[1]
    entries = need_ref.shape[1]
    edges = slot_ref.shape[1]
    per = entries // rows
    queries = dot(normed(latent_ref[...], gain_ref[...]), w_ref[...]).astype(bf16)
    eye = iota((rows, rows), 0) == iota((rows, rows), 1)
    counts = jnp.sum(jnp.where(eye, count_ref[...], 0), axis=1, keepdims=True)
    slots = jnp.where(iota((rows, edges), 1) < counts, slot_ref[...], 65535)
    need = need_ref[...]
    own = div(iota((rows, entries), 1), per) == iota((rows, entries), 0)
    extra = jnp.zeros((rows, LANES), f32)
    for i, part in enumerate((slots & 255, slots >> 8)):
        to = iota((edges, LANES), 1) == iota((edges, LANES), 0) + i * edges
        extra += dot(part.astype(f32).astype(bf16), to.astype(bf16))
    for i, part in enumerate((need & 255, need >> 8)):
        to = iota((entries, LANES), 1) == mod(iota((entries, LANES), 0), per) + 2 * edges + i * per
        spread = jnp.where(own, part.astype(f32), 0.0).astype(bf16)
        extra += dot(spread, to.astype(bf16))
    for i in range(out_ref.shape[0]):
        out_ref[i, :, :width] = queries
        out_ref[i, :, width:] = extra.astype(bf16)


def front_kernel(x_ref, gain_ref, w_kv_ref, w_q_ref, pairs_ref, query_ref):
    rows = normed(x_ref[...], gain_ref[...])
    pairs_ref[...] = dot(rows, w_kv_ref[...]).astype(bf16)
    query_ref[...] = dot(rows, w_q_ref[...]).T.astype(bf16)


def head_keys(keys, h, size):
    per = LANES // size
    part = keys[:, h // per * LANES : (h // per + 1) * LANES]
    return jnp.where(div(iota(part.shape, 1), size) == h % per, part, jnp.zeros_like(part))


def stat_parts(top, total):
    top_1 = top.astype(bf16).astype(f32)
    top_2 = (top - top_1).astype(bf16).astype(f32)
    total_1 = total.astype(bf16).astype(f32)
    return top_1, top_2, top - top_1 - top_2, total_1, total - total_1


def partial_kernel(cap, rows, edges, asked_ref, pairs_ref, out_ref, mixed_ref):
    me = lax.axis_index("dom")
    points, both = pairs_ref.shape
    peers = out_ref.shape[0]
    far = peers // 4
    width = both // 2
    size = width // HEADS
    per = cap * peers // rows
    scale = math.log2(math.e) / math.sqrt(size)
    all_nodes = asked_ref.shape[0]
    all_entries = peers * cap
    list_row, list_lane = div(me * cap, per), mod(me * cap, per)
    pick_shape = (all_entries, all_nodes)
    pick = iota(pick_shape, 1) == div(iota(pick_shape, 0), cap) * rows + list_row
    lane = iota((all_entries, LANES), 1)
    within = mod(iota((all_entries, LANES), 0), cap)
    low_lane = within + (2 * edges + list_lane)
    weights = jnp.where(lane == low_lane, 1.0, jnp.where(lane == low_lane + per, 256.0, 0.0))
    lists = dot(pick.astype(bf16), asked_ref[:, width:])
    index = jnp.sum(lists * weights, axis=1, keepdims=True).astype(jnp.int32)
    chosen = (index == iota((all_entries, points), 1)).astype(bf16)
    all_keys = dot(chosen, pairs_ref[:, :width]).astype(bf16)
    all_values = dot(chosen, pairs_ref[:, width:]).astype(bf16)

    nodes, entries = all_nodes // 2, all_entries // 2
    here = div(iota((entries, nodes), 0), cap) == div(iota((entries, nodes), 1), rows)
    listed = -(-cap // 8) * 8
    repeat = iota((entries, listed), 1) == mod(iota((entries, listed), 0), cap)
    for half in range(2):
        own = slice(half * nodes, (half + 1) * nodes)
        keys = all_keys[half * entries : (half + 1) * entries]
        values_t = all_values[half * entries : (half + 1) * entries].T
        extra_t = asked_ref[own, width:].astype(f32).T
        slots = (extra_t[:edges] + 256.0 * extra_t[edges : 2 * edges]).astype(jnp.int32) - me * cap
        uses = jnp.zeros((listed, nodes), f32)
        for j in range(edges):
            uses += jnp.where(slots[j : j + 1] == iota((listed, nodes), 0), 1.0, 0.0)
        uses = dot(repeat.astype(bf16), uses.astype(bf16))
        live = here & (uses > 0.5)
        bias = jnp.where(live, jnp.log2(jnp.where(live, uses, 1.0)), NEG)
        tops, totals = [], []
        for h in range(HEADS):
            at = h * size // LANES * LANES
            queries = asked_ref[own, at : at + LANES]
            scores = dot_t(head_keys(keys, h, size), queries) * scale + bias
            top = jnp.max(scores, axis=0, keepdims=True)
            raised = jnp.exp2(scores - top)
            tops.append(top)
            totals.append(jnp.sum(raised, axis=0, keepdims=True))
            mixed_ref[h * size : (h + 1) * size, :] = dot(
                values_t[h * size : (h + 1) * size, :], raised.astype(bf16)
            )
        stats = stat_parts(jnp.concatenate(tops, axis=0), jnp.concatenate(totals, axis=0))
        for i, part in enumerate(stats):
            mixed_ref[width + i * HEADS : width + (i + 1) * HEADS, :] = part
        rest = mixed_ref.shape[0] - width - len(stats) * HEADS
        mixed_ref[width + len(stats) * HEADS :, :] = jnp.zeros((rest, nodes), f32)
        result = mixed_ref[...].T.astype(bf16)
        for i in range(peers // 2):
            place = half * (peers // 2) + i
            out_ref[place % far * 4 + place // far] = result[i * rows : (i + 1) * rows]


def read_stats(stats):
    col, head = iota((LANES, LANES), 0), iota((LANES, LANES), 1)
    head_of = mod(col, HEADS) == head
    take_top = head_of & (col < 3 * HEADS)
    take_sum = head_of & (col >= 3 * HEADS) & (col < 5 * HEADS)
    return dot(stats, take_top.astype(bf16)), dot(stats, take_sum.astype(bf16))


def spread_heads(factor, width):
    size = width // HEADS
    spread = (div(iota((LANES, width), 1), size) == iota((LANES, width), 0)).astype(bf16)
    factor_1 = factor.astype(bf16)
    factor_2 = (factor - factor_1.astype(f32)).astype(bf16)
    return dot(factor_1, spread) + dot(factor_2, spread)


def combine_kernel(parts_ref, latent_ref, gain_ref, w_o_ref, w_kv_ref, latent_out_ref, out_ref):
    peers, rows, sent = parts_ref.shape
    width = w_o_ref.shape[0]
    parts = parts_ref[...].reshape(peers * rows, sent)
    top, total = read_stats(parts[:, width:])
    top = top.reshape(peers, rows, LANES)
    factor = jnp.exp2(top - jnp.max(top, axis=0, keepdims=True))
    total = jnp.sum(total.reshape(peers, rows, LANES) * factor, axis=0, keepdims=True)
    used = iota((1, rows, LANES), 2) < HEADS
    factor = factor * jnp.where(used, 1.0 / jnp.where(used, total, 1.0), 0.0)
    wide = spread_heads(factor.reshape(peers * rows, LANES), width)
    mixed = jnp.sum((parts[:, :width].astype(f32) * wide).reshape(peers, rows, width), axis=0)
    update = dot(mixed.astype(bf16), w_o_ref[...])
    latent_out = (latent_ref[...].astype(f32) + update).astype(bf16)
    latent_out_ref[...] = latent_out
    out_ref[...] = dot(normed(latent_out, gain_ref[...]), w_kv_ref[...]).astype(bf16)


def picks_kernel(cap, rows, far, need_ref, slot_ref, pick_ref):
    edges, nodes, points = pick_ref.shape
    high_count = need_ref.shape[0]
    need = need_ref[...].astype(f32).astype(bf16)
    for j in range(edges):
        slots = slot_ref[j : j + 1, :]
        row_of = (div(slots, LANES) == iota((high_count, points), 0)).astype(bf16)
        listed = lax.dot_general(need, row_of, (((0,), (0,)), ((), ())), preferred_element_type=f32)
        own = mod(slots, LANES) == iota((LANES, points), 0)
        found = jnp.sum(jnp.where(own, listed, 0.0), axis=0, keepdims=True).astype(jnp.int32)
        owner = div(slots, cap)
        node = (mod(owner, 4) * far + div(owner, 4)) * rows + found
        pick_ref[j] = (node == iota((nodes, points), 0)).astype(bf16)


def decode_kernel(x_ref, query_ref, pick_ref, nodes_ref, w_ref, out_ref, pairs_ref):
    width, points = query_ref.shape
    edges = pick_ref.shape[0]
    size = width // HEADS
    half = width // 2

    @pl.when(pl.program_id(0) == 0)
    def _():
        pairs_ref[...] = nodes_ref[...].T

    scores = []
    for j in range(edges):
        parts = []
        for start in (0, half):
            keys = dot(pairs_ref[start : start + half, :], pick_ref[j])
            products = keys * query_ref[start : start + half, :].astype(f32)
            parts.append(jnp.sum(products.reshape(HEADS // 2, size, points), axis=1))
        scores.append(jnp.concatenate(parts, axis=0) * (1.0 / math.sqrt(size)))
    highest = functools.reduce(jnp.maximum, scores)
    raised = [jnp.exp(score - highest) for score in scores]
    inverse = 1.0 / sum(raised)
    weights = [(one * inverse).astype(bf16).astype(f32) for one in raised]
    mixed = []
    for start in (0, half):
        total = jnp.zeros((HEADS // 2, size, points), f32)
        for j in range(edges):
            values = dot(pairs_ref[width + start : width + start + half, :], pick_ref[j])
            first = start // size
            weight = weights[j][first : first + HEADS // 2].reshape(HEADS // 2, 1, points)
            total += values.reshape(HEADS // 2, size, points) * weight
        mixed.append(total.reshape(half, points).T.astype(bf16))
    update = dot(jnp.concatenate(mixed, axis=1), w_ref[...])
    out_ref[...] = (x_ref[...].astype(f32) + update).astype(bf16)


def whole(*shape):
    return pl.BlockSpec(shape, lambda *_: (0,) * len(shape))


def on_device(
    grid,
    latent_in,
    grid_gain,
    node_gain,
    dec_gain,
    w_q_enc,
    w_kv_enc,
    w_o_enc,
    w_q_dec,
    w_kv_dec,
    w_o_dec,
    enc_need,
    enc_slot,
    enc_count,
    dec_need,
    dec_slot,
):
    peers = lax.axis_size("dom")
    far = peers // 4
    points, depth = grid.shape
    rows = latent_in.shape[0]
    width = w_q_enc.shape[1]
    nodes = peers * rows
    entries = enc_need.shape[1]
    edges = enc_slot.shape[0]
    cap = entries // peers
    sent = width + LANES
    block = math.gcd(points, 256)

    asked = pl.pallas_call(
        ask_kernel,
        out_shape=jax.ShapeDtypeStruct((far, rows, sent), bf16),
        compiler_params=params(58),
        cost_estimate=cost(2 * rows * depth * width, 2 * depth * width),
        name="ask",
    )(
        latent_in,
        node_gain.reshape(1, -1),
        w_q_enc,
        enc_slot.T,
        enc_count.reshape(1, -1),
        enc_need,
    )
    asked = lax.all_to_all(asked, "dom", 0, 0, tiled=True, axis_index_groups=column_groups(far))
    asked = jnp.broadcast_to(asked.reshape(1, far * rows, sent), (4, far * rows, sent))
    asked = lax.all_to_all(asked, "dom", 0, 0, tiled=True, axis_index_groups=plane_groups(far))

    pairs, queries = pl.pallas_call(
        front_kernel,
        grid=(points // block,),
        in_specs=[
            pl.BlockSpec((block, depth), lambda i: (i, 0)),
            whole(1, depth),
            whole(depth, 2 * width),
            whole(depth, width),
        ],
        out_specs=[
            pl.BlockSpec((block, 2 * width), lambda i: (i, 0)),
            pl.BlockSpec((width, block), lambda i: (0, i)),
        ],
        out_shape=[
            jax.ShapeDtypeStruct((points, 2 * width), bf16),
            jax.ShapeDtypeStruct((width, points), bf16),
        ],
        compiler_params=params(58, 1),
        cost_estimate=cost(6 * points * depth * width, 8 * points * depth),
        name="front",
    )(grid, grid_gain.reshape(1, -1), w_kv_enc, w_q_dec)

    parts = pl.pallas_call(
        functools.partial(partial_kernel, cap, rows, edges),
        out_shape=jax.ShapeDtypeStruct((peers, rows, sent), bf16),
        scratch_shapes=[pltpu.VMEM((sent, nodes // 2), f32)],
        compiler_params=params(58),
        cost_estimate=cost(4 * entries * points * width, 4 * points * width),
        name="partial",
    )(asked.reshape(nodes, sent), pairs)
    parts = lax.all_to_all(parts, "dom", split_axis=0, concat_axis=0, tiled=True)

    slot_total = dec_need.shape[1]
    picks = pl.pallas_call(
        functools.partial(picks_kernel, slot_total // peers, rows, far),
        out_shape=jax.ShapeDtypeStruct((dec_slot.shape[0], nodes, points), bf16),
        compiler_params=params(58),
        cost_estimate=cost(points * nodes * LANES, 8 * points * nodes),
        name="picks",
    )(dec_need.reshape(slot_total // LANES, LANES), dec_slot)

    latent_out, everyone = pl.pallas_call(
        combine_kernel,
        out_shape=[
            jax.ShapeDtypeStruct((rows, depth), bf16),
            jax.ShapeDtypeStruct((rows, 2 * width), bf16),
        ],
        compiler_params=params(24),
        cost_estimate=cost(6 * rows * depth * width, 6 * depth * width),
        name="combine",
    )(parts, latent_in, dec_gain.reshape(1, -1), w_o_enc, w_kv_dec)
    for groups in (column_groups(far), plane_groups(far)):
        everyone = lax.all_gather(everyone, "dom", tiled=True, axis_index_groups=groups)

    grid_out = pl.pallas_call(
        decode_kernel,
        grid=(points // block,),
        in_specs=[
            pl.BlockSpec((block, depth), lambda i: (i, 0)),
            pl.BlockSpec((width, block), lambda i: (0, i)),
            pl.BlockSpec((dec_slot.shape[0], nodes, block), lambda i: (0, 0, i)),
            whole(nodes, 2 * width),
            whole(width, depth),
        ],
        out_specs=pl.BlockSpec((block, depth), lambda i: (i, 0)),
        out_shape=jax.ShapeDtypeStruct((points, depth), bf16),
        scratch_shapes=[pltpu.VMEM((2 * width, nodes), bf16)],
        compiler_params=params(58, 1),
        cost_estimate=cost(8 * points * depth * width, 8 * points * depth),
        name="decode",
    )(grid, queries, picks, everyone, w_o_dec)
    return (latent_out, grid_out)


def solution(mesh):
    return jax.shard_map(
        on_device,
        mesh=mesh,
        in_specs=(
            P(("groups", "dom"), None),
            P(("groups", "dom"), None),
            P(),
            P(),
            P(),
            P(),
            P(),
            P(),
            P(),
            P(),
            P(),
            P("dom", None),
            P(None, "dom"),
            P("dom"),
            P("dom", None),
            P(None, "dom"),
        ),
        out_specs=(P(("groups", "dom"), None), P(("groups", "dom"), None)),
        check_vma=False,
    )
```

```python
import functools
import math

import jax
import jax.numpy as jnp
from jax import lax
from jax.experimental import pallas as pl
from jax.experimental.pallas import tpu as pltpu
from jax.sharding import PartitionSpec as P

HEADS = 8
LANES = 128
NEG = -1e30
norm_eps = 1e-06
f32 = jnp.float32
bf16 = jnp.bfloat16


def iota(shape, dim):
    return lax.broadcasted_iota(jnp.int32, shape, dim)


def div(values, by):
    if by & (by - 1) == 0:
        return values >> (by.bit_length() - 1)
    return values // by


def mod(values, by):
    if by & (by - 1) == 0:
        return values & (by - 1)
    return values % by


def dot(a, b):
    return jnp.dot(a, b, preferred_element_type=f32)


def dot_t(a, b):
    return lax.dot_general(a, b, (((1,), (1,)), ((), ())), preferred_element_type=f32)


def normed(values, gain):
    widened = values.astype(f32)
    spread = jnp.mean(widened * widened, axis=-1, keepdims=True)
    return (widened * lax.rsqrt(spread + norm_eps) * gain).astype(bf16)


def params(mib, grid_dims=0):
    return pltpu.CompilerParams(
        vmem_limit_bytes=mib * 2**20,
        dimension_semantics=("arbitrary",) * grid_dims if grid_dims else None,
    )


def cost(flops, read, exps=0):
    return pl.CostEstimate(flops=int(flops), bytes_accessed=int(read), transcendentals=int(exps))


def ask_kernel(latent_ref, gain_ref, w_ref, slot_ref, count_ref, need_ref, out_ref):
    rows = latent_ref.shape[0]
    width = w_ref.shape[1]
    entries = need_ref.shape[1]
    edges = slot_ref.shape[1]
    per = entries // rows
    queries = dot(normed(latent_ref[...], gain_ref[...]), w_ref[...]).astype(bf16)
    eye = iota((rows, rows), 0) == iota((rows, rows), 1)
    counts = jnp.sum(jnp.where(eye, count_ref[...], 0), axis=1, keepdims=True)
    slots = jnp.where(iota((rows, edges), 1) < counts, slot_ref[...], 65535)
    need = need_ref[...]
    own = div(iota((rows, entries), 1), per) == iota((rows, entries), 0)
    extra = jnp.zeros((rows, LANES), f32)
    for i, part in enumerate((slots & 255, slots >> 8)):
        to = iota((edges, LANES), 1) == iota((edges, LANES), 0) + i * edges
        extra += dot(part.astype(f32).astype(bf16), to.astype(bf16))
    for i, part in enumerate((need & 255, need >> 8)):
        to = iota((entries, LANES), 1) == mod(iota((entries, LANES), 0), per) + 2 * edges + i * per
        spread = jnp.where(own, part.astype(f32), 0.0).astype(bf16)
        extra += dot(spread, to.astype(bf16))
    for i in range(out_ref.shape[0]):
        out_ref[i, :, :width] = queries
        out_ref[i, :, width:] = extra.astype(bf16)


def front_kernel(x_ref, gain_ref, w_kv_ref, w_q_ref, pairs_ref, query_ref):
    rows = normed(x_ref[...], gain_ref[...])
    pairs_ref[...] = dot(rows, w_kv_ref[...]).astype(bf16)
    query_ref[...] = dot(rows, w_q_ref[...]).T.astype(bf16)


def stat_parts(top, total):
    top_1 = top.astype(bf16).astype(f32)
    top_2 = (top - top_1).astype(bf16).astype(f32)
    total_1 = total.astype(bf16).astype(f32)
    return top_1, top_2, top - top_1 - top_2, total_1, total - total_1


def partial_kernel(cap, rows, edges, asked_ref, pairs_ref, out_ref, mixed_ref):
    me = lax.axis_index("dom")
    points, both = pairs_ref.shape
    peers = out_ref.shape[0]
    width = both // 2
    size = width // HEADS
    per = cap * peers // rows
    scale = math.log2(math.e) / math.sqrt(size)
    all_nodes = asked_ref.shape[0]
    all_entries = peers * cap
    list_row, list_lane = div(me * cap, per), mod(me * cap, per)
    pick_shape = (all_entries, all_nodes)
    pick = iota(pick_shape, 1) == div(iota(pick_shape, 0), cap) * rows + list_row
    lane = iota((all_entries, LANES), 1)
    within = mod(iota((all_entries, LANES), 0), cap)
    low_lane = within + (2 * edges + list_lane)
    weights = jnp.where(lane == low_lane, 1.0, jnp.where(lane == low_lane + per, 256.0, 0.0))
    lists = dot(pick.astype(bf16), asked_ref[:, width:])
    index = jnp.sum(lists * weights, axis=1, keepdims=True).astype(jnp.int32)
    chosen = (index == iota((all_entries, points), 1)).astype(bf16)
    all_keys = dot(chosen, pairs_ref[:, :width]).astype(bf16)
    all_values = dot(chosen, pairs_ref[:, width:]).astype(bf16)

    nodes, entries = all_nodes // 2, all_entries // 2
    here = div(iota((entries, nodes), 0), cap) == div(iota((entries, nodes), 1), rows)
    listed = -(-cap // 8) * 8
    repeat = iota((entries, listed), 1) == mod(iota((entries, listed), 0), cap)
    for half in range(2):
        own = slice(half * nodes, (half + 1) * nodes)
        keys = all_keys[half * entries : (half + 1) * entries]
        values_t = all_values[half * entries : (half + 1) * entries].T
        extra_t = asked_ref[own, width:].astype(f32).T
        slots = (extra_t[:edges] + 256.0 * extra_t[edges : 2 * edges]).astype(jnp.int32) - me * cap
        uses = jnp.zeros((listed, nodes), f32)
        for j in range(edges):
            uses += jnp.where(slots[j : j + 1] == iota((listed, nodes), 0), 1.0, 0.0)
        uses = dot(repeat.astype(bf16), uses.astype(bf16))
        live = here & (uses > 0.5)
        bias = jnp.where(live, jnp.log2(jnp.where(live, uses, 1.0)), NEG)
        queries = asked_ref[own, :width]
        head = div(iota(queries.shape, 1), size)
        queries = jnp.concatenate(
            [jnp.where(head == h, queries, jnp.zeros_like(queries)) for h in range(HEADS)], axis=0
        )
        scores = dot_t(keys, queries) * scale + jnp.concatenate([bias] * HEADS, axis=1)
        top = jnp.max(scores, axis=0, keepdims=True)
        raised = jnp.exp2(scores - top)
        total = jnp.sum(raised, axis=0, keepdims=True)
        raised = raised.astype(bf16)
        for h in range(0, HEADS, 2):
            mixed = dot(
                values_t[h * size : (h + 2) * size, :], raised[:, h * nodes : (h + 2) * nodes]
            )
            mixed_ref[h * size : (h + 1) * size, :] = mixed[:size, :nodes]
            mixed_ref[(h + 1) * size : (h + 2) * size, :] = mixed[size:, nodes:]
        by_head = [
            jnp.concatenate([one[:, h * nodes : (h + 1) * nodes] for h in range(HEADS)], axis=0)
            for one in (top, total)
        ]
        stats = stat_parts(*by_head)
        for i, part in enumerate(stats):
            mixed_ref[width + i * HEADS : width + (i + 1) * HEADS, :] = part
        rest = mixed_ref.shape[0] - width - len(stats) * HEADS
        mixed_ref[width + len(stats) * HEADS :, :] = jnp.zeros((rest, nodes), f32)
        result = mixed_ref[...].T.astype(bf16)
        for i in range(peers // 2):
            out_ref[half * (peers // 2) + i] = result[i * rows : (i + 1) * rows]


def read_stats(stats):
    col, head = iota((LANES, LANES), 0), iota((LANES, LANES), 1)
    head_of = mod(col, HEADS) == head
    take_top = head_of & (col < 3 * HEADS)
    take_sum = head_of & (col >= 3 * HEADS) & (col < 5 * HEADS)
    return dot(stats, take_top.astype(bf16)), dot(stats, take_sum.astype(bf16))


def spread_heads(factor, width):
    size = width // HEADS
    spread = (div(iota((LANES, width), 1), size) == iota((LANES, width), 0)).astype(bf16)
    factor_1 = factor.astype(bf16)
    factor_2 = (factor - factor_1.astype(f32)).astype(bf16)
    return dot(factor_1, spread) + dot(factor_2, spread)


def combine_kernel(parts_ref, latent_ref, gain_ref, w_o_ref, w_kv_ref, latent_out_ref, out_ref):
    peers, rows, sent = parts_ref.shape
    width = w_o_ref.shape[0]
    parts = parts_ref[...].reshape(peers * rows, sent)
    top, total = read_stats(parts[:, width:])
    top = top.reshape(peers, rows, LANES)
    factor = jnp.exp2(top - jnp.max(top, axis=0, keepdims=True))
    total = jnp.sum(total.reshape(peers, rows, LANES) * factor, axis=0, keepdims=True)
    used = iota((1, rows, LANES), 2) < HEADS
    factor = factor * jnp.where(used, 1.0 / jnp.where(used, total, 1.0), 0.0)
    wide = spread_heads(factor.reshape(peers * rows, LANES), width)
    mixed = jnp.sum((parts[:, :width].astype(f32) * wide).reshape(peers, rows, width), axis=0)
    update = dot(mixed.astype(bf16), w_o_ref[...])
    latent_out = (latent_ref[...].astype(f32) + update).astype(bf16)
    latent_out_ref[...] = latent_out
    pairs = dot(normed(latent_out, gain_ref[...]), w_kv_ref[...]).astype(bf16)
    half = width // 2
    for p in range(peers):
        at = p % 2 * half
        out_ref[p, :, :half] = pairs[:, at : at + half]
        out_ref[p, :, half:] = pairs[:, width + at : width + at + half]


def picks_kernel(cap, rows, need_ref, slot_ref, pick_ref):
    edges, nodes, points = pick_ref.shape
    high_count = need_ref.shape[0]
    need = need_ref[...].astype(f32).astype(bf16)
    for j in range(edges):
        slots = slot_ref[j : j + 1, :]
        row_of = (div(slots, LANES) == iota((high_count, points), 0)).astype(bf16)
        listed = lax.dot_general(need, row_of, (((0,), (0,)), ((), ())), preferred_element_type=f32)
        own = mod(slots, LANES) == iota((LANES, points), 0)
        found = jnp.sum(jnp.where(own, listed, 0.0), axis=0, keepdims=True).astype(jnp.int32)
        node = div(slots, cap) * rows + found
        pick_ref[j] = (node == iota((nodes, points), 0)).astype(bf16)


def attend_half(pairs_ref, queries, pick_ref):
    half, points = queries.shape
    edges = pick_ref.shape[0]
    heads = HEADS // 2
    size = half // heads
    scores = []
    for j in range(edges):
        products = dot(pairs_ref[:half, :], pick_ref[j]) * queries.astype(f32)
        score = jnp.sum(products.reshape(heads, size, points), axis=1)
        scores.append(score * (1.0 / math.sqrt(size)))
    highest = functools.reduce(jnp.maximum, scores)
    raised = [jnp.exp(score - highest) for score in scores]
    inverse = 1.0 / sum(raised)
    mixed = jnp.zeros((heads, size, points), f32)
    for j in range(edges):
        weight = (raised[j] * inverse).astype(bf16).astype(f32).reshape(heads, 1, points)
        mixed += dot(pairs_ref[half:, :], pick_ref[j]).reshape(heads, size, points) * weight
    return mixed.reshape(half, points).T.astype(bf16)


def half_of(ref, first, half):
    return ref[pl.ds(pl.multiple_of(first, half), half), :]


def own_kernel(query_ref, pick_ref, nodes_ref, out_ref, pairs_ref):
    @pl.when(pl.program_id(0) == 0)
    def _():
        pairs_ref[...] = nodes_ref[...].T

    half = out_ref.shape[1]
    queries = half_of(query_ref, (lax.axis_index("dom") & 1) * half, half)
    out_ref[...] = attend_half(pairs_ref, queries, pick_ref)


def other_kernel(x_ref, query_ref, pick_ref, nodes_ref, own_ref, w_ref, out_ref, pairs_ref):
    @pl.when(pl.program_id(0) == 0)
    def _():
        pairs_ref[...] = nodes_ref[...].T

    half = own_ref.shape[1]
    core = lax.axis_index("dom") & 1
    update = dot(own_ref[...], half_of(w_ref, core * half, half))
    queries = half_of(query_ref, (1 - core) * half, half)
    update += dot(
        attend_half(pairs_ref, queries, pick_ref), half_of(w_ref, (1 - core) * half, half)
    )
    out_ref[...] = (x_ref[...].astype(f32) + update).astype(bf16)


def whole(*shape):
    return pl.BlockSpec(shape, lambda *_: (0,) * len(shape))


def on_device(
    grid,
    latent_in,
    grid_gain,
    node_gain,
    dec_gain,
    w_q_enc,
    w_kv_enc,
    w_o_enc,
    w_q_dec,
    w_kv_dec,
    w_o_dec,
    enc_need,
    enc_slot,
    enc_count,
    dec_need,
    dec_slot,
):
    peers = lax.axis_size("dom")
    points, depth = grid.shape
    rows = latent_in.shape[0]
    width = w_q_enc.shape[1]
    nodes = peers * rows
    entries = enc_need.shape[1]
    edges = enc_slot.shape[0]
    cap = entries // peers
    sent = width + LANES
    block = math.gcd(points, 256)

    asked = pl.pallas_call(
        ask_kernel,
        out_shape=jax.ShapeDtypeStruct((peers, rows, sent), bf16),
        compiler_params=params(58),
        cost_estimate=cost(2 * rows * depth * width, 2 * depth * width),
        name="ask",
    )(
        latent_in,
        node_gain.reshape(1, -1),
        w_q_enc,
        enc_slot.T,
        enc_count.reshape(1, -1),
        enc_need,
    )
    asked = lax.all_to_all(asked, "dom", split_axis=0, concat_axis=0, tiled=True)

    pairs, queries = pl.pallas_call(
        front_kernel,
        grid=(points // block,),
        in_specs=[
            pl.BlockSpec((block, depth), lambda i: (i, 0)),
            whole(1, depth),
            whole(depth, 2 * width),
            whole(depth, width),
        ],
        out_specs=[
            pl.BlockSpec((block, 2 * width), lambda i: (i, 0)),
            pl.BlockSpec((width, block), lambda i: (0, i)),
        ],
        out_shape=[
            jax.ShapeDtypeStruct((points, 2 * width), bf16),
            jax.ShapeDtypeStruct((width, points), bf16),
        ],
        compiler_params=params(58, 1),
        cost_estimate=cost(6 * points * depth * width, 8 * points * depth),
        name="front",
    )(grid, grid_gain.reshape(1, -1), w_kv_enc, w_q_dec)

    parts = pl.pallas_call(
        functools.partial(partial_kernel, cap, rows, edges),
        out_shape=jax.ShapeDtypeStruct((peers, rows, sent), bf16),
        scratch_shapes=[pltpu.VMEM((sent, nodes // 2), f32)],
        compiler_params=params(58),
        cost_estimate=cost(4 * entries * points * width, 4 * points * width),
        name="partial",
    )(asked.reshape(nodes, sent), pairs)
    parts = lax.all_to_all(parts, "dom", split_axis=0, concat_axis=0, tiled=True)

    slot_total = dec_need.shape[1]
    picks = pl.pallas_call(
        functools.partial(picks_kernel, slot_total // peers, rows),
        out_shape=jax.ShapeDtypeStruct((dec_slot.shape[0], nodes, points), bf16),
        compiler_params=params(58),
        cost_estimate=cost(points * nodes * LANES, 8 * points * nodes),
        name="picks",
    )(dec_need.reshape(slot_total // LANES, LANES), dec_slot)

    latent_out, everyone = pl.pallas_call(
        combine_kernel,
        out_shape=[
            jax.ShapeDtypeStruct((rows, depth), bf16),
            jax.ShapeDtypeStruct((peers, rows, width), bf16),
        ],
        compiler_params=params(24),
        cost_estimate=cost(6 * rows * depth * width, 6 * depth * width),
        name="combine",
    )(parts, latent_in, dec_gain.reshape(1, -1), w_o_enc, w_kv_dec)
    own = lax.all_to_all(everyone, "dom", split_axis=0, concat_axis=0, tiled=True)
    own = own.reshape(nodes, width)
    other = lax.ppermute(own, "dom", [(i, i ^ 1) for i in range(peers)])

    block = math.gcd(points, 512)
    point_rows = lambda columns: pl.BlockSpec((block, columns), lambda i: (i, 0))
    point_lanes = [
        pl.BlockSpec((width, block), lambda i: (0, i)),
        pl.BlockSpec((dec_slot.shape[0], nodes, block), lambda i: (0, 0, i)),
    ]
    own_mixed = pl.pallas_call(
        own_kernel,
        grid=(points // block,),
        in_specs=point_lanes + [whole(nodes, width)],
        out_specs=point_rows(width // 2),
        out_shape=jax.ShapeDtypeStruct((points, width // 2), bf16),
        scratch_shapes=[pltpu.VMEM((width, nodes), bf16)],
        compiler_params=params(58, 1),
        cost_estimate=cost(4 * points * nodes * width, 8 * points * nodes),
        name="own",
    )(queries, picks, own)
    grid_out = pl.pallas_call(
        other_kernel,
        grid=(points // block,),
        in_specs=[point_rows(depth)]
        + point_lanes
        + [whole(nodes, width), point_rows(width // 2), whole(width, depth)],
        out_specs=point_rows(depth),
        out_shape=jax.ShapeDtypeStruct((points, depth), bf16),
        scratch_shapes=[pltpu.VMEM((width, nodes), bf16)],
        compiler_params=params(58, 1),
        cost_estimate=cost(4 * points * depth * width, 8 * points * depth),
        name="other",
    )(grid, queries, picks, other, own_mixed, w_o_dec)
    return (latent_out, grid_out)


def solution(mesh):
    return jax.shard_map(
        on_device,
        mesh=mesh,
        in_specs=(
            P(("groups", "dom"), None),
            P(("groups", "dom"), None),
            P(),
            P(),
            P(),
            P(),
            P(),
            P(),
            P(),
            P(),
            P(),
            P("dom", None),
            P(None, "dom"),
            P("dom"),
            P("dom", None),
            P(None, "dom"),
        ),
        out_specs=(P(("groups", "dom"), None), P(("groups", "dom"), None)),
        check_vma=False,
    )
```

```python
import functools
import math

import jax
import jax.numpy as jnp
from jax import lax
from jax.experimental import pallas as pl
from jax.experimental.pallas import tpu as pltpu
from jax.sharding import PartitionSpec as P

HEADS = 8
LANES = 128
NEG = -1e30
norm_eps = 1e-06
f32 = jnp.float32
bf16 = jnp.bfloat16


def iota(shape, dim):
    return lax.broadcasted_iota(jnp.int32, shape, dim)


def div(values, by):
    if by & (by - 1) == 0:
        return values >> (by.bit_length() - 1)
    return values // by


def mod(values, by):
    if by & (by - 1) == 0:
        return values & (by - 1)
    return values % by


def dot(a, b):
    return jnp.dot(a, b, preferred_element_type=f32)


def dot_t(a, b):
    return lax.dot_general(a, b, (((1,), (1,)), ((), ())), preferred_element_type=f32)


def normed(values, gain):
    widened = values.astype(f32)
    spread = jnp.mean(widened * widened, axis=-1, keepdims=True)
    return (widened * lax.rsqrt(spread + norm_eps) * gain).astype(bf16)


def params(mib, grid_dims=0):
    return pltpu.CompilerParams(
        vmem_limit_bytes=mib * 2**20,
        dimension_semantics=("arbitrary",) * grid_dims if grid_dims else None,
    )


def cost(flops, read, exps=0):
    return pl.CostEstimate(flops=int(flops), bytes_accessed=int(read), transcendentals=int(exps))


def ask_kernel(latent_ref, gain_ref, w_ref, slot_ref, count_ref, need_ref, out_ref):
    rows = latent_ref.shape[0]
    width = w_ref.shape[1]
    entries = need_ref.shape[1]
    edges = slot_ref.shape[1]
    per = entries // rows
    queries = dot(normed(latent_ref[...], gain_ref[...]), w_ref[...]).astype(bf16)
    eye = iota((rows, rows), 0) == iota((rows, rows), 1)
    counts = jnp.sum(jnp.where(eye, count_ref[...], 0), axis=1, keepdims=True)
    slots = jnp.where(iota((rows, edges), 1) < counts, slot_ref[...], 65535)
    need = need_ref[...]
    own = div(iota((rows, entries), 1), per) == iota((rows, entries), 0)
    extra = jnp.zeros((rows, LANES), f32)
    for i, part in enumerate((slots & 255, slots >> 8)):
        to = iota((edges, LANES), 1) == iota((edges, LANES), 0) + i * edges
        extra += dot(part.astype(f32).astype(bf16), to.astype(bf16))
    for i, part in enumerate((need & 255, need >> 8)):
        to = iota((entries, LANES), 1) == mod(iota((entries, LANES), 0), per) + 2 * edges + i * per
        spread = jnp.where(own, part.astype(f32), 0.0).astype(bf16)
        extra += dot(spread, to.astype(bf16))
    half = width // 2
    for p in range(out_ref.shape[0]):
        out_ref[p, :, :half] = queries[:, p % 2 * half : (p % 2 + 1) * half]
        out_ref[p, :, half:] = extra.astype(bf16)


def half_columns(ref, core, half):
    return ref[:, pl.ds(pl.multiple_of(core * half, half), half)]


def front_kernel(steps, own_ref, other_ref, gain_ref, w_ref, pairs_ref, rows_ref):
    step = pl.program_id(0)

    @pl.when(step < steps)
    def _():
        rows_ref[...] = normed(own_ref[...], gain_ref[...])

    @pl.when(step >= steps)
    def _():
        rows_ref[...] = normed(other_ref[...], gain_ref[...])

    core = lax.axis_index("dom") & 1
    half = pairs_ref.shape[1] // 2
    rows = rows_ref[...]
    pairs_ref[:, :half] = dot(rows, half_columns(w_ref, core, half)).astype(bf16)
    pairs_ref[:, half:] = dot(rows, half_columns(w_ref, core + 2, half)).astype(bf16)


def stat_parts(top, total):
    top_1 = top.astype(bf16).astype(f32)
    top_2 = (top - top_1).astype(bf16).astype(f32)
    total_1 = total.astype(bf16).astype(f32)
    return top_1, top_2, top - top_1 - top_2, total_1, total - total_1


def partial_kernel(cap, edges, asked_hbm, pairs_hbm, out_ref, asked_ref, pairs_ref, mixed_ref, sems):
    copies = [
        pltpu.make_async_copy(asked_hbm, asked_ref, sems.at[0]),
        pltpu.make_async_copy(pairs_hbm, pairs_ref, sems.at[1]),
    ]
    for copy in copies:
        copy.start()
    me = lax.axis_index("dom")
    points, both = pairs_ref.shape
    points = points // 2
    peers, rows, _ = out_ref.shape
    width = both // 2
    heads = HEADS // 2
    size = width // heads
    per = cap * peers // rows
    scale = math.log2(math.e) / math.sqrt(size)
    all_nodes = asked_ref.shape[0]
    all_entries = peers * cap
    nodes, entries = all_nodes // 2, all_entries // 2
    pick_shape = (all_entries, all_nodes)
    pick_row = iota(pick_shape, 1) - div(iota(pick_shape, 0), cap) * rows
    lane = iota((all_entries, LANES), 1) - mod(iota((all_entries, LANES), 0), cap)
    here = div(iota((entries, nodes), 0), cap) == div(iota((entries, nodes), 1), rows)
    listed = -(-cap // 8) * 8
    repeat = iota((entries, listed), 1) == mod(iota((entries, listed), 0), cap)
    repeat = repeat.astype(bf16)
    copies[0].wait()
    extra = asked_ref[:, width:]
    extra_t = extra.astype(f32).T
    all_slots = (extra_t[:edges] + 256.0 * extra_t[edges : 2 * edges]).astype(jnp.int32)
    chosen, biases = [], []
    for other in range(2):
        first = (me ^ other) * cap
        list_row, low_lane = div(first, per), mod(first, per) + 2 * edges
        weights = jnp.where(lane == low_lane, 1.0, jnp.where(lane == low_lane + per, 256.0, 0.0))
        lists = dot((pick_row == list_row).astype(bf16), extra)
        index = jnp.sum(lists * weights, axis=1, keepdims=True).astype(jnp.int32)
        chosen.append((index == iota((all_entries, points), 1)).astype(bf16))
        slots = all_slots - first
        uses = jnp.zeros((listed, all_nodes), f32)
        for j in range(edges):
            uses += jnp.where(slots[j : j + 1] == iota((listed, all_nodes), 0), 1.0, 0.0)
        for half in range(2):
            used = dot(repeat, uses[:, half * nodes : (half + 1) * nodes].astype(bf16))
            live = here & (used > 0.5)
            biases.append(jnp.where(live, jnp.log2(jnp.where(live, used, 1.0)), NEG))
    copies[1].wait()
    gathered = [
        dot(chosen[other], pairs_ref[other * points : (other + 1) * points, :]).astype(bf16)
        for other in range(2)
    ]
    for half in range(2):
        part = slice(half * entries, (half + 1) * entries)
        pairs = jnp.concatenate([gathered[0][part], gathered[1][part]], axis=0)
        bias = jnp.concatenate([biases[half], biases[2 + half]], axis=0)
        keys, values_t = pairs[:, :width], pairs[:, width:].T
        queries = asked_ref[half * nodes : (half + 1) * nodes, :width]
        head = div(iota(queries.shape, 1), size)
        queries = jnp.concatenate(
            [jnp.where(head == h, queries, jnp.zeros_like(queries)) for h in range(heads)], axis=0
        )
        scores = dot_t(keys, queries) * scale + jnp.concatenate([bias] * heads, axis=1)
        top = jnp.max(scores, axis=0, keepdims=True)
        raised = jnp.exp2(scores - top)
        total = jnp.sum(raised, axis=0, keepdims=True)
        raised = raised.astype(bf16)
        for h in range(0, heads, 2):
            mixed = dot(
                values_t[h * size : (h + 2) * size, :], raised[:, h * nodes : (h + 2) * nodes]
            )
            mixed_ref[h * size : (h + 1) * size, :] = mixed[:size, :nodes]
            mixed_ref[(h + 1) * size : (h + 2) * size, :] = mixed[size:, nodes:]
        by_head = [
            jnp.concatenate([one[:, h * nodes : (h + 1) * nodes] for h in range(heads)], axis=0)
            for one in (top, total)
        ]
        stats = jnp.concatenate(stat_parts(*by_head), axis=0)
        rest = mixed_ref.shape[0] - width - stats.shape[0]
        mixed_ref[width:, :] = jnp.concatenate([stats, jnp.zeros((rest, nodes), f32)], axis=0)
        result = mixed_ref[...].T.astype(bf16)
        for i in range(peers // 2):
            out_ref[half * (peers // 2) + i] = result[i * rows : (i + 1) * rows]


def read_stats(stats):
    heads = HEADS // 2
    col, head = iota((LANES, LANES), 0), iota((LANES, LANES), 1)
    head_of = mod(col, heads) == head
    take_top = head_of & (col < 3 * heads)
    take_sum = head_of & (col >= 3 * heads) & (col < 5 * heads)
    return dot(stats, take_top.astype(bf16)), dot(stats, take_sum.astype(bf16))


def spread_heads(factor, width, size):
    spread = (div(iota((LANES, width), 1), size) == iota((LANES, width), 0)).astype(bf16)
    factor_1 = factor.astype(bf16)
    factor_2 = (factor - factor_1.astype(f32)).astype(bf16)
    return dot(factor_1, spread) + dot(factor_2, spread)


def combine_kernel(parts_ref, latent_ref, gain_ref, w_o_ref, w_kv_ref, latent_out_ref, out_ref):
    peers, rows, sent = parts_ref.shape
    width = w_o_ref.shape[0]
    half = width // 2
    chips = (peers // 2, 2, rows)
    parts = parts_ref[...].reshape(peers * rows, sent)
    top, total = read_stats(parts[:, half:])
    top = top.reshape(*chips, LANES)
    factor = jnp.exp2(top - jnp.max(top, axis=0, keepdims=True))
    total = jnp.sum(total.reshape(*chips, LANES) * factor, axis=0, keepdims=True)
    used = iota((1, 2, rows, LANES), 3) < HEADS // 2
    factor = factor * jnp.where(used, 1.0 / jnp.where(used, total, 1.0), 0.0)
    wide = spread_heads(factor.reshape(peers * rows, LANES), half, width // HEADS)
    mixed = jnp.sum((parts[:, :half].astype(f32) * wide).reshape(*chips, half), axis=0)
    mixed = jnp.concatenate([mixed[0], mixed[1]], axis=1)
    update = dot(mixed.astype(bf16), w_o_ref[...])
    latent_out = (latent_ref[...].astype(f32) + update).astype(bf16)
    latent_out_ref[...] = latent_out
    pairs = dot(normed(latent_out, gain_ref[...]), w_kv_ref[...]).astype(bf16)
    for p in range(peers):
        at = p % 2 * half
        out_ref[p, :, :half] = pairs[:, at : at + half]
        out_ref[p, :, half:] = pairs[:, width + at : width + at + half]


def middle_kernel(cap, rows, x_ref, gain_ref, w_ref, need_ref, slot_ref, query_ref, pick_ref):
    query_ref[...] = dot(normed(x_ref[...], gain_ref[...]), w_ref[...]).T.astype(bf16)
    edges, nodes, points = pick_ref.shape
    high_count = need_ref.shape[0]
    need = need_ref[...].astype(f32).astype(bf16)
    for j in range(edges):
        slots = slot_ref[j : j + 1, :]
        row_of = (div(slots, LANES) == iota((high_count, points), 0)).astype(bf16)
        listed = lax.dot_general(need, row_of, (((0,), (0,)), ((), ())), preferred_element_type=f32)
        own = mod(slots, LANES) == iota((LANES, points), 0)
        found = jnp.sum(jnp.where(own, listed, 0.0), axis=0, keepdims=True).astype(jnp.int32)
        node = div(slots, cap) * rows + found
        pick_ref[j] = (node == iota((nodes, points), 0)).astype(bf16)


def attend_half(pairs_ref, queries, pick_ref):
    half, points = queries.shape
    edges = pick_ref.shape[0]
    heads = HEADS // 2
    size = half // heads
    scores = []
    for j in range(edges):
        products = dot(pairs_ref[:half, :], pick_ref[j]) * queries.astype(f32)
        score = jnp.sum(products.reshape(heads, size, points), axis=1)
        scores.append(score * (1.0 / math.sqrt(size)))
    highest = functools.reduce(jnp.maximum, scores)
    raised = [jnp.exp(score - highest) for score in scores]
    inverse = 1.0 / sum(raised)
    mixed = jnp.zeros((heads, size, points), f32)
    for j in range(edges):
        weight = (raised[j] * inverse).astype(bf16).astype(f32).reshape(heads, 1, points)
        mixed += dot(pairs_ref[half:, :], pick_ref[j]).reshape(heads, size, points) * weight
    return mixed.reshape(half, points).T.astype(bf16)


def half_of(ref, first, half):
    return ref[pl.ds(pl.multiple_of(first, half), half), :]


def own_kernel(query_ref, pick_ref, nodes_hbm, out_ref, nodes_ref, pairs_ref, sem):
    @pl.when(pl.program_id(0) == 0)
    def _():
        copy = pltpu.make_async_copy(nodes_hbm, nodes_ref, sem)
        copy.start()
        copy.wait()
        pairs_ref[...] = nodes_ref[...].T

    half = out_ref.shape[1]
    queries = half_of(query_ref, (lax.axis_index("dom") & 1) * half, half)
    out_ref[...] = attend_half(pairs_ref, queries, pick_ref)


def other_kernel(
    x_ref, query_ref, pick_ref, nodes_hbm, own_ref, w_ref, out_ref, nodes_ref, pairs_ref, sem
):
    @pl.when(pl.program_id(0) == 0)
    def _():
        copy = pltpu.make_async_copy(nodes_hbm, nodes_ref, sem)
        copy.start()
        copy.wait()
        pairs_ref[...] = nodes_ref[...].T

    half = own_ref.shape[1]
    core = lax.axis_index("dom") & 1
    update = dot(own_ref[...], half_of(w_ref, core * half, half))
    queries = half_of(query_ref, (1 - core) * half, half)
    update += dot(
        attend_half(pairs_ref, queries, pick_ref), half_of(w_ref, (1 - core) * half, half)
    )
    out_ref[...] = (x_ref[...].astype(f32) + update).astype(bf16)


def whole(*shape):
    return pl.BlockSpec(shape, lambda *_: (0,) * len(shape))


def on_device(
    grid,
    latent_in,
    grid_gain,
    node_gain,
    dec_gain,
    w_q_enc,
    w_kv_enc,
    w_o_enc,
    w_q_dec,
    w_kv_dec,
    w_o_dec,
    enc_need,
    enc_slot,
    enc_count,
    dec_need,
    dec_slot,
):
    peers = lax.axis_size("dom")
    points, depth = grid.shape
    rows = latent_in.shape[0]
    width = w_q_enc.shape[1]
    nodes = peers * rows
    entries = enc_need.shape[1]
    edges = enc_slot.shape[0]
    cap = entries // peers
    half = width // 2
    sent = half + LANES
    swap = [(i, i ^ 1) for i in range(peers)]
    anywhere = pl.BlockSpec(memory_space=pl.ANY)

    other_grid = lax.ppermute(grid, "dom", swap)
    asked = pl.pallas_call(
        ask_kernel,
        out_shape=jax.ShapeDtypeStruct((peers, rows, sent), bf16),
        compiler_params=params(58),
        cost_estimate=cost(2 * rows * depth * width, 2 * depth * width),
        name="ask",
    )(
        latent_in,
        node_gain.reshape(1, -1),
        w_q_enc,
        enc_slot.T,
        enc_count.reshape(1, -1),
        enc_need,
    )
    asked = lax.all_to_all(asked, "dom", split_axis=0, concat_axis=0, tiled=True)

    block = math.gcd(points, 256)
    steps = points // block
    pairs = pl.pallas_call(
        functools.partial(front_kernel, steps),
        grid=(2 * steps,),
        in_specs=[
            pl.BlockSpec((block, depth), lambda i: (jnp.minimum(i, steps - 1), 0)),
            pl.BlockSpec((block, depth), lambda i: (jnp.maximum(i - steps, 0), 0)),
            whole(1, depth),
            whole(depth, 2 * width),
        ],
        out_specs=pl.BlockSpec((block, width), lambda i: (i, 0)),
        out_shape=jax.ShapeDtypeStruct((2 * points, width), bf16),
        scratch_shapes=[pltpu.VMEM((block, depth), bf16)],
        compiler_params=params(58, 1),
        cost_estimate=cost(4 * points * depth * width, 8 * points * depth),
        name="front",
    )(grid, other_grid, grid_gain.reshape(1, -1), w_kv_enc)

    parts = pl.pallas_call(
        functools.partial(partial_kernel, cap, edges),
        in_specs=[anywhere, anywhere],
        out_shape=jax.ShapeDtypeStruct((peers, rows, sent), bf16),
        scratch_shapes=[
            pltpu.VMEM((nodes, sent), bf16),
            pltpu.VMEM((2 * points, width), bf16),
            pltpu.VMEM((sent, nodes // 2), f32),
            pltpu.SemaphoreType.DMA((2,)),
        ],
        compiler_params=params(58),
        cost_estimate=cost(4 * entries * points * width, 4 * points * width),
        name="partial",
    )(asked.reshape(nodes, sent), pairs)
    parts = lax.all_to_all(parts, "dom", split_axis=0, concat_axis=0, tiled=True)

    slot_total = dec_need.shape[1]
    queries, picks = pl.pallas_call(
        functools.partial(middle_kernel, slot_total // peers, rows),
        out_shape=[
            jax.ShapeDtypeStruct((width, points), bf16),
            jax.ShapeDtypeStruct((dec_slot.shape[0], nodes, points), bf16),
        ],
        compiler_params=params(58),
        cost_estimate=cost(2 * points * depth * width, 8 * points * depth),
        name="middle",
    )(
        grid,
        grid_gain.reshape(1, -1),
        w_q_dec,
        dec_need.reshape(slot_total // LANES, LANES),
        dec_slot,
    )
    parts, queries, picks = lax.optimization_barrier((parts, queries, picks))

    latent_out, everyone = pl.pallas_call(
        combine_kernel,
        out_shape=[
            jax.ShapeDtypeStruct((rows, depth), bf16),
            jax.ShapeDtypeStruct((peers, rows, width), bf16),
        ],
        compiler_params=params(24),
        cost_estimate=cost(6 * rows * depth * width, 6 * depth * width),
        name="combine",
    )(parts, latent_in, dec_gain.reshape(1, -1), w_o_enc, w_kv_dec)
    own = lax.all_to_all(everyone, "dom", split_axis=0, concat_axis=0, tiled=True)
    own = own.reshape(nodes, width)
    other = lax.ppermute(own, "dom", swap)

    block = math.gcd(points, 512)
    point_rows = lambda columns: pl.BlockSpec((block, columns), lambda i: (i, 0))
    point_lanes = [
        pl.BlockSpec((width, block), lambda i: (0, i)),
        pl.BlockSpec((dec_slot.shape[0], nodes, block), lambda i: (0, 0, i)),
    ]
    own_mixed = pl.pallas_call(
        own_kernel,
        grid=(points // block,),
        in_specs=point_lanes + [anywhere],
        out_specs=point_rows(half),
        out_shape=jax.ShapeDtypeStruct((points, half), bf16),
        scratch_shapes=[
            pltpu.VMEM((nodes, width), bf16),
            pltpu.VMEM((width, nodes), bf16),
            pltpu.SemaphoreType.DMA,
        ],
        compiler_params=params(58, 1),
        cost_estimate=cost(4 * points * nodes * width, 8 * points * nodes),
        name="own",
    )(queries, picks, own)
    grid_out = pl.pallas_call(
        other_kernel,
        grid=(points // block,),
        in_specs=[point_rows(depth)]
        + point_lanes
        + [anywhere, point_rows(half), whole(width, depth)],
        out_specs=point_rows(depth),
        out_shape=jax.ShapeDtypeStruct((points, depth), bf16),
        scratch_shapes=[
            pltpu.VMEM((nodes, width), bf16),
            pltpu.VMEM((width, nodes), bf16),
            pltpu.SemaphoreType.DMA,
        ],
        compiler_params=params(58, 1),
        cost_estimate=cost(4 * points * depth * width, 8 * points * depth),
        name="other",
    )(grid, queries, picks, other, own_mixed, w_o_dec)
    return (latent_out, grid_out)


def solution(mesh):
    return jax.shard_map(
        on_device,
        mesh=mesh,
        in_specs=(
            P(("groups", "dom"), None),
            P(("groups", "dom"), None),
            P(),
            P(),
            P(),
            P(),
            P(),
            P(),
            P(),
            P(),
            P(),
            P("dom", None),
            P(None, "dom"),
            P("dom"),
            P("dom", None),
            P(None, "dom"),
        ),
        out_specs=(P(("groups", "dom"), None), P(("groups", "dom"), None)),
        check_vma=False,
    )
```

```python
import functools
import math

import jax
import jax.numpy as jnp
from jax import lax
from jax.experimental import pallas as pl
from jax.experimental.pallas import tpu as pltpu
from jax.sharding import PartitionSpec as P

HEADS = 8
LANES = 128
NEG = -1e30
norm_eps = 1e-06
f32 = jnp.float32
bf16 = jnp.bfloat16


def iota(shape, dim):
    return lax.broadcasted_iota(jnp.int32, shape, dim)


def div(values, by):
    if by & (by - 1) == 0:
        return values >> (by.bit_length() - 1)
    return values // by


def mod(values, by):
    if by & (by - 1) == 0:
        return values & (by - 1)
    return values % by


def dot(a, b):
    return jnp.dot(a, b, preferred_element_type=f32)


def dot_t(a, b):
    return lax.dot_general(a, b, (((1,), (1,)), ((), ())), preferred_element_type=f32)


def normed(values, gain):
    widened = values.astype(f32)
    spread = jnp.mean(widened * widened, axis=-1, keepdims=True)
    return (widened * lax.rsqrt(spread + norm_eps) * gain).astype(bf16)


def params(mib):
    return pltpu.CompilerParams(vmem_limit_bytes=mib * 2**20)


def cost(flops, read, exps=0):
    return pl.CostEstimate(flops=int(flops), bytes_accessed=int(read), transcendentals=int(exps))


def ask_kernel(
    latent_ref, gain_ref, slot_ref, count_ref, need_ref, w_hbm, out_ref, w_ref, sem
):
    copy = pltpu.make_async_copy(w_hbm, w_ref, sem)
    copy.start()
    rows = latent_ref.shape[0]
    width = w_ref.shape[1]
    entries = need_ref.shape[1]
    edges = slot_ref.shape[1]
    per = entries // rows
    rows_normed = normed(latent_ref[...], gain_ref[...])
    eye = iota((rows, rows), 0) == iota((rows, rows), 1)
    counts = jnp.sum(jnp.where(eye, count_ref[...], 0), axis=1, keepdims=True)
    slots = jnp.where(iota((rows, edges), 1) < counts, slot_ref[...], 65535)
    need = need_ref[...]
    own = div(iota((rows, entries), 1), per) == iota((rows, entries), 0)
    extra = jnp.zeros((rows, LANES), f32)
    for i, part in enumerate((slots & 255, slots >> 8)):
        to = iota((edges, LANES), 1) == iota((edges, LANES), 0) + i * edges
        extra += dot(part.astype(f32).astype(bf16), to.astype(bf16))
    for i, part in enumerate((need & 255, need >> 8)):
        to = iota((entries, LANES), 1) == mod(iota((entries, LANES), 0), per) + 2 * edges + i * per
        spread = jnp.where(own, part.astype(f32), 0.0).astype(bf16)
        extra += dot(spread, to.astype(bf16))
    copy.wait()
    queries = dot(rows_normed, w_ref[...]).astype(bf16)
    half = width // 2
    for p in range(out_ref.shape[0]):
        out_ref[p, :, :half] = queries[:, p % 2 * half : (p % 2 + 1) * half]
        out_ref[p, :, half:] = extra.astype(bf16)


def started(*copies):
    for copy in copies:
        copy.start()
    return copies


def front_kernel(steps, own_hbm, other_ref, gain_ref, w_hbm, pairs_ref, own_ref, w_ref, sems):
    points = own_ref.shape[0]
    block = points // steps
    half = pairs_ref.shape[1] // 2
    core = lax.axis_index("dom") & 1
    parts = [pl.ds(i * block, block) for i in range(steps)]
    weights = started(
        *[
            pltpu.make_async_copy(
                w_hbm.at[:, pl.ds(pl.multiple_of((core + 2 * i) * half, half), half)],
                w_ref.at[:, pl.ds(i * half, half)],
                sems.at[steps + i],
            )
            for i in range(2)
        ]
    )
    rows = started(
        *[
            pltpu.make_async_copy(own_hbm.at[part], own_ref.at[part], sems.at[i])
            for i, part in enumerate(parts)
        ]
    )
    gain = gain_ref[...]
    for copy in weights + rows:
        copy.wait()
    for start, ref in ((0, own_ref), (points, other_ref)):
        for i, part in enumerate(parts):
            pairs_ref[pl.ds(start + i * block, block), :] = dot(
                normed(ref[part, :], gain), w_ref[...]
            ).astype(bf16)


def stat_parts(top, total):
    top_1 = top.astype(bf16).astype(f32)
    top_2 = (top - top_1).astype(bf16).astype(f32)
    total_1 = total.astype(bf16).astype(f32)
    return top_1, top_2, top - top_1 - top_2, total_1, total - total_1


def partial_kernel(cap, edges, asked_ref, pairs_ref, out_ref, mixed_ref):
    me = lax.axis_index("dom")
    points, both = pairs_ref.shape
    points = points // 2
    peers, rows, _ = out_ref.shape
    width = both // 2
    heads = HEADS // 2
    size = width // heads
    per = cap * peers // rows
    scale = math.log2(math.e) / math.sqrt(size)
    all_nodes = asked_ref.shape[0]
    all_entries = peers * cap
    nodes, entries = all_nodes // 2, all_entries // 2
    pick_shape = (all_entries, all_nodes)
    pick_row = iota(pick_shape, 1) - div(iota(pick_shape, 0), cap) * rows
    lane = iota((all_entries, LANES), 1) - mod(iota((all_entries, LANES), 0), cap)
    here = div(iota((entries, nodes), 0), cap) == div(iota((entries, nodes), 1), rows)
    listed = -(-cap // 8) * 8
    repeat = iota((entries, listed), 1) == mod(iota((entries, listed), 0), cap)
    repeat = repeat.astype(f32)
    extra = asked_ref[:, width:]
    extra_t = extra.astype(f32).T
    all_slots = (extra_t[:edges] + 256.0 * extra_t[edges : 2 * edges]).astype(jnp.int32)
    chosen, biases = [], []
    for other in range(2):
        first = (me ^ other) * cap
        list_row, low_lane = div(first, per), mod(first, per) + 2 * edges
        weights = jnp.where(lane == low_lane, 1.0, jnp.where(lane == low_lane + per, 256.0, 0.0))
        lists = dot((pick_row == list_row).astype(bf16), extra)
        index = jnp.sum(lists * weights, axis=1, keepdims=True).astype(jnp.int32)
        chosen.append((index == iota((all_entries, points), 1)).astype(bf16))
        slots = all_slots - first
        uses = jnp.zeros((listed, all_nodes), f32)
        for j in range(edges):
            uses += jnp.where(slots[j : j + 1] == iota((listed, all_nodes), 0), 1.0, 0.0)
        live = uses > 0.5
        bias = jnp.where(live, jnp.log2(jnp.where(live, uses, 1.0)), NEG)
        for half in range(2):
            part = bias[:, half * nodes : (half + 1) * nodes]
            if cap == listed:
                repeated = jnp.concatenate([part] * (entries // cap), axis=0)
            else:
                repeated = lax.dot_general(
                    repeat, part, (((1,), (0,)), ((), ())), precision=lax.Precision.HIGHEST
                )
            biases.append(jnp.where(here, repeated, NEG))
    gathered = [
        dot(chosen[other], pairs_ref[other * points : (other + 1) * points, :]).astype(bf16)
        for other in range(2)
    ]
    for half in range(2):
        part = slice(half * entries, (half + 1) * entries)
        pairs = jnp.concatenate([gathered[0][part], gathered[1][part]], axis=0)
        bias = jnp.concatenate([biases[half], biases[2 + half]], axis=0)
        keys, values_t = pairs[:, :width], pairs[:, width:].T
        queries = asked_ref[half * nodes : (half + 1) * nodes, :width]
        head = div(iota(queries.shape, 1), size)
        queries = jnp.concatenate(
            [jnp.where(head == h, queries, jnp.zeros_like(queries)) for h in range(heads)], axis=0
        )
        scores = dot_t(keys, queries) * scale + jnp.concatenate([bias] * heads, axis=1)
        top = jnp.max(scores, axis=0, keepdims=True)
        raised = jnp.exp2(scores - top)
        total = jnp.sum(raised, axis=0, keepdims=True)
        raised = raised.astype(bf16)
        for h in range(0, heads, 2):
            mixed = dot(
                values_t[h * size : (h + 2) * size, :], raised[:, h * nodes : (h + 2) * nodes]
            )
            mixed_ref[h * size : (h + 1) * size, :] = mixed[:size, :nodes]
            mixed_ref[(h + 1) * size : (h + 2) * size, :] = mixed[size:, nodes:]
        by_head = [
            jnp.concatenate([one[:, h * nodes : (h + 1) * nodes] for h in range(heads)], axis=0)
            for one in (top, total)
        ]
        stats = jnp.concatenate(stat_parts(*by_head), axis=0)
        rest = mixed_ref.shape[0] - width - stats.shape[0]
        mixed_ref[width:, :] = jnp.concatenate([stats, jnp.zeros((rest, nodes), f32)], axis=0)
        result = mixed_ref[...].T.astype(bf16)
        for i in range(peers // 2):
            out_ref[half * (peers // 2) + i] = result[i * rows : (i + 1) * rows]


def read_stats(stats):
    heads = HEADS // 2
    col, head = iota((LANES, LANES), 0), iota((LANES, LANES), 1)
    head_of = mod(col, heads) == head
    take_top = head_of & (col < 3 * heads)
    take_sum = head_of & (col >= 3 * heads) & (col < 5 * heads)
    return dot(stats, take_top.astype(bf16)), dot(stats, take_sum.astype(bf16))


def spread_heads(factor, width, size):
    spread = (div(iota((LANES, width), 1), size) == iota((LANES, width), 0)).astype(bf16)
    factor_1 = factor.astype(bf16)
    factor_2 = (factor - factor_1.astype(f32)).astype(bf16)
    return dot(factor_1, spread) + dot(factor_2, spread)


def combine_kernel(parts_ref, latent_ref, gain_ref, w_o_ref, w_kv_ref, latent_out_ref, out_ref):
    peers, rows, sent = parts_ref.shape
    width = w_o_ref.shape[0]
    half = width // 2
    chips = (peers // 2, 2, rows)
    parts = parts_ref[...].reshape(peers * rows, sent)
    top, total = read_stats(parts[:, half:])
    top = top.reshape(*chips, LANES)
    factor = jnp.exp2(top - jnp.max(top, axis=0, keepdims=True))
    total = jnp.sum(total.reshape(*chips, LANES) * factor, axis=0, keepdims=True)
    used = iota((1, 2, rows, LANES), 3) < HEADS // 2
    factor = factor * jnp.where(used, 1.0 / jnp.where(used, total, 1.0), 0.0)
    wide = spread_heads(factor.reshape(peers * rows, LANES), half, width // HEADS)
    mixed = jnp.sum((parts[:, :half].astype(f32) * wide).reshape(*chips, half), axis=0)
    mixed = jnp.concatenate([mixed[0], mixed[1]], axis=1)
    update = dot(mixed.astype(bf16), w_o_ref[...])
    latent_out = (latent_ref[...].astype(f32) + update).astype(bf16)
    latent_out_ref[...] = latent_out
    pairs = dot(normed(latent_out, gain_ref[...]), w_kv_ref[...]).astype(bf16)
    for p in range(peers):
        at = p % 2 * half
        out_ref[p, :, :half] = pairs[:, at : at + half]
        out_ref[p, :, half:] = pairs[:, width + at : width + at + half]


def middle_kernel(cap, rows, x_ref, gain_ref, w_ref, need_ref, slot_ref, query_ref, pick_ref):
    query_ref[...] = dot(normed(x_ref[...], gain_ref[...]), w_ref[...]).T.astype(bf16)
    edges, nodes, points = pick_ref.shape
    high_count = need_ref.shape[0]
    need = need_ref[...].astype(f32).astype(bf16)
    for j in range(edges):
        slots = slot_ref[j : j + 1, :]
        row_of = (div(slots, LANES) == iota((high_count, points), 0)).astype(bf16)
        listed = lax.dot_general(need, row_of, (((0,), (0,)), ((), ())), preferred_element_type=f32)
        own = mod(slots, LANES) == iota((LANES, points), 0)
        found = jnp.sum(jnp.where(own, listed, 0.0), axis=0, keepdims=True).astype(jnp.int32)
        node = div(slots, cap) * rows + found
        pick_ref[j] = (node == iota((nodes, points), 0)).astype(bf16)


def attend_half(pairs, queries, pick_ref, part):
    half, points = queries.shape
    edges = pick_ref.shape[0]
    heads = HEADS // 2
    size = half // heads
    scores = []
    for j in range(edges):
        products = dot(pairs[:half], pick_ref[j, :, part]) * queries.astype(f32)
        score = jnp.sum(products.reshape(heads, size, points), axis=1)
        scores.append(score * (1.0 / math.sqrt(size)))
    highest = functools.reduce(jnp.maximum, scores)
    raised = [jnp.exp(score - highest) for score in scores]
    inverse = 1.0 / sum(raised)
    mixed = jnp.zeros((heads, size, points), f32)
    for j in range(edges):
        weight = (raised[j] * inverse).astype(bf16).astype(f32).reshape(heads, 1, points)
        mixed += dot(pairs[half:], pick_ref[j, :, part]).reshape(heads, size, points) * weight
    return mixed.reshape(half, points).T.astype(bf16)


def half_of(ref, first, half):
    return ref.at[pl.ds(pl.multiple_of(first, half), half)]


def own_kernel(steps, nodes_ref, query_hbm, pick_hbm, out_ref, query_ref, pick_ref, sems):
    points, half = out_ref.shape
    block = points // steps
    core = lax.axis_index("dom") & 1
    copies = started(
        pltpu.make_async_copy(half_of(query_hbm, core * half, half), query_ref, sems.at[0]),
        pltpu.make_async_copy(pick_hbm, pick_ref, sems.at[1]),
    )
    pairs = nodes_ref[...].T
    for copy in copies:
        copy.wait()
    for i in range(steps):
        part = pl.ds(i * block, block)
        out_ref[part, :] = attend_half(pairs, query_ref[:, part], pick_ref, part)


def other_kernel(
    steps, nodes_ref, own_ref, x_hbm, query_hbm, pick_hbm, w_hbm, out_hbm,
    x_ref, query_ref, pick_ref, w_ref, out_ref, sems, out_sems,
):
    points, half = own_ref.shape
    block = points // steps
    core = lax.axis_index("dom") & 1
    copies = started(
        pltpu.make_async_copy(half_of(w_hbm, core * half, half), w_ref.at[0], sems.at[0]),
        pltpu.make_async_copy(half_of(w_hbm, (1 - core) * half, half), w_ref.at[1], sems.at[1]),
        pltpu.make_async_copy(half_of(query_hbm, (1 - core) * half, half), query_ref, sems.at[2]),
        pltpu.make_async_copy(pick_hbm, pick_ref, sems.at[3]),
        pltpu.make_async_copy(x_hbm, x_ref, sems.at[4]),
    )
    pairs = nodes_ref[...].T
    for copy in copies:
        copy.wait()
    sends = []
    for i in range(steps):
        part = pl.ds(i * block, block)
        mixed = attend_half(pairs, query_ref[:, part], pick_ref, part)
        update = dot(own_ref[part, :], w_ref[0]) + dot(mixed, w_ref[1])
        out_ref[part, :] = (x_ref[part, :].astype(f32) + update).astype(bf16)
        sends += started(
            pltpu.make_async_copy(out_ref.at[part], out_hbm.at[part], out_sems.at[i])
        )
    for send in sends:
        send.wait()


def on_device(
    grid,
    latent_in,
    grid_gain,
    node_gain,
    dec_gain,
    w_q_enc,
    w_kv_enc,
    w_o_enc,
    w_q_dec,
    w_kv_dec,
    w_o_dec,
    enc_need,
    enc_slot,
    enc_count,
    dec_need,
    dec_slot,
):
    peers = lax.axis_size("dom")
    points, depth = grid.shape
    rows = latent_in.shape[0]
    width = w_q_enc.shape[1]
    nodes = peers * rows
    entries = enc_need.shape[1]
    edges = enc_slot.shape[0]
    cap = entries // peers
    half = width // 2
    sent = half + LANES
    swap = [(i, i ^ 1) for i in range(peers)]
    vmem = pl.BlockSpec(memory_space=pltpu.VMEM)
    hbm = pl.BlockSpec(memory_space=pltpu.HBM)

    other_grid = lax.ppermute(grid, "dom", swap)
    asked = pl.pallas_call(
        ask_kernel,
        in_specs=[vmem] * 5 + [hbm],
        out_shape=jax.ShapeDtypeStruct((peers, rows, sent), bf16),
        scratch_shapes=[pltpu.VMEM((depth, width), bf16), pltpu.SemaphoreType.DMA],
        compiler_params=params(58),
        cost_estimate=cost(2 * rows * depth * width, 2 * depth * width),
        name="ask",
    )(
        latent_in,
        node_gain.reshape(1, -1),
        enc_slot.T,
        enc_count.reshape(1, -1),
        enc_need,
        w_q_enc,
    )
    asked = lax.all_to_all(asked, "dom", split_axis=0, concat_axis=0, tiled=True)

    block = math.gcd(points, 256)
    steps = points // block
    pairs = pl.pallas_call(
        functools.partial(front_kernel, steps),
        in_specs=[hbm, vmem, vmem, hbm],
        out_shape=jax.ShapeDtypeStruct((2 * points, width), bf16),
        scratch_shapes=[
            pltpu.VMEM((points, depth), bf16),
            pltpu.VMEM((depth, width), bf16),
            pltpu.SemaphoreType.DMA((steps + 2,)),
        ],
        compiler_params=params(32),
        cost_estimate=cost(4 * points * depth * width, 8 * points * depth),
        name="front",
    )(grid, other_grid, grid_gain.reshape(1, -1), w_kv_enc)

    parts = pl.pallas_call(
        functools.partial(partial_kernel, cap, edges),
        out_shape=jax.ShapeDtypeStruct((peers, rows, sent), bf16),
        scratch_shapes=[pltpu.VMEM((sent, nodes // 2), f32)],
        compiler_params=params(40),
        cost_estimate=cost(4 * entries * points * width, 4 * points * width),
        name="partial",
    )(asked.reshape(nodes, sent), pairs)
    parts = lax.all_to_all(parts, "dom", split_axis=0, concat_axis=0, tiled=True)

    slot_total = dec_need.shape[1]
    queries, picks = pl.pallas_call(
        functools.partial(middle_kernel, slot_total // peers, rows),
        out_shape=[
            jax.ShapeDtypeStruct((width, points), bf16),
            jax.ShapeDtypeStruct((dec_slot.shape[0], nodes, points), bf16),
        ],
        compiler_params=params(58),
        cost_estimate=cost(2 * points * depth * width, 8 * points * depth),
        name="middle",
    )(
        grid,
        grid_gain.reshape(1, -1),
        w_q_dec,
        dec_need.reshape(slot_total // LANES, LANES),
        dec_slot,
    )
    parts, queries, picks = lax.optimization_barrier((parts, queries, picks))

    latent_out, everyone = pl.pallas_call(
        combine_kernel,
        out_shape=[
            jax.ShapeDtypeStruct((rows, depth), bf16),
            jax.ShapeDtypeStruct((peers, rows, width), bf16),
        ],
        compiler_params=params(24),
        cost_estimate=cost(6 * rows * depth * width, 6 * depth * width),
        name="combine",
    )(parts, latent_in, dec_gain.reshape(1, -1), w_o_enc, w_kv_dec)
    own = lax.all_to_all(everyone, "dom", split_axis=0, concat_axis=0, tiled=True)
    own = own.reshape(nodes, width)
    other = lax.ppermute(own, "dom", swap)

    steps = points // math.gcd(points, 512)
    edge_count = dec_slot.shape[0]
    own_mixed = pl.pallas_call(
        functools.partial(own_kernel, steps),
        in_specs=[vmem, hbm, hbm],
        out_shape=jax.ShapeDtypeStruct((points, half), bf16),
        scratch_shapes=[
            pltpu.VMEM((half, points), bf16),
            pltpu.VMEM((edge_count, nodes, points), bf16),
            pltpu.SemaphoreType.DMA((2,)),
        ],
        compiler_params=params(48),
        cost_estimate=cost(4 * points * nodes * width, 8 * points * nodes),
        name="own",
    )(own, queries, picks)
    grid_out = pl.pallas_call(
        functools.partial(other_kernel, steps),
        in_specs=[vmem, vmem] + [hbm] * 4,
        out_specs=hbm,
        out_shape=jax.ShapeDtypeStruct((points, depth), bf16),
        scratch_shapes=[
            pltpu.VMEM((points, depth), bf16),
            pltpu.VMEM((half, points), bf16),
            pltpu.VMEM((edge_count, nodes, points), bf16),
            pltpu.VMEM((2, half, depth), bf16),
            pltpu.VMEM((points, depth), bf16),
            pltpu.SemaphoreType.DMA((5,)),
            pltpu.SemaphoreType.DMA((steps,)),
        ],
        compiler_params=params(48),
        cost_estimate=cost(4 * points * depth * width, 8 * points * depth),
        name="other",
    )(other, own_mixed, grid, queries, picks, w_o_dec)
    return (latent_out, grid_out)


def solution(mesh):
    return jax.shard_map(
        on_device,
        mesh=mesh,
        in_specs=(
            P(("groups", "dom"), None),
            P(("groups", "dom"), None),
            P(),
            P(),
            P(),
            P(),
            P(),
            P(),
            P(),
            P(),
            P(),
            P("dom", None),
            P(None, "dom"),
            P("dom"),
            P("dom", None),
            P(None, "dom"),
        ),
        out_specs=(P(("groups", "dom"), None), P(("groups", "dom"), None)),
        check_vma=False,
    )
```

```python
import functools
import math

import jax
import jax.numpy as jnp
from jax import lax
from jax.experimental import pallas as pl
from jax.experimental.pallas import tpu as pltpu
from jax.sharding import PartitionSpec as P

HEADS = 8
LANES = 128
NEG = -1e30
norm_eps = 1e-06
f32 = jnp.float32
bf16 = jnp.bfloat16


def iota(shape, dim):
    return lax.broadcasted_iota(jnp.int32, shape, dim)


def div(values, by):
    if by & (by - 1) == 0:
        return values >> (by.bit_length() - 1)
    return values // by


def mod(values, by):
    if by & (by - 1) == 0:
        return values & (by - 1)
    return values % by


def dot(a, b):
    return jnp.dot(a, b, preferred_element_type=f32)


def dot_t(a, b):
    return lax.dot_general(a, b, (((1,), (1,)), ((), ())), preferred_element_type=f32)


def normed(values, gain):
    widened = values.astype(f32)
    spread = jnp.mean(widened * widened, axis=-1, keepdims=True)
    return (widened * lax.rsqrt(spread + norm_eps) * gain).astype(bf16)


def params(mib):
    return pltpu.CompilerParams(vmem_limit_bytes=mib * 2**20)


def started(*copies):
    for copy in copies:
        copy.start()
    return copies


def cost(flops, read, exps=0):
    return pl.CostEstimate(flops=int(flops), bytes_accessed=int(read), transcendentals=int(exps))


def ask_kernel(
    latent_ref, gain_ref, slot_ref, count_ref, need_ref, w_hbm, out_ref, w_ref, sem
):
    copy = pltpu.make_async_copy(w_hbm, w_ref, sem)
    copy.start()
    rows = latent_ref.shape[0]
    width = w_ref.shape[1]
    entries = need_ref.shape[1]
    edges = slot_ref.shape[1]
    per = entries // rows
    rows_normed = normed(latent_ref[...], gain_ref[...])
    eye = iota((rows, rows), 0) == iota((rows, rows), 1)
    counts = jnp.sum(jnp.where(eye, count_ref[...], 0), axis=1, keepdims=True)
    slots = jnp.where(iota((rows, edges), 1) < counts, slot_ref[...], 65535)
    need = need_ref[...]
    own = div(iota((rows, entries), 1), per) == iota((rows, entries), 0)
    extra = jnp.zeros((rows, LANES), f32)
    for i, part in enumerate((slots & 255, slots >> 8)):
        to = iota((edges, LANES), 1) == iota((edges, LANES), 0) + i * edges
        extra += dot(part.astype(f32).astype(bf16), to.astype(bf16))
    for i, part in enumerate((need & 255, need >> 8)):
        to = iota((entries, LANES), 1) == mod(iota((entries, LANES), 0), per) + 2 * edges + i * per
        spread = jnp.where(own, part.astype(f32), 0.0).astype(bf16)
        extra += dot(spread, to.astype(bf16))
    copy.wait()
    queries = dot(rows_normed, w_ref[...]).astype(bf16)
    half = width // 2
    for p in range(out_ref.shape[0]):
        out_ref[p, :, :half] = queries[:, p % 2 * half : (p % 2 + 1) * half]
        out_ref[p, :, half:] = extra.astype(bf16)


def front_kernel(
    steps, other_ref, gain_ref, own_hbm, w_hbm, out_hbm, own_ref, w_ref, pairs_ref, sems, out_sems
):
    points = own_ref.shape[0]
    block = points // steps
    half = pairs_ref.shape[1] // 2
    core = lax.axis_index("dom") & 1
    copies = started(
        *[
            pltpu.make_async_copy(
                w_hbm.at[:, pl.ds(pl.multiple_of((core + 2 * i) * half, half), half)],
                w_ref.at[:, pl.ds(i * half, half)],
                sems.at[i],
            )
            for i in range(2)
        ],
        pltpu.make_async_copy(own_hbm, own_ref, sems.at[2]),
    )
    gain = gain_ref[...]
    sends = []
    for step in range(2 * steps):
        rows_ref = other_ref if step < steps else own_ref
        if step == 0:
            copies[0].wait()
            copies[1].wait()
        if step == steps:
            copies[2].wait()
        part = pl.ds(step % steps * block, block)
        place = pl.ds((step + steps) % (2 * steps) * block, block)
        pairs_ref[place, :] = dot(normed(rows_ref[part, :], gain), w_ref[...]).astype(bf16)
        sends += started(
            pltpu.make_async_copy(pairs_ref.at[place], out_hbm.at[place], out_sems.at[step])
        )
    for send in sends:
        send.wait()


def stat_parts(top, total):
    top_1 = top.astype(bf16).astype(f32)
    top_2 = (top - top_1).astype(bf16).astype(f32)
    total_1 = total.astype(bf16).astype(f32)
    return top_1, top_2, top - top_1 - top_2, total_1, total - total_1


def partial_kernel(cap, edges, asked_ref, pairs_hbm, out_ref, pairs_ref, mixed_ref, sem):
    copy = pltpu.make_async_copy(pairs_hbm, pairs_ref, sem)
    copy.start()
    me = lax.axis_index("dom")
    points, both = pairs_ref.shape
    points = points // 2
    peers, rows, _ = out_ref.shape
    width = both // 2
    heads = HEADS // 2
    size = width // heads
    per = cap * peers // rows
    scale = math.log2(math.e) / math.sqrt(size)
    all_nodes = asked_ref.shape[0]
    all_entries = peers * cap
    nodes, entries = all_nodes // 2, all_entries // 2
    pick_shape = (all_entries, all_nodes)
    pick_row = iota(pick_shape, 1) - div(iota(pick_shape, 0), cap) * rows
    lane = iota((all_entries, LANES), 1) - mod(iota((all_entries, LANES), 0), cap)
    here = div(iota((entries, nodes), 0), cap) == div(iota((entries, nodes), 1), rows)
    listed = -(-cap // 8) * 8
    repeat = iota((entries, listed), 1) == mod(iota((entries, listed), 0), cap)
    repeat = repeat.astype(f32)
    extra = asked_ref[:, width:]
    extra_t = extra.astype(f32).T
    all_slots = (extra_t[:edges] + 256.0 * extra_t[edges : 2 * edges]).astype(jnp.int32)
    chosen, biases = [], []
    for other in range(2):
        first = (me ^ other) * cap
        list_row, low_lane = div(first, per), mod(first, per) + 2 * edges
        weights = jnp.where(lane == low_lane, 1.0, jnp.where(lane == low_lane + per, 256.0, 0.0))
        lists = dot((pick_row == list_row).astype(bf16), extra)
        index = jnp.sum(lists * weights, axis=1, keepdims=True).astype(jnp.int32)
        chosen.append((index == iota((all_entries, points), 1)).astype(bf16))
        slots = all_slots - first
        uses = jnp.zeros((listed, all_nodes), f32)
        for j in range(edges):
            uses += jnp.where(slots[j : j + 1] == iota((listed, all_nodes), 0), 1.0, 0.0)
        live = uses > 0.5
        bias = jnp.where(live, jnp.log2(jnp.where(live, uses, 1.0)), NEG)
        for half in range(2):
            part = bias[:, half * nodes : (half + 1) * nodes]
            if cap == listed:
                repeated = jnp.concatenate([part] * (entries // cap), axis=0)
            else:
                repeated = lax.dot_general(
                    repeat, part, (((1,), (0,)), ((), ())), precision=lax.Precision.HIGHEST
                )
            biases.append(jnp.where(here, repeated, NEG))
    copy.wait()
    gathered = [
        dot(chosen[other], pairs_ref[other * points : (other + 1) * points, :]).astype(bf16)
        for other in range(2)
    ]
    for half in range(2):
        part = slice(half * entries, (half + 1) * entries)
        pairs = jnp.concatenate([gathered[0][part], gathered[1][part]], axis=0)
        bias = jnp.concatenate([biases[half], biases[2 + half]], axis=0)
        keys, values_t = pairs[:, :width], pairs[:, width:].T
        queries = asked_ref[half * nodes : (half + 1) * nodes, :width]
        head = div(iota(queries.shape, 1), size)
        queries = jnp.concatenate(
            [jnp.where(head == h, queries, jnp.zeros_like(queries)) for h in range(heads)], axis=0
        )
        scores = dot_t(keys, queries) * scale + jnp.concatenate([bias] * heads, axis=1)
        top = jnp.max(scores, axis=0, keepdims=True)
        raised = jnp.exp2(scores - top)
        total = jnp.sum(raised, axis=0, keepdims=True)
        raised = raised.astype(bf16)
        for h in range(0, heads, 2):
            mixed = dot(
                values_t[h * size : (h + 2) * size, :], raised[:, h * nodes : (h + 2) * nodes]
            )
            mixed_ref[h * size : (h + 1) * size, :] = mixed[:size, :nodes]
            mixed_ref[(h + 1) * size : (h + 2) * size, :] = mixed[size:, nodes:]
        by_head = [
            jnp.concatenate([one[:, h * nodes : (h + 1) * nodes] for h in range(heads)], axis=0)
            for one in (top, total)
        ]
        stats = jnp.concatenate(stat_parts(*by_head), axis=0)
        rest = mixed_ref.shape[0] - width - stats.shape[0]
        mixed_ref[width:, :] = jnp.concatenate([stats, jnp.zeros((rest, nodes), f32)], axis=0)
        result = mixed_ref[...].T.astype(bf16)
        for i in range(peers // 2):
            out_ref[half * (peers // 2) + i] = result[i * rows : (i + 1) * rows]


def read_stats(stats):
    heads = HEADS // 2
    col, head = iota((LANES, LANES), 0), iota((LANES, LANES), 1)
    head_of = mod(col, heads) == head
    take_top = head_of & (col < 3 * heads)
    take_sum = head_of & (col >= 3 * heads) & (col < 5 * heads)
    return dot(stats, take_top.astype(bf16)), dot(stats, take_sum.astype(bf16))


def spread_heads(factor, width, size):
    spread = (div(iota((LANES, width), 1), size) == iota((LANES, width), 0)).astype(bf16)
    factor_1 = factor.astype(bf16)
    factor_2 = (factor - factor_1.astype(f32)).astype(bf16)
    return dot(factor_1, spread) + dot(factor_2, spread)


def combine_kernel(parts_ref, latent_ref, gain_ref, w_o_ref, w_kv_ref, latent_out_ref, out_ref):
    peers, rows, sent = parts_ref.shape
    width = w_o_ref.shape[0]
    half = width // 2
    chips = (peers // 2, 2, rows)
    parts = parts_ref[...].reshape(peers * rows, sent)
    top, total = read_stats(parts[:, half:])
    top = top.reshape(*chips, LANES)
    factor = jnp.exp2(top - jnp.max(top, axis=0, keepdims=True))
    total = jnp.sum(total.reshape(*chips, LANES) * factor, axis=0, keepdims=True)
    used = iota((1, 2, rows, LANES), 3) < HEADS // 2
    factor = factor * jnp.where(used, 1.0 / jnp.where(used, total, 1.0), 0.0)
    wide = spread_heads(factor.reshape(peers * rows, LANES), half, width // HEADS)
    mixed = jnp.sum((parts[:, :half].astype(f32) * wide).reshape(*chips, half), axis=0)
    mixed = jnp.concatenate([mixed[0], mixed[1]], axis=1)
    update = dot(mixed.astype(bf16), w_o_ref[...])
    latent_out = (latent_ref[...].astype(f32) + update).astype(bf16)
    latent_out_ref[...] = latent_out
    pairs = dot(normed(latent_out, gain_ref[...]), w_kv_ref[...]).astype(bf16)
    for p in range(peers):
        at = p % 2 * half
        out_ref[p, :, :half] = pairs[:, at : at + half]
        out_ref[p, :, half:] = pairs[:, width + at : width + at + half]


def middle_kernel(
    steps, cap, rows, gain_ref, need_ref, slot_ref, x_hbm, w_hbm, out_hbm, node_ref,
    x_ref, w_ref, query_ref, sems, out_sems,
):
    copies = started(
        pltpu.make_async_copy(w_hbm, w_ref, sems.at[0]),
        pltpu.make_async_copy(x_hbm, x_ref, sems.at[1]),
    )
    points = x_ref.shape[0]
    block = points // steps
    high_count = need_ref.shape[0]
    need = need_ref[...].astype(f32).astype(bf16)
    for j in range(slot_ref.shape[0]):
        slots = slot_ref[j : j + 1, :]
        row_of = (div(slots, LANES) == iota((high_count, points), 0)).astype(bf16)
        listed = lax.dot_general(need, row_of, (((0,), (0,)), ((), ())), preferred_element_type=f32)
        own = mod(slots, LANES) == iota((LANES, points), 0)
        found = jnp.sum(jnp.where(own, listed, 0.0), axis=0, keepdims=True).astype(jnp.int32)
        node_ref[j : j + 1, :] = div(slots, cap) * rows + found
    for copy in copies:
        copy.wait()
    sends = []
    for i in range(steps):
        part = pl.ds(i * block, block)
        queries = dot(normed(x_ref[part, :], gain_ref[...]), w_ref[...])
        query_ref[:, part] = queries.T.astype(bf16)
        sends += started(
            pltpu.make_async_copy(query_ref.at[:, part], out_hbm.at[:, part], out_sems.at[i])
        )
    for send in sends:
        send.wait()


def attend_half(pairs, queries, nodes):
    half, points = queries.shape
    edges = nodes.shape[0]
    heads = HEADS // 2
    size = half // heads
    node = iota((pairs.shape[1], points), 0)
    picks = [(nodes[j : j + 1] == node).astype(bf16) for j in range(edges)]
    scores = []
    for j in range(edges):
        products = dot(pairs[:half], picks[j]) * queries.astype(f32)
        score = jnp.sum(products.reshape(heads, size, points), axis=1)
        scores.append(score * (1.0 / math.sqrt(size)))
    highest = functools.reduce(jnp.maximum, scores)
    raised = [jnp.exp(score - highest) for score in scores]
    inverse = 1.0 / sum(raised)
    mixed = jnp.zeros((heads, size, points), f32)
    for j in range(edges):
        weight = (raised[j] * inverse).astype(bf16).astype(f32).reshape(heads, 1, points)
        mixed += dot(pairs[half:], picks[j]).reshape(heads, size, points) * weight
    return mixed.reshape(half, points).T.astype(bf16)


def half_of(ref, first, half):
    return ref.at[pl.ds(pl.multiple_of(first, half), half)]


def own_kernel(steps, pairs_ref, node_ref, query_hbm, out_ref, query_ref, sem):
    points, half = out_ref.shape
    block = points // steps
    core = lax.axis_index("dom") & 1
    copy = pltpu.make_async_copy(half_of(query_hbm, core * half, half), query_ref, sem)
    copy.start()
    pairs = pairs_ref[...].T
    copy.wait()
    for i in range(steps):
        part = pl.ds(i * block, block)
        out_ref[part, :] = attend_half(pairs, query_ref[:, part], node_ref[:, part])


def other_kernel(
    steps, pairs_ref, own_ref, node_ref, x_ref, w_ref, query_hbm, out_hbm,
    query_ref, out_ref, sem, out_sems,
):
    points, half = own_ref.shape
    block = points // steps
    core = lax.axis_index("dom") & 1
    copy = pltpu.make_async_copy(half_of(query_hbm, (1 - core) * half, half), query_ref, sem)
    copy.start()
    pairs = pairs_ref[...].T
    own_w = half_of(w_ref, core * half, half)
    other_w = half_of(w_ref, (1 - core) * half, half)
    copy.wait()
    sends = []
    for i in range(steps):
        part = pl.ds(i * block, block)
        mixed = attend_half(pairs, query_ref[:, part], node_ref[:, part])
        update = dot(own_ref[part, :], own_w[...]) + dot(mixed, other_w[...])
        out_ref[part, :] = (x_ref[part, :].astype(f32) + update).astype(bf16)
        sends += started(
            pltpu.make_async_copy(out_ref.at[part], out_hbm.at[part], out_sems.at[i])
        )
    for send in sends:
        send.wait()


def in_hbm(array):
    return pltpu.with_memory_space_constraint(array, pltpu.HBM)


def on_device(
    grid,
    latent_in,
    grid_gain,
    node_gain,
    dec_gain,
    w_q_enc,
    w_kv_enc,
    w_o_enc,
    w_q_dec,
    w_kv_dec,
    w_o_dec,
    enc_need,
    enc_slot,
    enc_count,
    dec_need,
    dec_slot,
):
    peers = lax.axis_size("dom")
    points, depth = grid.shape
    rows = latent_in.shape[0]
    width = w_q_enc.shape[1]
    nodes = peers * rows
    entries = enc_need.shape[1]
    edges = enc_slot.shape[0]
    cap = entries // peers
    half = width // 2
    sent = half + LANES
    swap = [(i, i ^ 1) for i in range(peers)]
    vmem = pl.BlockSpec(memory_space=pltpu.VMEM)
    hbm = pl.BlockSpec(memory_space=pltpu.HBM)

    other_grid = lax.ppermute(grid, "dom", swap)
    asked = pl.pallas_call(
        ask_kernel,
        in_specs=[vmem] * 5 + [hbm],
        out_shape=jax.ShapeDtypeStruct((peers, rows, sent), bf16),
        scratch_shapes=[pltpu.VMEM((depth, width), bf16), pltpu.SemaphoreType.DMA],
        compiler_params=params(58),
        cost_estimate=cost(2 * rows * depth * width, 2 * depth * width),
        name="ask",
    )(
        latent_in,
        node_gain.reshape(1, -1),
        enc_slot.T,
        enc_count.reshape(1, -1),
        enc_need,
        in_hbm(w_q_enc),
    )
    asked = lax.all_to_all(asked, "dom", split_axis=0, concat_axis=0, tiled=True)

    block = math.gcd(points, 256)
    steps = points // block
    pairs = pl.pallas_call(
        functools.partial(front_kernel, steps),
        in_specs=[vmem, vmem, hbm, hbm],
        out_specs=hbm,
        out_shape=pltpu.HBM((2 * points, width), bf16),
        scratch_shapes=[
            pltpu.VMEM((points, depth), bf16),
            pltpu.VMEM((depth, width), bf16),
            pltpu.VMEM((2 * points, width), bf16),
            pltpu.SemaphoreType.DMA((3,)),
            pltpu.SemaphoreType.DMA((2 * steps,)),
        ],
        compiler_params=params(40),
        cost_estimate=cost(4 * points * depth * width, 8 * points * depth),
        name="front",
    )(other_grid, grid_gain.reshape(1, -1), in_hbm(grid), in_hbm(w_kv_enc))

    parts = pl.pallas_call(
        functools.partial(partial_kernel, cap, edges),
        in_specs=[vmem, hbm],
        out_shape=jax.ShapeDtypeStruct((peers, rows, sent), bf16),
        scratch_shapes=[
            pltpu.VMEM((2 * points, width), bf16),
            pltpu.VMEM((sent, nodes // 2), f32),
            pltpu.SemaphoreType.DMA,
        ],
        compiler_params=params(40),
        cost_estimate=cost(4 * entries * points * width, 4 * points * width),
        name="partial",
    )(asked.reshape(nodes, sent), in_hbm(pairs))
    parts, dec_need, dec_slot = lax.optimization_barrier((parts, dec_need, dec_slot))
    parts = lax.all_to_all(parts, "dom", split_axis=0, concat_axis=0, tiled=True)

    slot_total = dec_need.shape[1]
    edge_count = dec_slot.shape[0]
    queries, node_of = pl.pallas_call(
        functools.partial(middle_kernel, steps, slot_total // peers, rows),
        in_specs=[vmem] * 3 + [hbm] * 2,
        out_specs=[hbm, vmem],
        out_shape=[
            pltpu.HBM((width, points), bf16),
            jax.ShapeDtypeStruct((edge_count, points), jnp.int32),
        ],
        scratch_shapes=[
            pltpu.VMEM((points, depth), bf16),
            pltpu.VMEM((depth, width), bf16),
            pltpu.VMEM((width, points), bf16),
            pltpu.SemaphoreType.DMA((2,)),
            pltpu.SemaphoreType.DMA((steps,)),
        ],
        compiler_params=params(40),
        cost_estimate=cost(2 * points * depth * width, 8 * points * depth),
        name="middle",
    )(
        grid_gain.reshape(1, -1),
        dec_need.reshape(slot_total // LANES, LANES),
        dec_slot,
        in_hbm(grid),
        in_hbm(w_q_dec),
    )
    parts, queries, node_of = lax.optimization_barrier((parts, queries, node_of))

    latent_out, everyone = pl.pallas_call(
        combine_kernel,
        out_shape=[
            jax.ShapeDtypeStruct((rows, depth), bf16),
            jax.ShapeDtypeStruct((peers, rows, width), bf16),
        ],
        compiler_params=params(24),
        cost_estimate=cost(6 * rows * depth * width, 6 * depth * width),
        name="combine",
    )(parts, latent_in, dec_gain.reshape(1, -1), w_o_enc, w_kv_dec)
    own = lax.all_to_all(everyone, "dom", split_axis=0, concat_axis=0, tiled=True)
    own = own.reshape(nodes, width)
    other = lax.ppermute(own, "dom", swap)

    own_mixed = pl.pallas_call(
        functools.partial(own_kernel, max(steps // 2, 1)),
        in_specs=[vmem, vmem, hbm],
        out_shape=jax.ShapeDtypeStruct((points, half), bf16),
        scratch_shapes=[pltpu.VMEM((half, points), bf16), pltpu.SemaphoreType.DMA],
        compiler_params=params(48),
        cost_estimate=cost(4 * points * nodes * width, 8 * points * nodes),
        name="own",
    )(own, node_of, in_hbm(queries))
    grid_out = pl.pallas_call(
        functools.partial(other_kernel, steps),
        in_specs=[vmem] * 5 + [hbm],
        out_specs=hbm,
        out_shape=pltpu.HBM((points, depth), bf16),
        scratch_shapes=[
            pltpu.VMEM((half, points), bf16),
            pltpu.VMEM((points, depth), bf16),
            pltpu.SemaphoreType.DMA,
            pltpu.SemaphoreType.DMA((steps,)),
        ],
        compiler_params=params(48),
        cost_estimate=cost(4 * points * depth * width, 8 * points * depth),
        name="other",
    )(other, own_mixed, node_of, grid, w_o_dec, in_hbm(queries))
    return (latent_out, grid_out)


def solution(mesh):
    return jax.shard_map(
        on_device,
        mesh=mesh,
        in_specs=(
            P(("groups", "dom"), None),
            P(("groups", "dom"), None),
            P(),
            P(),
            P(),
            P(),
            P(),
            P(),
            P(),
            P(),
            P(),
            P("dom", None),
            P(None, "dom"),
            P("dom"),
            P("dom", None),
            P(None, "dom"),
        ),
        out_specs=(P(("groups", "dom"), None), P(("groups", "dom"), None)),
        check_vma=False,
    )
```

```python
import functools
import math

import jax
import jax.numpy as jnp
from jax import lax
from jax.experimental import pallas as pl
from jax.experimental.pallas import tpu as pltpu
from jax.sharding import PartitionSpec as P

HEADS = 8
LANES = 128
NEG = -1e30
norm_eps = 1e-06
f32 = jnp.float32
bf16 = jnp.bfloat16


def iota(shape, dim):
    return lax.broadcasted_iota(jnp.int32, shape, dim)


def div(values, by):
    if by & (by - 1) == 0:
        return values >> (by.bit_length() - 1)
    return values // by


def mod(values, by):
    if by & (by - 1) == 0:
        return values & (by - 1)
    return values % by


def dot(a, b):
    return jnp.dot(a, b, preferred_element_type=f32)


def dot_t(a, b):
    return lax.dot_general(a, b, (((1,), (1,)), ((), ())), preferred_element_type=f32)


def normed(values, gain):
    widened = values.astype(f32)
    spread = jnp.mean(widened * widened, axis=-1, keepdims=True)
    return (widened * lax.rsqrt(spread + norm_eps) * gain).astype(bf16)


def params(mib):
    return pltpu.CompilerParams(vmem_limit_bytes=mib * 2**20)


def started(*copies):
    for copy in copies:
        copy.start()
    return copies


def cost(flops, read, exps=0):
    return pl.CostEstimate(flops=int(flops), bytes_accessed=int(read), transcendentals=int(exps))


def ask_kernel(*refs):
    sources, out_ref, held, sems = refs[:6], refs[6], refs[7:13], refs[13]
    copies = started(
        *[
            pltpu.make_async_copy(source, ref, sems.at[i])
            for i, (source, ref) in enumerate(zip(sources, held))
        ]
    )
    w_ref, latent_ref, gain_ref, slot_ref, count_ref, need_ref = held
    rows = latent_ref.shape[0]
    width = w_ref.shape[1]
    entries = need_ref.shape[1]
    edges = slot_ref.shape[1]
    per = entries // rows
    for copy in copies[1:]:
        copy.wait()
    rows_normed = normed(latent_ref[...], gain_ref[...])
    eye = iota((rows, rows), 0) == iota((rows, rows), 1)
    counts = jnp.sum(jnp.where(eye, count_ref[...], 0), axis=1, keepdims=True)
    slots = jnp.where(iota((rows, edges), 1) < counts, slot_ref[...], 65535)
    need = need_ref[...]
    own = div(iota((rows, entries), 1), per) == iota((rows, entries), 0)
    extra = jnp.zeros((rows, LANES), f32)
    for i, part in enumerate((slots & 255, slots >> 8)):
        to = iota((edges, LANES), 1) == iota((edges, LANES), 0) + i * edges
        extra += dot(part.astype(f32).astype(bf16), to.astype(bf16))
    for i, part in enumerate((need & 255, need >> 8)):
        to = iota((entries, LANES), 1) == mod(iota((entries, LANES), 0), per) + 2 * edges + i * per
        spread = jnp.where(own, part.astype(f32), 0.0).astype(bf16)
        extra += dot(spread, to.astype(bf16))
    copies[0].wait()
    queries = dot(rows_normed, w_ref[...]).astype(bf16)
    half = width // 2
    for p in range(out_ref.shape[0]):
        out_ref[p, :, :half] = queries[:, p % 2 * half : (p % 2 + 1) * half]
        out_ref[p, :, half:] = extra.astype(bf16)


def front_kernel(
    steps, other_ref, gain_hbm, own_hbm, w_hbm, pairs_ref, gain_ref, own_ref, w_ref, sems
):
    points = own_ref.shape[0]
    block = points // steps
    half = pairs_ref.shape[1] // 2
    core = lax.axis_index("dom") & 1
    copies = started(
        pltpu.make_async_copy(gain_hbm, gain_ref, sems.at[0]),
        *[
            pltpu.make_async_copy(
                w_hbm.at[:, pl.ds(pl.multiple_of((core + 2 * i) * half, half), half)],
                w_ref.at[:, pl.ds(i * half, half)],
                sems.at[1 + i],
            )
            for i in range(2)
        ],
        pltpu.make_async_copy(own_hbm, own_ref, sems.at[3]),
    )
    for copy in copies[:3]:
        copy.wait()
    gain = gain_ref[...]
    for start, rows_ref in ((points, other_ref), (0, own_ref)):
        if start == 0:
            copies[3].wait()
        for i in range(steps):
            rows = normed(rows_ref[pl.ds(i * block, block), :], gain)
            place = pl.ds(start + i * block, block)
            pairs_ref[place, :] = dot(rows, w_ref[...]).astype(bf16)


def stat_parts(top, total):
    top_1 = top.astype(bf16).astype(f32)
    top_2 = (top - top_1).astype(bf16).astype(f32)
    total_1 = total.astype(bf16).astype(f32)
    return top_1, top_2, top - top_1 - top_2, total_1, total - total_1


def partial_kernel(cap, edges, asked_ref, pairs_ref, out_ref, mixed_ref):
    me = lax.axis_index("dom")
    points, both = pairs_ref.shape
    points = points // 2
    peers, rows, _ = out_ref.shape
    width = both // 2
    heads = HEADS // 2
    size = width // heads
    per = cap * peers // rows
    scale = math.log2(math.e) / math.sqrt(size)
    all_nodes = asked_ref.shape[0]
    all_entries = peers * cap
    nodes, entries = all_nodes // 2, all_entries // 2
    pick_shape = (all_entries, all_nodes)
    pick_row = iota(pick_shape, 1) - div(iota(pick_shape, 0), cap) * rows
    lane = iota((all_entries, LANES), 1) - mod(iota((all_entries, LANES), 0), cap)
    here = div(iota((entries, nodes), 0), cap) == div(iota((entries, nodes), 1), rows)
    listed = -(-cap // 8) * 8
    repeat = iota((entries, listed), 1) == mod(iota((entries, listed), 0), cap)
    repeat = repeat.astype(f32)
    extra = asked_ref[:, width:]
    extra_t = extra.astype(f32).T
    all_slots = (extra_t[:edges] + 256.0 * extra_t[edges : 2 * edges]).astype(jnp.int32)
    chosen, biases = [], []
    for other in range(2):
        first = (me ^ other) * cap
        list_row, low_lane = div(first, per), mod(first, per) + 2 * edges
        weights = jnp.where(lane == low_lane, 1.0, jnp.where(lane == low_lane + per, 256.0, 0.0))
        lists = dot((pick_row == list_row).astype(bf16), extra)
        index = jnp.sum(lists * weights, axis=1, keepdims=True).astype(jnp.int32)
        chosen.append((index == iota((all_entries, points), 1)).astype(bf16))
        slots = all_slots - first
        uses = jnp.zeros((listed, all_nodes), f32)
        for j in range(edges):
            uses += jnp.where(slots[j : j + 1] == iota((listed, all_nodes), 0), 1.0, 0.0)
        live = uses > 0.5
        bias = jnp.where(live, jnp.log2(jnp.where(live, uses, 1.0)), NEG)
        for half in range(2):
            part = bias[:, half * nodes : (half + 1) * nodes]
            if cap == listed:
                repeated = jnp.concatenate([part] * (entries // cap), axis=0)
            else:
                repeated = lax.dot_general(
                    repeat, part, (((1,), (0,)), ((), ())), precision=lax.Precision.HIGHEST
                )
            biases.append(jnp.where(here, repeated, NEG))
    gathered = [
        dot(chosen[other], pairs_ref[other * points : (other + 1) * points, :]).astype(bf16)
        for other in range(2)
    ]
    for half in range(2):
        part = slice(half * entries, (half + 1) * entries)
        pairs = jnp.concatenate([gathered[0][part], gathered[1][part]], axis=0)
        bias = jnp.concatenate([biases[half], biases[2 + half]], axis=0)
        keys, values_t = pairs[:, :width], pairs[:, width:].T
        queries = asked_ref[half * nodes : (half + 1) * nodes, :width]
        head = div(iota(queries.shape, 1), size)
        queries = jnp.concatenate(
            [jnp.where(head == h, queries, jnp.zeros_like(queries)) for h in range(heads)], axis=0
        )
        scores = dot_t(keys, queries) * scale + jnp.concatenate([bias] * heads, axis=1)
        top = jnp.max(scores, axis=0, keepdims=True)
        raised = jnp.exp2(scores - top)
        total = jnp.sum(raised, axis=0, keepdims=True)
        raised = raised.astype(bf16)
        for h in range(0, heads, 2):
            mixed = dot(
                values_t[h * size : (h + 2) * size, :], raised[:, h * nodes : (h + 2) * nodes]
            )
            mixed_ref[h * size : (h + 1) * size, :] = mixed[:size, :nodes]
            mixed_ref[(h + 1) * size : (h + 2) * size, :] = mixed[size:, nodes:]
        by_head = [
            jnp.concatenate([one[:, h * nodes : (h + 1) * nodes] for h in range(heads)], axis=0)
            for one in (top, total)
        ]
        stats = jnp.concatenate(stat_parts(*by_head), axis=0)
        rest = mixed_ref.shape[0] - width - stats.shape[0]
        mixed_ref[width:, :] = jnp.concatenate([stats, jnp.zeros((rest, nodes), f32)], axis=0)
        result = mixed_ref[...].T.astype(bf16)
        for i in range(peers // 2):
            out_ref[half * (peers // 2) + i] = result[i * rows : (i + 1) * rows]


def read_stats(stats):
    heads = HEADS // 2
    col, head = iota((LANES, LANES), 0), iota((LANES, LANES), 1)
    head_of = mod(col, heads) == head
    take_top = head_of & (col < 3 * heads)
    take_sum = head_of & (col >= 3 * heads) & (col < 5 * heads)
    return dot(stats, take_top.astype(bf16)), dot(stats, take_sum.astype(bf16))


def spread_heads(factor, width, size):
    spread = (div(iota((LANES, width), 1), size) == iota((LANES, width), 0)).astype(bf16)
    factor_1 = factor.astype(bf16)
    factor_2 = (factor - factor_1.astype(f32)).astype(bf16)
    return dot(factor_1, spread) + dot(factor_2, spread)


def combine_kernel(parts_ref, latent_ref, gain_ref, w_o_ref, w_kv_ref, latent_out_ref, out_ref):
    peers, rows, sent = parts_ref.shape
    width = w_o_ref.shape[0]
    half = width // 2
    chips = (peers // 2, 2, rows)
    parts = parts_ref[...].reshape(peers * rows, sent)
    top, total = read_stats(parts[:, half:])
    top = top.reshape(*chips, LANES)
    factor = jnp.exp2(top - jnp.max(top, axis=0, keepdims=True))
    total = jnp.sum(total.reshape(*chips, LANES) * factor, axis=0, keepdims=True)
    used = iota((1, 2, rows, LANES), 3) < HEADS // 2
    factor = factor * jnp.where(used, 1.0 / jnp.where(used, total, 1.0), 0.0)
    wide = spread_heads(factor.reshape(peers * rows, LANES), half, width // HEADS)
    mixed = jnp.sum((parts[:, :half].astype(f32) * wide).reshape(*chips, half), axis=0)
    mixed = jnp.concatenate([mixed[0], mixed[1]], axis=1)
    update = dot(mixed.astype(bf16), w_o_ref[...])
    latent_out = (latent_ref[...].astype(f32) + update).astype(bf16)
    latent_out_ref[...] = latent_out
    pairs = dot(normed(latent_out, gain_ref[...]), w_kv_ref[...]).astype(bf16)
    for p in range(peers):
        at = p % 2 * half
        out_ref[p, :, :half] = pairs[:, at : at + half]
        out_ref[p, :, half:] = pairs[:, width + at : width + at + half]


def middle_kernel(
    steps, cap, rows, gain_ref, need_ref, slot_ref, x_hbm, w_hbm, query_ref, node_ref,
    x_ref, w_ref, sems,
):
    copies = started(
        pltpu.make_async_copy(w_hbm, w_ref, sems.at[0]),
        pltpu.make_async_copy(x_hbm, x_ref, sems.at[1]),
    )
    points = x_ref.shape[0]
    block = points // steps
    high_count = need_ref.shape[0]
    need = need_ref[...].astype(f32).astype(bf16)
    for j in range(slot_ref.shape[0]):
        slots = slot_ref[j : j + 1, :]
        row_of = (div(slots, LANES) == iota((high_count, points), 0)).astype(bf16)
        listed = lax.dot_general(need, row_of, (((0,), (0,)), ((), ())), preferred_element_type=f32)
        own = mod(slots, LANES) == iota((LANES, points), 0)
        found = jnp.sum(jnp.where(own, listed, 0.0), axis=0, keepdims=True).astype(jnp.int32)
        node_ref[j : j + 1, :] = div(slots, cap) * rows + found
    for copy in copies:
        copy.wait()
    for i in range(steps):
        part = pl.ds(i * block, block)
        queries = dot(normed(x_ref[part, :], gain_ref[...]), w_ref[...])
        query_ref[:, part] = queries.T.astype(bf16)


def attend_half(pairs, queries, nodes):
    half, points = queries.shape
    edges = nodes.shape[0]
    heads = HEADS // 2
    size = half // heads
    node = iota((pairs.shape[1], points), 0)
    picks = [(nodes[j : j + 1] == node).astype(bf16) for j in range(edges)]
    scores, values = [], []
    for j in range(edges):
        chosen = dot(pairs, picks[j])
        products = (chosen[:half] * queries.astype(f32)).reshape(heads, size, points)
        scores.append(jnp.sum(products, axis=1) * (1.0 / math.sqrt(size)))
        values.append(chosen[half:].reshape(heads, size, points))
    highest = functools.reduce(jnp.maximum, scores)
    raised = [jnp.exp(score - highest) for score in scores]
    inverse = 1.0 / sum(raised)
    mixed = jnp.zeros((heads, size, points), f32)
    for j in range(edges):
        weight = (raised[j] * inverse).astype(bf16).astype(f32).reshape(heads, 1, points)
        mixed += values[j] * weight
    return mixed.reshape(half, points).T.astype(bf16)


def half_of(ref, first, half):
    return ref.at[pl.ds(pl.multiple_of(first, half), half)]


def own_kernel(steps, pairs_ref, node_ref, query_ref, out_ref):
    points, half = out_ref.shape
    block = points // steps
    core = lax.axis_index("dom") & 1
    queries = half_of(query_ref, core * half, half)
    pairs = pairs_ref[...].T
    for i in range(steps):
        part = pl.ds(i * block, block)
        out_ref[part, :] = attend_half(pairs, queries[:, part], node_ref[:, part])


def other_kernel(
    steps, pairs_ref, own_ref, node_ref, query_ref, x_ref, w_ref, out_hbm, out_ref, sems
):
    points, half = own_ref.shape
    block = points // steps
    core = lax.axis_index("dom") & 1
    queries = half_of(query_ref, (1 - core) * half, half)
    own_w = half_of(w_ref, core * half, half)
    other_w = half_of(w_ref, (1 - core) * half, half)
    pairs = pairs_ref[...].T
    sends = []
    for i in range(steps):
        part = pl.ds(i * block, block)
        mixed = attend_half(pairs, queries[:, part], node_ref[:, part])
        update = dot(own_ref[part, :], own_w[...]) + dot(mixed, other_w[...])
        out_ref[part, :] = (x_ref[part, :].astype(f32) + update).astype(bf16)
        sends += started(pltpu.make_async_copy(out_ref.at[part], out_hbm.at[part], sems.at[i]))
    for send in sends:
        send.wait()


def in_hbm(array):
    return pltpu.with_memory_space_constraint(array, pltpu.HBM)


def in_vmem(array):
    return pltpu.with_memory_space_constraint(array, pltpu.VMEM)


def on_device(
    grid,
    latent_in,
    grid_gain,
    node_gain,
    dec_gain,
    w_q_enc,
    w_kv_enc,
    w_o_enc,
    w_q_dec,
    w_kv_dec,
    w_o_dec,
    enc_need,
    enc_slot,
    enc_count,
    dec_need,
    dec_slot,
):
    peers = lax.axis_size("dom")
    points, depth = grid.shape
    rows = latent_in.shape[0]
    width = w_q_enc.shape[1]
    nodes = peers * rows
    entries = enc_need.shape[1]
    edges = enc_slot.shape[0]
    cap = entries // peers
    half = width // 2
    sent = half + LANES
    swap = [(i, i ^ 1) for i in range(peers)]
    vmem = pl.BlockSpec(memory_space=pltpu.VMEM)
    hbm = pl.BlockSpec(memory_space=pltpu.HBM)

    other_grid = lax.ppermute(grid, "dom", swap)
    ask_inputs = (
        w_q_enc,
        latent_in,
        node_gain.reshape(1, -1),
        enc_slot.T,
        enc_count.reshape(1, -1),
        enc_need,
    )
    asked = pl.pallas_call(
        ask_kernel,
        in_specs=[hbm] * len(ask_inputs),
        out_shape=jax.ShapeDtypeStruct((peers, rows, sent), bf16),
        scratch_shapes=[pltpu.VMEM(one.shape, one.dtype) for one in ask_inputs]
        + [pltpu.SemaphoreType.DMA((len(ask_inputs),))],
        compiler_params=params(58),
        cost_estimate=cost(2 * rows * depth * width, 2 * depth * width),
        name="ask",
    )(*map(in_hbm, ask_inputs))
    asked = lax.all_to_all(asked, "dom", split_axis=0, concat_axis=0, tiled=True)

    block = math.gcd(points, 256)
    steps = points // block
    pairs = pl.pallas_call(
        functools.partial(front_kernel, steps),
        in_specs=[vmem, hbm, hbm, hbm],
        out_specs=vmem,
        out_shape=pltpu.VMEM((2 * points, width), bf16),
        scratch_shapes=[
            pltpu.VMEM((1, depth), f32),
            pltpu.VMEM((points, depth), bf16),
            pltpu.VMEM((depth, width), bf16),
            pltpu.SemaphoreType.DMA((4,)),
        ],
        compiler_params=params(40),
        cost_estimate=cost(4 * points * depth * width, 8 * points * depth),
        name="front",
    )(other_grid, in_hbm(grid_gain.reshape(1, -1)), in_hbm(grid), in_hbm(w_kv_enc))

    parts = pl.pallas_call(
        functools.partial(partial_kernel, cap, edges),
        in_specs=[vmem, vmem],
        out_shape=jax.ShapeDtypeStruct((peers, rows, sent), bf16),
        scratch_shapes=[pltpu.VMEM((sent, nodes // 2), f32)],
        compiler_params=params(40),
        cost_estimate=cost(4 * entries * points * width, 4 * points * width),
        name="partial",
    )(asked.reshape(nodes, sent), in_vmem(pairs))
    parts, dec_need, dec_slot = lax.optimization_barrier((parts, dec_need, dec_slot))
    parts = lax.all_to_all(parts, "dom", split_axis=0, concat_axis=0, tiled=True)

    slot_total = dec_need.shape[1]
    edge_count = dec_slot.shape[0]
    queries, node_of = pl.pallas_call(
        functools.partial(middle_kernel, steps, slot_total // peers, rows),
        in_specs=[vmem] * 3 + [hbm] * 2,
        out_specs=[vmem, vmem],
        out_shape=[
            pltpu.VMEM((width, points), bf16),
            jax.ShapeDtypeStruct((edge_count, points), jnp.int32),
        ],
        scratch_shapes=[
            pltpu.VMEM((points, depth), bf16),
            pltpu.VMEM((depth, width), bf16),
            pltpu.SemaphoreType.DMA((2,)),
        ],
        compiler_params=params(40),
        cost_estimate=cost(2 * points * depth * width, 8 * points * depth),
        name="middle",
    )(
        grid_gain.reshape(1, -1),
        dec_need.reshape(slot_total // LANES, LANES),
        dec_slot,
        in_hbm(grid),
        in_hbm(w_q_dec),
    )
    parts, queries, node_of = lax.optimization_barrier((parts, queries, node_of))

    latent_out, everyone = pl.pallas_call(
        combine_kernel,
        out_shape=[
            jax.ShapeDtypeStruct((rows, depth), bf16),
            jax.ShapeDtypeStruct((peers, rows, width), bf16),
        ],
        compiler_params=params(24),
        cost_estimate=cost(6 * rows * depth * width, 6 * depth * width),
        name="combine",
    )(parts, latent_in, dec_gain.reshape(1, -1), w_o_enc, w_kv_dec)
    own = lax.all_to_all(everyone, "dom", split_axis=0, concat_axis=0, tiled=True)
    own = own.reshape(nodes, width)
    other = lax.ppermute(own, "dom", swap)

    queries = in_vmem(queries)
    own_mixed = pl.pallas_call(
        functools.partial(own_kernel, steps),
        in_specs=[vmem] * 3,
        out_shape=jax.ShapeDtypeStruct((points, half), bf16),
        compiler_params=params(48),
        cost_estimate=cost(4 * points * nodes * width, 8 * points * nodes),
        name="own",
    )(own, node_of, queries)
    grid_out = pl.pallas_call(
        functools.partial(other_kernel, steps),
        in_specs=[vmem] * 6,
        out_specs=hbm,
        out_shape=pltpu.HBM((points, depth), bf16),
        scratch_shapes=[
            pltpu.VMEM((points, depth), bf16),
            pltpu.SemaphoreType.DMA((steps,)),
        ],
        compiler_params=params(48),
        cost_estimate=cost(4 * points * depth * width, 8 * points * depth),
        name="other",
    )(other, own_mixed, node_of, queries, grid, w_o_dec)
    return (latent_out, grid_out)


def solution(mesh):
    return jax.shard_map(
        on_device,
        mesh=mesh,
        in_specs=(
            P(("groups", "dom"), None),
            P(("groups", "dom"), None),
            P(),
            P(),
            P(),
            P(),
            P(),
            P(),
            P(),
            P(),
            P(),
            P("dom", None),
            P(None, "dom"),
            P("dom"),
            P("dom", None),
            P(None, "dom"),
        ),
        out_specs=(P(("groups", "dom"), None), P(("groups", "dom"), None)),
        check_vma=False,
    )
```

```python
import functools
import math

import jax
import jax.numpy as jnp
from jax import lax
from jax.experimental import pallas as pl
from jax.experimental.pallas import tpu as pltpu
from jax.sharding import PartitionSpec as P

HEADS = 8
LANES = 128
NEG = -1e30
norm_eps = 1e-06
f32 = jnp.float32
bf16 = jnp.bfloat16


def iota(shape, dim):
    return lax.broadcasted_iota(jnp.int32, shape, dim)


def div(values, by):
    if by & (by - 1) == 0:
        return values >> (by.bit_length() - 1)
    return values // by


def mod(values, by):
    if by & (by - 1) == 0:
        return values & (by - 1)
    return values % by


def dot(a, b):
    return jnp.dot(a, b, preferred_element_type=f32)


def dot_t(a, b):
    return lax.dot_general(a, b, (((1,), (1,)), ((), ())), preferred_element_type=f32)


def normed(values, gain):
    widened = values.astype(f32)
    spread = jnp.mean(widened * widened, axis=-1, keepdims=True)
    return (widened * lax.rsqrt(spread + norm_eps) * gain).astype(bf16)


def params(mib):
    return pltpu.CompilerParams(vmem_limit_bytes=mib * 2**20)


def started(*copies):
    for copy in copies:
        copy.start()
    return copies


def cost(flops, read, exps=0):
    return pl.CostEstimate(flops=int(flops), bytes_accessed=int(read), transcendentals=int(exps))


def columns_of(ref, where, rows, half):
    return [ref[where, i * rows : (i + 1) * rows, :] for i in range(half // LANES)]


def ask_kernel(*refs):
    sources, out_ref, held, sems = refs[:6], refs[6], refs[7:13], refs[13]
    copies = started(
        *[
            pltpu.make_async_copy(source, ref, sems.at[i])
            for i, (source, ref) in enumerate(zip(sources, held))
        ]
    )
    w_ref, latent_ref, gain_ref, slot_ref, count_ref, need_ref = held
    rows = latent_ref.shape[0]
    width = w_ref.shape[1]
    entries = need_ref.shape[1]
    edges = slot_ref.shape[1]
    peers = out_ref.shape[0]
    both = 2 * entries // peers
    tall = rows // 2
    for copy in copies[1:]:
        copy.wait()
    rows_normed = normed(latent_ref[...], gain_ref[...])
    live = iota((edges, rows), 0) < count_ref[...]
    slots = slot_ref[...].astype(f32).T.astype(jnp.int32)
    slots = jnp.where(live, slots, entries) - entries // 2
    slots = slots.astype(f32).astype(bf16)
    tile = jnp.zeros((tall, LANES), f32)
    for g in range(edges // tall):
        to = iota((rows, LANES), 1) == iota((rows, LANES), 0) + g * rows
        tile += dot(slots, to.astype(bf16))[g * tall : (g + 1) * tall]
    row, lane = iota((tall, LANES), 0), iota((tall, LANES), 1)
    in_list = (lane >= LANES // 2) & (lane < LANES // 2 + both)
    need = need_ref[...]
    tiles = []
    for chip in range(peers // 2):
        at = chip * both
        piece = need[:, at // LANES * LANES : at // LANES * LANES + LANES].astype(f32)
        piece = pltpu.roll(jnp.broadcast_to(piece, (tall, LANES)), (LANES // 2 - at) % LANES, 1)
        high = jnp.floor(piece * (1.0 / 256.0))
        piece = jnp.where(row == 0, piece - high * 256.0, jnp.where(row == 1, high, 0.0))
        tiles.append((tile + jnp.where(in_list, piece, 0.0)).astype(bf16))
    copies[0].wait()
    queries = dot(rows_normed, w_ref[...]).astype(bf16)
    half = width // 2
    for p in range(peers):
        for i in range(half // LANES):
            at = p % 2 * half + i * LANES
            out_ref[p, i * rows : (i + 1) * rows, :] = queries[:, at : at + LANES]
        out_ref[p, half // LANES * rows :, :] = tiles[p // 2]


def front_kernel(
    steps, gain_hbm, own_hbm, other_hbm, w_hbm, own_out_ref, other_out_ref,
    gain_ref, own_ref, other_ref, w_ref, sems,
):
    points = own_ref.shape[0]
    block = points // steps
    half = own_out_ref.shape[1] // 2
    core = lax.axis_index("dom") & 1
    copies = started(
        pltpu.make_async_copy(gain_hbm, gain_ref, sems.at[0]),
        *[
            pltpu.make_async_copy(
                w_hbm.at[:, pl.ds(pl.multiple_of((core + 2 * i) * half, half), half)],
                w_ref.at[:, pl.ds(i * half, half)],
                sems.at[1 + i],
            )
            for i in range(2)
        ],
        pltpu.make_async_copy(own_hbm, own_ref, sems.at[3]),
        pltpu.make_async_copy(other_hbm, other_ref, sems.at[4]),
    )
    for copy in copies[:3]:
        copy.wait()
    gain = gain_ref[...]
    for copy, rows_ref, out_ref in (
        (copies[3], own_ref, own_out_ref),
        (copies[4], other_ref, other_out_ref),
    ):
        copy.wait()
        for i in range(steps):
            part = pl.ds(i * block, block)
            out_ref[part, :] = dot(normed(rows_ref[part, :], gain), w_ref[...]).astype(bf16)


def stat_parts(top, total):
    top_1 = top.astype(bf16).astype(f32)
    top_2 = (top - top_1).astype(bf16).astype(f32)
    total_1 = total.astype(bf16).astype(f32)
    return top_1, top_2, top - top_1 - top_2, total_1, total - total_1


def partial_kernel(cap, rows, edges, asked_ref, *refs):
    pairs_refs, out_ref, mixed_ref = refs[:2], refs[2], refs[3]
    me = lax.axis_index("dom")
    points, both = pairs_refs[0].shape
    peers = out_ref.shape[0]
    width = both // 2
    heads = HEADS // 2
    size = width // heads
    tall = rows // 2
    stack = width // LANES * rows
    scale = math.log2(math.e) / math.sqrt(size)
    all_nodes, all_entries = peers * rows, peers * cap
    nodes, entries = all_nodes // 2, all_entries // 2
    tiles = asked_ref[:, stack:, :].astype(f32)

    group, across = div(iota((tall, LANES), 1), rows), LANES // rows
    slots = []
    for g in range(edges // tall):
        line = []
        for first in range(0, peers, across):
            merged = jnp.zeros((tall, LANES), f32)
            for w in range(across):
                merged = jnp.where(
                    group == w, pltpu.roll(tiles[first + w], (w - g) * rows % LANES, 1), merged
                )
            line.append(merged)
        slots.append(jnp.concatenate(line, axis=1))
    all_slots = jnp.concatenate(slots, axis=0).astype(jnp.int32) + all_entries // 2

    tile_rows = peers * tall
    pick_row = iota((all_entries, tile_rows), 1) - div(iota((all_entries, tile_rows), 0), cap) * tall
    pick = jnp.where(pick_row == 0, 1.0, jnp.where(pick_row == 1, 256.0, 0.0)).astype(bf16)
    lists = dot(pick, tiles.reshape(tile_rows, LANES).astype(bf16))
    lane = iota((all_entries, LANES), 1) - mod(iota((all_entries, LANES), 0), cap) - LANES // 2
    here = div(iota((entries, nodes), 0), cap) == div(iota((entries, nodes), 1), rows)
    listed = -(-cap // 8) * 8
    repeat = iota((entries, listed), 1) == mod(iota((entries, listed), 0), cap)
    repeat = repeat.astype(f32)
    chosen, biases = [], []
    for other in range(2):
        band = me ^ other
        mine = lane == (band & 1) * cap
        index = jnp.sum(jnp.where(mine, lists, 0.0), axis=1, keepdims=True).astype(jnp.int32)
        chosen.append((index == iota((all_entries, points), 1)).astype(bf16))
        slots = all_slots - band * cap
        uses = jnp.zeros((listed, all_nodes), f32)
        for j in range(edges):
            uses += jnp.where(slots[j : j + 1] == iota((listed, all_nodes), 0), 1.0, 0.0)
        live = uses > 0.5
        bias = jnp.where(live, jnp.log2(jnp.where(live, uses, 1.0)), NEG)
        for half in range(2):
            part = bias[:, half * nodes : (half + 1) * nodes]
            if cap == listed:
                repeated = jnp.concatenate([part] * (entries // cap), axis=0)
            else:
                repeated = lax.dot_general(
                    repeat, part, (((1,), (0,)), ((), ())), precision=lax.Precision.HIGHEST
                )
            biases.append(jnp.where(here, repeated, NEG))
    gathered = [dot(one, ref[...]).astype(bf16) for one, ref in zip(chosen, pairs_refs)]
    for half in range(2):
        part = slice(half * entries, (half + 1) * entries)
        pairs = jnp.concatenate([gathered[0][part], gathered[1][part]], axis=0)
        bias = jnp.concatenate([biases[half], biases[2 + half]], axis=0)
        keys, values_t = pairs[:, :width], pairs[:, width:].T
        windows = slice(half * (peers // 2), (half + 1) * (peers // 2))
        queries = [one.reshape(nodes, LANES) for one in columns_of(asked_ref, windows, rows, width)]
        queries = jnp.concatenate(queries, axis=1)
        head = div(iota(queries.shape, 1), size)
        queries = jnp.concatenate(
            [jnp.where(head == h, queries, jnp.zeros_like(queries)) for h in range(heads)], axis=0
        )
        scores = dot_t(keys, queries) * scale + jnp.concatenate([bias] * heads, axis=1)
        top = jnp.max(scores, axis=0, keepdims=True)
        raised = jnp.exp2(scores - top)
        total = jnp.sum(raised, axis=0, keepdims=True)
        raised = raised.astype(bf16)
        for h in range(0, heads, 2):
            mixed = dot(
                values_t[h * size : (h + 2) * size, :], raised[:, h * nodes : (h + 2) * nodes]
            )
            mixed_ref[h * size : (h + 1) * size, :] = mixed[:size, :nodes]
            mixed_ref[(h + 1) * size : (h + 2) * size, :] = mixed[size:, nodes:]
        by_head = [
            jnp.concatenate([one[:, h * nodes : (h + 1) * nodes] for h in range(heads)], axis=0)
            for one in (top, total)
        ]
        stats = jnp.concatenate(stat_parts(*by_head), axis=0)
        rest = mixed_ref.shape[0] - width - stats.shape[0]
        mixed_ref[width:, :] = jnp.concatenate([stats, jnp.zeros((rest, nodes), f32)], axis=0)
        result = mixed_ref[...].T
        mixed = result[:, :width].astype(bf16)
        for i in range(peers // 2):
            place = half * (peers // 2) + i
            for j in range(width // LANES):
                out_ref[place, j * rows : (j + 1) * rows, :] = mixed[
                    i * rows : (i + 1) * rows, j * LANES : (j + 1) * LANES
                ]
            upper = result[i * rows : i * rows + tall, width:]
            lower = result[i * rows + tall : (i + 1) * rows, width:]
            out_ref[place, stack:, :] = (upper + pltpu.roll(lower, LANES // 2, 1)).astype(bf16)


def read_stats(stats):
    heads = HEADS // 2
    col, head = iota((LANES, LANES), 0), iota((LANES, LANES), 1)
    head_of = mod(col, heads) == head
    take_top = head_of & (col < 3 * heads)
    take_sum = head_of & (col >= 3 * heads) & (col < 5 * heads)
    return dot(stats, take_top.astype(bf16)), dot(stats, take_sum.astype(bf16))


def spread_heads(factor, width, size):
    spread = (div(iota((LANES, width), 1), size) == iota((LANES, width), 0)).astype(bf16)
    factor_1 = factor.astype(bf16)
    factor_2 = (factor - factor_1.astype(f32)).astype(bf16)
    return dot(factor_1, spread) + dot(factor_2, spread)


def combine_kernel(parts_ref, latent_ref, gain_ref, w_o_ref, w_kv_ref, latent_out_ref, out_ref):
    peers = parts_ref.shape[0]
    rows = latent_ref.shape[0]
    width = w_o_ref.shape[0]
    half = width // 2
    chips = (peers // 2, 2, rows)
    parts = [
        one.reshape(peers * rows, LANES) for one in columns_of(parts_ref, slice(None), rows, half)
    ]
    parts = jnp.concatenate(parts, axis=1).astype(f32)
    tile = parts_ref[:, half // LANES * rows :, :].astype(f32)
    stats = jnp.concatenate([tile, pltpu.roll(tile, LANES // 2, 2)], axis=1)
    top, total = read_stats(stats.reshape(peers * rows, LANES).astype(bf16))
    top = top.reshape(*chips, LANES)
    factor = jnp.exp2(top - jnp.max(top, axis=0, keepdims=True))
    total = jnp.sum(total.reshape(*chips, LANES) * factor, axis=0, keepdims=True)
    used = iota((1, 2, rows, LANES), 3) < HEADS // 2
    factor = factor * jnp.where(used, 1.0 / jnp.where(used, total, 1.0), 0.0)
    wide = spread_heads(factor.reshape(peers * rows, LANES), half, width // HEADS)
    mixed = jnp.sum((parts * wide).reshape(*chips, half), axis=0)
    mixed = jnp.concatenate([mixed[0], mixed[1]], axis=1)
    update = dot(mixed.astype(bf16), w_o_ref[...])
    latent_out = (latent_ref[...].astype(f32) + update).astype(bf16)
    latent_out_ref[...] = latent_out
    pairs = dot(normed(latent_out, gain_ref[...]), w_kv_ref[...]).astype(bf16)
    for p in range(peers):
        at = p % 2 * half
        out_ref[p, :, :half] = pairs[:, at : at + half]
        out_ref[p, :, half:] = pairs[:, width + at : width + at + half]


def middle_kernel(
    steps, cap, rows, gain_ref, need_ref, slot_ref, x_hbm, w_hbm, query_ref, node_ref,
    x_ref, w_ref, sems,
):
    copies = started(
        pltpu.make_async_copy(w_hbm, w_ref, sems.at[0]),
        pltpu.make_async_copy(x_hbm, x_ref, sems.at[1]),
    )
    points = x_ref.shape[0]
    block = points // steps
    high_count = need_ref.shape[0]
    need = need_ref[...].astype(f32).astype(bf16)
    for j in range(slot_ref.shape[0]):
        slots = slot_ref[j : j + 1, :]
        row_of = (div(slots, LANES) == iota((high_count, points), 0)).astype(bf16)
        listed = lax.dot_general(need, row_of, (((0,), (0,)), ((), ())), preferred_element_type=f32)
        own = mod(slots, LANES) == iota((LANES, points), 0)
        found = jnp.sum(jnp.where(own, listed, 0.0), axis=0, keepdims=True).astype(jnp.int32)
        node_ref[j : j + 1, :] = div(slots, cap) * rows + found
    for copy in copies:
        copy.wait()
    for i in range(steps):
        part = pl.ds(i * block, block)
        queries = dot(normed(x_ref[part, :], gain_ref[...]), w_ref[...])
        query_ref[:, part] = queries.T.astype(bf16)


def attend_half(pairs, queries, nodes):
    half, points = queries.shape
    edges = nodes.shape[0]
    heads = HEADS // 2
    size = half // heads
    node = iota((pairs.shape[1], points), 0)
    picks = [(nodes[j : j + 1] == node).astype(bf16) for j in range(edges)]
    scores, values = [], []
    for j in range(edges):
        chosen = dot(pairs, picks[j])
        products = (chosen[:half] * queries.astype(f32)).reshape(heads, size, points)
        scores.append(jnp.sum(products, axis=1) * (1.0 / math.sqrt(size)))
        values.append(chosen[half:].reshape(heads, size, points))
    highest = functools.reduce(jnp.maximum, scores)
    raised = [jnp.exp(score - highest) for score in scores]
    inverse = 1.0 / sum(raised)
    mixed = jnp.zeros((heads, size, points), f32)
    for j in range(edges):
        weight = (raised[j] * inverse).astype(bf16).astype(f32).reshape(heads, 1, points)
        mixed += values[j] * weight
    return mixed.reshape(half, points).T.astype(bf16)


def half_of(ref, first, half):
    return ref.at[pl.ds(pl.multiple_of(first, half), half)]


def own_kernel(steps, pairs_ref, node_ref, query_ref, out_ref):
    points, half = out_ref.shape
    block = points // steps
    core = lax.axis_index("dom") & 1
    queries = half_of(query_ref, core * half, half)
    pairs = pairs_ref[...].T
    for i in range(steps):
        part = pl.ds(i * block, block)
        out_ref[part, :] = attend_half(pairs, queries[:, part], node_ref[:, part])


def other_kernel(
    steps, pairs_ref, own_ref, node_ref, query_ref, x_ref, w_ref, out_hbm, out_ref, sems
):
    points, half = own_ref.shape
    block = points // steps
    core = lax.axis_index("dom") & 1
    queries = half_of(query_ref, (1 - core) * half, half)
    own_w = half_of(w_ref, core * half, half)
    other_w = half_of(w_ref, (1 - core) * half, half)
    pairs = pairs_ref[...].T
    sends = []
    for i in range(steps):
        part = pl.ds(i * block, block)
        mixed = attend_half(pairs, queries[:, part], node_ref[:, part])
        update = dot(own_ref[part, :], own_w[...]) + dot(mixed, other_w[...])
        out_ref[part, :] = (x_ref[part, :].astype(f32) + update).astype(bf16)
        sends += started(pltpu.make_async_copy(out_ref.at[part], out_hbm.at[part], sems.at[i]))
    for send in sends:
        send.wait()


def in_hbm(array):
    return pltpu.with_memory_space_constraint(array, pltpu.HBM)


def in_vmem(array):
    return pltpu.with_memory_space_constraint(array, pltpu.VMEM)


def on_device(
    grid,
    latent_in,
    grid_gain,
    node_gain,
    dec_gain,
    w_q_enc,
    w_kv_enc,
    w_o_enc,
    w_q_dec,
    w_kv_dec,
    w_o_dec,
    enc_need,
    enc_slot,
    enc_count,
    dec_need,
    dec_slot,
):
    peers = lax.axis_size("dom")
    points, depth = grid.shape
    rows = latent_in.shape[0]
    width = w_q_enc.shape[1]
    nodes = peers * rows
    entries = enc_need.shape[1]
    edges = enc_slot.shape[0]
    cap = entries // peers
    half = width // 2
    sent = (peers, half // LANES * rows + rows // 2, LANES)
    swap = [(i, i ^ 1) for i in range(peers)]
    vmem = pl.BlockSpec(memory_space=pltpu.VMEM)
    hbm = pl.BlockSpec(memory_space=pltpu.HBM)

    other_grid = lax.ppermute(grid, "dom", swap)
    ask_inputs = (
        w_q_enc,
        latent_in,
        node_gain.reshape(1, -1),
        enc_slot.T,
        enc_count.reshape(1, -1),
        enc_need,
    )
    asked = pl.pallas_call(
        ask_kernel,
        in_specs=[hbm] * len(ask_inputs),
        out_shape=jax.ShapeDtypeStruct(sent, bf16),
        scratch_shapes=[pltpu.VMEM(one.shape, one.dtype) for one in ask_inputs]
        + [pltpu.SemaphoreType.DMA((len(ask_inputs),))],
        compiler_params=params(63),
        cost_estimate=cost(2 * rows * depth * width, 2 * depth * width),
        name="ask",
    )(*map(in_hbm, ask_inputs))
    asked = lax.all_to_all(asked, "dom", split_axis=0, concat_axis=0, tiled=True)

    block = math.gcd(points, 256)
    steps = points // block
    pairs = pl.pallas_call(
        functools.partial(front_kernel, steps),
        in_specs=[hbm] * 4,
        out_specs=[vmem] * 2,
        out_shape=[pltpu.VMEM((points, width), bf16)] * 2,
        scratch_shapes=[
            pltpu.VMEM((1, depth), f32),
            pltpu.VMEM((points, depth), bf16),
            pltpu.VMEM((points, depth), bf16),
            pltpu.VMEM((depth, width), bf16),
            pltpu.SemaphoreType.DMA((5,)),
        ],
        compiler_params=params(40),
        cost_estimate=cost(4 * points * depth * width, 8 * points * depth),
        name="front",
    )(*map(in_hbm, (grid_gain.reshape(1, -1), grid, other_grid, w_kv_enc)))

    parts = pl.pallas_call(
        functools.partial(partial_kernel, cap, rows, edges),
        in_specs=[vmem] * 3,
        out_shape=jax.ShapeDtypeStruct(sent, bf16),
        scratch_shapes=[pltpu.VMEM((half + LANES, nodes // 2), f32)],
        compiler_params=params(40),
        cost_estimate=cost(4 * entries * points * width, 4 * points * width),
        name="partial",
    )(asked, *map(in_vmem, pairs))
    parts, dec_need, dec_slot = lax.optimization_barrier((parts, dec_need, dec_slot))
    parts = lax.all_to_all(parts, "dom", split_axis=0, concat_axis=0, tiled=True)

    slot_total = dec_need.shape[1]
    edge_count = dec_slot.shape[0]
    queries, node_of = pl.pallas_call(
        functools.partial(middle_kernel, steps, slot_total // peers, rows),
        in_specs=[vmem] * 3 + [hbm] * 2,
        out_specs=[vmem, vmem],
        out_shape=[
            pltpu.VMEM((width, points), bf16),
            jax.ShapeDtypeStruct((edge_count, points), jnp.int32),
        ],
        scratch_shapes=[
            pltpu.VMEM((points, depth), bf16),
            pltpu.VMEM((depth, width), bf16),
            pltpu.SemaphoreType.DMA((2,)),
        ],
        compiler_params=params(40),
        cost_estimate=cost(2 * points * depth * width, 8 * points * depth),
        name="middle",
    )(
        grid_gain.reshape(1, -1),
        dec_need.reshape(slot_total // LANES, LANES),
        dec_slot,
        in_hbm(grid),
        in_hbm(w_q_dec),
    )
    parts, queries, node_of = lax.optimization_barrier((parts, queries, node_of))

    latent_out, everyone = pl.pallas_call(
        combine_kernel,
        out_shape=[
            jax.ShapeDtypeStruct((rows, depth), bf16),
            jax.ShapeDtypeStruct((peers, rows, width), bf16),
        ],
        compiler_params=params(24),
        cost_estimate=cost(6 * rows * depth * width, 6 * depth * width),
        name="combine",
    )(parts, latent_in, dec_gain.reshape(1, -1), w_o_enc, w_kv_dec)
    own = lax.all_to_all(everyone, "dom", split_axis=0, concat_axis=0, tiled=True)
    own = own.reshape(nodes, width)
    other = lax.ppermute(own, "dom", swap)

    queries = in_vmem(queries)
    own_mixed = pl.pallas_call(
        functools.partial(own_kernel, steps),
        in_specs=[vmem] * 3,
        out_shape=jax.ShapeDtypeStruct((points, half), bf16),
        compiler_params=params(48),
        cost_estimate=cost(4 * points * nodes * width, 8 * points * nodes),
        name="own",
    )(own, node_of, queries)
    grid_out = pl.pallas_call(
        functools.partial(other_kernel, steps),
        in_specs=[vmem] * 6,
        out_specs=hbm,
        out_shape=pltpu.HBM((points, depth), bf16),
        scratch_shapes=[
            pltpu.VMEM((points, depth), bf16),
            pltpu.SemaphoreType.DMA((steps,)),
        ],
        compiler_params=params(48),
        cost_estimate=cost(4 * points * depth * width, 8 * points * depth),
        name="other",
    )(other, own_mixed, node_of, queries, grid, w_o_dec)
    return (latent_out, grid_out)


def solution(mesh):
    return jax.shard_map(
        on_device,
        mesh=mesh,
        in_specs=(
            P(("groups", "dom"), None),
            P(("groups", "dom"), None),
            P(),
            P(),
            P(),
            P(),
            P(),
            P(),
            P(),
            P(),
            P(),
            P("dom", None),
            P(None, "dom"),
            P("dom"),
            P("dom", None),
            P(None, "dom"),
        ),
        out_specs=(P(("groups", "dom"), None), P(("groups", "dom"), None)),
        check_vma=False,
    )
```

```python
import functools
import math

import jax
import jax.numpy as jnp
from jax import lax
from jax.experimental import pallas as pl
from jax.experimental.pallas import tpu as pltpu
from jax.sharding import PartitionSpec as P

HEADS = 8
LANES = 128
NEG = -1e30
norm_eps = 1e-06
f32 = jnp.float32
bf16 = jnp.bfloat16


def iota(shape, dim):
    return lax.broadcasted_iota(jnp.int32, shape, dim)


def div(values, by):
    if by & (by - 1) == 0:
        return values >> (by.bit_length() - 1)
    return values // by


def mod(values, by):
    if by & (by - 1) == 0:
        return values & (by - 1)
    return values % by


def dot(a, b):
    return jnp.dot(a, b, preferred_element_type=f32)


def dot_t(a, b):
    return lax.dot_general(a, b, (((1,), (1,)), ((), ())), preferred_element_type=f32)


def normed(values, gain):
    widened = values.astype(f32)
    spread = jnp.mean(widened * widened, axis=-1, keepdims=True)
    return (widened * lax.rsqrt(spread + norm_eps) * gain).astype(bf16)


def params(mib):
    return pltpu.CompilerParams(vmem_limit_bytes=mib * 2**20)


def started(*copies):
    for copy in copies:
        copy.start()
    return copies


def cost(flops, read, exps=0):
    return pl.CostEstimate(flops=int(flops), bytes_accessed=int(read), transcendentals=int(exps))


def place_of(index, peers):
    if isinstance(index, int):
        return (index + index % 2 * (peers // 2)) % peers
    return mod(index + (index & 1) * (peers // 2), peers)


def exchange(blocks, peers):
    order = [place_of(i, peers) for i in range(peers)]
    return lax.all_to_all(
        blocks, "dom", split_axis=0, concat_axis=0, tiled=True, axis_index_groups=[order]
    )


def columns_of(ref, where, rows, half):
    return [ref[where, i * rows : (i + 1) * rows, :] for i in range(half // LANES)]


def ask_kernel(*refs):
    sources, out_ref, held, sems = refs[:6], refs[6], refs[7:13], refs[13]
    copies = started(
        *[
            pltpu.make_async_copy(source, ref, sems.at[i])
            for i, (source, ref) in enumerate(zip(sources, held))
        ]
    )
    w_ref, latent_ref, gain_ref, slot_ref, count_ref, need_ref = held
    rows = latent_ref.shape[0]
    width = w_ref.shape[1]
    entries = need_ref.shape[1]
    edges = slot_ref.shape[1]
    peers = out_ref.shape[0]
    both = 2 * entries // peers
    tall = rows // 2
    for copy in copies[1:]:
        copy.wait()
    rows_normed = normed(latent_ref[...], gain_ref[...])
    live = iota((edges, rows), 0) < count_ref[...]
    slots = slot_ref[...].astype(f32).T.astype(jnp.int32)
    slots = jnp.where(live, slots, entries) - entries // 2
    slots = slots.astype(f32).astype(bf16)
    tile = jnp.zeros((tall, LANES), f32)
    for g in range(edges // tall):
        to = iota((rows, LANES), 1) == iota((rows, LANES), 0) + g * rows
        tile += dot(slots, to.astype(bf16))[g * tall : (g + 1) * tall]
    row, lane = iota((tall, LANES), 0), iota((tall, LANES), 1)
    in_list = (lane >= LANES // 2) & (lane < LANES // 2 + both)
    need = need_ref[...]
    tiles = []
    for chip in range(peers // 2):
        at = chip * both
        piece = need[:, at // LANES * LANES : at // LANES * LANES + LANES].astype(f32)
        piece = pltpu.roll(jnp.broadcast_to(piece, (tall, LANES)), (LANES // 2 - at) % LANES, 1)
        high = jnp.floor(piece * (1.0 / 256.0))
        piece = jnp.where(row == 0, piece - high * 256.0, jnp.where(row == 1, high, 0.0))
        tiles.append((tile + jnp.where(in_list, piece, 0.0)).astype(bf16))
    copies[0].wait()
    queries = dot(rows_normed, w_ref[...]).astype(bf16)
    half = width // 2
    for p in range(peers):
        for i in range(half // LANES):
            at = p % 2 * half + i * LANES
            out_ref[p, i * rows : (i + 1) * rows, :] = queries[:, at : at + LANES]
        out_ref[p, half // LANES * rows :, :] = tiles[place_of(p, peers) // 2]


def front_kernel(
    steps, gain_hbm, own_hbm, other_hbm, w_hbm, own_out_ref, other_out_ref,
    gain_ref, own_ref, other_ref, w_ref, sems,
):
    points = own_ref.shape[0]
    block = points // steps
    half = own_out_ref.shape[1] // 2
    core = lax.axis_index("dom") & 1
    copies = started(
        pltpu.make_async_copy(gain_hbm, gain_ref, sems.at[0]),
        *[
            pltpu.make_async_copy(
                w_hbm.at[:, pl.ds(pl.multiple_of((core + 2 * i) * half, half), half)],
                w_ref.at[:, pl.ds(i * half, half)],
                sems.at[1 + i],
            )
            for i in range(2)
        ],
    )
    parts = [pl.ds(i * block, block) for i in range(steps)]
    sides = ((own_hbm, own_ref, own_out_ref), (other_hbm, other_ref, other_out_ref))
    rows = started(
        *[
            pltpu.make_async_copy(hbm.at[part], ref.at[part], sems.at[3 + side * steps + i])
            for side, (hbm, ref, _) in enumerate(sides)
            for i, part in enumerate(parts)
        ]
    )
    for copy in copies:
        copy.wait()
    gain = gain_ref[...]
    for side, (_, ref, out_ref) in enumerate(sides):
        for i, part in enumerate(parts):
            rows[side * steps + i].wait()
            out_ref[part, :] = dot(normed(ref[part, :], gain), w_ref[...]).astype(bf16)


def stat_parts(top, total):
    top_1 = top.astype(bf16).astype(f32)
    top_2 = (top - top_1).astype(bf16).astype(f32)
    total_1 = total.astype(bf16).astype(f32)
    return top_1, top_2, top - top_1 - top_2, total_1, total - total_1


def partial_kernel(cap, rows, edges, asked_ref, *refs):
    pairs_refs, out_ref, mixed_ref = refs[:2], refs[2], refs[3]
    me = lax.axis_index("dom")
    points, both = pairs_refs[0].shape
    peers = out_ref.shape[0]
    width = both // 2
    heads = HEADS // 2
    size = width // heads
    tall = rows // 2
    stack = width // LANES * rows
    scale = math.log2(math.e) / math.sqrt(size)
    all_nodes, all_entries = peers * rows, peers * cap
    nodes, entries = all_nodes // 2, all_entries // 2
    tiles = asked_ref[:, stack:, :].astype(f32)

    tile_rows = peers * tall
    pick_row = iota((all_entries, tile_rows), 1) - div(iota((all_entries, tile_rows), 0), cap) * tall
    pick = jnp.where(pick_row == 0, 1.0, jnp.where(pick_row == 1, 256.0, 0.0)).astype(bf16)
    lists = dot(pick, tiles.reshape(tile_rows, LANES).astype(bf16))
    lane = iota((all_entries, LANES), 1) - mod(iota((all_entries, LANES), 0), cap) - LANES // 2
    gathered = []
    for other, ref in enumerate(pairs_refs):
        mine = lane == ((me ^ other) & 1) * cap
        index = jnp.sum(jnp.where(mine, lists, 0.0), axis=1, keepdims=True).astype(jnp.int32)
        chosen = (index == iota((all_entries, points), 1)).astype(bf16)
        gathered.append(dot(chosen, ref[...]).astype(bf16))

    group, across = div(iota((tall, LANES), 1), rows), LANES // rows
    slots = []
    for g in range(edges // tall):
        line = []
        for first in range(0, peers, across):
            merged = jnp.zeros((tall, LANES), f32)
            for w in range(across):
                merged = jnp.where(
                    group == w, pltpu.roll(tiles[first + w], (w - g) * rows % LANES, 1), merged
                )
            line.append(merged)
        slots.append(jnp.concatenate(line, axis=1))
    all_slots = jnp.concatenate(slots, axis=0).astype(jnp.int32) + all_entries // 2

    here = div(iota((entries, nodes), 0), cap) == div(iota((entries, nodes), 1), rows)
    listed = -(-cap // 8) * 8
    repeat = iota((entries, listed), 1) == mod(iota((entries, listed), 0), cap)
    repeat = repeat.astype(f32)
    biases = []
    for other in range(2):
        slots = all_slots - (me ^ other) * cap
        uses = jnp.zeros((listed, all_nodes), f32)
        for j in range(edges):
            uses += jnp.where(slots[j : j + 1] == iota((listed, all_nodes), 0), 1.0, 0.0)
        live = uses > 0.5
        bias = jnp.where(live, jnp.log2(jnp.where(live, uses, 1.0)), NEG)
        for half in range(2):
            part = bias[:, half * nodes : (half + 1) * nodes]
            if cap == listed:
                repeated = jnp.concatenate([part] * (entries // cap), axis=0)
            else:
                repeated = lax.dot_general(
                    repeat, part, (((1,), (0,)), ((), ())), precision=lax.Precision.HIGHEST
                )
            biases.append(jnp.where(here, repeated, NEG))
    for half in range(2):
        part = slice(half * entries, (half + 1) * entries)
        pairs = jnp.concatenate([gathered[0][part], gathered[1][part]], axis=0)
        bias = jnp.concatenate([biases[half], biases[2 + half]], axis=0)
        keys, values_t = pairs[:, :width], pairs[:, width:].T
        windows = slice(half * (peers // 2), (half + 1) * (peers // 2))
        queries = [one.reshape(nodes, LANES) for one in columns_of(asked_ref, windows, rows, width)]
        queries = jnp.concatenate(queries, axis=1)
        head = div(iota(queries.shape, 1), size)
        queries = jnp.concatenate(
            [jnp.where(head == h, queries, jnp.zeros_like(queries)) for h in range(heads)], axis=0
        )
        scores = dot_t(keys, queries) * scale + jnp.concatenate([bias] * heads, axis=1)
        top = jnp.max(scores, axis=0, keepdims=True)
        raised = jnp.exp2(scores - top)
        total = jnp.sum(raised, axis=0, keepdims=True)
        raised = raised.astype(bf16)
        for h in range(0, heads, 2):
            mixed = dot(
                values_t[h * size : (h + 2) * size, :], raised[:, h * nodes : (h + 2) * nodes]
            )
            mixed_ref[h * size : (h + 1) * size, :] = mixed[:size, :nodes]
            mixed_ref[(h + 1) * size : (h + 2) * size, :] = mixed[size:, nodes:]
        by_head = [
            jnp.concatenate([one[:, h * nodes : (h + 1) * nodes] for h in range(heads)], axis=0)
            for one in (top, total)
        ]
        stats = jnp.concatenate(stat_parts(*by_head), axis=0)
        rest = mixed_ref.shape[0] - width - stats.shape[0]
        mixed_ref[width:, :] = jnp.concatenate([stats, jnp.zeros((rest, nodes), f32)], axis=0)
        result = mixed_ref[...].T
        mixed = result[:, :width].astype(bf16)
        for i in range(peers // 2):
            place = half * (peers // 2) + i
            for j in range(width // LANES):
                out_ref[place, j * rows : (j + 1) * rows, :] = mixed[
                    i * rows : (i + 1) * rows, j * LANES : (j + 1) * LANES
                ]
            upper = result[i * rows : i * rows + tall, width:]
            lower = result[i * rows + tall : (i + 1) * rows, width:]
            out_ref[place, stack:, :] = (upper + pltpu.roll(lower, LANES // 2, 1)).astype(bf16)


def combine_kernel(parts_ref, latent_ref, gain_ref, w_o_ref, w_kv_ref, latent_out_ref, out_ref):
    peers = parts_ref.shape[0]
    rows = latent_ref.shape[0]
    width = w_o_ref.shape[0]
    half = width // 2
    heads, size, tall = HEADS // 2, width // HEADS, rows // 2
    chips = (peers // 2, 2, tall, LANES)
    tile = parts_ref[:, half // LANES * rows :, :].astype(f32)

    def moved(columns):
        return pltpu.roll(tile, LANES - columns, 2)

    top = (tile + moved(heads) + moved(2 * heads)).reshape(chips)
    total = (moved(3 * heads) + moved(4 * heads)).reshape(chips)
    factor = jnp.exp2(top - jnp.max(top, axis=0, keepdims=True))
    factor = factor / jnp.sum(total * factor, axis=0, keepdims=True)
    head = div(iota(chips, 3), size)
    blocks = []
    for i, block in enumerate(columns_of(parts_ref, slice(None), rows, half)):
        block = block.astype(f32)
        nodes = []
        for g in range(2):
            wide = jnp.zeros(chips, f32)
            for h in range(LANES // size):
                at = g * (LANES // 2) + i * (LANES // size) + h
                wide = jnp.where(head == h, factor[..., at : at + 1], wide)
            part = block[:, g * tall : (g + 1) * tall].reshape(chips)
            nodes.append(jnp.sum(part * wide, axis=0))
        blocks.append(jnp.concatenate(nodes, axis=1))
    mixed = jnp.concatenate([block[h] for h in range(2) for block in blocks], axis=1)
    update = dot(mixed.astype(bf16), w_o_ref[...])
    latent_out = (latent_ref[...].astype(f32) + update).astype(bf16)
    latent_out_ref[...] = latent_out
    pairs = dot(normed(latent_out, gain_ref[...]), w_kv_ref[...]).astype(bf16)
    for p in range(peers):
        at = p % 2 * half
        out_ref[p, :, :half] = pairs[:, at : at + half]
        out_ref[p, :, half:] = pairs[:, width + at : width + at + half]


def middle_kernel(
    steps, peers, rows, gain_ref, need_ref, slot_ref, x_hbm, w_hbm, query_ref, node_ref,
    x_ref, w_ref, sems,
):
    copies = started(
        pltpu.make_async_copy(w_hbm, w_ref, sems.at[0]),
        pltpu.make_async_copy(x_hbm, x_ref, sems.at[1]),
    )
    points = x_ref.shape[0]
    block = points // steps
    high_count = need_ref.shape[0]
    cap = high_count * LANES // peers
    need = need_ref[...].astype(f32).astype(bf16)
    for j in range(slot_ref.shape[0]):
        slots = slot_ref[j : j + 1, :]
        row_of = (div(slots, LANES) == iota((high_count, points), 0)).astype(bf16)
        listed = lax.dot_general(need, row_of, (((0,), (0,)), ((), ())), preferred_element_type=f32)
        own = mod(slots, LANES) == iota((LANES, points), 0)
        found = jnp.sum(jnp.where(own, listed, 0.0), axis=0, keepdims=True).astype(jnp.int32)
        node_ref[j : j + 1, :] = place_of(div(slots, cap), peers) * rows + found
    for copy in copies:
        copy.wait()
    for i in range(steps):
        part = pl.ds(i * block, block)
        queries = dot(normed(x_ref[part, :], gain_ref[...]), w_ref[...])
        query_ref[:, part] = queries.T.astype(bf16)


def attend_half(pairs, queries, nodes):
    half, points = queries.shape
    edges = nodes.shape[0]
    heads = HEADS // 2
    size = half // heads
    node = iota((pairs.shape[1], points), 0)
    picks = [(nodes[j : j + 1] == node).astype(bf16) for j in range(edges)]
    scores, values = [], []
    for j in range(edges):
        chosen = dot(pairs, picks[j])
        products = (chosen[:half] * queries.astype(f32)).reshape(heads, size, points)
        scores.append(jnp.sum(products, axis=1) * (1.0 / math.sqrt(size)))
        values.append(chosen[half:].reshape(heads, size, points))
    highest = functools.reduce(jnp.maximum, scores)
    raised = [jnp.exp(score - highest) for score in scores]
    inverse = 1.0 / sum(raised)
    mixed = jnp.zeros((heads, size, points), f32)
    for j in range(edges):
        weight = (raised[j] * inverse).astype(bf16).astype(f32).reshape(heads, 1, points)
        mixed += values[j] * weight
    return mixed.reshape(half, points).T.astype(bf16)


def half_of(ref, first, half):
    return ref.at[pl.ds(pl.multiple_of(first, half), half)]


def own_kernel(steps, pairs_ref, node_ref, query_ref, out_ref):
    points, half = out_ref.shape
    block = points // steps
    core = lax.axis_index("dom") & 1
    queries = half_of(query_ref, core * half, half)
    pairs = pairs_ref[...].T
    for i in range(steps):
        part = pl.ds(i * block, block)
        out_ref[part, :] = attend_half(pairs, queries[:, part], node_ref[:, part])


def other_kernel(
    steps, pairs_ref, own_ref, node_ref, query_ref, x_ref, w_ref, out_hbm, out_ref, sems
):
    points, half = own_ref.shape
    block = points // steps
    core = lax.axis_index("dom") & 1
    queries = half_of(query_ref, (1 - core) * half, half)
    pairs = pairs_ref[...].T
    sends = []
    for i in range(steps):
        part = pl.ds(i * block, block)
        mixed = attend_half(pairs, queries[:, part], node_ref[:, part])
        own = own_ref[part, :]
        both = [jnp.where(core == 0, own, mixed), jnp.where(core == 0, mixed, own)]
        update = dot(jnp.concatenate(both, axis=1), w_ref[...])
        out_ref[part, :] = (x_ref[part, :].astype(f32) + update).astype(bf16)
        sends += started(pltpu.make_async_copy(out_ref.at[part], out_hbm.at[part], sems.at[i]))
    for send in sends:
        send.wait()


def in_hbm(array):
    return pltpu.with_memory_space_constraint(array, pltpu.HBM)


def in_vmem(array):
    return pltpu.with_memory_space_constraint(array, pltpu.VMEM)


def on_device(
    grid,
    latent_in,
    grid_gain,
    node_gain,
    dec_gain,
    w_q_enc,
    w_kv_enc,
    w_o_enc,
    w_q_dec,
    w_kv_dec,
    w_o_dec,
    enc_need,
    enc_slot,
    enc_count,
    dec_need,
    dec_slot,
):
    peers = lax.axis_size("dom")
    points, depth = grid.shape
    rows = latent_in.shape[0]
    width = w_q_enc.shape[1]
    nodes = peers * rows
    entries = enc_need.shape[1]
    edges = enc_slot.shape[0]
    cap = entries // peers
    half = width // 2
    sent = (peers, half // LANES * rows + rows // 2, LANES)
    swap = [(i, i ^ 1) for i in range(peers)]
    vmem = pl.BlockSpec(memory_space=pltpu.VMEM)
    hbm = pl.BlockSpec(memory_space=pltpu.HBM)

    other_grid = lax.ppermute(grid, "dom", swap)
    ask_inputs = (
        w_q_enc,
        latent_in,
        node_gain.reshape(1, -1),
        enc_slot.T,
        enc_count.reshape(1, -1),
        enc_need,
    )
    asked = pl.pallas_call(
        ask_kernel,
        in_specs=[hbm] * len(ask_inputs),
        out_shape=jax.ShapeDtypeStruct(sent, bf16),
        scratch_shapes=[pltpu.VMEM(one.shape, one.dtype) for one in ask_inputs]
        + [pltpu.SemaphoreType.DMA((len(ask_inputs),))],
        compiler_params=params(63),
        cost_estimate=cost(2 * rows * depth * width, 2 * depth * width),
        name="ask",
    )(*map(in_hbm, ask_inputs))
    asked = exchange(asked, peers)

    block = math.gcd(points, 256)
    steps = points // block
    pairs = pl.pallas_call(
        functools.partial(front_kernel, steps),
        in_specs=[hbm] * 4,
        out_specs=[vmem] * 2,
        out_shape=[pltpu.VMEM((points, width), bf16)] * 2,
        scratch_shapes=[
            pltpu.VMEM((1, depth), f32),
            pltpu.VMEM((points, depth), bf16),
            pltpu.VMEM((points, depth), bf16),
            pltpu.VMEM((depth, width), bf16),
            pltpu.SemaphoreType.DMA((3 + 2 * steps,)),
        ],
        compiler_params=params(40),
        cost_estimate=cost(4 * points * depth * width, 8 * points * depth),
        name="front",
    )(*map(in_hbm, (grid_gain.reshape(1, -1), grid, other_grid, w_kv_enc)))

    parts = pl.pallas_call(
        functools.partial(partial_kernel, cap, rows, edges),
        in_specs=[vmem] * 3,
        out_shape=jax.ShapeDtypeStruct(sent, bf16),
        scratch_shapes=[pltpu.VMEM((half + LANES, nodes // 2), f32)],
        compiler_params=params(40),
        cost_estimate=cost(4 * entries * points * width, 4 * points * width),
        name="partial",
    )(asked, *map(in_vmem, pairs))
    parts, dec_need, dec_slot = lax.optimization_barrier((parts, dec_need, dec_slot))
    parts = exchange(parts, peers)

    slot_total = dec_need.shape[1]
    edge_count = dec_slot.shape[0]
    queries, node_of = pl.pallas_call(
        functools.partial(middle_kernel, steps, peers, rows),
        in_specs=[vmem] * 3 + [hbm] * 2,
        out_specs=[vmem, vmem],
        out_shape=[
            pltpu.VMEM((width, points), bf16),
            jax.ShapeDtypeStruct((edge_count, points), jnp.int32),
        ],
        scratch_shapes=[
            pltpu.VMEM((points, depth), bf16),
            pltpu.VMEM((depth, width), bf16),
            pltpu.SemaphoreType.DMA((2,)),
        ],
        compiler_params=params(40),
        cost_estimate=cost(2 * points * depth * width, 8 * points * depth),
        name="middle",
    )(
        grid_gain.reshape(1, -1),
        dec_need.reshape(slot_total // LANES, LANES),
        dec_slot,
        in_hbm(grid),
        in_hbm(w_q_dec),
    )
    parts, queries, node_of = lax.optimization_barrier((parts, queries, node_of))

    latent_out, everyone = pl.pallas_call(
        combine_kernel,
        out_shape=[
            jax.ShapeDtypeStruct((rows, depth), bf16),
            jax.ShapeDtypeStruct((peers, rows, width), bf16),
        ],
        compiler_params=params(24),
        cost_estimate=cost(6 * rows * depth * width, 6 * depth * width),
        name="combine",
    )(parts, latent_in, dec_gain.reshape(1, -1), w_o_enc, w_kv_dec)
    own = exchange(everyone, peers).reshape(nodes, width)
    other = lax.ppermute(own, "dom", swap)

    queries = in_vmem(queries)
    own_mixed = pl.pallas_call(
        functools.partial(own_kernel, steps),
        in_specs=[vmem] * 3,
        out_shape=jax.ShapeDtypeStruct((points, half), bf16),
        compiler_params=params(48),
        cost_estimate=cost(4 * points * nodes * width, 8 * points * nodes),
        name="own",
    )(own, node_of, queries)
    grid_out = pl.pallas_call(
        functools.partial(other_kernel, steps),
        in_specs=[vmem] * 6,
        out_specs=hbm,
        out_shape=pltpu.HBM((points, depth), bf16),
        scratch_shapes=[
            pltpu.VMEM((points, depth), bf16),
            pltpu.SemaphoreType.DMA((steps,)),
        ],
        compiler_params=params(48),
        cost_estimate=cost(4 * points * depth * width, 8 * points * depth),
        name="other",
    )(other, own_mixed, node_of, queries, grid, w_o_dec)
    return (latent_out, grid_out)


def solution(mesh):
    return jax.shard_map(
        on_device,
        mesh=mesh,
        in_specs=(
            P(("groups", "dom"), None),
            P(("groups", "dom"), None),
            P(),
            P(),
            P(),
            P(),
            P(),
            P(),
            P(),
            P(),
            P(),
            P("dom", None),
            P(None, "dom"),
            P("dom"),
            P("dom", None),
            P(None, "dom"),
        ),
        out_specs=(P(("groups", "dom"), None), P(("groups", "dom"), None)),
        check_vma=False,
    )
```

```python
import functools
import math

import jax
import jax.numpy as jnp
from jax import lax
from jax.experimental import pallas as pl
from jax.experimental.pallas import tpu as pltpu
from jax.sharding import PartitionSpec as P

HEADS = 8
LANES = 128
NEG = -1e30
norm_eps = 1e-06
f32 = jnp.float32
bf16 = jnp.bfloat16


def iota(shape, dim):
    return lax.broadcasted_iota(jnp.int32, shape, dim)


def div(values, by):
    if by & (by - 1) == 0:
        return values >> (by.bit_length() - 1)
    return values // by


def mod(values, by):
    if by & (by - 1) == 0:
        return values & (by - 1)
    return values % by


def dot(a, b):
    return jnp.dot(a, b, preferred_element_type=f32)


def dot_t(a, b):
    return lax.dot_general(a, b, (((1,), (1,)), ((), ())), preferred_element_type=f32)


def normed(values, gain):
    widened = values.astype(f32)
    spread = jnp.mean(widened * widened, axis=-1, keepdims=True)
    return (widened * lax.rsqrt(spread + norm_eps) * gain).astype(bf16)


def params(mib):
    return pltpu.CompilerParams(vmem_limit_bytes=mib * 2**20)


def started(*copies):
    for copy in copies:
        copy.start()
    return copies


def cost(flops, read, exps=0):
    return pl.CostEstimate(flops=int(flops), bytes_accessed=int(read), transcendentals=int(exps))


def place_of(index, peers):
    if isinstance(index, int):
        return (index + index % 2 * (peers // 2)) % peers
    return mod(index + (index & 1) * (peers // 2), peers)


def exchange(blocks, peers):
    order = [place_of(i, peers) for i in range(peers)]
    return lax.all_to_all(
        blocks, "dom", split_axis=0, concat_axis=0, tiled=True, axis_index_groups=[order]
    )


def columns_of(ref, where, rows, half):
    return [ref[where, i * rows : (i + 1) * rows, :] for i in range(half // LANES)]


def ask_kernel(*refs):
    sources, out_ref, held, sems = refs[:6], refs[6], refs[7:13], refs[13]
    copies = started(
        *[
            pltpu.make_async_copy(source, ref, sems.at[i])
            for i, (source, ref) in enumerate(zip(sources, held))
        ]
    )
    w_ref, latent_ref, gain_ref, slot_ref, count_ref, need_ref = held
    rows = latent_ref.shape[0]
    width = w_ref.shape[1]
    entries = need_ref.shape[1]
    edges = slot_ref.shape[1]
    peers = out_ref.shape[0]
    both = 2 * entries // peers
    tall = rows // 2
    for copy in copies[1:]:
        copy.wait()
    rows_normed = normed(latent_ref[...], gain_ref[...])
    live = iota((edges, rows), 0) < count_ref[...]
    slots = slot_ref[...].astype(f32).T.astype(jnp.int32)
    slots = jnp.where(live, slots, entries) - entries // 2
    slots = slots.astype(f32).astype(bf16)
    tile = jnp.zeros((tall, LANES), f32)
    for g in range(edges // tall):
        to = iota((rows, LANES), 1) == iota((rows, LANES), 0) + g * rows
        tile += dot(slots, to.astype(bf16))[g * tall : (g + 1) * tall]
    row, lane = iota((tall, LANES), 0), iota((tall, LANES), 1)
    in_list = (lane >= LANES // 2) & (lane < LANES // 2 + both)
    need = need_ref[...]
    tiles = []
    for chip in range(peers // 2):
        at = chip * both
        piece = need[:, at // LANES * LANES : at // LANES * LANES + LANES].astype(f32)
        piece = pltpu.roll(jnp.broadcast_to(piece, (tall, LANES)), (LANES // 2 - at) % LANES, 1)
        high = jnp.floor(piece * (1.0 / 256.0))
        piece = jnp.where(row == 0, piece - high * 256.0, jnp.where(row == 1, high, 0.0))
        tiles.append((tile + jnp.where(in_list, piece, 0.0)).astype(bf16))
    copies[0].wait()
    queries = dot(rows_normed, w_ref[...]).astype(bf16)
    half = width // 2
    for p in range(peers):
        for i in range(half // LANES):
            at = p % 2 * half + i * LANES
            out_ref[p, i * rows : (i + 1) * rows, :] = queries[:, at : at + LANES]
        out_ref[p, half // LANES * rows :, :] = tiles[place_of(p, peers) // 2]


def front_kernel(
    steps, gain_hbm, own_hbm, other_hbm, w_hbm, own_out_ref, other_out_ref,
    gain_ref, own_ref, other_ref, w_ref, sems,
):
    points = own_ref.shape[0]
    block = points // steps
    half = own_out_ref.shape[1] // 2
    core = lax.axis_index("dom") & 1
    copies = started(
        pltpu.make_async_copy(gain_hbm, gain_ref, sems.at[0]),
        pltpu.make_async_copy(own_hbm, own_ref, sems.at[1]),
        *[
            pltpu.make_async_copy(
                w_hbm.at[:, pl.ds(pl.multiple_of((core + 2 * i) * half, half), half)],
                w_ref.at[:, pl.ds(i * half, half)],
                sems.at[2 + i],
            )
            for i in range(2)
        ],
        pltpu.make_async_copy(other_hbm, other_ref, sems.at[4]),
    )
    parts = [pl.ds(i * block, block) for i in range(steps)]
    copies[0].wait()
    copies[1].wait()
    gain = gain_ref[...]
    own_rows = [normed(own_ref[part, :], gain) for part in parts]
    copies[2].wait()
    copies[3].wait()
    for part, rows in zip(parts, own_rows):
        own_out_ref[part, :] = dot(rows, w_ref[...]).astype(bf16)
    copies[4].wait()
    for part in parts:
        other_out_ref[part, :] = dot(normed(other_ref[part, :], gain), w_ref[...]).astype(bf16)


def stat_parts(top, total):
    top_1 = top.astype(bf16).astype(f32)
    top_2 = (top - top_1).astype(bf16).astype(f32)
    total_1 = total.astype(bf16).astype(f32)
    return top_1, top_2, top - top_1 - top_2, total_1, total - total_1


def partial_kernel(cap, rows, edges, asked_ref, *refs):
    pairs_refs, out_ref, mixed_ref = refs[:2], refs[2], refs[3]
    me = lax.axis_index("dom")
    points, both = pairs_refs[0].shape
    peers = out_ref.shape[0]
    width = both // 2
    heads = HEADS // 2
    size = width // heads
    tall = rows // 2
    stack = width // LANES * rows
    scale = math.log2(math.e) / math.sqrt(size)
    all_nodes, all_entries = peers * rows, peers * cap
    nodes, entries = all_nodes // 2, all_entries // 2
    tiles = asked_ref[:, stack:, :].astype(f32)

    tile_rows = peers * tall
    pick_row = iota((all_entries, tile_rows), 1) - div(iota((all_entries, tile_rows), 0), cap) * tall
    pick = jnp.where(pick_row == 0, 1.0, jnp.where(pick_row == 1, 256.0, 0.0)).astype(bf16)
    lists = dot(pick, tiles.reshape(tile_rows, LANES).astype(bf16))
    lane = iota((all_entries, LANES), 1) - mod(iota((all_entries, LANES), 0), cap) - LANES // 2
    gathered = []
    for other, ref in enumerate(pairs_refs):
        mine = lane == ((me ^ other) & 1) * cap
        index = jnp.sum(jnp.where(mine, lists, 0.0), axis=1, keepdims=True).astype(jnp.int32)
        chosen = (index == iota((all_entries, points), 1)).astype(bf16)
        gathered.append(dot(chosen, ref[...]).astype(bf16))

    group, across = div(iota((tall, LANES), 1), rows), LANES // rows
    slots = []
    for g in range(edges // tall):
        line = []
        for first in range(0, peers, across):
            merged = jnp.zeros((tall, LANES), f32)
            for w in range(across):
                merged = jnp.where(
                    group == w, pltpu.roll(tiles[first + w], (w - g) * rows % LANES, 1), merged
                )
            line.append(merged)
        slots.append(jnp.concatenate(line, axis=1))
    all_slots = jnp.concatenate(slots, axis=0).astype(jnp.int32) + all_entries // 2

    here = div(iota((entries, nodes), 0), cap) == div(iota((entries, nodes), 1), rows)
    listed = -(-cap // 8) * 8
    repeat = iota((entries, listed), 1) == mod(iota((entries, listed), 0), cap)
    repeat = repeat.astype(f32)
    biases = []
    for other in range(2):
        slots = all_slots - (me ^ other) * cap
        uses = jnp.zeros((listed, all_nodes), f32)
        for j in range(edges):
            uses += jnp.where(slots[j : j + 1] == iota((listed, all_nodes), 0), 1.0, 0.0)
        live = uses > 0.5
        bias = jnp.where(live, jnp.log2(jnp.where(live, uses, 1.0)), NEG)
        for half in range(2):
            part = bias[:, half * nodes : (half + 1) * nodes]
            if cap == listed:
                repeated = jnp.concatenate([part] * (entries // cap), axis=0)
            else:
                repeated = lax.dot_general(
                    repeat, part, (((1,), (0,)), ((), ())), precision=lax.Precision.HIGHEST
                )
            biases.append(jnp.where(here, repeated, NEG))
    for half in range(2):
        part = slice(half * entries, (half + 1) * entries)
        pairs = jnp.concatenate([gathered[0][part], gathered[1][part]], axis=0)
        bias = jnp.concatenate([biases[half], biases[2 + half]], axis=0)
        keys, values_t = pairs[:, :width], pairs[:, width:].T
        windows = slice(half * (peers // 2), (half + 1) * (peers // 2))
        queries = [one.reshape(nodes, LANES) for one in columns_of(asked_ref, windows, rows, width)]
        queries = jnp.concatenate(queries, axis=1)
        head = div(iota(queries.shape, 1), size)
        queries = jnp.concatenate(
            [jnp.where(head == h, queries, jnp.zeros_like(queries)) for h in range(heads)], axis=0
        )
        scores = dot_t(keys, queries) * scale + jnp.concatenate([bias] * heads, axis=1)
        top = jnp.max(scores, axis=0, keepdims=True)
        raised = jnp.exp2(scores - top)
        total = jnp.sum(raised, axis=0, keepdims=True)
        raised = raised.astype(bf16)
        for h in range(0, heads, 2):
            mixed = dot(
                values_t[h * size : (h + 2) * size, :], raised[:, h * nodes : (h + 2) * nodes]
            )
            mixed_ref[h * size : (h + 1) * size, :] = mixed[:size, :nodes]
            mixed_ref[(h + 1) * size : (h + 2) * size, :] = mixed[size:, nodes:]
        by_head = [
            jnp.concatenate([one[:, h * nodes : (h + 1) * nodes] for h in range(heads)], axis=0)
            for one in (top, total)
        ]
        stats = jnp.concatenate(stat_parts(*by_head), axis=0)
        rest = mixed_ref.shape[0] - width - stats.shape[0]
        mixed_ref[width:, :] = jnp.concatenate([stats, jnp.zeros((rest, nodes), f32)], axis=0)
        result = mixed_ref[...].T
        mixed = result[:, :width].astype(bf16)
        for i in range(peers // 2):
            place = half * (peers // 2) + i
            for j in range(width // LANES):
                out_ref[place, j * rows : (j + 1) * rows, :] = mixed[
                    i * rows : (i + 1) * rows, j * LANES : (j + 1) * LANES
                ]
            upper = result[i * rows : i * rows + tall, width:]
            lower = result[i * rows + tall : (i + 1) * rows, width:]
            out_ref[place, stack:, :] = (upper + pltpu.roll(lower, LANES // 2, 1)).astype(bf16)


def combine_kernel(parts_ref, latent_ref, gain_ref, w_o_ref, w_kv_ref, latent_out_ref, out_ref):
    peers = parts_ref.shape[0]
    rows = latent_ref.shape[0]
    width = w_o_ref.shape[0]
    half = width // 2
    heads, size, tall = HEADS // 2, width // HEADS, rows // 2
    chips = (peers // 2, 2, tall, LANES)
    tile = parts_ref[:, half // LANES * rows :, :].astype(f32)

    def moved(columns):
        return pltpu.roll(tile, LANES - columns, 2)

    top = (tile + moved(heads) + moved(2 * heads)).reshape(chips)
    total = (moved(3 * heads) + moved(4 * heads)).reshape(chips)
    factor = jnp.exp2(top - jnp.max(top, axis=0, keepdims=True))
    factor = factor / jnp.sum(total * factor, axis=0, keepdims=True)
    head = div(iota(chips, 3), size)
    blocks = []
    for i, block in enumerate(columns_of(parts_ref, slice(None), rows, half)):
        block = block.astype(f32)
        nodes = []
        for g in range(2):
            wide = jnp.zeros(chips, f32)
            for h in range(LANES // size):
                at = g * (LANES // 2) + i * (LANES // size) + h
                wide = jnp.where(head == h, factor[..., at : at + 1], wide)
            part = block[:, g * tall : (g + 1) * tall].reshape(chips)
            nodes.append(jnp.sum(part * wide, axis=0))
        blocks.append(jnp.concatenate(nodes, axis=1))
    mixed = jnp.concatenate([block[h] for h in range(2) for block in blocks], axis=1)
    update = dot(mixed.astype(bf16), w_o_ref[...])
    latent_out = (latent_ref[...].astype(f32) + update).astype(bf16)
    latent_out_ref[...] = latent_out
    pairs = dot(normed(latent_out, gain_ref[...]), w_kv_ref[...]).astype(bf16)
    for p in range(peers):
        at = p % 2 * half
        out_ref[p, :, :half] = pairs[:, at : at + half]
        out_ref[p, :, half:] = pairs[:, width + at : width + at + half]


def middle_kernel(
    steps, peers, rows, gain_ref, need_ref, slot_ref, x_hbm, w_hbm, query_ref, node_ref,
    x_ref, w_ref, sems,
):
    copies = started(
        pltpu.make_async_copy(w_hbm, w_ref, sems.at[0]),
        pltpu.make_async_copy(x_hbm, x_ref, sems.at[1]),
    )
    points = x_ref.shape[0]
    block = points // steps
    high_count = need_ref.shape[0]
    cap = high_count * LANES // peers
    need = need_ref[...].astype(f32).astype(bf16)
    for j in range(slot_ref.shape[0]):
        slots = slot_ref[j : j + 1, :]
        row_of = (div(slots, LANES) == iota((high_count, points), 0)).astype(bf16)
        listed = lax.dot_general(need, row_of, (((0,), (0,)), ((), ())), preferred_element_type=f32)
        own = mod(slots, LANES) == iota((LANES, points), 0)
        found = jnp.sum(jnp.where(own, listed, 0.0), axis=0, keepdims=True).astype(jnp.int32)
        node_ref[j : j + 1, :] = place_of(div(slots, cap), peers) * rows + found
    for copy in copies:
        copy.wait()
    for i in range(steps):
        part = pl.ds(i * block, block)
        queries = dot(normed(x_ref[part, :], gain_ref[...]), w_ref[...])
        query_ref[:, part] = queries.T.astype(bf16)


def attend_half(pairs, queries, nodes):
    half, points = queries.shape
    edges = nodes.shape[0]
    heads = HEADS // 2
    size = half // heads
    node = iota((pairs.shape[1], points), 0)
    picks = [(nodes[j : j + 1] == node).astype(bf16) for j in range(edges)]
    scores, values = [], []
    for j in range(edges):
        chosen = dot(pairs, picks[j])
        products = (chosen[:half] * queries.astype(f32)).reshape(heads, size, points)
        scores.append(jnp.sum(products, axis=1) * (1.0 / math.sqrt(size)))
        values.append(chosen[half:].reshape(heads, size, points))
    highest = functools.reduce(jnp.maximum, scores)
    raised = [jnp.exp(score - highest) for score in scores]
    inverse = 1.0 / sum(raised)
    mixed = jnp.zeros((heads, size, points), f32)
    for j in range(edges):
        weight = (raised[j] * inverse).astype(bf16).astype(f32).reshape(heads, 1, points)
        mixed += values[j] * weight
    return mixed.reshape(half, points).T.astype(bf16)


def half_of(ref, first, half):
    return ref.at[pl.ds(pl.multiple_of(first, half), half)]


def own_kernel(steps, pairs_ref, node_ref, query_ref, out_ref):
    points, half = out_ref.shape
    block = points // steps
    core = lax.axis_index("dom") & 1
    queries = half_of(query_ref, core * half, half)
    pairs = pairs_ref[...].T
    for i in range(steps):
        part = pl.ds(i * block, block)
        out_ref[part, :] = attend_half(pairs, queries[:, part], node_ref[:, part])


def other_kernel(
    steps, pairs_ref, own_ref, node_ref, query_ref, x_ref, w_ref, out_hbm, out_ref, sems
):
    points, half = own_ref.shape
    block = points // steps
    core = lax.axis_index("dom") & 1
    queries = half_of(query_ref, (1 - core) * half, half)
    pairs = pairs_ref[...].T
    sends = []
    parts = [pl.ds(i * block, block) for i in range(steps)]

    def attended(part):
        return attend_half(pairs, queries[:, part], node_ref[:, part])

    mixed = attended(parts[0])
    for i, part in enumerate(parts):
        following = attended(parts[i + 1]) if i + 1 < steps else None
        own = own_ref[part, :]
        both = [jnp.where(core == 0, own, mixed), jnp.where(core == 0, mixed, own)]
        update = dot(jnp.concatenate(both, axis=1), w_ref[...])
        out_ref[part, :] = (x_ref[part, :].astype(f32) + update).astype(bf16)
        sends += started(pltpu.make_async_copy(out_ref.at[part], out_hbm.at[part], sems.at[i]))
        mixed = following
    for send in sends:
        send.wait()


def in_hbm(array):
    return pltpu.with_memory_space_constraint(array, pltpu.HBM)


def in_vmem(array):
    return pltpu.with_memory_space_constraint(array, pltpu.VMEM)


def on_device(
    grid,
    latent_in,
    grid_gain,
    node_gain,
    dec_gain,
    w_q_enc,
    w_kv_enc,
    w_o_enc,
    w_q_dec,
    w_kv_dec,
    w_o_dec,
    enc_need,
    enc_slot,
    enc_count,
    dec_need,
    dec_slot,
):
    peers = lax.axis_size("dom")
    points, depth = grid.shape
    rows = latent_in.shape[0]
    width = w_q_enc.shape[1]
    nodes = peers * rows
    entries = enc_need.shape[1]
    edges = enc_slot.shape[0]
    cap = entries // peers
    half = width // 2
    sent = (peers, half // LANES * rows + rows // 2, LANES)
    swap = [(i, i ^ 1) for i in range(peers)]
    vmem = pl.BlockSpec(memory_space=pltpu.VMEM)
    hbm = pl.BlockSpec(memory_space=pltpu.HBM)

    other_grid = lax.ppermute(grid, "dom", swap)
    ask_inputs = (
        w_q_enc,
        latent_in,
        node_gain.reshape(1, -1),
        enc_slot.T,
        enc_count.reshape(1, -1),
        enc_need,
    )
    asked = pl.pallas_call(
        ask_kernel,
        in_specs=[hbm] * len(ask_inputs),
        out_shape=jax.ShapeDtypeStruct(sent, bf16),
        scratch_shapes=[pltpu.VMEM(one.shape, one.dtype) for one in ask_inputs]
        + [pltpu.SemaphoreType.DMA((len(ask_inputs),))],
        compiler_params=params(63),
        cost_estimate=cost(2 * rows * depth * width, 2 * depth * width),
        name="ask",
    )(*map(in_hbm, ask_inputs))
    asked = exchange(asked, peers)

    block = math.gcd(points, 256)
    steps = points // block
    pairs = pl.pallas_call(
        functools.partial(front_kernel, steps),
        in_specs=[hbm] * 4,
        out_specs=[vmem] * 2,
        out_shape=[pltpu.VMEM((points, width), bf16)] * 2,
        scratch_shapes=[
            pltpu.VMEM((1, depth), f32),
            pltpu.VMEM((points, depth), bf16),
            pltpu.VMEM((points, depth), bf16),
            pltpu.VMEM((depth, width), bf16),
            pltpu.SemaphoreType.DMA((5,)),
        ],
        compiler_params=params(40),
        cost_estimate=cost(4 * points * depth * width, 8 * points * depth),
        name="front",
    )(*map(in_hbm, (grid_gain.reshape(1, -1), grid, other_grid, w_kv_enc)))

    parts = pl.pallas_call(
        functools.partial(partial_kernel, cap, rows, edges),
        in_specs=[vmem] * 3,
        out_shape=jax.ShapeDtypeStruct(sent, bf16),
        scratch_shapes=[pltpu.VMEM((half + LANES, nodes // 2), f32)],
        compiler_params=params(40),
        cost_estimate=cost(4 * entries * points * width, 4 * points * width),
        name="partial",
    )(asked, *map(in_vmem, pairs))
    parts, dec_need, dec_slot = lax.optimization_barrier((parts, dec_need, dec_slot))
    parts = exchange(parts, peers)

    slot_total = dec_need.shape[1]
    edge_count = dec_slot.shape[0]
    queries, node_of = pl.pallas_call(
        functools.partial(middle_kernel, steps, peers, rows),
        in_specs=[vmem] * 3 + [hbm] * 2,
        out_specs=[vmem, vmem],
        out_shape=[
            pltpu.VMEM((width, points), bf16),
            jax.ShapeDtypeStruct((edge_count, points), jnp.int32),
        ],
        scratch_shapes=[
            pltpu.VMEM((points, depth), bf16),
            pltpu.VMEM((depth, width), bf16),
            pltpu.SemaphoreType.DMA((2,)),
        ],
        compiler_params=params(40),
        cost_estimate=cost(2 * points * depth * width, 8 * points * depth),
        name="middle",
    )(
        grid_gain.reshape(1, -1),
        dec_need.reshape(slot_total // LANES, LANES),
        dec_slot,
        in_hbm(grid),
        in_hbm(w_q_dec),
    )
    parts, queries, node_of = lax.optimization_barrier((parts, queries, node_of))

    latent_out, everyone = pl.pallas_call(
        combine_kernel,
        out_shape=[
            jax.ShapeDtypeStruct((rows, depth), bf16),
            jax.ShapeDtypeStruct((peers, rows, width), bf16),
        ],
        compiler_params=params(24),
        cost_estimate=cost(6 * rows * depth * width, 6 * depth * width),
        name="combine",
    )(parts, latent_in, dec_gain.reshape(1, -1), w_o_enc, w_kv_dec)
    own = exchange(everyone, peers).reshape(nodes, width)
    other = lax.ppermute(own, "dom", swap)

    queries = in_vmem(queries)
    own_mixed = pl.pallas_call(
        functools.partial(own_kernel, steps),
        in_specs=[vmem] * 3,
        out_shape=jax.ShapeDtypeStruct((points, half), bf16),
        compiler_params=params(48),
        cost_estimate=cost(4 * points * nodes * width, 8 * points * nodes),
        name="own",
    )(own, node_of, queries)
    grid_out = pl.pallas_call(
        functools.partial(other_kernel, steps),
        in_specs=[vmem] * 6,
        out_specs=hbm,
        out_shape=pltpu.HBM((points, depth), bf16),
        scratch_shapes=[
            pltpu.VMEM((points, depth), bf16),
            pltpu.SemaphoreType.DMA((steps,)),
        ],
        compiler_params=params(48),
        cost_estimate=cost(4 * points * depth * width, 8 * points * depth),
        name="other",
    )(other, own_mixed, node_of, queries, grid, w_o_dec)
    return (latent_out, grid_out)


def solution(mesh):
    return jax.shard_map(
        on_device,
        mesh=mesh,
        in_specs=(
            P(("groups", "dom"), None),
            P(("groups", "dom"), None),
            P(),
            P(),
            P(),
            P(),
            P(),
            P(),
            P(),
            P(),
            P(),
            P("dom", None),
            P(None, "dom"),
            P("dom"),
            P("dom", None),
            P(None, "dom"),
        ),
        out_specs=(P(("groups", "dom"), None), P(("groups", "dom"), None)),
        check_vma=False,
    )
```

```python
import functools
import math

import jax
import jax.numpy as jnp
from jax import lax
from jax.experimental import pallas as pl
from jax.experimental.pallas import tpu as pltpu
from jax.sharding import PartitionSpec as P

HEADS = 8
LANES = 128
NEG = -1e30
norm_eps = 1e-06
f32 = jnp.float32
bf16 = jnp.bfloat16


def iota(shape, dim):
    return lax.broadcasted_iota(jnp.int32, shape, dim)


def one_hot(places, shape, dim):
    return (places.astype(jnp.int16) == iota(shape, dim).astype(jnp.int16)).astype(bf16)


def div(values, by):
    if by & (by - 1) == 0:
        return values >> (by.bit_length() - 1)
    return values // by


def mod(values, by):
    if by & (by - 1) == 0:
        return values & (by - 1)
    return values % by


def dot(a, b):
    return jnp.dot(a, b, preferred_element_type=f32)


def dot_t(a, b):
    return lax.dot_general(a, b, (((1,), (1,)), ((), ())), preferred_element_type=f32)


def normed(values, gain):
    widened = values.astype(f32)
    spread = jnp.mean(widened * widened, axis=-1, keepdims=True)
    return (widened * lax.rsqrt(spread + norm_eps) * gain).astype(bf16)


def params(mib):
    return pltpu.CompilerParams(vmem_limit_bytes=mib * 2**20)


def started(*copies):
    for copy in copies:
        copy.start()
    return copies


def cost(flops, read, exps=0):
    return pl.CostEstimate(flops=int(flops), bytes_accessed=int(read), transcendentals=int(exps))


def place_of(index, peers):
    if isinstance(index, int):
        return (index + index % 2 * (peers // 2)) % peers
    return mod(index + (index & 1) * (peers // 2), peers)


def exchange(blocks, peers):
    order = [place_of(i, peers) for i in range(peers)]
    return lax.all_to_all(
        blocks, "dom", split_axis=0, concat_axis=0, tiled=True, axis_index_groups=[order]
    )


def columns_of(ref, where, rows, half):
    return [ref[where, i * rows : (i + 1) * rows, :] for i in range(half // LANES)]


def ask_kernel(*refs):
    sources, out_ref, held, sems = refs[:6], refs[6], refs[7:13], refs[13]
    copies = started(
        *[
            pltpu.make_async_copy(source, ref, sems.at[i])
            for i, (source, ref) in enumerate(zip(sources, held))
        ]
    )
    w_ref, latent_ref, gain_ref, slot_ref, count_ref, need_ref = held
    rows = latent_ref.shape[0]
    width = w_ref.shape[1]
    entries = need_ref.shape[1]
    edges = slot_ref.shape[1]
    peers = out_ref.shape[0]
    both = 2 * entries // peers
    tall = rows // 2
    for copy in copies[1:]:
        copy.wait()
    rows_normed = normed(latent_ref[...], gain_ref[...])
    live = iota((edges, rows), 0) < count_ref[...]
    slots = slot_ref[...].astype(f32).T.astype(jnp.int32)
    slots = jnp.where(live, slots, entries) - entries // 2
    slots = slots.astype(f32).astype(bf16)
    tile = jnp.zeros((tall, LANES), f32)
    for g in range(edges // tall):
        to = iota((rows, LANES), 1) == iota((rows, LANES), 0) + g * rows
        tile += dot(slots, to.astype(bf16))[g * tall : (g + 1) * tall]
    row, lane = iota((tall, LANES), 0), iota((tall, LANES), 1)
    in_list = (lane >= LANES // 2) & (lane < LANES // 2 + both)
    need = need_ref[...]
    tiles = []
    for chip in range(peers // 2):
        at = chip * both
        piece = need[:, at // LANES * LANES : at // LANES * LANES + LANES].astype(f32)
        piece = pltpu.roll(jnp.broadcast_to(piece, (tall, LANES)), (LANES // 2 - at) % LANES, 1)
        high = jnp.floor(piece * (1.0 / 256.0))
        piece = jnp.where(row == 0, piece - high * 256.0, jnp.where(row == 1, high, 0.0))
        tiles.append((tile + jnp.where(in_list, piece, 0.0)).astype(bf16))
    copies[0].wait()
    queries = dot(rows_normed, w_ref[...]).astype(bf16)
    half = width // 2
    for p in range(peers):
        for i in range(half // LANES):
            at = p % 2 * half + i * LANES
            out_ref[p, i * rows : (i + 1) * rows, :] = queries[:, at : at + LANES]
        out_ref[p, half // LANES * rows :, :] = tiles[place_of(p, peers) // 2]


def front_kernel(
    steps, gain_hbm, own_hbm, other_hbm, w_hbm, own_out_ref, other_out_ref,
    gain_ref, own_ref, other_ref, w_ref, sems,
):
    points = own_ref.shape[0]
    block = points // steps
    half = own_out_ref.shape[1] // 2
    core = lax.axis_index("dom") & 1
    copies = started(
        pltpu.make_async_copy(gain_hbm, gain_ref, sems.at[0]),
        *[
            pltpu.make_async_copy(
                w_hbm.at[:, pl.ds(pl.multiple_of((core + 2 * i) * half, half), half)],
                w_ref.at[:, pl.ds(i * half, half)],
                sems.at[1 + i],
            )
            for i in range(2)
        ],
        pltpu.make_async_copy(own_hbm, own_ref, sems.at[3]),
        pltpu.make_async_copy(other_hbm, other_ref, sems.at[4]),
    )
    parts = [pl.ds(i * block, block) for i in range(steps)]
    for copy in copies[:3]:
        copy.wait()
    gain = gain_ref[...]
    sides = ((own_ref, own_out_ref), (other_ref, other_out_ref))
    for copy, (rows_ref, out_ref) in zip(copies[3:], sides):
        copy.wait()
        for part in parts:
            out_ref[part, :] = dot(normed(rows_ref[part, :], gain), w_ref[...]).astype(bf16)


def stat_parts(top, total):
    top_1 = top.astype(bf16).astype(f32)
    top_2 = (top - top_1).astype(bf16).astype(f32)
    total_1 = total.astype(bf16).astype(f32)
    return top_1, top_2, top - top_1 - top_2, total_1, total - total_1


def partial_kernel(cap, rows, edges, asked_ref, *refs):
    pairs_refs, out_ref = refs[:2], refs[2]
    me = lax.axis_index("dom")
    points, both = pairs_refs[0].shape
    peers = out_ref.shape[0]
    width = both // 2
    heads = HEADS // 2
    size = width // heads
    tall = rows // 2
    stack = width // LANES * rows
    scale = math.log2(math.e) / math.sqrt(size)
    all_nodes, all_entries = peers * rows, peers * cap
    some = LANES // (heads * rows)
    nodes, entries = some * rows, some * cap
    tiles = asked_ref[:, stack:, :].astype(f32)

    tile_rows = peers * tall
    pick_row = iota((all_entries, tile_rows), 1) - div(iota((all_entries, tile_rows), 0), cap) * tall
    pick = jnp.where(pick_row == 0, 1.0, jnp.where(pick_row == 1, 256.0, 0.0)).astype(bf16)
    lists = dot(pick, tiles.reshape(tile_rows, LANES).astype(bf16))
    lane = iota((all_entries, LANES), 1) - mod(iota((all_entries, LANES), 0), cap) - LANES // 2
    gathered = []
    for other, ref in enumerate(pairs_refs):
        mine = lane == ((me ^ other) & 1) * cap
        index = jnp.sum(jnp.where(mine, lists, 0.0), axis=1, keepdims=True).astype(jnp.int32)
        gathered.append(dot(one_hot(index, (all_entries, points), 1), ref[...]))

    group, across = div(iota((tall, LANES), 1), rows), LANES // rows
    slots = []
    for g in range(edges // tall):
        line = []
        for first in range(0, peers, across):
            merged = jnp.zeros((tall, LANES), f32)
            for w in range(across):
                merged = jnp.where(
                    group == w, pltpu.roll(tiles[first + w], (w - g) * rows % LANES, 1), merged
                )
            line.append(merged)
        slots.append(jnp.concatenate(line, axis=1))
    all_slots = jnp.concatenate(slots, axis=0).astype(jnp.int32) + all_entries // 2

    listed = -(-cap // 8) * 8
    biases = []
    for other in range(2):
        slots = all_slots - (me ^ other) * cap
        uses = jnp.zeros((listed, all_nodes), f32)
        for j in range(edges):
            uses += jnp.where(slots[j : j + 1] == iota((listed, all_nodes), 0), 1.0, 0.0)
        live = uses > 0.5
        biases.append(jnp.where(live, jnp.log2(jnp.where(live, uses, 1.0)), NEG))

    window = mod(div(iota((listed, LANES), 1), rows), some)
    first_nodes = iota((listed, LANES), 1) < nodes
    first_head = iota((nodes, LANES), 1) < size
    tops, totals = [], []
    for start in range(0, peers, some):
        bias = []
        for one in biases:
            at = start * rows
            one = one[:, at // LANES * LANES : at // LANES * LANES + LANES]
            one = jnp.where(first_nodes, pltpu.roll(one, -at % LANES, 1), 0.0)
            spread = nodes
            while spread < LANES:
                one += pltpu.roll(one, spread, 1)
                spread *= 2
            bias += [jnp.where(window == w, one, NEG)[:cap] for w in range(some)]
        part = slice(start * cap, start * cap + entries)
        pairs = jnp.concatenate([one[part] for one in gathered], axis=0).astype(bf16)
        windows = slice(start, start + some)
        queries = [one.reshape(nodes, LANES) for one in columns_of(asked_ref, windows, rows, width)]
        queries = jnp.concatenate(queries, axis=1)
        head = div(iota(queries.shape, 1), size)
        queries = jnp.concatenate(
            [jnp.where(head == h, queries, jnp.zeros_like(queries)) for h in range(heads)], axis=0
        )
        scores = dot_t(pairs[:, :width], queries) * scale + jnp.concatenate(bias, axis=0)
        top = jnp.max(scores, axis=0, keepdims=True)
        raised = jnp.exp2(scores - top)
        tops.append(top)
        totals.append(jnp.sum(raised, axis=0, keepdims=True))
        mixed = dot(raised.T.astype(bf16), pairs[:, width:])
        for j in range(width // LANES):
            block = mixed[:, j * LANES : (j + 1) * LANES]
            h = j * (LANES // size)
            block = jnp.where(
                first_head, block[h * nodes : (h + 1) * nodes], block[(h + 1) * nodes : (h + 2) * nodes]
            ).astype(bf16)
            for w in range(some):
                out_ref[start + w, j * rows : (j + 1) * rows, :] = block[w * rows : (w + 1) * rows]

    row_lane = iota((tall, LANES), 1)
    for first in range(0, len(tops), 8):
        parts = stat_parts(
            jnp.concatenate(tops[first : first + 8], axis=0),
            jnp.concatenate(totals[first : first + 8], axis=0),
        )
        rest = jnp.zeros((LANES - 8 * len(parts), LANES), f32)
        columns = jnp.concatenate([*parts, rest], axis=0).T
        for g in range(8):
            for w in range(some):
                tile = jnp.zeros((tall, LANES), f32)
                for h in range(heads):
                    for late in range(2):
                        at = h * nodes + w * rows + late * tall
                        move = late * (LANES // 2) + h - g
                        here = (mod(row_lane, 8) == h) & (div(row_lane, LANES // 2) == late)
                        piece = pltpu.roll(columns[at : at + tall], move % LANES, 1)
                        tile = jnp.where(here, piece, tile)
                out_ref[(first + g) * some + w, stack:, :] = tile.astype(bf16)


def combine_kernel(parts_ref, latent_ref, gain_ref, w_o_ref, w_kv_ref, latent_out_ref, out_ref):
    peers = parts_ref.shape[0]
    rows = latent_ref.shape[0]
    width = w_o_ref.shape[0]
    half = width // 2
    size, tall = width // HEADS, rows // 2
    chips = (peers // 2, 2, tall, LANES)
    tile = parts_ref[:, half // LANES * rows :, :].astype(f32)

    def moved(columns):
        return pltpu.roll(tile, LANES - columns, 2)

    top = (tile + moved(8) + moved(16)).reshape(chips)
    total = (moved(24) + moved(32)).reshape(chips)
    factor = jnp.exp2(top - jnp.max(top, axis=0, keepdims=True))
    factor = factor / jnp.sum(total * factor, axis=0, keepdims=True)
    head = div(iota(chips, 3), size)
    blocks = []
    for i, block in enumerate(columns_of(parts_ref, slice(None), rows, half)):
        block = block.astype(f32)
        nodes = []
        for g in range(2):
            wide = jnp.zeros(chips, f32)
            for h in range(LANES // size):
                at = g * (LANES // 2) + i * (LANES // size) + h
                wide = jnp.where(head == h, factor[..., at : at + 1], wide)
            part = block[:, g * tall : (g + 1) * tall].reshape(chips)
            nodes.append(jnp.sum(part * wide, axis=0))
        blocks.append(jnp.concatenate(nodes, axis=1))
    mixed = jnp.concatenate([block[h] for h in range(2) for block in blocks], axis=1)
    update = dot(mixed.astype(bf16), w_o_ref[...])
    latent_out = (latent_ref[...].astype(f32) + update).astype(bf16)
    latent_out_ref[...] = latent_out
    pairs = dot(normed(latent_out, gain_ref[...]), w_kv_ref[...]).astype(bf16)
    for p in range(peers):
        at = p % 2 * half
        out_ref[p, :, :half] = pairs[:, at : at + half]
        out_ref[p, :, half:] = pairs[:, width + at : width + at + half]


def middle_kernel(
    steps, peers, rows, gain_ref, need_ref, slot_ref, x_hbm, w_hbm, query_ref, node_ref,
    x_ref, w_ref, sems,
):
    copies = started(
        pltpu.make_async_copy(w_hbm, w_ref, sems.at[0]),
        pltpu.make_async_copy(x_hbm, x_ref, sems.at[1]),
    )
    points = x_ref.shape[0]
    block = points // steps
    high_count = need_ref.shape[0]
    cap = high_count * LANES // peers
    need = need_ref[...].astype(f32).astype(bf16)
    for j in range(slot_ref.shape[0]):
        slots = slot_ref[j : j + 1, :]
        row_of = (div(slots, LANES) == iota((high_count, points), 0)).astype(bf16)
        listed = lax.dot_general(need, row_of, (((0,), (0,)), ((), ())), preferred_element_type=f32)
        own = mod(slots, LANES) == iota((LANES, points), 0)
        found = jnp.sum(jnp.where(own, listed, 0.0), axis=0, keepdims=True).astype(jnp.int32)
        node_ref[j : j + 1, :] = place_of(div(slots, cap), peers) * rows + found
    for copy in copies:
        copy.wait()
    for i in range(steps):
        part = pl.ds(i * block, block)
        queries = dot(normed(x_ref[part, :], gain_ref[...]), w_ref[...])
        query_ref[:, part] = queries.T.astype(bf16)


def attend_half(pairs, queries, nodes):
    half, points = queries.shape
    edges = nodes.shape[0]
    heads = HEADS // 2
    size = half // heads
    picks = [one_hot(nodes[j : j + 1], (pairs.shape[1], points), 0) for j in range(edges)]
    scores, values = [], []
    for j in range(edges):
        chosen = dot(pairs, picks[j])
        products = (chosen[:half] * queries.astype(f32)).reshape(heads, size, points)
        scores.append(jnp.sum(products, axis=1) * (1.0 / math.sqrt(size)))
        values.append(chosen[half:].reshape(heads, size, points))
    highest = functools.reduce(jnp.maximum, scores)
    raised = [jnp.exp(score - highest) for score in scores]
    inverse = 1.0 / sum(raised)
    mixed = jnp.zeros((heads, size, points), f32)
    for j in range(edges):
        weight = (raised[j] * inverse).astype(bf16).astype(f32).reshape(heads, 1, points)
        mixed += values[j] * weight
    return mixed.reshape(half, points).T.astype(bf16)


def half_of(ref, first, half):
    return ref.at[pl.ds(pl.multiple_of(first, half), half)]


def own_kernel(steps, pairs_ref, node_ref, query_ref, out_ref):
    points, half = out_ref.shape
    block = points // steps
    core = lax.axis_index("dom") & 1
    queries = half_of(query_ref, core * half, half)
    pairs = pairs_ref[...].T
    for i in range(steps):
        part = pl.ds(i * block, block)
        out_ref[part, :] = attend_half(pairs, queries[:, part], node_ref[:, part])


def other_kernel(
    steps, pairs_ref, own_ref, node_ref, query_ref, x_ref, w_ref, out_hbm, out_ref, sems
):
    points, half = own_ref.shape
    block = points // steps
    core = lax.axis_index("dom") & 1
    queries = half_of(query_ref, (1 - core) * half, half)
    pairs = pairs_ref[...].T
    sends = []
    parts = [pl.ds(i * block, block) for i in range(steps)]

    def attended(part):
        return attend_half(pairs, queries[:, part], node_ref[:, part])

    mixed = attended(parts[0])
    for i, part in enumerate(parts):
        following = attended(parts[i + 1]) if i + 1 < steps else None
        own = own_ref[part, :]
        both = [jnp.where(core == 0, own, mixed), jnp.where(core == 0, mixed, own)]
        update = dot(jnp.concatenate(both, axis=1), w_ref[...])
        out_ref[part, :] = (x_ref[part, :].astype(f32) + update).astype(bf16)
        sends += started(pltpu.make_async_copy(out_ref.at[part], out_hbm.at[part], sems.at[i]))
        mixed = following
    for send in sends:
        send.wait()


def in_hbm(array):
    return pltpu.with_memory_space_constraint(array, pltpu.HBM)


def in_vmem(array):
    return pltpu.with_memory_space_constraint(array, pltpu.VMEM)


def on_device(
    grid,
    latent_in,
    grid_gain,
    node_gain,
    dec_gain,
    w_q_enc,
    w_kv_enc,
    w_o_enc,
    w_q_dec,
    w_kv_dec,
    w_o_dec,
    enc_need,
    enc_slot,
    enc_count,
    dec_need,
    dec_slot,
):
    peers = lax.axis_size("dom")
    points, depth = grid.shape
    rows = latent_in.shape[0]
    width = w_q_enc.shape[1]
    nodes = peers * rows
    entries = enc_need.shape[1]
    edges = enc_slot.shape[0]
    cap = entries // peers
    half = width // 2
    sent = (peers, half // LANES * rows + rows // 2, LANES)
    swap = [(i, i ^ 1) for i in range(peers)]
    vmem = pl.BlockSpec(memory_space=pltpu.VMEM)
    hbm = pl.BlockSpec(memory_space=pltpu.HBM)

    other_grid = lax.ppermute(grid, "dom", swap)
    ask_inputs = (
        w_q_enc,
        latent_in,
        node_gain.reshape(1, -1),
        enc_slot.T,
        enc_count.reshape(1, -1),
        enc_need,
    )
    asked = pl.pallas_call(
        ask_kernel,
        in_specs=[hbm] * len(ask_inputs),
        out_shape=jax.ShapeDtypeStruct(sent, bf16),
        scratch_shapes=[pltpu.VMEM(one.shape, one.dtype) for one in ask_inputs]
        + [pltpu.SemaphoreType.DMA((len(ask_inputs),))],
        compiler_params=params(63),
        cost_estimate=cost(2 * rows * depth * width, 2 * depth * width),
        name="ask",
    )(*map(in_hbm, ask_inputs))
    asked = exchange(asked, peers)

    block = math.gcd(points, 256)
    steps = points // block
    pairs = pl.pallas_call(
        functools.partial(front_kernel, steps),
        in_specs=[hbm] * 4,
        out_specs=[vmem] * 2,
        out_shape=[pltpu.VMEM((points, width), bf16)] * 2,
        scratch_shapes=[
            pltpu.VMEM((1, depth), f32),
            pltpu.VMEM((points, depth), bf16),
            pltpu.VMEM((points, depth), bf16),
            pltpu.VMEM((depth, width), bf16),
            pltpu.SemaphoreType.DMA((5,)),
        ],
        compiler_params=params(40),
        cost_estimate=cost(4 * points * depth * width, 8 * points * depth),
        name="front",
    )(*map(in_hbm, (grid_gain.reshape(1, -1), grid, other_grid, w_kv_enc)))

    parts = pl.pallas_call(
        functools.partial(partial_kernel, cap, rows, edges),
        in_specs=[vmem] * 3,
        out_shape=jax.ShapeDtypeStruct(sent, bf16),
        compiler_params=params(40),
        cost_estimate=cost(4 * entries * points * width, 4 * points * width),
        name="partial",
    )(asked, *map(in_vmem, pairs))
    parts, dec_need, dec_slot = lax.optimization_barrier((parts, dec_need, dec_slot))
    parts = exchange(parts, peers)

    slot_total = dec_need.shape[1]
    edge_count = dec_slot.shape[0]
    queries, node_of = pl.pallas_call(
        functools.partial(middle_kernel, steps, peers, rows),
        in_specs=[vmem] * 3 + [hbm] * 2,
        out_specs=[vmem, vmem],
        out_shape=[
            pltpu.VMEM((width, points), bf16),
            jax.ShapeDtypeStruct((edge_count, points), jnp.int32),
        ],
        scratch_shapes=[
            pltpu.VMEM((points, depth), bf16),
            pltpu.VMEM((depth, width), bf16),
            pltpu.SemaphoreType.DMA((2,)),
        ],
        compiler_params=params(40),
        cost_estimate=cost(2 * points * depth * width, 8 * points * depth),
        name="middle",
    )(
        grid_gain.reshape(1, -1),
        dec_need.reshape(slot_total // LANES, LANES),
        dec_slot,
        in_hbm(grid),
        in_hbm(w_q_dec),
    )
    parts, queries, node_of = lax.optimization_barrier((parts, queries, node_of))

    latent_out, everyone = pl.pallas_call(
        combine_kernel,
        out_shape=[
            jax.ShapeDtypeStruct((rows, depth), bf16),
            jax.ShapeDtypeStruct((peers, rows, width), bf16),
        ],
        compiler_params=params(24),
        cost_estimate=cost(6 * rows * depth * width, 6 * depth * width),
        name="combine",
    )(parts, latent_in, dec_gain.reshape(1, -1), w_o_enc, w_kv_dec)
    own = exchange(everyone, peers).reshape(nodes, width)
    other = lax.ppermute(own, "dom", swap)

    queries = in_vmem(queries)
    own_mixed = pl.pallas_call(
        functools.partial(own_kernel, steps),
        in_specs=[vmem] * 3,
        out_shape=jax.ShapeDtypeStruct((points, half), bf16),
        compiler_params=params(48),
        cost_estimate=cost(4 * points * nodes * width, 8 * points * nodes),
        name="own",
    )(own, node_of, queries)
    grid_out = pl.pallas_call(
        functools.partial(other_kernel, steps),
        in_specs=[vmem] * 6,
        out_specs=hbm,
        out_shape=pltpu.HBM((points, depth), bf16),
        scratch_shapes=[
            pltpu.VMEM((points, depth), bf16),
            pltpu.SemaphoreType.DMA((steps,)),
        ],
        compiler_params=params(48),
        cost_estimate=cost(4 * points * depth * width, 8 * points * depth),
        name="other",
    )(other, own_mixed, node_of, queries, grid, w_o_dec)
    return (latent_out, grid_out)


def solution(mesh):
    return jax.shard_map(
        on_device,
        mesh=mesh,
        in_specs=(
            P(("groups", "dom"), None),
            P(("groups", "dom"), None),
            P(),
            P(),
            P(),
            P(),
            P(),
            P(),
            P(),
            P(),
            P(),
            P("dom", None),
            P(None, "dom"),
            P("dom"),
            P("dom", None),
            P(None, "dom"),
        ),
        out_specs=(P(("groups", "dom"), None), P(("groups", "dom"), None)),
        check_vma=False,
    )
```

```python
import functools
import math

import jax
import jax.numpy as jnp
from jax import lax
from jax.experimental import pallas as pl
from jax.experimental.pallas import tpu as pltpu
from jax.sharding import PartitionSpec as P

HEADS = 8
LANES = 128
NEG = -1e30
norm_eps = 1e-06
f32 = jnp.float32
bf16 = jnp.bfloat16


def iota(shape, dim):
    return lax.broadcasted_iota(jnp.int32, shape, dim)


def one_hot(places, shape, dim):
    return (places == iota(shape, dim)).astype(bf16)


def div(values, by):
    if by & (by - 1) == 0:
        return values >> (by.bit_length() - 1)
    return values // by


def mod(values, by):
    if by & (by - 1) == 0:
        return values & (by - 1)
    return values % by


def dot(a, b):
    return jnp.dot(a, b, preferred_element_type=f32)


def dot_t(a, b):
    return lax.dot_general(a, b, (((1,), (1,)), ((), ())), preferred_element_type=f32)


def normed(values, gain):
    widened = values.astype(f32)
    spread = jnp.mean(widened * widened, axis=-1, keepdims=True)
    return (widened * lax.rsqrt(spread + norm_eps) * gain).astype(bf16)


def params(mib):
    return pltpu.CompilerParams(vmem_limit_bytes=mib * 2**20)


def started(*copies):
    for copy in copies:
        copy.start()
    return copies


def cost(flops, read, exps=0):
    return pl.CostEstimate(flops=int(flops), bytes_accessed=int(read), transcendentals=int(exps))


def place_of(index, peers):
    if isinstance(index, int):
        return (index + index % 2 * (peers // 2)) % peers
    return mod(index + (index & 1) * (peers // 2), peers)


def exchange(blocks, order=None):
    return lax.all_to_all(
        blocks, "dom", split_axis=0, concat_axis=0, tiled=True, axis_index_groups=order
    )


def columns_of(ref, where, rows, half):
    return [ref[where, i * rows : (i + 1) * rows, :] for i in range(half // LANES)]


def ask_kernel(*refs):
    sources, out_ref, held, sems = refs[:6], refs[6], refs[7:13], refs[13]
    copies = started(
        *[
            pltpu.make_async_copy(source, ref, sems.at[i])
            for i, (source, ref) in enumerate(zip(sources, held))
        ]
    )
    w_ref, latent_ref, gain_ref, slot_ref, count_ref, need_ref = held
    rows = latent_ref.shape[0]
    width = w_ref.shape[1]
    entries = need_ref.shape[1]
    edges = slot_ref.shape[1]
    peers = out_ref.shape[0]
    both = 2 * entries // peers
    tall = rows // 2
    for copy in copies[1:]:
        copy.wait()
    rows_normed = normed(latent_ref[...], gain_ref[...])
    live = iota((edges, rows), 0) < count_ref[...]
    slots = slot_ref[...].astype(f32).T.astype(jnp.int32)
    slots = jnp.where(live, slots, entries) - entries // 2
    slots = slots.astype(f32).astype(bf16)
    tile = jnp.zeros((tall, LANES), f32)
    for g in range(edges // tall):
        to = iota((rows, LANES), 1) == iota((rows, LANES), 0) + g * rows
        tile += dot(slots, to.astype(bf16))[g * tall : (g + 1) * tall]
    row, lane = iota((tall, LANES), 0), iota((tall, LANES), 1)
    in_list = (lane >= LANES // 2) & (lane < LANES // 2 + both)
    need = need_ref[...]
    tiles = []
    for chip in range(peers // 2):
        at = chip * both
        piece = need[:, at // LANES * LANES : at // LANES * LANES + LANES].astype(f32)
        piece = pltpu.roll(jnp.broadcast_to(piece, (tall, LANES)), (LANES // 2 - at) % LANES, 1)
        high = jnp.floor(piece * (1.0 / 256.0))
        piece = jnp.where(row == 0, piece - high * 256.0, jnp.where(row == 1, high, 0.0))
        tiles.append((tile + jnp.where(in_list, piece, 0.0)).astype(bf16))
    copies[0].wait()
    queries = dot(rows_normed, w_ref[...]).astype(bf16)
    half = width // 2
    for p in range(peers):
        for i in range(half // LANES):
            at = p % 2 * half + i * LANES
            out_ref[p, i * rows : (i + 1) * rows, :] = queries[:, at : at + LANES]
        out_ref[p, half // LANES * rows :, :] = tiles[p // 2]


def front_kernel(
    steps, gain_hbm, own_hbm, other_hbm, w_hbm, own_out_ref, other_out_ref,
    gain_ref, own_ref, other_ref, w_ref, sems,
):
    points = own_ref.shape[0]
    block = points // steps
    half = own_out_ref.shape[1] // 2
    core = lax.axis_index("dom") & 1
    copies = started(
        pltpu.make_async_copy(gain_hbm, gain_ref, sems.at[0]),
        *[
            pltpu.make_async_copy(
                w_hbm.at[:, pl.ds(pl.multiple_of((core + 2 * i) * half, half), half)],
                w_ref.at[:, pl.ds(i * half, half)],
                sems.at[1 + i],
            )
            for i in range(2)
        ],
        pltpu.make_async_copy(own_hbm, own_ref, sems.at[3]),
        pltpu.make_async_copy(other_hbm, other_ref, sems.at[4]),
    )
    parts = [pl.ds(i * block, block) for i in range(steps)]
    for copy in copies[:3]:
        copy.wait()
    gain = gain_ref[...]
    sides = ((own_ref, own_out_ref), (other_ref, other_out_ref))
    for copy, (rows_ref, out_ref) in zip(copies[3:], sides):
        copy.wait()
        for part in parts:
            out_ref[part, :] = dot(normed(rows_ref[part, :], gain), w_ref[...]).astype(bf16)


def stat_parts(top, total):
    top_1 = top.astype(bf16).astype(f32)
    top_2 = (top - top_1).astype(bf16).astype(f32)
    total_1 = total.astype(bf16).astype(f32)
    return top_1, top_2, top - top_1 - top_2, total_1, total - total_1


def partial_kernel(cap, rows, edges, asked_ref, *refs):
    pairs_refs, out_ref = refs[:2], refs[2]
    me = lax.axis_index("dom")
    points, both = pairs_refs[0].shape
    peers = out_ref.shape[0]
    width = both // 2
    heads = HEADS // 2
    size = width // heads
    tall = rows // 2
    stack = width // LANES * rows
    scale = math.log2(math.e) / math.sqrt(size)
    all_nodes, all_entries = peers * rows, peers * cap
    some = LANES // (heads * rows)
    nodes, entries = some * rows, some * cap
    tiles = asked_ref[:, stack:, :].astype(f32)

    tile_rows = peers * tall
    pick_row = iota((all_entries, tile_rows), 1) - div(iota((all_entries, tile_rows), 0), cap) * tall
    pick = jnp.where(pick_row == 0, 1.0, jnp.where(pick_row == 1, 256.0, 0.0)).astype(bf16)
    lists = dot(pick, tiles.reshape(tile_rows, LANES).astype(bf16))
    lane = iota((all_entries, LANES), 1) - mod(iota((all_entries, LANES), 0), cap) - LANES // 2
    gathered = []
    for other, ref in enumerate(pairs_refs):
        mine = lane == ((me ^ other) & 1) * cap
        index = jnp.sum(jnp.where(mine, lists, 0.0), axis=1, keepdims=True).astype(jnp.int32)
        gathered.append(dot(one_hot(index, (all_entries, points), 1), ref[...]))

    group, across = div(iota((tall, LANES), 1), rows), LANES // rows
    slots = []
    for g in range(edges // tall):
        line = []
        for first in range(0, peers, across):
            merged = jnp.zeros((tall, LANES), f32)
            for w in range(across):
                merged = jnp.where(
                    group == w, pltpu.roll(tiles[first + w], (w - g) * rows % LANES, 1), merged
                )
            line.append(merged)
        slots.append(jnp.concatenate(line, axis=1))
    all_slots = jnp.concatenate(slots, axis=0).astype(jnp.int32) + all_entries // 2

    listed = -(-cap // 8) * 8
    biases = []
    for other in range(2):
        slots = all_slots - (me ^ other) * cap
        uses = jnp.zeros((listed, all_nodes), f32)
        for j in range(edges):
            uses += jnp.where(slots[j : j + 1] == iota((listed, all_nodes), 0), 1.0, 0.0)
        live = uses > 0.5
        biases.append(jnp.where(live, jnp.log2(jnp.where(live, uses, 1.0)), NEG))

    window = mod(div(iota((listed, LANES), 1), rows), some)
    first_nodes = iota((listed, LANES), 1) < nodes
    first_head = iota((nodes, LANES), 1) < size
    tops, totals = [], []
    for start in range(0, peers, some):
        bias = []
        for one in biases:
            at = start * rows
            one = one[:, at // LANES * LANES : at // LANES * LANES + LANES]
            one = jnp.where(first_nodes, pltpu.roll(one, -at % LANES, 1), 0.0)
            spread = nodes
            while spread < LANES:
                one += pltpu.roll(one, spread, 1)
                spread *= 2
            bias += [jnp.where(window == w, one, NEG)[:cap] for w in range(some)]
        part = slice(start * cap, start * cap + entries)
        pairs = jnp.concatenate([one[part] for one in gathered], axis=0).astype(bf16)
        windows = slice(start, start + some)
        queries = [one.reshape(nodes, LANES) for one in columns_of(asked_ref, windows, rows, width)]
        queries = jnp.concatenate(queries, axis=1)
        head = div(iota(queries.shape, 1), size)
        queries = jnp.concatenate(
            [jnp.where(head == h, queries, jnp.zeros_like(queries)) for h in range(heads)], axis=0
        )
        scores = dot_t(pairs[:, :width], queries) * scale + jnp.concatenate(bias, axis=0)
        top = jnp.max(scores, axis=0, keepdims=True)
        raised = jnp.exp2(scores - top)
        tops.append(top)
        totals.append(jnp.sum(raised, axis=0, keepdims=True))
        mixed = dot(raised.T.astype(bf16), pairs[:, width:])
        for j in range(width // LANES):
            block = mixed[:, j * LANES : (j + 1) * LANES]
            h = j * (LANES // size)
            block = jnp.where(
                first_head, block[h * nodes : (h + 1) * nodes], block[(h + 1) * nodes : (h + 2) * nodes]
            ).astype(bf16)
            for w in range(some):
                out_ref[place_of(start + w, peers), j * rows : (j + 1) * rows, :] = block[w * rows : (w + 1) * rows]

    row_lane = iota((tall, LANES), 1)
    for first in range(0, len(tops), 8):
        parts = stat_parts(
            jnp.concatenate(tops[first : first + 8], axis=0),
            jnp.concatenate(totals[first : first + 8], axis=0),
        )
        rest = jnp.zeros((LANES - 8 * len(parts), LANES), f32)
        columns = jnp.concatenate([*parts, rest], axis=0).T
        for g in range(8):
            for w in range(some):
                tile = jnp.zeros((tall, LANES), f32)
                for h in range(heads):
                    for late in range(2):
                        at = h * nodes + w * rows + late * tall
                        move = late * (LANES // 2) + h - g
                        here = (mod(row_lane, 8) == h) & (div(row_lane, LANES // 2) == late)
                        piece = pltpu.roll(columns[at : at + tall], move % LANES, 1)
                        tile = jnp.where(here, piece, tile)
                out_ref[place_of((first + g) * some + w, peers), stack:, :] = tile.astype(bf16)


def combine_kernel(parts_ref, latent_ref, gain_ref, w_o_ref, w_kv_ref, latent_out_ref, out_ref):
    peers = parts_ref.shape[0]
    rows = latent_ref.shape[0]
    width = w_o_ref.shape[0]
    half = width // 2
    size, tall = width // HEADS, rows // 2
    chips = (peers // 2, 2, tall, LANES)
    tile = parts_ref[:, half // LANES * rows :, :].astype(f32)

    def moved(columns):
        return pltpu.roll(tile, LANES - columns, 2)

    top = (tile + moved(8) + moved(16)).reshape(chips)
    total = (moved(24) + moved(32)).reshape(chips)
    factor = jnp.exp2(top - jnp.max(top, axis=0, keepdims=True))
    factor = factor / jnp.sum(total * factor, axis=0, keepdims=True)
    head = div(iota(chips, 3), size)
    blocks = []
    for i, block in enumerate(columns_of(parts_ref, slice(None), rows, half)):
        block = block.astype(f32)
        nodes = []
        for g in range(2):
            wide = jnp.zeros(chips, f32)
            for h in range(LANES // size):
                at = g * (LANES // 2) + i * (LANES // size) + h
                wide = jnp.where(head == h, factor[..., at : at + 1], wide)
            part = block[:, g * tall : (g + 1) * tall].reshape(chips)
            nodes.append(jnp.sum(part * wide, axis=0))
        blocks.append(jnp.concatenate(nodes, axis=1))
    mixed = jnp.concatenate([block[h] for h in range(2) for block in blocks], axis=1)
    update = dot(mixed.astype(bf16), w_o_ref[...])
    latent_out = (latent_ref[...].astype(f32) + update).astype(bf16)
    latent_out_ref[...] = latent_out
    pairs = dot(normed(latent_out, gain_ref[...]), w_kv_ref[...]).astype(bf16)
    for p in range(peers):
        at = p % 2 * half
        out_ref[p, :, :half] = pairs[:, at : at + half]
        out_ref[p, :, half:] = pairs[:, width + at : width + at + half]


def middle_kernel(
    steps, peers, rows, gain_ref, need_ref, slot_ref, x_hbm, w_hbm, query_ref, node_ref,
    x_ref, w_ref, sems,
):
    copies = started(
        pltpu.make_async_copy(w_hbm, w_ref, sems.at[0]),
        pltpu.make_async_copy(x_hbm, x_ref, sems.at[1]),
    )
    points = x_ref.shape[0]
    block = points // steps
    high_count = need_ref.shape[0]
    cap = high_count * LANES // peers
    need = need_ref[...].astype(f32).astype(bf16)
    for j in range(slot_ref.shape[0]):
        slots = slot_ref[j : j + 1, :]
        row_of = (div(slots, LANES) == iota((high_count, points), 0)).astype(bf16)
        listed = lax.dot_general(need, row_of, (((0,), (0,)), ((), ())), preferred_element_type=f32)
        own = mod(slots, LANES) == iota((LANES, points), 0)
        found = jnp.sum(jnp.where(own, listed, 0.0), axis=0, keepdims=True).astype(jnp.int32)
        node_ref[j : j + 1, :] = place_of(div(slots, cap), peers) * rows + found
    for copy in copies:
        copy.wait()
    for i in range(steps):
        part = pl.ds(i * block, block)
        queries = dot(normed(x_ref[part, :], gain_ref[...]), w_ref[...])
        query_ref[:, part] = queries.T.astype(bf16)


def attend_half(pairs, queries, nodes):
    half, points = queries.shape
    edges = nodes.shape[0]
    heads = HEADS // 2
    size = half // heads
    picks = [one_hot(nodes[j : j + 1], (pairs.shape[1], points), 0) for j in range(edges)]
    scores, values = [], []
    for j in range(edges):
        chosen = dot(pairs, picks[j])
        products = (chosen[:half] * queries.astype(f32)).reshape(heads, size, points)
        scores.append(jnp.sum(products, axis=1) * (1.0 / math.sqrt(size)))
        values.append(chosen[half:].reshape(heads, size, points))
    highest = functools.reduce(jnp.maximum, scores)
    raised = [jnp.exp(score - highest) for score in scores]
    inverse = 1.0 / sum(raised)
    mixed = jnp.zeros((heads, size, points), f32)
    for j in range(edges):
        weight = (raised[j] * inverse).astype(bf16).astype(f32).reshape(heads, 1, points)
        mixed += values[j] * weight
    return mixed.reshape(half, points).T.astype(bf16)


def half_of(ref, first, half):
    return ref.at[pl.ds(pl.multiple_of(first, half), half)]


def own_kernel(steps, pairs_ref, node_ref, query_ref, out_ref):
    points, half = out_ref.shape
    block = points // steps
    core = lax.axis_index("dom") & 1
    queries = half_of(query_ref, core * half, half)
    pairs = pairs_ref[...].T
    for i in range(steps):
        part = pl.ds(i * block, block)
        out_ref[part, :] = attend_half(pairs, queries[:, part], node_ref[:, part])


def other_kernel(
    steps, pairs_ref, own_ref, node_ref, query_ref, x_ref, w_ref, out_hbm, out_ref, sems
):
    points, half = own_ref.shape
    block = points // steps
    core = lax.axis_index("dom") & 1
    queries = half_of(query_ref, (1 - core) * half, half)
    pairs = pairs_ref[...].T
    sends = []
    parts = [pl.ds(i * block, block) for i in range(steps)]

    def attended(part):
        return attend_half(pairs, queries[:, part], node_ref[:, part])

    mixed = attended(parts[0])
    for i, part in enumerate(parts):
        following = attended(parts[i + 1]) if i + 1 < steps else None
        own = own_ref[part, :]
        both = [jnp.where(core == 0, own, mixed), jnp.where(core == 0, mixed, own)]
        update = dot(jnp.concatenate(both, axis=1), w_ref[...])
        out_ref[part, :] = (x_ref[part, :].astype(f32) + update).astype(bf16)
        sends += started(pltpu.make_async_copy(out_ref.at[part], out_hbm.at[part], sems.at[i]))
        mixed = following
    for send in sends:
        send.wait()


def in_hbm(array):
    return pltpu.with_memory_space_constraint(array, pltpu.HBM)


def in_vmem(array):
    return pltpu.with_memory_space_constraint(array, pltpu.VMEM)


def on_device(
    grid,
    latent_in,
    grid_gain,
    node_gain,
    dec_gain,
    w_q_enc,
    w_kv_enc,
    w_o_enc,
    w_q_dec,
    w_kv_dec,
    w_o_dec,
    enc_need,
    enc_slot,
    enc_count,
    dec_need,
    dec_slot,
):
    peers = lax.axis_size("dom")
    points, depth = grid.shape
    rows = latent_in.shape[0]
    width = w_q_enc.shape[1]
    nodes = peers * rows
    entries = enc_need.shape[1]
    edges = enc_slot.shape[0]
    cap = entries // peers
    half = width // 2
    sent = (peers, half // LANES * rows + rows // 2, LANES)
    swap = [(i, i ^ 1) for i in range(peers)]
    vmem = pl.BlockSpec(memory_space=pltpu.VMEM)
    hbm = pl.BlockSpec(memory_space=pltpu.HBM)

    other_grid = lax.ppermute(grid, "dom", swap)
    ask_inputs = (
        w_q_enc,
        latent_in,
        node_gain.reshape(1, -1),
        enc_slot.T,
        enc_count.reshape(1, -1),
        enc_need,
    )
    asked = pl.pallas_call(
        ask_kernel,
        in_specs=[hbm] * len(ask_inputs),
        out_shape=jax.ShapeDtypeStruct(sent, bf16),
        scratch_shapes=[pltpu.VMEM(one.shape, one.dtype) for one in ask_inputs]
        + [pltpu.SemaphoreType.DMA((len(ask_inputs),))],
        compiler_params=params(63),
        cost_estimate=cost(2 * rows * depth * width, 2 * depth * width),
        name="ask",
    )(*map(in_hbm, ask_inputs))
    asked = exchange(asked)

    block = math.gcd(points, 256)
    steps = points // block
    pairs = pl.pallas_call(
        functools.partial(front_kernel, steps),
        in_specs=[hbm] * 4,
        out_specs=[vmem] * 2,
        out_shape=[pltpu.VMEM((points, width), bf16)] * 2,
        scratch_shapes=[
            pltpu.VMEM((1, depth), f32),
            pltpu.VMEM((points, depth), bf16),
            pltpu.VMEM((points, depth), bf16),
            pltpu.VMEM((depth, width), bf16),
            pltpu.SemaphoreType.DMA((5,)),
        ],
        compiler_params=params(40),
        cost_estimate=cost(4 * points * depth * width, 8 * points * depth),
        name="front",
    )(*map(in_hbm, (grid_gain.reshape(1, -1), grid, other_grid, w_kv_enc)))

    parts = pl.pallas_call(
        functools.partial(partial_kernel, cap, rows, edges),
        in_specs=[vmem] * 3,
        out_shape=jax.ShapeDtypeStruct(sent, bf16),
        compiler_params=params(40),
        cost_estimate=cost(4 * entries * points * width, 4 * points * width),
        name="partial",
    )(asked, *map(in_vmem, pairs))
    parts, dec_need, dec_slot = lax.optimization_barrier((parts, dec_need, dec_slot))
    order = [[place_of(i, peers) for i in range(peers)]]
    parts = exchange(parts, order)

    slot_total = dec_need.shape[1]
    edge_count = dec_slot.shape[0]
    queries, node_of = pl.pallas_call(
        functools.partial(middle_kernel, steps, peers, rows),
        in_specs=[vmem] * 3 + [hbm] * 2,
        out_specs=[vmem, vmem],
        out_shape=[
            pltpu.VMEM((width, points), bf16),
            jax.ShapeDtypeStruct((edge_count, points), jnp.int32),
        ],
        scratch_shapes=[
            pltpu.VMEM((points, depth), bf16),
            pltpu.VMEM((depth, width), bf16),
            pltpu.SemaphoreType.DMA((2,)),
        ],
        compiler_params=params(40),
        cost_estimate=cost(2 * points * depth * width, 8 * points * depth),
        name="middle",
    )(
        grid_gain.reshape(1, -1),
        dec_need.reshape(slot_total // LANES, LANES),
        dec_slot,
        in_hbm(grid),
        in_hbm(w_q_dec),
    )
    parts, queries, node_of = lax.optimization_barrier((parts, queries, node_of))

    latent_out, everyone = pl.pallas_call(
        combine_kernel,
        out_shape=[
            pltpu.VMEM((rows, depth), bf16),
            jax.ShapeDtypeStruct((peers, rows, width), bf16),
        ],
        compiler_params=params(24),
        cost_estimate=cost(6 * rows * depth * width, 6 * depth * width),
        name="combine",
    )(parts, latent_in, dec_gain.reshape(1, -1), w_o_enc, w_kv_dec)
    own = exchange(everyone, order).reshape(nodes, width)
    other = lax.ppermute(own, "dom", swap)

    queries = in_vmem(queries)
    own_mixed = pl.pallas_call(
        functools.partial(own_kernel, steps),
        in_specs=[vmem] * 3,
        out_shape=jax.ShapeDtypeStruct((points, half), bf16),
        compiler_params=params(48),
        cost_estimate=cost(4 * points * nodes * width, 8 * points * nodes),
        name="own",
    )(own, node_of, queries)
    grid_out = pl.pallas_call(
        functools.partial(other_kernel, steps),
        in_specs=[vmem] * 6,
        out_specs=hbm,
        out_shape=pltpu.HBM((points, depth), bf16),
        scratch_shapes=[
            pltpu.VMEM((points, depth), bf16),
            pltpu.SemaphoreType.DMA((steps,)),
        ],
        compiler_params=params(48),
        cost_estimate=cost(4 * points * depth * width, 8 * points * depth),
        name="other",
    )(other, own_mixed, node_of, queries, grid, w_o_dec)
    return (latent_out, grid_out)


def solution(mesh):
    return jax.shard_map(
        on_device,
        mesh=mesh,
        in_specs=(
            P(("groups", "dom"), None),
            P(("groups", "dom"), None),
            P(),
            P(),
            P(),
            P(),
            P(),
            P(),
            P(),
            P(),
            P(),
            P("dom", None),
            P(None, "dom"),
            P("dom"),
            P("dom", None),
            P(None, "dom"),
        ),
        out_specs=(P(("groups", "dom"), None), P(("groups", "dom"), None)),
        check_vma=False,
    )
```

```python
import functools
import math

import jax
import jax.numpy as jnp
from jax import lax
from jax.experimental import pallas as pl
from jax.experimental.pallas import tpu as pltpu
from jax.sharding import PartitionSpec as P

HEADS = 8
LANES = 128
NEG = -1e30
norm_eps = 1e-06
f32 = jnp.float32
bf16 = jnp.bfloat16


def iota(shape, dim):
    return lax.broadcasted_iota(jnp.int32, shape, dim)


def one_hot(places, shape, dim):
    return (places == iota(shape, dim)).astype(bf16)


def div(values, by):
    if by & (by - 1) == 0:
        return values >> (by.bit_length() - 1)
    return values // by


def mod(values, by):
    if by & (by - 1) == 0:
        return values & (by - 1)
    return values % by


def dot(a, b):
    return jnp.dot(a, b, preferred_element_type=f32)


def dot_t(a, b):
    return lax.dot_general(a, b, (((1,), (1,)), ((), ())), preferred_element_type=f32)


def normed(values, gain):
    widened = values.astype(f32)
    spread = jnp.mean(widened * widened, axis=-1, keepdims=True)
    return (widened * lax.rsqrt(spread + norm_eps) * gain).astype(bf16)


def params(mib):
    return pltpu.CompilerParams(vmem_limit_bytes=mib * 2**20)


def started(*copies):
    for copy in copies:
        copy.start()
    return copies


def cost(flops, read, exps=0):
    return pl.CostEstimate(flops=int(flops), bytes_accessed=int(read), transcendentals=int(exps))


def place_of(index, peers):
    if isinstance(index, int):
        return (index + index % 2 * (peers // 2)) % peers
    return mod(index + (index & 1) * (peers // 2), peers)


def exchange(blocks, order=None):
    return lax.all_to_all(
        blocks, "dom", split_axis=0, concat_axis=0, tiled=True, axis_index_groups=order
    )


def slab(values, i, late, tall):
    return values[late * tall : (late + 1) * tall, i * LANES : (i + 1) * LANES]


def ask_kernel(*refs):
    sources, out_ref, held, sems = refs[:6], refs[6], refs[7:13], refs[13]
    copies = started(
        *[
            pltpu.make_async_copy(source, ref, sems.at[i])
            for i, (source, ref) in enumerate(zip(sources, held))
        ]
    )
    w_ref, latent_ref, gain_ref, slot_ref, count_ref, need_ref = held
    rows = latent_ref.shape[0]
    width = w_ref.shape[1]
    entries = need_ref.shape[1]
    edges = slot_ref.shape[1]
    peers = out_ref.shape[0]
    both = 2 * entries // peers
    tall = rows // 2
    for copy in copies[1:]:
        copy.wait()
    rows_normed = normed(latent_ref[...], gain_ref[...])
    live = iota((edges, rows), 0) < count_ref[...]
    slots = slot_ref[...].astype(f32).T.astype(jnp.int32)
    slots = jnp.where(live, slots, entries) - entries // 2
    slots = slots.astype(f32).astype(bf16)
    tile = jnp.zeros((tall, LANES), f32)
    for g in range(edges // tall):
        to = iota((rows, LANES), 1) == iota((rows, LANES), 0) + g * rows
        tile += dot(slots, to.astype(bf16))[g * tall : (g + 1) * tall]
    row, lane = iota((tall, LANES), 0), iota((tall, LANES), 1)
    in_list = (lane >= LANES // 2) & (lane < LANES // 2 + both)
    need = need_ref[...]
    tiles = []
    for chip in range(peers // 2):
        at = chip * both
        piece = need[:, at // LANES * LANES : at // LANES * LANES + LANES].astype(f32)
        piece = pltpu.roll(jnp.broadcast_to(piece, (tall, LANES)), (LANES // 2 - at) % LANES, 1)
        high = jnp.floor(piece * (1.0 / 256.0))
        piece = jnp.where(row == 0, piece - high * 256.0, jnp.where(row == 1, high, 0.0))
        tiles.append((tile + jnp.where(in_list, piece, 0.0)).astype(bf16))
    copies[0].wait()
    queries = dot(rows_normed, w_ref[...])
    blocks = width // 2 // LANES
    slabs = [
        slab(queries, i, late, tall).astype(bf16) for i in range(2 * blocks) for late in range(2)
    ]
    for p in range(peers):
        for i in range(2 * blocks):
            out_ref[p, i] = slabs[p % 2 * 2 * blocks + i]
        out_ref[p, 2 * blocks] = tiles[p // 2]


def front_kernel(
    steps, gain_hbm, own_hbm, other_hbm, w_hbm, own_out_ref, other_out_ref,
    gain_ref, own_ref, other_ref, w_ref, sems,
):
    points = own_ref.shape[0]
    block = points // steps
    half = own_out_ref.shape[1] // 2
    core = lax.axis_index("dom") & 1
    copies = started(
        pltpu.make_async_copy(gain_hbm, gain_ref, sems.at[0]),
        *[
            pltpu.make_async_copy(
                w_hbm.at[:, pl.ds(pl.multiple_of((core + 2 * i) * half, half), half)],
                w_ref.at[:, pl.ds(i * half, half)],
                sems.at[1 + i],
            )
            for i in range(2)
        ],
        pltpu.make_async_copy(own_hbm, own_ref, sems.at[3]),
        pltpu.make_async_copy(other_hbm, other_ref, sems.at[4]),
    )
    parts = [pl.ds(i * block, block) for i in range(steps)]
    for copy in copies[:3]:
        copy.wait()
    gain = gain_ref[...]
    sides = ((own_ref, own_out_ref), (other_ref, other_out_ref))
    for copy, (rows_ref, out_ref) in zip(copies[3:], sides):
        copy.wait()
        for part in parts:
            out_ref[part, :] = dot(normed(rows_ref[part, :], gain), w_ref[...]).astype(bf16)


def stat_parts(top, total):
    top_1 = top.astype(bf16).astype(f32)
    top_2 = (top - top_1).astype(bf16).astype(f32)
    total_1 = total.astype(bf16).astype(f32)
    return top_1, top_2, top - top_1 - top_2, total_1, total - total_1


def partial_kernel(cap, rows, edges, asked_ref, *refs):
    pairs_refs, out_ref = refs[:2], refs[2]
    me = lax.axis_index("dom")
    points, both = pairs_refs[0].shape
    peers = out_ref.shape[0]
    width = both // 2
    heads = HEADS // 2
    size = width // heads
    tall = rows // 2
    blocks = width // LANES
    scale = math.log2(math.e) / math.sqrt(size)
    all_nodes, all_entries = peers * rows, peers * cap
    some = LANES // (heads * rows)
    nodes, entries = some * rows, some * cap
    tiles = asked_ref[:, 2 * blocks].astype(f32)

    tile_rows = peers * tall
    pick_row = iota((all_entries, tile_rows), 1) - div(iota((all_entries, tile_rows), 0), cap) * tall
    pick = jnp.where(pick_row == 0, 1.0, jnp.where(pick_row == 1, 256.0, 0.0)).astype(bf16)
    lists = dot(pick, tiles.reshape(tile_rows, LANES).astype(bf16))
    lane = iota((all_entries, LANES), 1) - mod(iota((all_entries, LANES), 0), cap) - LANES // 2
    gathered = []
    for other, ref in enumerate(pairs_refs):
        mine = lane == ((me ^ other) & 1) * cap
        index = jnp.sum(jnp.where(mine, lists, 0.0), axis=1, keepdims=True).astype(jnp.int32)
        gathered.append(dot(one_hot(index, (all_entries, points), 1), ref[...]))

    group, across = div(iota((tall, LANES), 1), rows), LANES // rows
    slots = []
    for g in range(edges // tall):
        line = []
        for first in range(0, peers, across):
            merged = jnp.zeros((tall, LANES), f32)
            for w in range(across):
                merged = jnp.where(
                    group == w, pltpu.roll(tiles[first + w], (w - g) * rows % LANES, 1), merged
                )
            line.append(merged)
        slots.append(jnp.concatenate(line, axis=1))
    all_slots = jnp.concatenate(slots, axis=0).astype(jnp.int32) + all_entries // 2

    listed = -(-cap // 8) * 8
    biases = []
    for other in range(2):
        slots = all_slots - (me ^ other) * cap
        uses = jnp.zeros((listed, all_nodes), f32)
        for j in range(edges):
            uses += jnp.where(slots[j : j + 1] == iota((listed, all_nodes), 0), 1.0, 0.0)
        live = uses > 0.5
        biases.append(jnp.where(live, jnp.log2(jnp.where(live, uses, 1.0)), NEG))

    window = mod(div(iota((listed, LANES), 1), rows), some)
    first_nodes = iota((listed, LANES), 1) < nodes
    first_head = iota((nodes, LANES), 1) < size
    tops, totals = [], []
    for start in range(0, peers, some):
        bias = []
        for one in biases:
            at = start * rows
            one = one[:, at // LANES * LANES : at // LANES * LANES + LANES]
            one = jnp.where(first_nodes, pltpu.roll(one, -at % LANES, 1), 0.0)
            spread = nodes
            while spread < LANES:
                one += pltpu.roll(one, spread, 1)
                spread *= 2
            bias += [jnp.where(window == w, one, NEG)[:cap] for w in range(some)]
        part = slice(start * cap, start * cap + entries)
        pairs = jnp.concatenate([one[part] for one in gathered], axis=0).astype(bf16)
        queries = [
            jnp.concatenate(
                [asked_ref[start + n // 2, 2 * i + n % 2].astype(f32) for n in range(2 * some)], axis=0
            )
            for i in range(blocks)
        ]
        queries = jnp.concatenate(queries, axis=1).astype(bf16)
        head = div(iota(queries.shape, 1), size)
        queries = jnp.concatenate(
            [jnp.where(head == h, queries, jnp.zeros_like(queries)) for h in range(heads)], axis=0
        )
        scores = dot_t(pairs[:, :width], queries) * scale + jnp.concatenate(bias, axis=0)
        top = jnp.max(scores, axis=0, keepdims=True)
        raised = jnp.exp2(scores - top)
        tops.append(top)
        totals.append(jnp.sum(raised, axis=0, keepdims=True))
        mixed = dot(raised.T.astype(bf16), pairs[:, width:])
        for i in range(blocks):
            block = mixed[:, i * LANES : (i + 1) * LANES]
            h = i * (LANES // size)
            block = jnp.where(
                first_head, block[h * nodes : (h + 1) * nodes], block[(h + 1) * nodes : (h + 2) * nodes]
            )
            for n in range(2 * some):
                place = place_of(start + n // 2, peers)
                out_ref[place, 2 * i + n % 2] = slab(block, 0, n, tall).astype(bf16)

    row_lane = iota((tall, LANES), 1)
    for first in range(0, len(tops), 8):
        parts = stat_parts(
            jnp.concatenate(tops[first : first + 8], axis=0),
            jnp.concatenate(totals[first : first + 8], axis=0),
        )
        rest = jnp.zeros((LANES - 8 * len(parts), LANES), f32)
        columns = jnp.concatenate([*parts, rest], axis=0).T
        for g in range(8):
            for w in range(some):
                tile = jnp.zeros((tall, LANES), f32)
                for h in range(heads):
                    for late in range(2):
                        at = h * nodes + w * rows + late * tall
                        move = late * (LANES // 2) + h - g
                        here = (mod(row_lane, 8) == h) & (div(row_lane, LANES // 2) == late)
                        piece = pltpu.roll(columns[at : at + tall], move % LANES, 1)
                        tile = jnp.where(here, piece, tile)
                out_ref[place_of((first + g) * some + w, peers), 2 * blocks] = tile.astype(bf16)


def combine_kernel(
    parts_ref, latent_ref, gain_ref, w_o_ref, w_kv_ref, latent_hbm, out_ref, latent_out_ref, sem
):
    peers = parts_ref.shape[0]
    rows = latent_ref.shape[0]
    width = w_o_ref.shape[0]
    half = width // 2
    size, tall = width // HEADS, rows // 2
    chips = (peers // 2, 2, tall, LANES)
    tile = parts_ref[:, 2 * (half // LANES)].astype(f32)

    def moved(columns):
        return pltpu.roll(tile, LANES - columns, 2)

    top = (tile + moved(8) + moved(16)).reshape(chips)
    total = (moved(24) + moved(32)).reshape(chips)
    factor = jnp.exp2(top - jnp.max(top, axis=0, keepdims=True))
    factor = factor / jnp.sum(total * factor, axis=0, keepdims=True)
    head = div(iota(chips, 3), size)
    blocks = []
    for i in range(half // LANES):
        nodes = []
        for late in range(2):
            wide = jnp.zeros(chips, f32)
            for h in range(LANES // size):
                at = late * (LANES // 2) + i * (LANES // size) + h
                wide = jnp.where(head == h, factor[..., at : at + 1], wide)
            part = parts_ref[:, 2 * i + late].astype(f32).reshape(chips)
            nodes.append(jnp.sum(part * wide, axis=0))
        blocks.append(jnp.concatenate(nodes, axis=1))
    mixed = jnp.concatenate([block[h] for h in range(2) for block in blocks], axis=1)
    update = dot(mixed.astype(bf16), w_o_ref[...])
    latent_out = (latent_ref[...].astype(f32) + update).astype(bf16)
    latent_out_ref[...] = latent_out
    copy = pltpu.make_async_copy(latent_out_ref, latent_hbm, sem)
    copy.start()
    pairs = dot(normed(latent_out, gain_ref[...]), w_kv_ref[...]).astype(bf16)
    for p in range(peers):
        at = p % 2 * half
        out_ref[p, :, :half] = pairs[:, at : at + half]
        out_ref[p, :, half:] = pairs[:, width + at : width + at + half]
    copy.wait()


def middle_kernel(
    steps, peers, rows, gain_ref, need_ref, slot_ref, x_hbm, w_hbm, query_ref, node_ref,
    x_ref, w_ref, sems,
):
    copies = started(
        pltpu.make_async_copy(w_hbm, w_ref, sems.at[0]),
        pltpu.make_async_copy(x_hbm, x_ref, sems.at[1]),
    )
    points = x_ref.shape[0]
    block = points // steps
    high_count = need_ref.shape[0]
    cap = high_count * LANES // peers
    need = need_ref[...].astype(f32).astype(bf16)
    for j in range(slot_ref.shape[0]):
        slots = slot_ref[j : j + 1, :]
        row_of = (div(slots, LANES) == iota((high_count, points), 0)).astype(bf16)
        listed = lax.dot_general(need, row_of, (((0,), (0,)), ((), ())), preferred_element_type=f32)
        own = mod(slots, LANES) == iota((LANES, points), 0)
        found = jnp.sum(jnp.where(own, listed, 0.0), axis=0, keepdims=True).astype(jnp.int32)
        node_ref[j : j + 1, :] = place_of(div(slots, cap), peers) * rows + found
    for copy in copies:
        copy.wait()
    for i in range(steps):
        part = pl.ds(i * block, block)
        queries = dot(normed(x_ref[part, :], gain_ref[...]), w_ref[...])
        query_ref[:, part] = queries.T.astype(bf16)


def attend_half(pairs, queries, nodes):
    half, points = queries.shape
    edges = nodes.shape[0]
    heads = HEADS // 2
    size = half // heads
    picks = [one_hot(nodes[j : j + 1], (pairs.shape[1], points), 0) for j in range(edges)]
    scores, values = [], []
    for j in range(edges):
        chosen = dot(pairs, picks[j])
        products = (chosen[:half] * queries.astype(f32)).reshape(heads, size, points)
        scores.append(jnp.sum(products, axis=1) * (1.0 / math.sqrt(size)))
        values.append(chosen[half:].reshape(heads, size, points))
    highest = functools.reduce(jnp.maximum, scores)
    raised = [jnp.exp(score - highest) for score in scores]
    inverse = 1.0 / sum(raised)
    mixed = jnp.zeros((heads, size, points), f32)
    for j in range(edges):
        weight = (raised[j] * inverse).astype(bf16).astype(f32).reshape(heads, 1, points)
        mixed += values[j] * weight
    return mixed.reshape(half, points).T.astype(bf16)


def half_of(ref, first, half):
    return ref.at[pl.ds(pl.multiple_of(first, half), half)]


def own_kernel(steps, pairs_ref, node_ref, query_ref, out_ref):
    points, half = out_ref.shape
    block = points // steps
    core = lax.axis_index("dom") & 1
    queries = half_of(query_ref, core * half, half)
    pairs = pairs_ref[...].T
    for i in range(steps):
        part = pl.ds(i * block, block)
        out_ref[part, :] = attend_half(pairs, queries[:, part], node_ref[:, part])


def other_kernel(
    steps, pairs_ref, own_ref, node_ref, query_ref, x_ref, w_ref, out_hbm, out_ref, sems
):
    points, half = own_ref.shape
    block = points // steps
    core = lax.axis_index("dom") & 1
    queries = half_of(query_ref, (1 - core) * half, half)
    pairs = pairs_ref[...].T
    sends = []
    parts = [pl.ds(i * block, block) for i in range(steps)]

    def attended(part):
        return attend_half(pairs, queries[:, part], node_ref[:, part])

    mixed = attended(parts[0])
    for i, part in enumerate(parts):
        following = attended(parts[i + 1]) if i + 1 < steps else None
        own = own_ref[part, :]
        both = [jnp.where(core == 0, own, mixed), jnp.where(core == 0, mixed, own)]
        update = dot(jnp.concatenate(both, axis=1), w_ref[...])
        out_ref[part, :] = (x_ref[part, :].astype(f32) + update).astype(bf16)
        sends += started(pltpu.make_async_copy(out_ref.at[part], out_hbm.at[part], sems.at[i]))
        mixed = following
    for send in sends:
        send.wait()


def in_hbm(array):
    return pltpu.with_memory_space_constraint(array, pltpu.HBM)


def in_vmem(array):
    return pltpu.with_memory_space_constraint(array, pltpu.VMEM)


def on_device(
    grid,
    latent_in,
    grid_gain,
    node_gain,
    dec_gain,
    w_q_enc,
    w_kv_enc,
    w_o_enc,
    w_q_dec,
    w_kv_dec,
    w_o_dec,
    enc_need,
    enc_slot,
    enc_count,
    dec_need,
    dec_slot,
):
    peers = lax.axis_size("dom")
    points, depth = grid.shape
    rows = latent_in.shape[0]
    width = w_q_enc.shape[1]
    nodes = peers * rows
    entries = enc_need.shape[1]
    edges = enc_slot.shape[0]
    cap = entries // peers
    half = width // 2
    sent = (peers, 2 * (half // LANES) + 1, rows // 2, LANES)
    swap = [(i, i ^ 1) for i in range(peers)]
    vmem = pl.BlockSpec(memory_space=pltpu.VMEM)
    hbm = pl.BlockSpec(memory_space=pltpu.HBM)

    other_grid = lax.ppermute(grid, "dom", swap)
    ask_inputs = (
        w_q_enc,
        latent_in,
        node_gain.reshape(1, -1),
        enc_slot.T,
        enc_count.reshape(1, -1),
        enc_need,
    )
    asked = pl.pallas_call(
        ask_kernel,
        in_specs=[hbm] * len(ask_inputs),
        out_shape=jax.ShapeDtypeStruct(sent, bf16),
        scratch_shapes=[pltpu.VMEM(one.shape, one.dtype) for one in ask_inputs]
        + [pltpu.SemaphoreType.DMA((len(ask_inputs),))],
        compiler_params=params(63),
        cost_estimate=cost(2 * rows * depth * width, 2 * depth * width),
        name="ask",
    )(*map(in_hbm, ask_inputs))
    asked = exchange(asked)

    block = math.gcd(points, 256)
    steps = points // block
    pairs = pl.pallas_call(
        functools.partial(front_kernel, steps),
        in_specs=[hbm] * 4,
        out_specs=[vmem] * 2,
        out_shape=[pltpu.VMEM((points, width), bf16)] * 2,
        scratch_shapes=[
            pltpu.VMEM((1, depth), f32),
            pltpu.VMEM((points, depth), bf16),
            pltpu.VMEM((points, depth), bf16),
            pltpu.VMEM((depth, width), bf16),
            pltpu.SemaphoreType.DMA((5,)),
        ],
        compiler_params=params(40),
        cost_estimate=cost(4 * points * depth * width, 8 * points * depth),
        name="front",
    )(*map(in_hbm, (grid_gain.reshape(1, -1), grid, other_grid, w_kv_enc)))

    parts = pl.pallas_call(
        functools.partial(partial_kernel, cap, rows, edges),
        in_specs=[vmem] * 3,
        out_shape=jax.ShapeDtypeStruct(sent, bf16),
        compiler_params=params(40),
        cost_estimate=cost(4 * entries * points * width, 4 * points * width),
        name="partial",
    )(asked, *map(in_vmem, pairs))
    parts, dec_need, dec_slot = lax.optimization_barrier((parts, dec_need, dec_slot))
    order = [[place_of(i, peers) for i in range(peers)]]
    parts = exchange(parts, order)

    slot_total = dec_need.shape[1]
    edge_count = dec_slot.shape[0]
    queries, node_of = pl.pallas_call(
        functools.partial(middle_kernel, steps, peers, rows),
        in_specs=[vmem] * 3 + [hbm] * 2,
        out_specs=[vmem, vmem],
        out_shape=[
            pltpu.VMEM((width, points), bf16),
            jax.ShapeDtypeStruct((edge_count, points), jnp.int32),
        ],
        scratch_shapes=[
            pltpu.VMEM((points, depth), bf16),
            pltpu.VMEM((depth, width), bf16),
            pltpu.SemaphoreType.DMA((2,)),
        ],
        compiler_params=params(40),
        cost_estimate=cost(2 * points * depth * width, 8 * points * depth),
        name="middle",
    )(
        grid_gain.reshape(1, -1),
        dec_need.reshape(slot_total // LANES, LANES),
        dec_slot,
        in_hbm(grid),
        in_hbm(w_q_dec),
    )
    parts, queries, node_of = lax.optimization_barrier((parts, queries, node_of))

    latent_out, everyone = pl.pallas_call(
        combine_kernel,
        in_specs=[vmem] * 5,
        out_specs=[hbm, vmem],
        out_shape=[
            pltpu.HBM((rows, depth), bf16),
            jax.ShapeDtypeStruct((peers, rows, width), bf16),
        ],
        scratch_shapes=[pltpu.VMEM((rows, depth), bf16), pltpu.SemaphoreType.DMA],
        compiler_params=params(24),
        cost_estimate=cost(6 * rows * depth * width, 6 * depth * width),
        name="combine",
    )(parts, latent_in, dec_gain.reshape(1, -1), w_o_enc, w_kv_dec)
    own = exchange(everyone, order).reshape(nodes, width)
    other = lax.ppermute(own, "dom", swap)

    queries = in_vmem(queries)
    own_mixed = pl.pallas_call(
        functools.partial(own_kernel, steps),
        in_specs=[vmem] * 3,
        out_shape=jax.ShapeDtypeStruct((points, half), bf16),
        compiler_params=params(48),
        cost_estimate=cost(4 * points * nodes * width, 8 * points * nodes),
        name="own",
    )(own, node_of, queries)
    grid_out = pl.pallas_call(
        functools.partial(other_kernel, steps),
        in_specs=[vmem] * 6,
        out_specs=hbm,
        out_shape=pltpu.HBM((points, depth), bf16),
        scratch_shapes=[
            pltpu.VMEM((points, depth), bf16),
            pltpu.SemaphoreType.DMA((steps,)),
        ],
        compiler_params=params(48),
        cost_estimate=cost(4 * points * depth * width, 8 * points * depth),
        name="other",
    )(other, own_mixed, node_of, queries, grid, w_o_dec)
    return (latent_out, grid_out)


def solution(mesh):
    return jax.shard_map(
        on_device,
        mesh=mesh,
        in_specs=(
            P(("groups", "dom"), None),
            P(("groups", "dom"), None),
            P(),
            P(),
            P(),
            P(),
            P(),
            P(),
            P(),
            P(),
            P(),
            P("dom", None),
            P(None, "dom"),
            P("dom"),
            P("dom", None),
            P(None, "dom"),
        ),
        out_specs=(P(("groups", "dom"), None), P(("groups", "dom"), None)),
        check_vma=False,
    )
```

```python
import functools
import math

import jax
import jax.numpy as jnp
from jax import lax
from jax.experimental import pallas as pl
from jax.experimental.pallas import tpu as pltpu
from jax.sharding import PartitionSpec as P

HEADS = 8
LANES = 128
NEG = -1e30
norm_eps = 1e-06
f32 = jnp.float32
bf16 = jnp.bfloat16


def iota(shape, dim):
    return lax.broadcasted_iota(jnp.int32, shape, dim)


def one_hot(places, shape, dim):
    return (places == iota(shape, dim)).astype(bf16)


def div(values, by):
    if by & (by - 1) == 0:
        return values >> (by.bit_length() - 1)
    return values // by


def mod(values, by):
    if by & (by - 1) == 0:
        return values & (by - 1)
    return values % by


def dot(a, b):
    return jnp.dot(a, b, preferred_element_type=f32)


def dot_t(a, b):
    return lax.dot_general(a, b, (((1,), (1,)), ((), ())), preferred_element_type=f32)


def normed(values, gain):
    widened = values.astype(f32)
    spread = jnp.mean(widened * widened, axis=-1, keepdims=True)
    return (widened * lax.rsqrt(spread + norm_eps) * gain).astype(bf16)


def params(mib):
    return pltpu.CompilerParams(vmem_limit_bytes=mib * 2**20)


def started(*copies):
    for copy in copies:
        copy.start()
    return copies


def cost(flops, read, exps=0):
    return pl.CostEstimate(flops=int(flops), bytes_accessed=int(read), transcendentals=int(exps))


def place_of(index, peers):
    if isinstance(index, int):
        return (index + index % 2 * (peers // 2)) % peers
    return mod(index + (index & 1) * (peers // 2), peers)


def exchange(blocks, order=None):
    return lax.all_to_all(
        blocks, "dom", split_axis=0, concat_axis=0, tiled=True, axis_index_groups=order
    )


def slab(values, i, late, tall):
    return values[late * tall : (late + 1) * tall, i * LANES : (i + 1) * LANES]


def ask_kernel(*refs):
    sources, out_ref, held, sems = refs[:6], refs[6], refs[7:13], refs[13]
    copies = started(
        *[
            pltpu.make_async_copy(source, ref, sems.at[i])
            for i, (source, ref) in enumerate(zip(sources, held))
        ]
    )
    w_ref, latent_ref, gain_ref, slot_ref, count_ref, need_ref = held
    rows = latent_ref.shape[0]
    width = w_ref.shape[1]
    entries = need_ref.shape[1]
    edges = slot_ref.shape[1]
    peers = out_ref.shape[0]
    both = 2 * entries // peers
    tall = rows // 2
    for copy in copies[1:]:
        copy.wait()
    rows_normed = normed(latent_ref[...], gain_ref[...])
    live = iota((edges, rows), 0) < count_ref[...]
    slots = slot_ref[...].astype(f32).T.astype(jnp.int32)
    slots = jnp.where(live, slots, entries) - entries // 2
    slots = slots.astype(f32).astype(bf16)
    tile = jnp.zeros((tall, LANES), f32)
    for g in range(edges // tall):
        to = iota((rows, LANES), 1) == iota((rows, LANES), 0) + g * rows
        tile += dot(slots, to.astype(bf16))[g * tall : (g + 1) * tall]
    row, lane = iota((tall, LANES), 0), iota((tall, LANES), 1)
    in_list = (lane >= LANES // 2) & (lane < LANES // 2 + both)
    need = need_ref[...]
    tiles = []
    for chip in range(peers // 2):
        at = chip * both
        piece = need[:, at // LANES * LANES : at // LANES * LANES + LANES].astype(f32)
        piece = pltpu.roll(jnp.broadcast_to(piece, (tall, LANES)), (LANES // 2 - at) % LANES, 1)
        high = jnp.floor(piece * (1.0 / 256.0))
        piece = jnp.where(row == 0, piece - high * 256.0, jnp.where(row == 1, high, 0.0))
        tiles.append((tile + jnp.where(in_list, piece, 0.0)).astype(bf16))
    copies[0].wait()
    queries = dot(rows_normed, w_ref[...])
    blocks = width // 2 // LANES
    slabs = [
        slab(queries, i, late, tall).astype(bf16) for i in range(2 * blocks) for late in range(2)
    ]
    for p in range(peers):
        for i in range(2 * blocks):
            out_ref[p, i] = slabs[p % 2 * 2 * blocks + i]
        out_ref[p, 2 * blocks] = tiles[p // 2]


def front_kernel(
    steps, gain_hbm, own_hbm, other_hbm, w_hbm, own_out_ref, other_out_ref,
    gain_ref, own_ref, other_ref, w_ref, sems,
):
    points = own_ref.shape[0]
    block = points // steps
    half = own_out_ref.shape[1] // 2
    core = lax.axis_index("dom") & 1
    copies = started(
        pltpu.make_async_copy(gain_hbm, gain_ref, sems.at[0]),
        *[
            pltpu.make_async_copy(
                w_hbm.at[:, pl.ds(pl.multiple_of((core + 2 * i) * half, half), half)],
                w_ref.at[:, pl.ds(i * half, half)],
                sems.at[1 + i],
            )
            for i in range(2)
        ],
        pltpu.make_async_copy(own_hbm, own_ref, sems.at[3]),
        pltpu.make_async_copy(other_hbm, other_ref, sems.at[4]),
    )
    parts = [pl.ds(i * block, block) for i in range(steps)]
    for copy in copies[:3]:
        copy.wait()
    gain = gain_ref[...]
    sides = ((own_ref, own_out_ref), (other_ref, other_out_ref))
    for copy, (rows_ref, out_ref) in zip(copies[3:], sides):
        copy.wait()
        for part in parts:
            out_ref[part, :] = dot(normed(rows_ref[part, :], gain), w_ref[...]).astype(bf16)


def stat_parts(top, total):
    top_1 = top.astype(bf16).astype(f32)
    top_2 = (top - top_1).astype(bf16).astype(f32)
    total_1 = total.astype(bf16).astype(f32)
    return top_1, top_2, top - top_1 - top_2, total_1, total - total_1


def partial_kernel(cap, rows, edges, asked_ref, *refs):
    pairs_refs, out_ref = refs[:2], refs[2]
    me = lax.axis_index("dom")
    points, both = pairs_refs[0].shape
    peers = out_ref.shape[0]
    width = both // 2
    heads = HEADS // 2
    size = width // heads
    tall = rows // 2
    blocks = width // LANES
    scale = math.log2(math.e) / math.sqrt(size)
    all_nodes, all_entries = peers * rows, peers * cap
    some = LANES // (heads * rows)
    nodes, entries = some * rows, some * cap
    tiles = asked_ref[:, 2 * blocks].astype(f32)

    tile_rows = peers * tall
    pick_row = iota((all_entries, tile_rows), 1) - div(iota((all_entries, tile_rows), 0), cap) * tall
    pick = jnp.where(pick_row == 0, 1.0, jnp.where(pick_row == 1, 256.0, 0.0)).astype(bf16)
    lists = dot(pick, tiles.reshape(tile_rows, LANES).astype(bf16))
    lane = iota((all_entries, LANES), 1) - mod(iota((all_entries, LANES), 0), cap) - LANES // 2
    gathered = []
    for other, ref in enumerate(pairs_refs):
        mine = lane == ((me ^ other) & 1) * cap
        index = jnp.sum(jnp.where(mine, lists, 0.0), axis=1, keepdims=True).astype(jnp.int32)
        gathered.append(dot(one_hot(index, (all_entries, points), 1), ref[...]))

    group, across = div(iota((tall, LANES), 1), rows), LANES // rows
    slots = []
    for g in range(edges // tall):
        line = []
        for first in range(0, peers, across):
            merged = jnp.zeros((tall, LANES), f32)
            for w in range(across):
                merged = jnp.where(
                    group == w, pltpu.roll(tiles[first + w], (w - g) * rows % LANES, 1), merged
                )
            line.append(merged)
        slots.append(jnp.concatenate(line, axis=1))
    all_slots = jnp.concatenate(slots, axis=0).astype(jnp.int32) + all_entries // 2

    listed = -(-cap // 8) * 8
    biases = []
    for other in range(2):
        slots = all_slots - (me ^ other) * cap
        uses = jnp.zeros((listed, all_nodes), f32)
        for j in range(edges):
            uses += jnp.where(slots[j : j + 1] == iota((listed, all_nodes), 0), 1.0, 0.0)
        live = uses > 0.5
        biases.append(jnp.where(live, jnp.log2(jnp.where(live, uses, 1.0)), NEG))

    window = mod(div(iota((listed, LANES), 1), rows), some)
    first_nodes = iota((listed, LANES), 1) < nodes
    first_head = iota((nodes, LANES), 1) < size
    tops, totals = [], []
    for start in range(0, peers, some):
        bias = []
        for one in biases:
            at = start * rows
            one = one[:, at // LANES * LANES : at // LANES * LANES + LANES]
            one = jnp.where(first_nodes, pltpu.roll(one, -at % LANES, 1), 0.0)
            spread = nodes
            while spread < LANES:
                one += pltpu.roll(one, spread, 1)
                spread *= 2
            bias += [jnp.where(window == w, one, NEG)[:cap] for w in range(some)]
        part = slice(start * cap, start * cap + entries)
        pairs = jnp.concatenate([one[part] for one in gathered], axis=0).astype(bf16)
        queries = [
            jnp.concatenate(
                [asked_ref[start + n // 2, 2 * i + n % 2].astype(f32) for n in range(2 * some)], axis=0
            )
            for i in range(blocks)
        ]
        queries = jnp.concatenate(queries, axis=1).astype(bf16)
        head = div(iota(queries.shape, 1), size)
        queries = jnp.concatenate(
            [jnp.where(head == h, queries, jnp.zeros_like(queries)) for h in range(heads)], axis=0
        )
        scores = dot_t(pairs[:, :width], queries) * scale + jnp.concatenate(bias, axis=0)
        top = jnp.max(scores, axis=0, keepdims=True)
        raised = jnp.exp2(scores - top)
        tops.append(top)
        totals.append(jnp.sum(raised, axis=0, keepdims=True))
        mixed = dot(raised.T.astype(bf16), pairs[:, width:])
        for i in range(blocks):
            block = mixed[:, i * LANES : (i + 1) * LANES]
            h = i * (LANES // size)
            block = jnp.where(
                first_head, block[h * nodes : (h + 1) * nodes], block[(h + 1) * nodes : (h + 2) * nodes]
            )
            for n in range(2 * some):
                place = place_of(start + n // 2, peers)
                out_ref[place, 2 * i + n % 2] = slab(block, 0, n, tall).astype(bf16)

    row_lane = iota((tall, LANES), 1)
    for first in range(0, len(tops), 8):
        parts = stat_parts(
            jnp.concatenate(tops[first : first + 8], axis=0),
            jnp.concatenate(totals[first : first + 8], axis=0),
        )
        rest = jnp.zeros((LANES - 8 * len(parts), LANES), f32)
        columns = jnp.concatenate([*parts, rest], axis=0).T
        for g in range(8):
            for w in range(some):
                tile = jnp.zeros((tall, LANES), f32)
                for h in range(heads):
                    for late in range(2):
                        at = h * nodes + w * rows + late * tall
                        move = late * (LANES // 2) + h - g
                        here = (mod(row_lane, 8) == h) & (div(row_lane, LANES // 2) == late)
                        piece = pltpu.roll(columns[at : at + tall], move % LANES, 1)
                        tile = jnp.where(here, piece, tile)
                out_ref[place_of((first + g) * some + w, peers), 2 * blocks] = tile.astype(bf16)


def combine_kernel(parts_ref, latent_ref, gain_ref, w_o_ref, w_kv_ref, latent_out_ref, out_ref):
    peers = parts_ref.shape[0]
    rows = latent_ref.shape[0]
    width = w_o_ref.shape[0]
    half = width // 2
    size, tall = width // HEADS, rows // 2
    chips = (peers // 2, 2, tall, LANES)
    tile = parts_ref[:, 2 * (half // LANES)].astype(f32)

    def moved(columns):
        return pltpu.roll(tile, LANES - columns, 2)

    top = (tile + moved(8) + moved(16)).reshape(chips)
    total = (moved(24) + moved(32)).reshape(chips)
    factor = jnp.exp2(top - jnp.max(top, axis=0, keepdims=True))
    factor = factor / jnp.sum(total * factor, axis=0, keepdims=True)
    head = div(iota(chips, 3), size)
    blocks = []
    for i in range(half // LANES):
        nodes = []
        for late in range(2):
            wide = jnp.zeros(chips, f32)
            for h in range(LANES // size):
                at = late * (LANES // 2) + i * (LANES // size) + h
                wide = jnp.where(head == h, factor[..., at : at + 1], wide)
            part = parts_ref[:, 2 * i + late].astype(f32).reshape(chips)
            nodes.append(jnp.sum(part * wide, axis=0))
        blocks.append(jnp.concatenate(nodes, axis=1))
    mixed = jnp.concatenate([block[h] for h in range(2) for block in blocks], axis=1)
    update = dot(mixed.astype(bf16), w_o_ref[...])
    latent_out = (latent_ref[...].astype(f32) + update).astype(bf16)
    latent_out_ref[...] = latent_out
    pairs = dot(normed(latent_out, gain_ref[...]), w_kv_ref[...]).astype(bf16)
    for p in range(peers):
        at = p % 2 * half
        out_ref[p, :, :half] = pairs[:, at : at + half]
        out_ref[p, :, half:] = pairs[:, width + at : width + at + half]


def middle_kernel(
    steps, peers, rows, gain_ref, need_ref, slot_ref, x_hbm, w_hbm, query_ref, node_ref,
    x_ref, w_ref, sems,
):
    copies = started(
        pltpu.make_async_copy(w_hbm, w_ref, sems.at[0]),
        pltpu.make_async_copy(x_hbm, x_ref, sems.at[1]),
    )
    points = x_ref.shape[0]
    block = points // steps
    high_count = need_ref.shape[0]
    cap = high_count * LANES // peers
    need = need_ref[...].astype(f32).astype(bf16)
    for j in range(slot_ref.shape[0]):
        slots = slot_ref[j : j + 1, :]
        row_of = (div(slots, LANES) == iota((high_count, points), 0)).astype(bf16)
        listed = lax.dot_general(need, row_of, (((0,), (0,)), ((), ())), preferred_element_type=f32)
        own = mod(slots, LANES) == iota((LANES, points), 0)
        found = jnp.sum(jnp.where(own, listed, 0.0), axis=0, keepdims=True).astype(jnp.int32)
        node_ref[j : j + 1, :] = place_of(div(slots, cap), peers) * rows + found
    for copy in copies:
        copy.wait()
    for i in range(steps):
        part = pl.ds(i * block, block)
        queries = dot(normed(x_ref[part, :], gain_ref[...]), w_ref[...])
        query_ref[:, part] = queries.T.astype(bf16)


def attend_half(pairs, queries, nodes):
    half, points = queries.shape
    edges = nodes.shape[0]
    heads = HEADS // 2
    size = half // heads
    picks = [one_hot(nodes[j : j + 1], (pairs.shape[1], points), 0) for j in range(edges)]
    scores, values = [], []
    for j in range(edges):
        chosen = dot(pairs, picks[j])
        products = (chosen[:half] * queries.astype(f32)).reshape(heads, size, points)
        scores.append(jnp.sum(products, axis=1) * (1.0 / math.sqrt(size)))
        values.append(chosen[half:].reshape(heads, size, points))
    highest = functools.reduce(jnp.maximum, scores)
    raised = [jnp.exp(score - highest) for score in scores]
    inverse = 1.0 / sum(raised)
    mixed = jnp.zeros((heads, size, points), f32)
    for j in range(edges):
        weight = (raised[j] * inverse).astype(bf16).astype(f32).reshape(heads, 1, points)
        mixed += values[j] * weight
    return mixed.reshape(half, points).T.astype(bf16)


def half_of(ref, first, half):
    return ref.at[pl.ds(pl.multiple_of(first, half), half)]


def own_kernel(steps, pairs_ref, node_ref, query_ref, out_ref):
    points, half = out_ref.shape
    block = points // steps
    core = lax.axis_index("dom") & 1
    queries = half_of(query_ref, core * half, half)
    pairs = pairs_ref[...].T
    for i in range(steps):
        part = pl.ds(i * block, block)
        out_ref[part, :] = attend_half(pairs, queries[:, part], node_ref[:, part])


def other_kernel(
    steps, pairs_ref, own_ref, node_ref, query_ref, x_ref, w_ref, latent_ref,
    out_hbm, latent_hbm, out_ref, sems,
):
    latent_copy = pltpu.make_async_copy(latent_ref, latent_hbm, sems.at[steps])
    latent_copy.start()
    points, half = own_ref.shape
    block = points // steps
    core = lax.axis_index("dom") & 1
    queries = half_of(query_ref, (1 - core) * half, half)
    pairs = pairs_ref[...].T
    sends = []
    parts = [pl.ds(i * block, block) for i in range(steps)]

    def attended(part):
        return attend_half(pairs, queries[:, part], node_ref[:, part])

    mixed = attended(parts[0])
    for i, part in enumerate(parts):
        following = attended(parts[i + 1]) if i + 1 < steps else None
        own = own_ref[part, :]
        both = [jnp.where(core == 0, own, mixed), jnp.where(core == 0, mixed, own)]
        update = dot(jnp.concatenate(both, axis=1), w_ref[...])
        out_ref[part, :] = (x_ref[part, :].astype(f32) + update).astype(bf16)
        sends += started(pltpu.make_async_copy(out_ref.at[part], out_hbm.at[part], sems.at[i]))
        mixed = following
    for send in sends:
        send.wait()
    latent_copy.wait()


def in_hbm(array):
    return pltpu.with_memory_space_constraint(array, pltpu.HBM)


def in_vmem(array):
    return pltpu.with_memory_space_constraint(array, pltpu.VMEM)


def on_device(
    grid,
    latent_in,
    grid_gain,
    node_gain,
    dec_gain,
    w_q_enc,
    w_kv_enc,
    w_o_enc,
    w_q_dec,
    w_kv_dec,
    w_o_dec,
    enc_need,
    enc_slot,
    enc_count,
    dec_need,
    dec_slot,
):
    peers = lax.axis_size("dom")
    points, depth = grid.shape
    rows = latent_in.shape[0]
    width = w_q_enc.shape[1]
    nodes = peers * rows
    entries = enc_need.shape[1]
    edges = enc_slot.shape[0]
    cap = entries // peers
    half = width // 2
    sent = (peers, 2 * (half // LANES) + 1, rows // 2, LANES)
    swap = [(i, i ^ 1) for i in range(peers)]
    vmem = pl.BlockSpec(memory_space=pltpu.VMEM)
    hbm = pl.BlockSpec(memory_space=pltpu.HBM)

    other_grid = lax.ppermute(grid, "dom", swap)
    ask_inputs = (
        w_q_enc,
        latent_in,
        node_gain.reshape(1, -1),
        enc_slot.T,
        enc_count.reshape(1, -1),
        enc_need,
    )
    asked = pl.pallas_call(
        ask_kernel,
        in_specs=[hbm] * len(ask_inputs),
        out_shape=jax.ShapeDtypeStruct(sent, bf16),
        scratch_shapes=[pltpu.VMEM(one.shape, one.dtype) for one in ask_inputs]
        + [pltpu.SemaphoreType.DMA((len(ask_inputs),))],
        compiler_params=params(63),
        cost_estimate=cost(2 * rows * depth * width, 2 * depth * width),
        name="ask",
    )(*map(in_hbm, ask_inputs))
    asked = exchange(asked)

    block = math.gcd(points, 256)
    steps = points // block
    pairs = pl.pallas_call(
        functools.partial(front_kernel, steps),
        in_specs=[hbm] * 4,
        out_specs=[vmem] * 2,
        out_shape=[pltpu.VMEM((points, width), bf16)] * 2,
        scratch_shapes=[
            pltpu.VMEM((1, depth), f32),
            pltpu.VMEM((points, depth), bf16),
            pltpu.VMEM((points, depth), bf16),
            pltpu.VMEM((depth, width), bf16),
            pltpu.SemaphoreType.DMA((5,)),
        ],
        compiler_params=params(40),
        cost_estimate=cost(4 * points * depth * width, 8 * points * depth),
        name="front",
    )(*map(in_hbm, (grid_gain.reshape(1, -1), grid, other_grid, w_kv_enc)))

    parts = pl.pallas_call(
        functools.partial(partial_kernel, cap, rows, edges),
        in_specs=[vmem] * 3,
        out_shape=jax.ShapeDtypeStruct(sent, bf16),
        compiler_params=params(40),
        cost_estimate=cost(4 * entries * points * width, 4 * points * width),
        name="partial",
    )(asked, *map(in_vmem, pairs))
    parts, dec_need, dec_slot = lax.optimization_barrier((parts, dec_need, dec_slot))
    order = [[place_of(i, peers) for i in range(peers)]]
    parts = exchange(parts, order)

    slot_total = dec_need.shape[1]
    edge_count = dec_slot.shape[0]
    queries, node_of = pl.pallas_call(
        functools.partial(middle_kernel, steps, peers, rows),
        in_specs=[vmem] * 3 + [hbm] * 2,
        out_specs=[vmem, vmem],
        out_shape=[
            pltpu.VMEM((width, points), bf16),
            jax.ShapeDtypeStruct((edge_count, points), jnp.int32),
        ],
        scratch_shapes=[
            pltpu.VMEM((points, depth), bf16),
            pltpu.VMEM((depth, width), bf16),
            pltpu.SemaphoreType.DMA((2,)),
        ],
        compiler_params=params(40),
        cost_estimate=cost(2 * points * depth * width, 8 * points * depth),
        name="middle",
    )(
        grid_gain.reshape(1, -1),
        dec_need.reshape(slot_total // LANES, LANES),
        dec_slot,
        in_hbm(grid),
        in_hbm(w_q_dec),
    )
    parts, queries, node_of = lax.optimization_barrier((parts, queries, node_of))

    latent_out, everyone = pl.pallas_call(
        combine_kernel,
        in_specs=[vmem] * 5,
        out_specs=[vmem] * 2,
        out_shape=[
            pltpu.VMEM((rows, depth), bf16),
            jax.ShapeDtypeStruct((peers, rows, width), bf16),
        ],
        compiler_params=params(24),
        cost_estimate=cost(6 * rows * depth * width, 6 * depth * width),
        name="combine",
    )(parts, latent_in, dec_gain.reshape(1, -1), w_o_enc, w_kv_dec)
    own = exchange(everyone, order).reshape(nodes, width)
    other = lax.ppermute(own, "dom", swap)

    queries = in_vmem(queries)
    own_mixed = pl.pallas_call(
        functools.partial(own_kernel, steps),
        in_specs=[vmem] * 3,
        out_shape=jax.ShapeDtypeStruct((points, half), bf16),
        compiler_params=params(48),
        cost_estimate=cost(4 * points * nodes * width, 8 * points * nodes),
        name="own",
    )(own, node_of, queries)
    grid_out, latent_out = pl.pallas_call(
        functools.partial(other_kernel, steps),
        in_specs=[vmem] * 7,
        out_specs=[hbm] * 2,
        out_shape=[pltpu.HBM((points, depth), bf16), pltpu.HBM((rows, depth), bf16)],
        scratch_shapes=[
            pltpu.VMEM((points, depth), bf16),
            pltpu.SemaphoreType.DMA((steps + 1,)),
        ],
        compiler_params=params(48),
        cost_estimate=cost(4 * points * depth * width, 8 * points * depth),
        name="other",
    )(other, own_mixed, node_of, queries, grid, w_o_dec, in_vmem(latent_out))
    return (latent_out, grid_out)


def solution(mesh):
    return jax.shard_map(
        on_device,
        mesh=mesh,
        in_specs=(
            P(("groups", "dom"), None),
            P(("groups", "dom"), None),
            P(),
            P(),
            P(),
            P(),
            P(),
            P(),
            P(),
            P(),
            P(),
            P("dom", None),
            P(None, "dom"),
            P("dom"),
            P("dom", None),
            P(None, "dom"),
        ),
        out_specs=(P(("groups", "dom"), None), P(("groups", "dom"), None)),
        check_vma=False,
    )
```

```python
import functools
import math

import jax
import jax.numpy as jnp
from jax import lax
from jax.experimental import pallas as pl
from jax.experimental.pallas import tpu as pltpu
from jax.sharding import PartitionSpec as P

HEADS = 8
LANES = 128
NEG = -1e30
norm_eps = 1e-06
f32 = jnp.float32
bf16 = jnp.bfloat16


def iota(shape, dim):
    return lax.broadcasted_iota(jnp.int32, shape, dim)


def one_hot(places, shape, dim):
    return (places == iota(shape, dim)).astype(bf16)


def div(values, by):
    if by & (by - 1) == 0:
        return values >> (by.bit_length() - 1)
    return values // by


def mod(values, by):
    if by & (by - 1) == 0:
        return values & (by - 1)
    return values % by


def dot(a, b):
    return jnp.dot(a, b, preferred_element_type=f32)


def dot_t(a, b):
    return lax.dot_general(a, b, (((1,), (1,)), ((), ())), preferred_element_type=f32)


def normed(values, gain):
    widened = values.astype(f32)
    spread = jnp.mean(widened * widened, axis=-1, keepdims=True)
    return (widened * lax.rsqrt(spread + norm_eps) * gain).astype(bf16)


def params(mib):
    return pltpu.CompilerParams(vmem_limit_bytes=mib * 2**20)


def started(*copies):
    for copy in copies:
        copy.start()
    return copies


def cost(flops, read, exps=0):
    return pl.CostEstimate(flops=int(flops), bytes_accessed=int(read), transcendentals=int(exps))


def place_of(index, peers):
    if isinstance(index, int):
        return (index + index % 2 * (peers // 2)) % peers
    return mod(index + (index & 1) * (peers // 2), peers)


def exchange(blocks, order=None):
    return lax.all_to_all(
        blocks, "dom", split_axis=0, concat_axis=0, tiled=True, axis_index_groups=order
    )


def slab(values, i, late, tall):
    return values[late * tall : (late + 1) * tall, i * LANES : (i + 1) * LANES]


def ask_kernel(*refs):
    sources, out_ref, held, sems = refs[:6], refs[6], refs[7:13], refs[13]
    copies = started(
        *[
            pltpu.make_async_copy(source, ref, sems.at[i])
            for i, (source, ref) in enumerate(zip(sources, held))
        ]
    )
    w_ref, latent_ref, gain_ref, slot_ref, count_ref, need_ref = held
    rows = latent_ref.shape[0]
    width = w_ref.shape[1]
    entries = need_ref.shape[1]
    edges = slot_ref.shape[1]
    peers = out_ref.shape[0]
    both = 2 * entries // peers
    tall = rows // 2
    for copy in copies[1:]:
        copy.wait()
    rows_normed = normed(latent_ref[...], gain_ref[...])
    live = iota((edges, rows), 0) < count_ref[...]
    slots = slot_ref[...].astype(f32).T.astype(jnp.int32)
    slots = jnp.where(live, slots, entries) - entries // 2
    slots = slots.astype(f32).astype(bf16)
    tile = jnp.zeros((tall, LANES), f32)
    for g in range(edges // tall):
        to = iota((rows, LANES), 1) == iota((rows, LANES), 0) + g * rows
        tile += dot(slots, to.astype(bf16))[g * tall : (g + 1) * tall]
    row, lane = iota((tall, LANES), 0), iota((tall, LANES), 1)
    in_list = (lane >= LANES // 2) & (lane < LANES // 2 + both)
    need = need_ref[...]
    tiles = []
    for chip in range(peers // 2):
        at = chip * both
        piece = need[:, at // LANES * LANES : at // LANES * LANES + LANES].astype(f32)
        piece = pltpu.roll(jnp.broadcast_to(piece, (tall, LANES)), (LANES // 2 - at) % LANES, 1)
        high = jnp.floor(piece * (1.0 / 256.0))
        piece = jnp.where(row == 0, piece - high * 256.0, jnp.where(row == 1, high, 0.0))
        tiles.append((tile + jnp.where(in_list, piece, 0.0)).astype(bf16))
    copies[0].wait()
    queries = dot(rows_normed, w_ref[...])
    blocks = width // 2 // LANES
    slabs = [
        slab(queries, i, late, tall).astype(bf16) for i in range(2 * blocks) for late in range(2)
    ]
    for p in range(peers):
        for i in range(2 * blocks):
            out_ref[p, i] = slabs[p % 2 * 2 * blocks + i]
        out_ref[p, 2 * blocks] = tiles[p // 2]


def front_kernel(
    steps, gain_hbm, own_hbm, other_hbm, w_hbm, own_out_ref, other_out_ref,
    gain_ref, own_ref, other_ref, w_ref, sems,
):
    points = own_ref.shape[0]
    block = points // steps
    half = own_out_ref.shape[1] // 2
    core = lax.axis_index("dom") & 1
    copies = started(
        pltpu.make_async_copy(gain_hbm, gain_ref, sems.at[0]),
        *[
            pltpu.make_async_copy(
                w_hbm.at[:, pl.ds(pl.multiple_of((core + 2 * i) * half, half), half)],
                w_ref.at[:, pl.ds(i * half, half)],
                sems.at[1 + i],
            )
            for i in range(2)
        ],
        pltpu.make_async_copy(own_hbm, own_ref, sems.at[3]),
        pltpu.make_async_copy(other_hbm, other_ref, sems.at[4]),
    )
    parts = [pl.ds(i * block, block) for i in range(steps)]
    for copy in copies[:3]:
        copy.wait()
    gain = gain_ref[...]
    sides = ((own_ref, own_out_ref), (other_ref, other_out_ref))
    for copy, (rows_ref, out_ref) in zip(copies[3:], sides):
        copy.wait()
        for part in parts:
            out_ref[part, :] = dot(normed(rows_ref[part, :], gain), w_ref[...]).astype(bf16)


def stat_parts(top, total):
    top_1 = top.astype(bf16).astype(f32)
    top_2 = (top - top_1).astype(bf16).astype(f32)
    total_1 = total.astype(bf16).astype(f32)
    return top_1, top_2, top - top_1 - top_2, total_1, total - total_1


def partial_kernel(cap, rows, edges, asked_ref, *refs):
    pairs_refs, out_ref = refs[:2], refs[2]
    me = lax.axis_index("dom")
    points, both = pairs_refs[0].shape
    peers = out_ref.shape[0]
    width = both // 2
    heads = HEADS // 2
    size = width // heads
    tall = rows // 2
    blocks = width // LANES
    scale = math.log2(math.e) / math.sqrt(size)
    all_nodes, all_entries = peers * rows, peers * cap
    some = LANES // (heads * rows)
    nodes, entries = some * rows, some * cap
    tiles = asked_ref[:, 2 * blocks].astype(f32)

    tile_rows = peers * tall
    pick_row = iota((all_entries, tile_rows), 1) - div(iota((all_entries, tile_rows), 0), cap) * tall
    pick = jnp.where(pick_row == 0, 1.0, jnp.where(pick_row == 1, 256.0, 0.0)).astype(bf16)
    lists = dot(pick, tiles.reshape(tile_rows, LANES).astype(bf16))
    lane = iota((all_entries, LANES), 1) - mod(iota((all_entries, LANES), 0), cap) - LANES // 2
    gathered = []
    for other, ref in enumerate(pairs_refs):
        mine = lane == ((me ^ other) & 1) * cap
        index = jnp.sum(jnp.where(mine, lists, 0.0), axis=1, keepdims=True).astype(jnp.int32)
        gathered.append(dot(one_hot(index, (all_entries, points), 1), ref[...]))

    group, across = div(iota((tall, LANES), 1), rows), LANES // rows
    slots = []
    for g in range(edges // tall):
        line = []
        for first in range(0, peers, across):
            merged = jnp.zeros((tall, LANES), f32)
            for w in range(across):
                merged = jnp.where(
                    group == w, pltpu.roll(tiles[first + w], (w - g) * rows % LANES, 1), merged
                )
            line.append(merged)
        slots.append(jnp.concatenate(line, axis=1))
    all_slots = jnp.concatenate(slots, axis=0).astype(jnp.int32) + all_entries // 2

    listed = -(-cap // 8) * 8
    biases = []
    for other in range(2):
        slots = all_slots - (me ^ other) * cap
        uses = jnp.zeros((listed, all_nodes), f32)
        for j in range(edges):
            uses += jnp.where(slots[j : j + 1] == iota((listed, all_nodes), 0), 1.0, 0.0)
        live = uses > 0.5
        biases.append(jnp.where(live, jnp.log2(jnp.where(live, uses, 1.0)), NEG))

    window = mod(div(iota((listed, LANES), 1), rows), some)
    first_nodes = iota((listed, LANES), 1) < nodes
    first_head = iota((nodes, LANES), 1) < size
    tops, totals = [], []
    for start in range(0, peers, some):
        bias = []
        for one in biases:
            at = start * rows
            one = one[:, at // LANES * LANES : at // LANES * LANES + LANES]
            one = jnp.where(first_nodes, pltpu.roll(one, -at % LANES, 1), 0.0)
            spread = nodes
            while spread < LANES:
                one += pltpu.roll(one, spread, 1)
                spread *= 2
            bias += [jnp.where(window == w, one, NEG)[:cap] for w in range(some)]
        part = slice(start * cap, start * cap + entries)
        pairs = jnp.concatenate([one[part] for one in gathered], axis=0).astype(bf16)
        queries = [
            jnp.concatenate(
                [asked_ref[start + n // 2, 2 * i + n % 2].astype(f32) for n in range(2 * some)], axis=0
            )
            for i in range(blocks)
        ]
        queries = jnp.concatenate(queries, axis=1).astype(bf16)
        head = div(iota(queries.shape, 1), size)
        queries = jnp.concatenate(
            [jnp.where(head == h, queries, jnp.zeros_like(queries)) for h in range(heads)], axis=0
        )
        scores = dot_t(pairs[:, :width], queries) * scale + jnp.concatenate(bias, axis=0)
        top = jnp.max(scores, axis=0, keepdims=True)
        raised = jnp.exp2(scores - top)
        tops.append(top)
        totals.append(jnp.sum(raised, axis=0, keepdims=True))
        mixed = dot(raised.T.astype(bf16), pairs[:, width:])
        for i in range(blocks):
            block = mixed[:, i * LANES : (i + 1) * LANES]
            h = i * (LANES // size)
            block = jnp.where(
                first_head, block[h * nodes : (h + 1) * nodes], block[(h + 1) * nodes : (h + 2) * nodes]
            )
            for n in range(2 * some):
                place = place_of(start + n // 2, peers)
                out_ref[place, 2 * i + n % 2] = slab(block, 0, n, tall).astype(bf16)

    row_lane = iota((tall, LANES), 1)
    for first in range(0, len(tops), 8):
        parts = stat_parts(
            jnp.concatenate(tops[first : first + 8], axis=0),
            jnp.concatenate(totals[first : first + 8], axis=0),
        )
        rest = jnp.zeros((LANES - 8 * len(parts), LANES), f32)
        columns = jnp.concatenate([*parts, rest], axis=0).T
        for g in range(8):
            for w in range(some):
                tile = jnp.zeros((tall, LANES), f32)
                for h in range(heads):
                    for late in range(2):
                        at = h * nodes + w * rows + late * tall
                        move = late * (LANES // 2) + h - g
                        here = (mod(row_lane, 8) == h) & (div(row_lane, LANES // 2) == late)
                        piece = pltpu.roll(columns[at : at + tall], move % LANES, 1)
                        tile = jnp.where(here, piece, tile)
                out_ref[place_of((first + g) * some + w, peers), 2 * blocks] = tile.astype(bf16)


def combine_kernel(parts_ref, latent_ref, gain_ref, w_o_ref, w_kv_ref, latent_out_ref, out_ref):
    peers = parts_ref.shape[0]
    rows = latent_ref.shape[0]
    width = w_o_ref.shape[0]
    half = width // 2
    size, tall = width // HEADS, rows // 2
    chips = (peers // 2, 2, tall, LANES)
    tile = parts_ref[:, 2 * (half // LANES)].astype(f32)

    def moved(columns):
        return pltpu.roll(tile, LANES - columns, 2)

    top = (tile + moved(8) + moved(16)).reshape(chips)
    total = (moved(24) + moved(32)).reshape(chips)
    factor = jnp.exp2(top - jnp.max(top, axis=0, keepdims=True))
    factor = factor / jnp.sum(total * factor, axis=0, keepdims=True)
    head = div(iota(chips, 3), size)
    blocks = []
    for i in range(half // LANES):
        nodes = []
        for late in range(2):
            wide = jnp.zeros(chips, f32)
            for h in range(LANES // size):
                at = late * (LANES // 2) + i * (LANES // size) + h
                wide = jnp.where(head == h, factor[..., at : at + 1], wide)
            part = parts_ref[:, 2 * i + late].astype(f32).reshape(chips)
            nodes.append(jnp.sum(part * wide, axis=0))
        blocks.append(jnp.concatenate(nodes, axis=1))
    mixed = jnp.concatenate([block[h] for h in range(2) for block in blocks], axis=1)
    update = dot(mixed.astype(bf16), w_o_ref[...])
    latent_out = (latent_ref[...].astype(f32) + update).astype(bf16)
    latent_out_ref[...] = latent_out
    pairs = dot(normed(latent_out, gain_ref[...]), w_kv_ref[...]).astype(bf16)
    for p in range(peers):
        at = p % 2 * half
        out_ref[p, :, :half] = pairs[:, at : at + half]
        out_ref[p, :, half:] = pairs[:, width + at : width + at + half]


def middle_kernel(
    steps, peers, rows, gain_ref, need_ref, slot_ref, x_hbm, w_hbm, query_ref, node_ref,
    x_ref, w_ref, sems,
):
    copies = started(
        pltpu.make_async_copy(w_hbm, w_ref, sems.at[0]),
        pltpu.make_async_copy(x_hbm, x_ref, sems.at[1]),
    )
    points = x_ref.shape[0]
    block = points // steps
    high_count = need_ref.shape[0]
    cap = high_count * LANES // peers
    need = need_ref[...].astype(f32).astype(bf16)
    for j in range(slot_ref.shape[0]):
        slots = slot_ref[j : j + 1, :]
        row_of = (div(slots, LANES) == iota((high_count, points), 0)).astype(bf16)
        listed = lax.dot_general(need, row_of, (((0,), (0,)), ((), ())), preferred_element_type=f32)
        own = mod(slots, LANES) == iota((LANES, points), 0)
        found = jnp.sum(jnp.where(own, listed, 0.0), axis=0, keepdims=True).astype(jnp.int32)
        node_ref[j : j + 1, :] = place_of(div(slots, cap), peers) * rows + found
    for copy in copies:
        copy.wait()
    for i in range(steps):
        part = pl.ds(i * block, block)
        queries = dot(normed(x_ref[part, :], gain_ref[...]), w_ref[...])
        query_ref[:, part] = queries.T.astype(bf16)


def attend_half(pairs, queries, nodes):
    half, points = queries.shape
    edges = nodes.shape[0]
    heads = HEADS // 2
    size = half // heads
    picks = [one_hot(nodes[j : j + 1], (pairs.shape[1], points), 0) for j in range(edges)]
    scores, values = [], []
    for j in range(edges):
        chosen = dot(pairs, picks[j])
        products = (chosen[:half] * queries.astype(f32)).reshape(heads, size, points)
        scores.append(jnp.sum(products, axis=1) * (1.0 / math.sqrt(size)))
        values.append(chosen[half:].reshape(heads, size, points))
    highest = functools.reduce(jnp.maximum, scores)
    raised = [jnp.exp(score - highest) for score in scores]
    inverse = 1.0 / sum(raised)
    mixed = jnp.zeros((heads, size, points), f32)
    for j in range(edges):
        weight = (raised[j] * inverse).astype(bf16).astype(f32).reshape(heads, 1, points)
        mixed += values[j] * weight
    return mixed.reshape(half, points).T.astype(bf16)


def half_of(ref, first, half):
    return ref.at[pl.ds(pl.multiple_of(first, half), half)]


def own_kernel(steps, pairs_ref, node_ref, query_ref, out_ref):
    points, half = out_ref.shape
    block = points // steps
    core = lax.axis_index("dom") & 1
    queries = half_of(query_ref, core * half, half)
    pairs = pairs_ref[...].T
    for i in range(steps):
        part = pl.ds(i * block, block)
        out_ref[part, :] = attend_half(pairs, queries[:, part], node_ref[:, part])


def other_kernel(
    steps, pairs_ref, own_ref, node_ref, query_ref, x_ref, w_ref, latent_ref,
    out_hbm, latent_hbm, out_ref, sems,
):
    latent_copy = pltpu.make_async_copy(latent_ref, latent_hbm, sems.at[steps])
    latent_copy.start()
    points, half = own_ref.shape
    block = points // steps
    core = lax.axis_index("dom") & 1
    queries = half_of(query_ref, (1 - core) * half, half)
    pairs = pairs_ref[...].T
    sends = []
    parts = [pl.ds(i * block, block) for i in range(steps)]

    def attended(part):
        return attend_half(pairs, queries[:, part], node_ref[:, part])

    mixed = attended(parts[0])
    for i, part in enumerate(parts):
        following = attended(parts[i + 1]) if i + 1 < steps else None
        own = own_ref[part, :]
        both = [jnp.where(core == 0, own, mixed), jnp.where(core == 0, mixed, own)]
        update = dot(jnp.concatenate(both, axis=1), w_ref[...])
        out_ref[part, :] = (x_ref[part, :].astype(f32) + update).astype(bf16)
        sends += started(pltpu.make_async_copy(out_ref.at[part], out_hbm.at[part], sems.at[i]))
        mixed = following
    for send in sends:
        send.wait()
    latent_copy.wait()


def in_hbm(array):
    return pltpu.with_memory_space_constraint(array, pltpu.HBM)


def in_vmem(array):
    return pltpu.with_memory_space_constraint(array, pltpu.VMEM)


def on_device(
    grid,
    latent_in,
    grid_gain,
    node_gain,
    dec_gain,
    w_q_enc,
    w_kv_enc,
    w_o_enc,
    w_q_dec,
    w_kv_dec,
    w_o_dec,
    enc_need,
    enc_slot,
    enc_count,
    dec_need,
    dec_slot,
):
    peers = lax.axis_size("dom")
    points, depth = grid.shape
    rows = latent_in.shape[0]
    width = w_q_enc.shape[1]
    nodes = peers * rows
    entries = enc_need.shape[1]
    edges = enc_slot.shape[0]
    cap = entries // peers
    half = width // 2
    sent = (peers, 2 * (half // LANES) + 1, rows // 2, LANES)
    swap = [(i, i ^ 1) for i in range(peers)]
    vmem = pl.BlockSpec(memory_space=pltpu.VMEM)
    hbm = pl.BlockSpec(memory_space=pltpu.HBM)

    other_grid = lax.ppermute(grid, "dom", swap)
    ask_inputs = (
        w_q_enc,
        latent_in,
        node_gain.reshape(1, -1),
        enc_slot.T,
        enc_count.reshape(1, -1),
        enc_need,
    )
    asked = pl.pallas_call(
        ask_kernel,
        in_specs=[hbm] * len(ask_inputs),
        out_specs=vmem,
        out_shape=pltpu.VMEM(sent, bf16),
        scratch_shapes=[pltpu.VMEM(one.shape, one.dtype) for one in ask_inputs]
        + [pltpu.SemaphoreType.DMA((len(ask_inputs),))],
        compiler_params=params(62),
        cost_estimate=cost(2 * rows * depth * width, 2 * depth * width),
        name="ask",
    )(*map(in_hbm, ask_inputs))
    asked = exchange(asked)

    block = math.gcd(points, 256)
    steps = points // block
    pairs = pl.pallas_call(
        functools.partial(front_kernel, steps),
        in_specs=[hbm] * 4,
        out_specs=[vmem] * 2,
        out_shape=[pltpu.VMEM((points, width), bf16)] * 2,
        scratch_shapes=[
            pltpu.VMEM((1, depth), f32),
            pltpu.VMEM((points, depth), bf16),
            pltpu.VMEM((points, depth), bf16),
            pltpu.VMEM((depth, width), bf16),
            pltpu.SemaphoreType.DMA((5,)),
        ],
        compiler_params=params(40),
        cost_estimate=cost(4 * points * depth * width, 8 * points * depth),
        name="front",
    )(*map(in_hbm, (grid_gain.reshape(1, -1), grid, other_grid, w_kv_enc)))

    parts = pl.pallas_call(
        functools.partial(partial_kernel, cap, rows, edges),
        in_specs=[vmem] * 3,
        out_specs=vmem,
        out_shape=pltpu.VMEM(sent, bf16),
        compiler_params=params(40),
        cost_estimate=cost(4 * entries * points * width, 4 * points * width),
        name="partial",
    )(asked, *map(in_vmem, pairs))
    parts, dec_need, dec_slot = lax.optimization_barrier((parts, dec_need, dec_slot))
    order = [[place_of(i, peers) for i in range(peers)]]
    parts = exchange(parts, order)

    slot_total = dec_need.shape[1]
    edge_count = dec_slot.shape[0]
    queries, node_of = pl.pallas_call(
        functools.partial(middle_kernel, steps, peers, rows),
        in_specs=[vmem] * 3 + [hbm] * 2,
        out_specs=[vmem, vmem],
        out_shape=[
            pltpu.VMEM((width, points), bf16),
            jax.ShapeDtypeStruct((edge_count, points), jnp.int32),
        ],
        scratch_shapes=[
            pltpu.VMEM((points, depth), bf16),
            pltpu.VMEM((depth, width), bf16),
            pltpu.SemaphoreType.DMA((2,)),
        ],
        compiler_params=params(40),
        cost_estimate=cost(2 * points * depth * width, 8 * points * depth),
        name="middle",
    )(
        grid_gain.reshape(1, -1),
        dec_need.reshape(slot_total // LANES, LANES),
        dec_slot,
        in_hbm(grid),
        in_hbm(w_q_dec),
    )
    parts, queries, node_of = lax.optimization_barrier((parts, queries, node_of))

    latent_out, everyone = pl.pallas_call(
        combine_kernel,
        in_specs=[vmem] * 5,
        out_specs=[vmem] * 2,
        out_shape=[
            pltpu.VMEM((rows, depth), bf16),
            jax.ShapeDtypeStruct((peers, rows, width), bf16),
        ],
        compiler_params=params(24),
        cost_estimate=cost(6 * rows * depth * width, 6 * depth * width),
        name="combine",
    )(parts, latent_in, dec_gain.reshape(1, -1), w_o_enc, w_kv_dec)
    own = exchange(everyone, order).reshape(nodes, width)
    other = lax.ppermute(own, "dom", swap)

    queries = in_vmem(queries)
    own_mixed = pl.pallas_call(
        functools.partial(own_kernel, steps),
        in_specs=[vmem] * 3,
        out_shape=jax.ShapeDtypeStruct((points, half), bf16),
        compiler_params=params(48),
        cost_estimate=cost(4 * points * nodes * width, 8 * points * nodes),
        name="own",
    )(own, node_of, queries)
    grid_out, latent_out = pl.pallas_call(
        functools.partial(other_kernel, steps),
        in_specs=[vmem] * 7,
        out_specs=[hbm] * 2,
        out_shape=[pltpu.HBM((points, depth), bf16), pltpu.HBM((rows, depth), bf16)],
        scratch_shapes=[
            pltpu.VMEM((points, depth), bf16),
            pltpu.SemaphoreType.DMA((steps + 1,)),
        ],
        compiler_params=params(48),
        cost_estimate=cost(4 * points * depth * width, 8 * points * depth),
        name="other",
    )(other, own_mixed, node_of, queries, grid, w_o_dec, in_vmem(latent_out))
    return (latent_out, grid_out)


def solution(mesh):
    return jax.shard_map(
        on_device,
        mesh=mesh,
        in_specs=(
            P(("groups", "dom"), None),
            P(("groups", "dom"), None),
            P(),
            P(),
            P(),
            P(),
            P(),
            P(),
            P(),
            P(),
            P(),
            P("dom", None),
            P(None, "dom"),
            P("dom"),
            P("dom", None),
            P(None, "dom"),
        ),
        out_specs=(P(("groups", "dom"), None), P(("groups", "dom"), None)),
        check_vma=False,
    )
```

```python
import functools
import math

import jax
import jax.numpy as jnp
from jax import lax
from jax.experimental import pallas as pl
from jax.experimental.pallas import tpu as pltpu
from jax.sharding import PartitionSpec as P

HEADS = 8
LANES = 128
NEG = -1e30
norm_eps = 1e-06
f32 = jnp.float32
bf16 = jnp.bfloat16


def iota(shape, dim):
    return lax.broadcasted_iota(jnp.int32, shape, dim)


def one_hot(places, shape, dim):
    return (places == iota(shape, dim)).astype(bf16)


def div(values, by):
    if by & (by - 1) == 0:
        return values >> (by.bit_length() - 1)
    return values // by


def mod(values, by):
    if by & (by - 1) == 0:
        return values & (by - 1)
    return values % by


def dot(a, b):
    return jnp.dot(a, b, preferred_element_type=f32)


def dot_t(a, b):
    return lax.dot_general(a, b, (((1,), (1,)), ((), ())), preferred_element_type=f32)


def normed(values, gain):
    widened = values.astype(f32)
    spread = jnp.mean(widened * widened, axis=-1, keepdims=True)
    return (widened * lax.rsqrt(spread + norm_eps) * gain).astype(bf16)


def params(mib):
    return pltpu.CompilerParams(vmem_limit_bytes=mib * 2**20)


def started(*copies):
    for copy in copies:
        copy.start()
    return copies


def split_copy(source, target, sems, count=4):
    rows = target.shape[0] // count
    parts = [pl.ds(i * rows, rows) for i in range(count)]
    return [
        pltpu.make_async_copy(source.at[part], target.at[part], sems.at[i])
        for i, part in enumerate(parts)
    ]


def cost(flops, read, exps=0):
    return pl.CostEstimate(flops=int(flops), bytes_accessed=int(read), transcendentals=int(exps))


def place_of(index, peers):
    if isinstance(index, int):
        return (index + index % 2 * (peers // 2)) % peers
    return mod(index + (index & 1) * (peers // 2), peers)


def exchange(blocks, order=None):
    return lax.all_to_all(
        blocks, "dom", split_axis=0, concat_axis=0, tiled=True, axis_index_groups=order
    )


def slab(values, i, late, tall):
    return values[late * tall : (late + 1) * tall, i * LANES : (i + 1) * LANES]


def ask_kernel(*refs):
    sources, out_ref, held, sems = refs[:6], refs[6], refs[7:13], refs[13]
    weights = started(*split_copy(sources[0], held[0], sems.at[pl.ds(0, 4)]))
    copies = started(
        *[
            pltpu.make_async_copy(source, ref, sems.at[4 + i])
            for i, (source, ref) in enumerate(zip(sources[1:], held[1:]))
        ]
    )
    w_ref, latent_ref, gain_ref, slot_ref, count_ref, need_ref = held
    rows = latent_ref.shape[0]
    width = w_ref.shape[1]
    entries = need_ref.shape[1]
    edges = slot_ref.shape[1]
    peers = out_ref.shape[0]
    both = 2 * entries // peers
    tall = rows // 2
    for copy in copies:
        copy.wait()
    rows_normed = normed(latent_ref[...], gain_ref[...])
    live = iota((edges, rows), 0) < count_ref[...]
    slots = slot_ref[...].astype(f32).T.astype(jnp.int32)
    slots = jnp.where(live, slots, entries) - entries // 2
    slots = slots.astype(f32).astype(bf16)
    tile = jnp.zeros((tall, LANES), f32)
    for g in range(edges // tall):
        to = iota((rows, LANES), 1) == iota((rows, LANES), 0) + g * rows
        tile += dot(slots, to.astype(bf16))[g * tall : (g + 1) * tall]
    row, lane = iota((tall, LANES), 0), iota((tall, LANES), 1)
    in_list = (lane >= LANES // 2) & (lane < LANES // 2 + both)
    need = need_ref[...]
    tiles = []
    for chip in range(peers // 2):
        at = chip * both
        piece = need[:, at // LANES * LANES : at // LANES * LANES + LANES].astype(f32)
        piece = pltpu.roll(jnp.broadcast_to(piece, (tall, LANES)), (LANES // 2 - at) % LANES, 1)
        high = jnp.floor(piece * (1.0 / 256.0))
        piece = jnp.where(row == 0, piece - high * 256.0, jnp.where(row == 1, high, 0.0))
        tiles.append((tile + jnp.where(in_list, piece, 0.0)).astype(bf16))
    for copy in weights:
        copy.wait()
    queries = dot(rows_normed, w_ref[...])
    blocks = width // 2 // LANES
    slabs = [
        slab(queries, i, late, tall).astype(bf16) for i in range(2 * blocks) for late in range(2)
    ]
    for p in range(peers):
        for i in range(2 * blocks):
            out_ref[p, i] = slabs[p % 2 * 2 * blocks + i]
        out_ref[p, 2 * blocks] = tiles[p // 2]


def front_kernel(
    steps, gain_hbm, own_hbm, other_hbm, w_hbm, own_out_ref, other_out_ref,
    gain_ref, own_ref, other_ref, w_ref, sems,
):
    points = own_ref.shape[0]
    block = points // steps
    half = own_out_ref.shape[1] // 2
    core = lax.axis_index("dom") & 1
    first = [pltpu.make_async_copy(gain_hbm, gain_ref, sems.at[0])]
    for i in range(2):
        source = w_hbm.at[:, pl.ds(pl.multiple_of((core + 2 * i) * half, half), half)]
        target = w_ref.at[:, pl.ds(i * half, half)]
        first += split_copy(source, target, sems.at[pl.ds(1 + 4 * i, 4)])
    first += split_copy(own_hbm, own_ref, sems.at[pl.ds(9, 4)])
    second = split_copy(other_hbm, other_ref, sems.at[pl.ds(13, 4)])
    started(*first, *second)
    parts = [pl.ds(i * block, block) for i in range(steps)]
    for copies, rows_ref, out_ref in (
        (first, own_ref, own_out_ref),
        (second, other_ref, other_out_ref),
    ):
        for copy in copies:
            copy.wait()
        gain = gain_ref[...]
        for part in parts:
            out_ref[part, :] = dot(normed(rows_ref[part, :], gain), w_ref[...]).astype(bf16)


def stat_parts(top, total):
    top_1 = top.astype(bf16).astype(f32)
    top_2 = (top - top_1).astype(bf16).astype(f32)
    total_1 = total.astype(bf16).astype(f32)
    return top_1, top_2, top - top_1 - top_2, total_1, total - total_1


def partial_kernel(cap, rows, edges, asked_ref, *refs):
    pairs_refs, out_ref = refs[:2], refs[2]
    me = lax.axis_index("dom")
    points, both = pairs_refs[0].shape
    peers = out_ref.shape[0]
    width = both // 2
    heads = HEADS // 2
    size = width // heads
    tall = rows // 2
    blocks = width // LANES
    scale = math.log2(math.e) / math.sqrt(size)
    all_nodes, all_entries = peers * rows, peers * cap
    some = LANES // (heads * rows)
    nodes, entries = some * rows, some * cap
    tiles = asked_ref[:, 2 * blocks].astype(f32)

    tile_rows = peers * tall
    pick_row = iota((all_entries, tile_rows), 1) - div(iota((all_entries, tile_rows), 0), cap) * tall
    pick = jnp.where(pick_row == 0, 1.0, jnp.where(pick_row == 1, 256.0, 0.0)).astype(bf16)
    lists = dot(pick, tiles.reshape(tile_rows, LANES).astype(bf16))
    lane = iota((all_entries, LANES), 1) - mod(iota((all_entries, LANES), 0), cap) - LANES // 2
    gathered = []
    for other, ref in enumerate(pairs_refs):
        mine = lane == ((me ^ other) & 1) * cap
        index = jnp.sum(jnp.where(mine, lists, 0.0), axis=1, keepdims=True).astype(jnp.int32)
        gathered.append(dot(one_hot(index, (all_entries, points), 1), ref[...]))

    group, across = div(iota((tall, LANES), 1), rows), LANES // rows
    slots = []
    for g in range(edges // tall):
        line = []
        for first in range(0, peers, across):
            merged = jnp.zeros((tall, LANES), f32)
            for w in range(across):
                merged = jnp.where(
                    group == w, pltpu.roll(tiles[first + w], (w - g) * rows % LANES, 1), merged
                )
            line.append(merged)
        slots.append(jnp.concatenate(line, axis=1))
    all_slots = jnp.concatenate(slots, axis=0).astype(jnp.int32) + all_entries // 2

    listed = -(-cap // 8) * 8
    biases = []
    for other in range(2):
        slots = all_slots - (me ^ other) * cap
        uses = jnp.zeros((listed, all_nodes), f32)
        for j in range(edges):
            uses += jnp.where(slots[j : j + 1] == iota((listed, all_nodes), 0), 1.0, 0.0)
        live = uses > 0.5
        biases.append(jnp.where(live, jnp.log2(jnp.where(live, uses, 1.0)), NEG))

    window = mod(div(iota((listed, LANES), 1), rows), some)
    first_nodes = iota((listed, LANES), 1) < nodes
    first_head = iota((nodes, LANES), 1) < size
    tops, totals = [], []
    for start in range(0, peers, some):
        bias = []
        for one in biases:
            at = start * rows
            one = one[:, at // LANES * LANES : at // LANES * LANES + LANES]
            one = jnp.where(first_nodes, pltpu.roll(one, -at % LANES, 1), 0.0)
            spread = nodes
            while spread < LANES:
                one += pltpu.roll(one, spread, 1)
                spread *= 2
            bias += [jnp.where(window == w, one, NEG)[:cap] for w in range(some)]
        part = slice(start * cap, start * cap + entries)
        pairs = jnp.concatenate([one[part] for one in gathered], axis=0).astype(bf16)
        queries = [
            jnp.concatenate(
                [asked_ref[start + n // 2, 2 * i + n % 2].astype(f32) for n in range(2 * some)], axis=0
            )
            for i in range(blocks)
        ]
        queries = jnp.concatenate(queries, axis=1).astype(bf16)
        head = div(iota(queries.shape, 1), size)
        queries = jnp.concatenate(
            [jnp.where(head == h, queries, jnp.zeros_like(queries)) for h in range(heads)], axis=0
        )
        scores = dot_t(pairs[:, :width], queries) * scale + jnp.concatenate(bias, axis=0)
        top = jnp.max(scores, axis=0, keepdims=True)
        raised = jnp.exp2(scores - top)
        tops.append(top)
        totals.append(jnp.sum(raised, axis=0, keepdims=True))
        mixed = dot(raised.T.astype(bf16), pairs[:, width:])
        for i in range(blocks):
            block = mixed[:, i * LANES : (i + 1) * LANES]
            h = i * (LANES // size)
            block = jnp.where(
                first_head, block[h * nodes : (h + 1) * nodes], block[(h + 1) * nodes : (h + 2) * nodes]
            )
            for n in range(2 * some):
                place = place_of(start + n // 2, peers)
                out_ref[place, 2 * i + n % 2] = slab(block, 0, n, tall).astype(bf16)

    row_lane = iota((tall, LANES), 1)
    for first in range(0, len(tops), 8):
        parts = stat_parts(
            jnp.concatenate(tops[first : first + 8], axis=0),
            jnp.concatenate(totals[first : first + 8], axis=0),
        )
        rest = jnp.zeros((LANES - 8 * len(parts), LANES), f32)
        columns = jnp.concatenate([*parts, rest], axis=0).T
        for g in range(8):
            for w in range(some):
                tile = jnp.zeros((tall, LANES), f32)
                for h in range(heads):
                    for late in range(2):
                        at = h * nodes + w * rows + late * tall
                        move = late * (LANES // 2) + h - g
                        here = (mod(row_lane, 8) == h) & (div(row_lane, LANES // 2) == late)
                        piece = pltpu.roll(columns[at : at + tall], move % LANES, 1)
                        tile = jnp.where(here, piece, tile)
                out_ref[place_of((first + g) * some + w, peers), 2 * blocks] = tile.astype(bf16)


def combine_kernel(parts_ref, latent_ref, gain_ref, w_o_ref, w_kv_ref, latent_out_ref, out_ref):
    peers = parts_ref.shape[0]
    rows = latent_ref.shape[0]
    width = w_o_ref.shape[0]
    half = width // 2
    size, tall = width // HEADS, rows // 2
    chips = (peers // 2, 2, tall, LANES)
    tile = parts_ref[:, 2 * (half // LANES)].astype(f32)

    def moved(columns):
        return pltpu.roll(tile, LANES - columns, 2)

    top = (tile + moved(8) + moved(16)).reshape(chips)
    total = (moved(24) + moved(32)).reshape(chips)
    factor = jnp.exp2(top - jnp.max(top, axis=0, keepdims=True))
    factor = factor / jnp.sum(total * factor, axis=0, keepdims=True)
    head = div(iota(chips, 3), size)
    blocks = []
    for i in range(half // LANES):
        nodes = []
        for late in range(2):
            wide = jnp.zeros(chips, f32)
            for h in range(LANES // size):
                at = late * (LANES // 2) + i * (LANES // size) + h
                wide = jnp.where(head == h, factor[..., at : at + 1], wide)
            part = parts_ref[:, 2 * i + late].astype(f32).reshape(chips)
            nodes.append(jnp.sum(part * wide, axis=0))
        blocks.append(jnp.concatenate(nodes, axis=1))
    mixed = jnp.concatenate([block[h] for h in range(2) for block in blocks], axis=1)
    update = dot(mixed.astype(bf16), w_o_ref[...])
    latent_out = (latent_ref[...].astype(f32) + update).astype(bf16)
    latent_out_ref[...] = latent_out
    pairs = dot(normed(latent_out, gain_ref[...]), w_kv_ref[...]).astype(bf16)
    for p in range(peers):
        at = p % 2 * half
        out_ref[p, :, :half] = pairs[:, at : at + half]
        out_ref[p, :, half:] = pairs[:, width + at : width + at + half]


def middle_kernel(
    steps, peers, rows, gain_ref, need_ref, slot_ref, x_hbm, w_hbm, query_ref, node_ref,
    x_ref, w_ref, sems,
):
    copies = started(
        *split_copy(w_hbm, w_ref, sems.at[pl.ds(0, 4)]),
        *split_copy(x_hbm, x_ref, sems.at[pl.ds(4, 4)]),
    )
    points = x_ref.shape[0]
    block = points // steps
    high_count = need_ref.shape[0]
    cap = high_count * LANES // peers
    need = need_ref[...].astype(f32).astype(bf16)
    for j in range(slot_ref.shape[0]):
        slots = slot_ref[j : j + 1, :]
        row_of = (div(slots, LANES) == iota((high_count, points), 0)).astype(bf16)
        listed = lax.dot_general(need, row_of, (((0,), (0,)), ((), ())), preferred_element_type=f32)
        own = mod(slots, LANES) == iota((LANES, points), 0)
        found = jnp.sum(jnp.where(own, listed, 0.0), axis=0, keepdims=True).astype(jnp.int32)
        node_ref[j : j + 1, :] = place_of(div(slots, cap), peers) * rows + found
    for copy in copies:
        copy.wait()
    for i in range(steps):
        part = pl.ds(i * block, block)
        queries = dot(normed(x_ref[part, :], gain_ref[...]), w_ref[...])
        query_ref[:, part] = queries.T.astype(bf16)


def attend_half(pairs, queries, nodes):
    half, points = queries.shape
    edges = nodes.shape[0]
    heads = HEADS // 2
    size = half // heads
    picks = [one_hot(nodes[j : j + 1], (pairs.shape[1], points), 0) for j in range(edges)]
    scores, values = [], []
    for j in range(edges):
        chosen = dot(pairs, picks[j])
        products = (chosen[:half] * queries.astype(f32)).reshape(heads, size, points)
        scores.append(jnp.sum(products, axis=1) * (1.0 / math.sqrt(size)))
        values.append(chosen[half:].reshape(heads, size, points))
    highest = functools.reduce(jnp.maximum, scores)
    raised = [jnp.exp(score - highest) for score in scores]
    inverse = 1.0 / sum(raised)
    mixed = jnp.zeros((heads, size, points), f32)
    for j in range(edges):
        weight = (raised[j] * inverse).astype(bf16).astype(f32).reshape(heads, 1, points)
        mixed += values[j] * weight
    return mixed.reshape(half, points).T.astype(bf16)


def half_of(ref, first, half):
    return ref.at[pl.ds(pl.multiple_of(first, half), half)]


def own_kernel(steps, pairs_ref, node_ref, query_ref, out_ref):
    points, half = out_ref.shape
    block = points // steps
    core = lax.axis_index("dom") & 1
    queries = half_of(query_ref, core * half, half)
    pairs = pairs_ref[...].T
    for i in range(steps):
        part = pl.ds(i * block, block)
        out_ref[part, :] = attend_half(pairs, queries[:, part], node_ref[:, part])


def other_kernel(
    steps, pairs_ref, own_ref, node_ref, query_ref, x_ref, w_ref, latent_ref,
    out_hbm, latent_hbm, out_ref, sems,
):
    latent_copy = pltpu.make_async_copy(latent_ref, latent_hbm, sems.at[steps])
    latent_copy.start()
    points, half = own_ref.shape
    block = points // steps
    core = lax.axis_index("dom") & 1
    queries = half_of(query_ref, (1 - core) * half, half)
    pairs = pairs_ref[...].T
    sends = []
    parts = [pl.ds(i * block, block) for i in range(steps)]

    def attended(part):
        return attend_half(pairs, queries[:, part], node_ref[:, part])

    mixed = attended(parts[0])
    for i, part in enumerate(parts):
        following = attended(parts[i + 1]) if i + 1 < steps else None
        own = own_ref[part, :]
        both = [jnp.where(core == 0, own, mixed), jnp.where(core == 0, mixed, own)]
        update = dot(jnp.concatenate(both, axis=1), w_ref[...])
        out_ref[part, :] = (x_ref[part, :].astype(f32) + update).astype(bf16)
        sends += started(pltpu.make_async_copy(out_ref.at[part], out_hbm.at[part], sems.at[i]))
        mixed = following
    for send in sends:
        send.wait()
    latent_copy.wait()


def in_hbm(array):
    return pltpu.with_memory_space_constraint(array, pltpu.HBM)


def in_vmem(array):
    return pltpu.with_memory_space_constraint(array, pltpu.VMEM)


def on_device(
    grid,
    latent_in,
    grid_gain,
    node_gain,
    dec_gain,
    w_q_enc,
    w_kv_enc,
    w_o_enc,
    w_q_dec,
    w_kv_dec,
    w_o_dec,
    enc_need,
    enc_slot,
    enc_count,
    dec_need,
    dec_slot,
):
    peers = lax.axis_size("dom")
    points, depth = grid.shape
    rows = latent_in.shape[0]
    width = w_q_enc.shape[1]
    nodes = peers * rows
    entries = enc_need.shape[1]
    edges = enc_slot.shape[0]
    cap = entries // peers
    half = width // 2
    sent = (peers, 2 * (half // LANES) + 1, rows // 2, LANES)
    swap = [(i, i ^ 1) for i in range(peers)]
    vmem = pl.BlockSpec(memory_space=pltpu.VMEM)
    hbm = pl.BlockSpec(memory_space=pltpu.HBM)

    other_grid = lax.ppermute(grid, "dom", swap)
    ask_inputs = (
        w_q_enc,
        latent_in,
        node_gain.reshape(1, -1),
        enc_slot.T,
        enc_count.reshape(1, -1),
        enc_need,
    )
    asked = pl.pallas_call(
        ask_kernel,
        in_specs=[hbm] * len(ask_inputs),
        out_specs=vmem,
        out_shape=pltpu.VMEM(sent, bf16),
        scratch_shapes=[pltpu.VMEM(one.shape, one.dtype) for one in ask_inputs]
        + [pltpu.SemaphoreType.DMA((len(ask_inputs) + 3,))],
        compiler_params=params(62),
        cost_estimate=cost(2 * rows * depth * width, 2 * depth * width),
        name="ask",
    )(*map(in_hbm, ask_inputs))
    asked = exchange(asked)

    block = math.gcd(points, 256)
    steps = points // block
    pairs = pl.pallas_call(
        functools.partial(front_kernel, steps),
        in_specs=[hbm] * 4,
        out_specs=[vmem] * 2,
        out_shape=[pltpu.VMEM((points, width), bf16)] * 2,
        scratch_shapes=[
            pltpu.VMEM((1, depth), f32),
            pltpu.VMEM((points, depth), bf16),
            pltpu.VMEM((points, depth), bf16),
            pltpu.VMEM((depth, width), bf16),
            pltpu.SemaphoreType.DMA((17,)),
        ],
        compiler_params=params(40),
        cost_estimate=cost(4 * points * depth * width, 8 * points * depth),
        name="front",
    )(*map(in_hbm, (grid_gain.reshape(1, -1), grid, other_grid, w_kv_enc)))

    parts = pl.pallas_call(
        functools.partial(partial_kernel, cap, rows, edges),
        in_specs=[vmem] * 3,
        out_specs=vmem,
        out_shape=pltpu.VMEM(sent, bf16),
        compiler_params=params(40),
        cost_estimate=cost(4 * entries * points * width, 4 * points * width),
        name="partial",
    )(asked, *map(in_vmem, pairs))
    parts, dec_need, dec_slot = lax.optimization_barrier((parts, dec_need, dec_slot))
    order = [[place_of(i, peers) for i in range(peers)]]
    parts = exchange(parts, order)

    slot_total = dec_need.shape[1]
    edge_count = dec_slot.shape[0]
    queries, node_of = pl.pallas_call(
        functools.partial(middle_kernel, steps, peers, rows),
        in_specs=[vmem] * 3 + [hbm] * 2,
        out_specs=[vmem, vmem],
        out_shape=[
            pltpu.VMEM((width, points), bf16),
            jax.ShapeDtypeStruct((edge_count, points), jnp.int32),
        ],
        scratch_shapes=[
            pltpu.VMEM((points, depth), bf16),
            pltpu.VMEM((depth, width), bf16),
            pltpu.SemaphoreType.DMA((8,)),
        ],
        compiler_params=params(40),
        cost_estimate=cost(2 * points * depth * width, 8 * points * depth),
        name="middle",
    )(
        grid_gain.reshape(1, -1),
        dec_need.reshape(slot_total // LANES, LANES),
        dec_slot,
        in_hbm(grid),
        in_hbm(w_q_dec),
    )
    parts, queries, node_of = lax.optimization_barrier((parts, queries, node_of))

    latent_out, everyone = pl.pallas_call(
        combine_kernel,
        in_specs=[vmem] * 5,
        out_specs=[vmem] * 2,
        out_shape=[
            pltpu.VMEM((rows, depth), bf16),
            jax.ShapeDtypeStruct((peers, rows, width), bf16),
        ],
        compiler_params=params(24),
        cost_estimate=cost(6 * rows * depth * width, 6 * depth * width),
        name="combine",
    )(parts, latent_in, dec_gain.reshape(1, -1), w_o_enc, w_kv_dec)
    own = exchange(everyone, order).reshape(nodes, width)
    other = lax.ppermute(own, "dom", swap)

    queries = in_vmem(queries)
    own_mixed = pl.pallas_call(
        functools.partial(own_kernel, max(steps // 2, 1)),
        in_specs=[vmem] * 3,
        out_shape=jax.ShapeDtypeStruct((points, half), bf16),
        compiler_params=params(48),
        cost_estimate=cost(4 * points * nodes * width, 8 * points * nodes),
        name="own",
    )(own, node_of, queries)
    grid_out, latent_out = pl.pallas_call(
        functools.partial(other_kernel, steps),
        in_specs=[vmem] * 7,
        out_specs=[hbm] * 2,
        out_shape=[pltpu.HBM((points, depth), bf16), pltpu.HBM((rows, depth), bf16)],
        scratch_shapes=[
            pltpu.VMEM((points, depth), bf16),
            pltpu.SemaphoreType.DMA((steps + 1,)),
        ],
        compiler_params=params(48),
        cost_estimate=cost(4 * points * depth * width, 8 * points * depth),
        name="other",
    )(other, own_mixed, node_of, queries, grid, w_o_dec, in_vmem(latent_out))
    return (latent_out, grid_out)


def solution(mesh):
    return jax.shard_map(
        on_device,
        mesh=mesh,
        in_specs=(
            P(("groups", "dom"), None),
            P(("groups", "dom"), None),
            P(),
            P(),
            P(),
            P(),
            P(),
            P(),
            P(),
            P(),
            P(),
            P("dom", None),
            P(None, "dom"),
            P("dom"),
            P("dom", None),
            P(None, "dom"),
        ),
        out_specs=(P(("groups", "dom"), None), P(("groups", "dom"), None)),
        check_vma=False,
    )
```

```python
import functools
import math

import jax
import jax.numpy as jnp
from jax import lax
from jax.experimental import pallas as pl
from jax.experimental.pallas import tpu as pltpu
from jax.sharding import PartitionSpec as P

HEADS = 8
LANES = 128
NEG = -1e30
norm_eps = 1e-06
f32 = jnp.float32
bf16 = jnp.bfloat16


def iota(shape, dim):
    return lax.broadcasted_iota(jnp.int32, shape, dim)


def one_hot(places, shape, dim):
    return (places == iota(shape, dim)).astype(bf16)


def div(values, by):
    if by & (by - 1) == 0:
        return values >> (by.bit_length() - 1)
    return values // by


def mod(values, by):
    if by & (by - 1) == 0:
        return values & (by - 1)
    return values % by


def dot(a, b):
    return jnp.dot(a, b, preferred_element_type=f32)


def dot_t(a, b):
    return lax.dot_general(a, b, (((1,), (1,)), ((), ())), preferred_element_type=f32)


def normed(values, gain):
    widened = values.astype(f32)
    spread = jnp.mean(widened * widened, axis=-1, keepdims=True)
    return (widened * lax.rsqrt(spread + norm_eps) * gain).astype(bf16)


def params(mib):
    return pltpu.CompilerParams(vmem_limit_bytes=mib * 2**20)


def started(*copies):
    for copy in copies:
        copy.start()
    return copies


def cost(flops, read, exps=0):
    return pl.CostEstimate(flops=int(flops), bytes_accessed=int(read), transcendentals=int(exps))


def exchange(blocks, groups=None):
    return lax.all_to_all(
        blocks, "dom", split_axis=0, concat_axis=0, tiled=True, axis_index_groups=groups
    )


def slab(values, i, late, tall):
    return values[late * tall : (late + 1) * tall, i * LANES : (i + 1) * LANES]


def ask_kernel(*refs):
    sources, out_ref, held, sems = refs[:6], refs[6], refs[7:13], refs[13]
    copies = started(
        *[
            pltpu.make_async_copy(source, ref, sems.at[i])
            for i, (source, ref) in enumerate(zip(sources, held))
        ]
    )
    w_ref, latent_ref, gain_ref, slot_ref, count_ref, need_ref = held
    rows = latent_ref.shape[0]
    width = w_ref.shape[1]
    entries = need_ref.shape[1]
    edges = slot_ref.shape[1]
    peers = out_ref.shape[0]
    both = 2 * entries // peers
    tall = rows // 2
    for copy in copies[1:]:
        copy.wait()
    rows_normed = normed(latent_ref[...], gain_ref[...])
    live = iota((edges, rows), 0) < count_ref[...]
    slots = slot_ref[...].astype(f32).T.astype(jnp.int32)
    slots = jnp.where(live, slots, entries) - entries // 2
    slots = slots.astype(f32).astype(bf16)
    tile = jnp.zeros((tall, LANES), f32)
    for g in range(edges // tall):
        to = iota((rows, LANES), 1) == iota((rows, LANES), 0) + g * rows
        tile += dot(slots, to.astype(bf16))[g * tall : (g + 1) * tall]
    row, lane = iota((tall, LANES), 0), iota((tall, LANES), 1)
    in_list = (lane >= LANES // 2) & (lane < LANES // 2 + both)
    need = need_ref[...]
    tiles = []
    for chip in range(peers // 2):
        at = chip * both
        piece = need[:, at // LANES * LANES : at // LANES * LANES + LANES].astype(f32)
        piece = pltpu.roll(jnp.broadcast_to(piece, (tall, LANES)), (LANES // 2 - at) % LANES, 1)
        high = jnp.floor(piece * (1.0 / 256.0))
        piece = jnp.where(row == 0, piece - high * 256.0, jnp.where(row == 1, high, 0.0))
        tiles.append((tile + jnp.where(in_list, piece, 0.0)).astype(bf16))
    copies[0].wait()
    queries = dot(rows_normed, w_ref[...])
    blocks = width // 2 // LANES
    slabs = [
        slab(queries, i, late, tall).astype(bf16) for i in range(2 * blocks) for late in range(2)
    ]
    for p in range(peers):
        for i in range(2 * blocks):
            out_ref[p, i] = slabs[p % 2 * 2 * blocks + i]
        out_ref[p, 2 * blocks] = tiles[p // 2]


def front_kernel(
    steps, gain_hbm, own_hbm, other_hbm, w_hbm, own_out_ref, other_out_ref,
    gain_ref, own_ref, other_ref, w_ref, sems,
):
    points = own_ref.shape[0]
    block = points // steps
    half = own_out_ref.shape[1] // 2
    core = lax.axis_index("dom") & 1
    copies = started(
        pltpu.make_async_copy(gain_hbm, gain_ref, sems.at[0]),
        *[
            pltpu.make_async_copy(
                w_hbm.at[:, pl.ds(pl.multiple_of((core + 2 * i) * half, half), half)],
                w_ref.at[:, pl.ds(i * half, half)],
                sems.at[1 + i],
            )
            for i in range(2)
        ],
        pltpu.make_async_copy(own_hbm, own_ref, sems.at[3]),
        pltpu.make_async_copy(other_hbm, other_ref, sems.at[4]),
    )
    parts = [pl.ds(i * block, block) for i in range(steps)]
    for copy in copies[:3]:
        copy.wait()
    gain = gain_ref[...]
    sides = ((own_ref, own_out_ref), (other_ref, other_out_ref))
    for copy, (rows_ref, out_ref) in zip(copies[3:], sides):
        copy.wait()
        for part in parts:
            out_ref[part, :] = dot(normed(rows_ref[part, :], gain), w_ref[...]).astype(bf16)


def stat_parts(top, total):
    top_1 = top.astype(bf16).astype(f32)
    top_2 = (top - top_1).astype(bf16).astype(f32)
    total_1 = total.astype(bf16).astype(f32)
    return top_1, top_2, top - top_1 - top_2, total_1, total - total_1


def partial_kernel(cap, rows, edges, asked_ref, *refs):
    pairs_refs, out_ref = refs[:2], refs[2]
    me = lax.axis_index("dom")
    points, both = pairs_refs[0].shape
    peers = out_ref.shape[0]
    width = both // 2
    heads = HEADS // 2
    size = width // heads
    tall = rows // 2
    blocks = width // LANES
    scale = math.log2(math.e) / math.sqrt(size)
    all_nodes, all_entries = peers * rows, peers * cap
    some = LANES // (heads * rows)
    nodes, entries = some * rows, some * cap
    tiles = asked_ref[:, 2 * blocks].astype(f32)

    tile_rows = peers * tall
    pick_row = iota((all_entries, tile_rows), 1) - div(iota((all_entries, tile_rows), 0), cap) * tall
    pick = jnp.where(pick_row == 0, 1.0, jnp.where(pick_row == 1, 256.0, 0.0)).astype(bf16)
    lists = dot(pick, tiles.reshape(tile_rows, LANES).astype(bf16))
    lane = iota((all_entries, LANES), 1) - mod(iota((all_entries, LANES), 0), cap) - LANES // 2
    gathered = []
    for other, ref in enumerate(pairs_refs):
        mine = lane == ((me ^ other) & 1) * cap
        index = jnp.sum(jnp.where(mine, lists, 0.0), axis=1, keepdims=True).astype(jnp.int32)
        gathered.append(dot(one_hot(index, (all_entries, points), 1), ref[...]))

    group, across = div(iota((tall, LANES), 1), rows), LANES // rows
    slots = []
    for g in range(edges // tall):
        line = []
        for first in range(0, peers, across):
            merged = jnp.zeros((tall, LANES), f32)
            for w in range(across):
                merged = jnp.where(
                    group == w, pltpu.roll(tiles[first + w], (w - g) * rows % LANES, 1), merged
                )
            line.append(merged)
        slots.append(jnp.concatenate(line, axis=1))
    all_slots = jnp.concatenate(slots, axis=0).astype(jnp.int32) + all_entries // 2

    listed = -(-cap // 8) * 8
    biases = []
    for other in range(2):
        slots = all_slots - (me ^ other) * cap
        uses = jnp.zeros((listed, all_nodes), f32)
        for j in range(edges):
            uses += jnp.where(slots[j : j + 1] == iota((listed, all_nodes), 0), 1.0, 0.0)
        live = uses > 0.5
        biases.append(jnp.where(live, jnp.log2(jnp.where(live, uses, 1.0)), NEG))

    window = mod(div(iota((listed, LANES), 1), rows), some)
    first_nodes = iota((listed, LANES), 1) < nodes
    first_head = iota((nodes, LANES), 1) < size
    tops, totals = [], []
    for start in range(0, peers, some):
        bias = []
        for one in biases:
            at = start * rows
            one = one[:, at // LANES * LANES : at // LANES * LANES + LANES]
            one = jnp.where(first_nodes, pltpu.roll(one, -at % LANES, 1), 0.0)
            spread = nodes
            while spread < LANES:
                one += pltpu.roll(one, spread, 1)
                spread *= 2
            bias += [jnp.where(window == w, one, NEG)[:cap] for w in range(some)]
        part = slice(start * cap, start * cap + entries)
        pairs = jnp.concatenate([one[part] for one in gathered], axis=0).astype(bf16)
        queries = [
            jnp.concatenate(
                [asked_ref[start + n // 2, 2 * i + n % 2].astype(f32) for n in range(2 * some)], axis=0
            )
            for i in range(blocks)
        ]
        queries = jnp.concatenate(queries, axis=1).astype(bf16)
        head = div(iota(queries.shape, 1), size)
        queries = jnp.concatenate(
            [jnp.where(head == h, queries, jnp.zeros_like(queries)) for h in range(heads)], axis=0
        )
        scores = dot_t(pairs[:, :width], queries) * scale + jnp.concatenate(bias, axis=0)
        top = jnp.max(scores, axis=0, keepdims=True)
        raised = jnp.exp2(scores - top)
        tops.append(top)
        totals.append(jnp.sum(raised, axis=0, keepdims=True))
        mixed = dot(raised.T.astype(bf16), pairs[:, width:])
        for i in range(blocks):
            block = mixed[:, i * LANES : (i + 1) * LANES]
            h = i * (LANES // size)
            block = jnp.where(
                first_head, block[h * nodes : (h + 1) * nodes], block[(h + 1) * nodes : (h + 2) * nodes]
            )
            for n in range(2 * some):
                place = start + n // 2
                out_ref[place, 2 * i + n % 2] = slab(block, 0, n, tall).astype(bf16)

    row_lane = iota((tall, LANES), 1)
    for first in range(0, len(tops), 8):
        parts = stat_parts(
            jnp.concatenate(tops[first : first + 8], axis=0),
            jnp.concatenate(totals[first : first + 8], axis=0),
        )
        rest = jnp.zeros((LANES - 8 * len(parts), LANES), f32)
        columns = jnp.concatenate([*parts, rest], axis=0).T
        for g in range(8):
            for w in range(some):
                tile = jnp.zeros((tall, LANES), f32)
                for h in range(heads):
                    for late in range(2):
                        at = h * nodes + w * rows + late * tall
                        move = late * (LANES // 2) + h - g
                        here = (mod(row_lane, 8) == h) & (div(row_lane, LANES // 2) == late)
                        piece = pltpu.roll(columns[at : at + tall], move % LANES, 1)
                        tile = jnp.where(here, piece, tile)
                out_ref[(first + g) * some + w, 2 * blocks] = tile.astype(bf16)


def merge_kernel(parts_ref, out_ref):
    chips, windows, slabs, tall, _ = parts_ref.shape
    half = out_ref.shape[1]
    size = half // (HEADS // 2)
    tile = parts_ref[:, :, slabs - 1].astype(f32)

    def moved(columns):
        return pltpu.roll(tile, LANES - columns, 3)

    top = tile + moved(8) + moved(16)
    factor = jnp.exp2(top - jnp.max(top, axis=0, keepdims=True))
    factor = factor / jnp.sum((moved(24) + moved(32)) * factor, axis=0, keepdims=True)
    head = div(iota(tile.shape, 3), size)
    blocks = []
    for i in range(half // LANES):
        nodes = []
        for late in range(2):
            wide = jnp.zeros(tile.shape, f32)
            for h in range(LANES // size):
                at = late * (LANES // 2) + i * (LANES // size) + h
                wide = jnp.where(head == h, factor[..., at : at + 1], wide)
            part = parts_ref[:, :, 2 * i + late].astype(f32)
            nodes.append(jnp.sum(part * wide, axis=0))
        blocks.append(jnp.concatenate(nodes, axis=1))
    mixed = jnp.concatenate(blocks, axis=2)
    out_ref[...] = mixed.reshape(windows * 2 * tall, half).astype(bf16)


def combine_kernel(
    mixed_ref, other_mixed_ref, latent_ref, other_latent_ref, gain_ref, w_o_ref, w_kv_ref,
    latent_out_ref, out_ref,
):
    chips = out_ref.shape[0]
    rows = latent_ref.shape[0]
    width, half = w_o_ref.shape[0], w_o_ref.shape[0] // 2
    core = lax.axis_index("dom") & 1

    def in_order(own_ref, other_ref, axis):
        own, other = own_ref[...], other_ref[...]
        both = [jnp.where(core == 0, own, other), jnp.where(core == 0, other, own)]
        return jnp.concatenate(both, axis=axis)

    update = dot(in_order(mixed_ref, other_mixed_ref, 1), w_o_ref[...])
    latent_in = in_order(latent_ref, other_latent_ref, 0)
    latent_out = (latent_in.astype(f32) + update).astype(bf16)
    latent_out_ref[...] = jnp.where(core == 0, latent_out[:rows], latent_out[rows:])
    latent_rows = normed(latent_out, gain_ref[...])
    for c in range(2):

        @pl.when(core == c)
        def _():
            for i in range(2):
                at = i * width + c * half
                pairs = dot(latent_rows, w_kv_ref[:, at : at + half]).astype(bf16)
                for k in range(chips):
                    out_ref[k, :, i * half : (i + 1) * half] = pairs


def middle_kernel(
    steps, peers, rows, gain_ref, need_ref, slot_ref, x_hbm, w_hbm, query_ref, node_ref,
    x_ref, w_ref, sems,
):
    copies = started(
        pltpu.make_async_copy(w_hbm, w_ref, sems.at[0]),
        pltpu.make_async_copy(x_hbm, x_ref, sems.at[1]),
    )
    points = x_ref.shape[0]
    block = points // steps
    high_count = need_ref.shape[0]
    cap = high_count * LANES // peers
    need = need_ref[...].astype(f32).astype(bf16)
    for j in range(slot_ref.shape[0]):
        slots = slot_ref[j : j + 1, :]
        row_of = (div(slots, LANES) == iota((high_count, points), 0)).astype(bf16)
        listed = lax.dot_general(need, row_of, (((0,), (0,)), ((), ())), preferred_element_type=f32)
        own = mod(slots, LANES) == iota((LANES, points), 0)
        found = jnp.sum(jnp.where(own, listed, 0.0), axis=0, keepdims=True).astype(jnp.int32)
        node_ref[j : j + 1, :] = div(slots, cap) * rows + found
    for copy in copies:
        copy.wait()
    for i in range(steps):
        part = pl.ds(i * block, block)
        queries = dot(normed(x_ref[part, :], gain_ref[...]), w_ref[...])
        query_ref[:, part] = queries.T.astype(bf16)


def attend_half(pairs, queries, nodes):
    half, points = queries.shape
    edges = nodes.shape[0]
    heads = HEADS // 2
    size = half // heads
    picks = [one_hot(nodes[j : j + 1], (pairs.shape[1], points), 0) for j in range(edges)]
    scores, values = [], []
    for j in range(edges):
        chosen = dot(pairs, picks[j])
        products = (chosen[:half] * queries.astype(f32)).reshape(heads, size, points)
        scores.append(jnp.sum(products, axis=1) * (1.0 / math.sqrt(size)))
        values.append(chosen[half:].reshape(heads, size, points))
    highest = functools.reduce(jnp.maximum, scores)
    raised = [jnp.exp(score - highest) for score in scores]
    inverse = 1.0 / sum(raised)
    mixed = jnp.zeros((heads, size, points), f32)
    for j in range(edges):
        weight = (raised[j] * inverse).astype(bf16).astype(f32).reshape(heads, 1, points)
        mixed += values[j] * weight
    return mixed.reshape(half, points).T.astype(bf16)


def half_of(ref, first, half):
    return ref.at[pl.ds(pl.multiple_of(first, half), half)]


def own_kernel(steps, pairs_ref, node_ref, query_ref, out_ref):
    points, half = out_ref.shape
    block = points // steps
    core = lax.axis_index("dom") & 1
    queries = half_of(query_ref, core * half, half)
    pairs = pairs_ref[...].T
    for i in range(steps):
        part = pl.ds(i * block, block)
        out_ref[part, :] = attend_half(pairs, queries[:, part], node_ref[:, part])


def other_kernel(
    steps, pairs_ref, own_ref, node_ref, query_ref, x_ref, w_ref, latent_ref,
    out_hbm, latent_hbm, out_ref, sems,
):
    latent_copy = pltpu.make_async_copy(latent_ref, latent_hbm, sems.at[steps])
    latent_copy.start()
    points, half = own_ref.shape
    block = points // steps
    core = lax.axis_index("dom") & 1
    queries = half_of(query_ref, (1 - core) * half, half)
    pairs = pairs_ref[...].T
    sends = []
    parts = [pl.ds(i * block, block) for i in range(steps)]

    def attended(part):
        return attend_half(pairs, queries[:, part], node_ref[:, part])

    mixed = attended(parts[0])
    for i, part in enumerate(parts):
        following = attended(parts[i + 1]) if i + 1 < steps else None
        own = own_ref[part, :]
        both = [jnp.where(core == 0, own, mixed), jnp.where(core == 0, mixed, own)]
        update = dot(jnp.concatenate(both, axis=1), w_ref[...])
        out_ref[part, :] = (x_ref[part, :].astype(f32) + update).astype(bf16)
        sends += started(pltpu.make_async_copy(out_ref.at[part], out_hbm.at[part], sems.at[i]))
        mixed = following
    for send in sends:
        send.wait()
    latent_copy.wait()


def in_hbm(array):
    return pltpu.with_memory_space_constraint(array, pltpu.HBM)


def in_vmem(array):
    return pltpu.with_memory_space_constraint(array, pltpu.VMEM)


def on_device(
    grid,
    latent_in,
    grid_gain,
    node_gain,
    dec_gain,
    w_q_enc,
    w_kv_enc,
    w_o_enc,
    w_q_dec,
    w_kv_dec,
    w_o_dec,
    enc_need,
    enc_slot,
    enc_count,
    dec_need,
    dec_slot,
):
    peers = lax.axis_size("dom")
    points, depth = grid.shape
    rows = latent_in.shape[0]
    width = w_q_enc.shape[1]
    nodes = peers * rows
    entries = enc_need.shape[1]
    edges = enc_slot.shape[0]
    cap = entries // peers
    half = width // 2
    sent = (peers, 2 * (half // LANES) + 1, rows // 2, LANES)
    swap = [(i, i ^ 1) for i in range(peers)]
    vmem = pl.BlockSpec(memory_space=pltpu.VMEM)
    hbm = pl.BlockSpec(memory_space=pltpu.HBM)

    other_grid = lax.ppermute(grid, "dom", swap)
    other_latent = lax.ppermute(latent_in, "dom", swap)
    ask_inputs = (
        w_q_enc,
        latent_in,
        node_gain.reshape(1, -1),
        enc_slot.T,
        enc_count.reshape(1, -1),
        enc_need,
    )
    asked = pl.pallas_call(
        ask_kernel,
        in_specs=[hbm] * len(ask_inputs),
        out_specs=vmem,
        out_shape=pltpu.VMEM(sent, bf16),
        scratch_shapes=[pltpu.VMEM(one.shape, one.dtype) for one in ask_inputs]
        + [pltpu.SemaphoreType.DMA((len(ask_inputs),))],
        compiler_params=params(62),
        cost_estimate=cost(2 * rows * depth * width, 2 * depth * width),
        name="ask",
    )(*map(in_hbm, ask_inputs))
    asked = exchange(asked)

    block = math.gcd(points, 256)
    steps = points // block
    pairs = pl.pallas_call(
        functools.partial(front_kernel, steps),
        in_specs=[hbm] * 4,
        out_specs=[vmem] * 2,
        out_shape=[pltpu.VMEM((points, width), bf16)] * 2,
        scratch_shapes=[
            pltpu.VMEM((1, depth), f32),
            pltpu.VMEM((points, depth), bf16),
            pltpu.VMEM((points, depth), bf16),
            pltpu.VMEM((depth, width), bf16),
            pltpu.SemaphoreType.DMA((5,)),
        ],
        compiler_params=params(40),
        cost_estimate=cost(4 * points * depth * width, 8 * points * depth),
        name="front",
    )(*map(in_hbm, (grid_gain.reshape(1, -1), grid, other_grid, w_kv_enc)))

    parts = pl.pallas_call(
        functools.partial(partial_kernel, cap, rows, edges),
        in_specs=[vmem] * 3,
        out_specs=vmem,
        out_shape=pltpu.VMEM(sent, bf16),
        compiler_params=params(40),
        cost_estimate=cost(4 * entries * points * width, 4 * points * width),
        name="partial",
    )(asked, *map(in_vmem, pairs))
    parts, dec_need, dec_slot = lax.optimization_barrier((parts, dec_need, dec_slot))
    same_core = [list(range(c, peers, 2)) for c in range(2)]
    parts = parts.reshape(peers // 2, 2 * sent[1], *sent[2:])
    parts = exchange(parts, same_core).reshape(peers // 2, 2, *sent[1:])

    slot_total = dec_need.shape[1]
    edge_count = dec_slot.shape[0]
    queries, node_of = pl.pallas_call(
        functools.partial(middle_kernel, steps, peers, rows),
        in_specs=[vmem] * 3 + [hbm] * 2,
        out_specs=[vmem, vmem],
        out_shape=[
            pltpu.VMEM((width, points), bf16),
            jax.ShapeDtypeStruct((edge_count, points), jnp.int32),
        ],
        scratch_shapes=[
            pltpu.VMEM((points, depth), bf16),
            pltpu.VMEM((depth, width), bf16),
            pltpu.SemaphoreType.DMA((2,)),
        ],
        compiler_params=params(40),
        cost_estimate=cost(2 * points * depth * width, 8 * points * depth),
        name="middle",
    )(
        grid_gain.reshape(1, -1),
        dec_need.reshape(slot_total // LANES, LANES),
        dec_slot,
        in_hbm(grid),
        in_hbm(w_q_dec),
    )
    parts, queries, node_of = lax.optimization_barrier((parts, queries, node_of))

    mixed = pl.pallas_call(
        merge_kernel,
        in_specs=[vmem],
        out_specs=vmem,
        out_shape=jax.ShapeDtypeStruct((2 * rows, half), bf16),
        compiler_params=params(24),
        cost_estimate=cost(8 * nodes * half, 8 * nodes * half),
        name="merge",
    )(parts)
    latent_out, everyone = pl.pallas_call(
        combine_kernel,
        in_specs=[vmem] * 7,
        out_specs=[vmem] * 2,
        out_shape=[
            pltpu.VMEM((rows, depth), bf16),
            jax.ShapeDtypeStruct((peers // 2, 2 * rows, width), bf16),
        ],
        compiler_params=params(24),
        cost_estimate=cost(6 * rows * depth * width, 6 * depth * width),
        name="combine",
    )(
        mixed,
        lax.ppermute(mixed, "dom", swap),
        latent_in,
        other_latent,
        dec_gain.reshape(1, -1),
        w_o_enc,
        w_kv_dec,
    )
    own = exchange(everyone, same_core).reshape(nodes, width)
    other = lax.ppermute(own, "dom", swap)

    queries = in_vmem(queries)
    own_mixed = pl.pallas_call(
        functools.partial(own_kernel, steps),
        in_specs=[vmem] * 3,
        out_shape=jax.ShapeDtypeStruct((points, half), bf16),
        compiler_params=params(48),
        cost_estimate=cost(4 * points * nodes * width, 8 * points * nodes),
        name="own",
    )(own, node_of, queries)
    grid_out, latent_out = pl.pallas_call(
        functools.partial(other_kernel, steps),
        in_specs=[vmem] * 7,
        out_specs=[hbm] * 2,
        out_shape=[pltpu.HBM((points, depth), bf16), pltpu.HBM((rows, depth), bf16)],
        scratch_shapes=[
            pltpu.VMEM((points, depth), bf16),
            pltpu.SemaphoreType.DMA((steps + 1,)),
        ],
        compiler_params=params(48),
        cost_estimate=cost(4 * points * depth * width, 8 * points * depth),
        name="other",
    )(other, own_mixed, node_of, queries, grid, w_o_dec, in_vmem(latent_out))
    return (latent_out, grid_out)


def solution(mesh):
    return jax.shard_map(
        on_device,
        mesh=mesh,
        in_specs=(
            P(("groups", "dom"), None),
            P(("groups", "dom"), None),
            P(),
            P(),
            P(),
            P(),
            P(),
            P(),
            P(),
            P(),
            P(),
            P("dom", None),
            P(None, "dom"),
            P("dom"),
            P("dom", None),
            P(None, "dom"),
        ),
        out_specs=(P(("groups", "dom"), None), P(("groups", "dom"), None)),
        check_vma=False,
    )
```

```python
import functools
import math

import jax
import jax.numpy as jnp
from jax import lax
from jax.experimental import pallas as pl
from jax.experimental.pallas import tpu as pltpu
from jax.sharding import PartitionSpec as P

HEADS = 8
LANES = 128
NEG = -1e30
norm_eps = 1e-06
f32 = jnp.float32
bf16 = jnp.bfloat16


def iota(shape, dim):
    return lax.broadcasted_iota(jnp.int32, shape, dim)


def one_hot(places, shape, dim):
    return (places == iota(shape, dim)).astype(bf16)


def div(values, by):
    if by & (by - 1) == 0:
        return values >> (by.bit_length() - 1)
    return values // by


def mod(values, by):
    if by & (by - 1) == 0:
        return values & (by - 1)
    return values % by


def dot(a, b):
    return jnp.dot(a, b, preferred_element_type=f32)


def dot_t(a, b):
    return lax.dot_general(a, b, (((1,), (1,)), ((), ())), preferred_element_type=f32)


def normed(values, gain):
    widened = values.astype(f32)
    spread = jnp.mean(widened * widened, axis=-1, keepdims=True)
    return (widened * lax.rsqrt(spread + norm_eps) * gain).astype(bf16)


def params(mib):
    return pltpu.CompilerParams(vmem_limit_bytes=mib * 2**20)


def started(*copies):
    for copy in copies:
        copy.start()
    return copies


def cost(flops, read, exps=0):
    return pl.CostEstimate(flops=int(flops), bytes_accessed=int(read), transcendentals=int(exps))


def exchange(blocks, groups=None):
    return lax.all_to_all(
        blocks, "dom", split_axis=0, concat_axis=0, tiled=True, axis_index_groups=groups
    )


def slab(values, i, late, tall):
    return values[late * tall : (late + 1) * tall, i * LANES : (i + 1) * LANES]


def ask_kernel(*refs):
    sources, out_ref, held, sems = refs[:6], refs[6], refs[7:13], refs[13]
    copies = started(
        *[
            pltpu.make_async_copy(source, ref, sems.at[i])
            for i, (source, ref) in enumerate(zip(sources, held))
        ]
    )
    w_ref, latent_ref, gain_ref, slot_ref, count_ref, need_ref = held
    rows = latent_ref.shape[0]
    width = w_ref.shape[1]
    entries = need_ref.shape[1]
    edges = slot_ref.shape[1]
    peers = out_ref.shape[0]
    both = 2 * entries // peers
    tall = rows // 2
    for copy in copies[1:]:
        copy.wait()
    rows_normed = normed(latent_ref[...], gain_ref[...])
    live = iota((edges, rows), 0) < count_ref[...]
    slots = slot_ref[...].astype(f32).T.astype(jnp.int32)
    slots = jnp.where(live, slots, entries) - entries // 2
    slots = slots.astype(f32).astype(bf16)
    tile = jnp.zeros((tall, LANES), f32)
    for g in range(edges // tall):
        to = iota((rows, LANES), 1) == iota((rows, LANES), 0) + g * rows
        tile += dot(slots, to.astype(bf16))[g * tall : (g + 1) * tall]
    row, lane = iota((tall, LANES), 0), iota((tall, LANES), 1)
    in_list = (lane >= LANES // 2) & (lane < LANES // 2 + both)
    need = need_ref[...]
    tiles = []
    for chip in range(peers // 2):
        at = chip * both
        piece = need[:, at // LANES * LANES : at // LANES * LANES + LANES].astype(f32)
        piece = pltpu.roll(jnp.broadcast_to(piece, (tall, LANES)), (LANES // 2 - at) % LANES, 1)
        high = jnp.floor(piece * (1.0 / 256.0))
        piece = jnp.where(row == 0, piece - high * 256.0, jnp.where(row == 1, high, 0.0))
        tiles.append((tile + jnp.where(in_list, piece, 0.0)).astype(bf16))
    copies[0].wait()
    queries = dot(rows_normed, w_ref[...])
    blocks = width // 2 // LANES
    slabs = [
        slab(queries, i, late, tall).astype(bf16) for i in range(2 * blocks) for late in range(2)
    ]
    for p in range(peers):
        for i in range(2 * blocks):
            out_ref[p, i] = slabs[p % 2 * 2 * blocks + i]
        out_ref[p, 2 * blocks] = tiles[p // 2]


def front_kernel(
    steps, gain_hbm, own_hbm, other_hbm, w_hbm, own_out_ref, other_out_ref,
    gain_ref, own_ref, other_ref, w_ref, sems,
):
    points = own_ref.shape[0]
    block = points // steps
    half = own_out_ref.shape[1] // 2
    core = lax.axis_index("dom") & 1
    copies = started(
        pltpu.make_async_copy(gain_hbm, gain_ref, sems.at[0]),
        *[
            pltpu.make_async_copy(
                w_hbm.at[:, pl.ds(pl.multiple_of((core + 2 * i) * half, half), half)],
                w_ref.at[:, pl.ds(i * half, half)],
                sems.at[1 + i],
            )
            for i in range(2)
        ],
        pltpu.make_async_copy(own_hbm, own_ref, sems.at[3]),
        pltpu.make_async_copy(other_hbm, other_ref, sems.at[4]),
    )
    parts = [pl.ds(i * block, block) for i in range(steps)]
    for copy in copies[:3]:
        copy.wait()
    gain = gain_ref[...]
    sides = ((own_ref, own_out_ref), (other_ref, other_out_ref))
    for copy, (rows_ref, out_ref) in zip(copies[3:], sides):
        copy.wait()
        for part in parts:
            out_ref[part, :] = dot(normed(rows_ref[part, :], gain), w_ref[...]).astype(bf16)


def stat_parts(top, total):
    top_1 = top.astype(bf16).astype(f32)
    top_2 = (top - top_1).astype(bf16).astype(f32)
    total_1 = total.astype(bf16).astype(f32)
    return top_1, top_2, top - top_1 - top_2, total_1, total - total_1


def partial_kernel(cap, rows, edges, asked_ref, *refs):
    pairs_refs, out_ref = refs[:2], refs[2]
    me = lax.axis_index("dom")
    points, both = pairs_refs[0].shape
    peers = out_ref.shape[0]
    width = both // 2
    heads = HEADS // 2
    size = width // heads
    tall = rows // 2
    blocks = width // LANES
    scale = math.log2(math.e) / math.sqrt(size)
    all_nodes, all_entries = peers * rows, peers * cap
    some = LANES // (heads * rows)
    nodes, entries = some * rows, some * cap
    tiles = asked_ref[:, 2 * blocks].astype(f32)

    tile_rows = peers * tall
    pick_row = iota((all_entries, tile_rows), 1) - div(iota((all_entries, tile_rows), 0), cap) * tall
    pick = jnp.where(pick_row == 0, 1.0, jnp.where(pick_row == 1, 256.0, 0.0)).astype(bf16)
    lists = dot(pick, tiles.reshape(tile_rows, LANES).astype(bf16))
    lane = iota((all_entries, LANES), 1) - mod(iota((all_entries, LANES), 0), cap) - LANES // 2
    gathered = []
    for other, ref in enumerate(pairs_refs):
        mine = lane == ((me ^ other) & 1) * cap
        index = jnp.sum(jnp.where(mine, lists, 0.0), axis=1, keepdims=True).astype(jnp.int32)
        gathered.append(dot(one_hot(index, (all_entries, points), 1), ref[...]))

    group, across = div(iota((tall, LANES), 1), rows), LANES // rows
    slots = []
    for g in range(edges // tall):
        line = []
        for first in range(0, peers, across):
            merged = jnp.zeros((tall, LANES), f32)
            for w in range(across):
                merged = jnp.where(
                    group == w, pltpu.roll(tiles[first + w], (w - g) * rows % LANES, 1), merged
                )
            line.append(merged)
        slots.append(jnp.concatenate(line, axis=1))
    all_slots = jnp.concatenate(slots, axis=0).astype(jnp.int32) + all_entries // 2

    listed = -(-cap // 8) * 8
    biases = []
    for other in range(2):
        slots = all_slots - (me ^ other) * cap
        uses = jnp.zeros((listed, all_nodes), f32)
        for j in range(edges):
            uses += jnp.where(slots[j : j + 1] == iota((listed, all_nodes), 0), 1.0, 0.0)
        live = uses > 0.5
        biases.append(jnp.where(live, jnp.log2(jnp.where(live, uses, 1.0)), NEG))

    window = mod(div(iota((listed, LANES), 1), rows), some)
    first_nodes = iota((listed, LANES), 1) < nodes
    first_head = iota((nodes, LANES), 1) < size
    tops, totals = [], []
    for start in range(0, peers, some):
        bias = []
        for one in biases:
            at = start * rows
            one = one[:, at // LANES * LANES : at // LANES * LANES + LANES]
            one = jnp.where(first_nodes, pltpu.roll(one, -at % LANES, 1), 0.0)
            spread = nodes
            while spread < LANES:
                one += pltpu.roll(one, spread, 1)
                spread *= 2
            bias += [jnp.where(window == w, one, NEG)[:cap] for w in range(some)]
        part = slice(start * cap, start * cap + entries)
        pairs = jnp.concatenate([one[part] for one in gathered], axis=0).astype(bf16)
        queries = [
            jnp.concatenate(
                [asked_ref[start + n // 2, 2 * i + n % 2].astype(f32) for n in range(2 * some)], axis=0
            )
            for i in range(blocks)
        ]
        queries = jnp.concatenate(queries, axis=1).astype(bf16)
        head = div(iota(queries.shape, 1), size)
        queries = jnp.concatenate(
            [jnp.where(head == h, queries, jnp.zeros_like(queries)) for h in range(heads)], axis=0
        )
        scores = dot_t(pairs[:, :width], queries) * scale + jnp.concatenate(bias, axis=0)
        top = jnp.max(scores, axis=0, keepdims=True)
        raised = jnp.exp2(scores - top)
        tops.append(top)
        totals.append(jnp.sum(raised, axis=0, keepdims=True))
        mixed = dot(raised.T.astype(bf16), pairs[:, width:])
        for i in range(blocks):
            block = mixed[:, i * LANES : (i + 1) * LANES]
            h = i * (LANES // size)
            block = jnp.where(
                first_head, block[h * nodes : (h + 1) * nodes], block[(h + 1) * nodes : (h + 2) * nodes]
            )
            for n in range(2 * some):
                place = start + n // 2
                out_ref[place, 2 * i + n % 2] = slab(block, 0, n, tall).astype(bf16)

    row_lane = iota((tall, LANES), 1)
    for first in range(0, len(tops), 8):
        parts = stat_parts(
            jnp.concatenate(tops[first : first + 8], axis=0),
            jnp.concatenate(totals[first : first + 8], axis=0),
        )
        rest = jnp.zeros((LANES - 8 * len(parts), LANES), f32)
        columns = jnp.concatenate([*parts, rest], axis=0).T
        for g in range(8):
            for w in range(some):
                tile = jnp.zeros((tall, LANES), f32)
                for h in range(heads):
                    for late in range(2):
                        at = h * nodes + w * rows + late * tall
                        move = late * (LANES // 2) + h - g
                        here = (mod(row_lane, 8) == h) & (div(row_lane, LANES // 2) == late)
                        piece = pltpu.roll(columns[at : at + tall], move % LANES, 1)
                        tile = jnp.where(here, piece, tile)
                out_ref[(first + g) * some + w, 2 * blocks] = tile.astype(bf16)


def merge_kernel(parts_ref, out_ref):
    chips, windows, slabs, tall, _ = parts_ref.shape
    half = out_ref.shape[1]
    size = half // (HEADS // 2)
    tile = parts_ref[:, :, slabs - 1].astype(f32)

    def moved(columns):
        return pltpu.roll(tile, LANES - columns, 3)

    top = tile + moved(8) + moved(16)
    factor = jnp.exp2(top - jnp.max(top, axis=0, keepdims=True))
    factor = factor / jnp.sum((moved(24) + moved(32)) * factor, axis=0, keepdims=True)
    head = div(iota(tile.shape, 3), size)
    blocks = []
    for i in range(half // LANES):
        nodes = []
        for late in range(2):
            wide = jnp.zeros(tile.shape, f32)
            for h in range(LANES // size):
                at = late * (LANES // 2) + i * (LANES // size) + h
                wide = jnp.where(head == h, factor[..., at : at + 1], wide)
            part = parts_ref[:, :, 2 * i + late].astype(f32)
            nodes.append(jnp.sum(part * wide, axis=0))
        blocks.append(jnp.concatenate(nodes, axis=1))
    mixed = jnp.concatenate(blocks, axis=2)
    out_ref[...] = mixed.reshape(windows * 2 * tall, half).astype(bf16)


def combine_kernel(
    mixed_ref, other_mixed_ref, latent_ref, other_latent_ref, gain_ref, w_o_ref, w_kv_ref,
    latent_out_ref, out_ref,
):
    rows = latent_ref.shape[0]
    core = lax.axis_index("dom") & 1

    def in_order(own_ref, other_ref, axis):
        own, other = own_ref[...], other_ref[...]
        both = [jnp.where(core == 0, own, other), jnp.where(core == 0, other, own)]
        return jnp.concatenate(both, axis=axis)

    update = dot(in_order(mixed_ref, other_mixed_ref, 1), w_o_ref[...])
    latent_in = in_order(latent_ref, other_latent_ref, 0)
    latent_out = (latent_in.astype(f32) + update).astype(bf16)
    latent_out_ref[...] = jnp.where(core == 0, latent_out[:rows], latent_out[rows:])
    latent_rows = normed(latent_out, gain_ref[...])
    pairs = dot(latent_rows, w_kv_ref[...]).astype(bf16)
    for k in range(out_ref.shape[0]):
        out_ref[k] = pairs


def middle_kernel(
    steps, peers, rows, gain_ref, need_ref, slot_ref, x_hbm, w_hbm, w_kv_hbm,
    query_ref, node_ref, w_kv_ref, x_ref, w_ref, sems,
):
    copies = started(
        pltpu.make_async_copy(w_hbm, w_ref, sems.at[0]),
        pltpu.make_async_copy(x_hbm, x_ref, sems.at[1]),
    )
    half = w_kv_ref.shape[1] // 2
    core = lax.axis_index("dom") & 1
    later = started(
        *[
            pltpu.make_async_copy(
                w_kv_hbm.at[:, pl.ds(pl.multiple_of((core + 2 * i) * half, half), half)],
                w_kv_ref.at[:, pl.ds(i * half, half)],
                sems.at[2 + i],
            )
            for i in range(2)
        ]
    )
    points = x_ref.shape[0]
    block = points // steps
    high_count = need_ref.shape[0]
    cap = high_count * LANES // peers
    need = need_ref[...].astype(f32).astype(bf16)
    for j in range(slot_ref.shape[0]):
        slots = slot_ref[j : j + 1, :]
        row_of = (div(slots, LANES) == iota((high_count, points), 0)).astype(bf16)
        listed = lax.dot_general(need, row_of, (((0,), (0,)), ((), ())), preferred_element_type=f32)
        own = mod(slots, LANES) == iota((LANES, points), 0)
        found = jnp.sum(jnp.where(own, listed, 0.0), axis=0, keepdims=True).astype(jnp.int32)
        node_ref[j : j + 1, :] = div(slots, cap) * rows + found
    for copy in copies:
        copy.wait()
    for i in range(steps):
        part = pl.ds(i * block, block)
        queries = dot(normed(x_ref[part, :], gain_ref[...]), w_ref[...])
        query_ref[:, part] = queries.T.astype(bf16)
    for copy in later:
        copy.wait()


def attend_half(pairs, queries, nodes):
    half, points = queries.shape
    edges = nodes.shape[0]
    heads = HEADS // 2
    size = half // heads
    picks = [one_hot(nodes[j : j + 1], (pairs.shape[1], points), 0) for j in range(edges)]
    scores, values = [], []
    for j in range(edges):
        chosen = dot(pairs, picks[j])
        products = (chosen[:half] * queries.astype(f32)).reshape(heads, size, points)
        scores.append(jnp.sum(products, axis=1) * (1.0 / math.sqrt(size)))
        values.append(chosen[half:].reshape(heads, size, points))
    highest = functools.reduce(jnp.maximum, scores)
    raised = [jnp.exp(score - highest) for score in scores]
    inverse = 1.0 / sum(raised)
    mixed = jnp.zeros((heads, size, points), f32)
    for j in range(edges):
        weight = (raised[j] * inverse).astype(bf16).astype(f32).reshape(heads, 1, points)
        mixed += values[j] * weight
    return mixed.reshape(half, points).T.astype(bf16)


def half_of(ref, first, half):
    return ref.at[pl.ds(pl.multiple_of(first, half), half)]


def own_kernel(steps, pairs_ref, node_ref, query_ref, out_ref):
    points, half = out_ref.shape
    block = points // steps
    core = lax.axis_index("dom") & 1
    queries = half_of(query_ref, core * half, half)
    pairs = pairs_ref[...].T
    for i in range(steps):
        part = pl.ds(i * block, block)
        out_ref[part, :] = attend_half(pairs, queries[:, part], node_ref[:, part])


def other_kernel(
    steps, pairs_ref, own_ref, node_ref, query_ref, x_ref, w_ref, latent_ref,
    out_hbm, latent_hbm, out_ref, sems,
):
    latent_copy = pltpu.make_async_copy(latent_ref, latent_hbm, sems.at[steps])
    latent_copy.start()
    points, half = own_ref.shape
    block = points // steps
    core = lax.axis_index("dom") & 1
    queries = half_of(query_ref, (1 - core) * half, half)
    pairs = pairs_ref[...].T
    sends = []
    parts = [pl.ds(i * block, block) for i in range(steps)]

    def attended(part):
        return attend_half(pairs, queries[:, part], node_ref[:, part])

    mixed = attended(parts[0])
    for i, part in enumerate(parts):
        following = attended(parts[i + 1]) if i + 1 < steps else None
        own = own_ref[part, :]
        both = [jnp.where(core == 0, own, mixed), jnp.where(core == 0, mixed, own)]
        update = dot(jnp.concatenate(both, axis=1), w_ref[...])
        out_ref[part, :] = (x_ref[part, :].astype(f32) + update).astype(bf16)
        sends += started(pltpu.make_async_copy(out_ref.at[part], out_hbm.at[part], sems.at[i]))
        mixed = following
    for send in sends:
        send.wait()
    latent_copy.wait()


def in_hbm(array):
    return pltpu.with_memory_space_constraint(array, pltpu.HBM)


def in_vmem(array):
    return pltpu.with_memory_space_constraint(array, pltpu.VMEM)


def on_device(
    grid,
    latent_in,
    grid_gain,
    node_gain,
    dec_gain,
    w_q_enc,
    w_kv_enc,
    w_o_enc,
    w_q_dec,
    w_kv_dec,
    w_o_dec,
    enc_need,
    enc_slot,
    enc_count,
    dec_need,
    dec_slot,
):
    peers = lax.axis_size("dom")
    points, depth = grid.shape
    rows = latent_in.shape[0]
    width = w_q_enc.shape[1]
    nodes = peers * rows
    entries = enc_need.shape[1]
    edges = enc_slot.shape[0]
    cap = entries // peers
    half = width // 2
    sent = (peers, 2 * (half // LANES) + 1, rows // 2, LANES)
    swap = [(i, i ^ 1) for i in range(peers)]
    vmem = pl.BlockSpec(memory_space=pltpu.VMEM)
    hbm = pl.BlockSpec(memory_space=pltpu.HBM)

    other_grid = lax.ppermute(grid, "dom", swap)
    other_latent = lax.ppermute(latent_in, "dom", swap)
    ask_inputs = (
        w_q_enc,
        latent_in,
        node_gain.reshape(1, -1),
        enc_slot.T,
        enc_count.reshape(1, -1),
        enc_need,
    )
    asked = pl.pallas_call(
        ask_kernel,
        in_specs=[hbm] * len(ask_inputs),
        out_specs=vmem,
        out_shape=pltpu.VMEM(sent, bf16),
        scratch_shapes=[pltpu.VMEM(one.shape, one.dtype) for one in ask_inputs]
        + [pltpu.SemaphoreType.DMA((len(ask_inputs),))],
        compiler_params=params(62),
        cost_estimate=cost(2 * rows * depth * width, 2 * depth * width),
        name="ask",
    )(*map(in_hbm, ask_inputs))
    asked = exchange(asked)

    block = math.gcd(points, 256)
    steps = points // block
    pairs = pl.pallas_call(
        functools.partial(front_kernel, steps),
        in_specs=[hbm] * 4,
        out_specs=[vmem] * 2,
        out_shape=[pltpu.VMEM((points, width), bf16)] * 2,
        scratch_shapes=[
            pltpu.VMEM((1, depth), f32),
            pltpu.VMEM((points, depth), bf16),
            pltpu.VMEM((points, depth), bf16),
            pltpu.VMEM((depth, width), bf16),
            pltpu.SemaphoreType.DMA((5,)),
        ],
        compiler_params=params(40),
        cost_estimate=cost(4 * points * depth * width, 8 * points * depth),
        name="front",
    )(*map(in_hbm, (grid_gain.reshape(1, -1), grid, other_grid, w_kv_enc)))

    parts = pl.pallas_call(
        functools.partial(partial_kernel, cap, rows, edges),
        in_specs=[vmem] * 3,
        out_specs=vmem,
        out_shape=pltpu.VMEM(sent, bf16),
        compiler_params=params(40),
        cost_estimate=cost(4 * entries * points * width, 4 * points * width),
        name="partial",
    )(asked, *map(in_vmem, pairs))
    parts, dec_need, dec_slot = lax.optimization_barrier((parts, dec_need, dec_slot))
    same_core = [list(range(c, peers, 2)) for c in range(2)]
    parts = parts.reshape(peers // 2, 2 * sent[1], *sent[2:])
    parts = exchange(parts, same_core).reshape(peers // 2, 2, *sent[1:])

    slot_total = dec_need.shape[1]
    edge_count = dec_slot.shape[0]
    queries, node_of, w_kv_half = pl.pallas_call(
        functools.partial(middle_kernel, steps, peers, rows),
        in_specs=[vmem] * 3 + [hbm] * 3,
        out_specs=[vmem] * 3,
        out_shape=[
            pltpu.VMEM((width, points), bf16),
            jax.ShapeDtypeStruct((edge_count, points), jnp.int32),
            pltpu.VMEM((depth, width), bf16),
        ],
        scratch_shapes=[
            pltpu.VMEM((points, depth), bf16),
            pltpu.VMEM((depth, width), bf16),
            pltpu.SemaphoreType.DMA((4,)),
        ],
        compiler_params=params(40),
        cost_estimate=cost(2 * points * depth * width, 8 * points * depth),
        name="middle",
    )(
        grid_gain.reshape(1, -1),
        dec_need.reshape(slot_total // LANES, LANES),
        dec_slot,
        in_hbm(grid),
        in_hbm(w_q_dec),
        in_hbm(w_kv_dec),
    )
    parts, queries, node_of = lax.optimization_barrier((parts, queries, node_of))

    mixed = pl.pallas_call(
        merge_kernel,
        in_specs=[vmem],
        out_specs=vmem,
        out_shape=jax.ShapeDtypeStruct((2 * rows, half), bf16),
        compiler_params=params(24),
        cost_estimate=cost(8 * nodes * half, 8 * nodes * half),
        name="merge",
    )(parts)
    latent_out, everyone = pl.pallas_call(
        combine_kernel,
        in_specs=[vmem] * 7,
        out_specs=[vmem] * 2,
        out_shape=[
            pltpu.VMEM((rows, depth), bf16),
            jax.ShapeDtypeStruct((peers // 2, 2 * rows, width), bf16),
        ],
        compiler_params=params(24),
        cost_estimate=cost(6 * rows * depth * width, 6 * depth * width),
        name="combine",
    )(
        mixed,
        lax.ppermute(mixed, "dom", swap),
        latent_in,
        other_latent,
        dec_gain.reshape(1, -1),
        w_o_enc,
        in_vmem(w_kv_half),
    )
    own = exchange(everyone, same_core).reshape(nodes, width)
    other = lax.ppermute(own, "dom", swap)

    queries = in_vmem(queries)
    own_mixed = pl.pallas_call(
        functools.partial(own_kernel, steps),
        in_specs=[vmem] * 3,
        out_shape=jax.ShapeDtypeStruct((points, half), bf16),
        compiler_params=params(48),
        cost_estimate=cost(4 * points * nodes * width, 8 * points * nodes),
        name="own",
    )(own, node_of, queries)
    grid_out, latent_out = pl.pallas_call(
        functools.partial(other_kernel, steps),
        in_specs=[vmem] * 7,
        out_specs=[hbm] * 2,
        out_shape=[pltpu.HBM((points, depth), bf16), pltpu.HBM((rows, depth), bf16)],
        scratch_shapes=[
            pltpu.VMEM((points, depth), bf16),
            pltpu.SemaphoreType.DMA((steps + 1,)),
        ],
        compiler_params=params(48),
        cost_estimate=cost(4 * points * depth * width, 8 * points * depth),
        name="other",
    )(other, own_mixed, node_of, queries, grid, w_o_dec, in_vmem(latent_out))
    return (latent_out, grid_out)


def solution(mesh):
    return jax.shard_map(
        on_device,
        mesh=mesh,
        in_specs=(
            P(("groups", "dom"), None),
            P(("groups", "dom"), None),
            P(),
            P(),
            P(),
            P(),
            P(),
            P(),
            P(),
            P(),
            P(),
            P("dom", None),
            P(None, "dom"),
            P("dom"),
            P("dom", None),
            P(None, "dom"),
        ),
        out_specs=(P(("groups", "dom"), None), P(("groups", "dom"), None)),
        check_vma=False,
    )
```

```python
import functools
import math

import jax
import jax.numpy as jnp
from jax import lax
from jax.experimental import pallas as pl
from jax.experimental.pallas import tpu as pltpu
from jax.sharding import PartitionSpec as P

HEADS = 8
LANES = 128
NEG = -1e30
norm_eps = 1e-06
f32 = jnp.float32
bf16 = jnp.bfloat16


def iota(shape, dim):
    return lax.broadcasted_iota(jnp.int32, shape, dim)


def one_hot(places, shape, dim):
    return (places == iota(shape, dim)).astype(bf16)


def div(values, by):
    if by & (by - 1) == 0:
        return values >> (by.bit_length() - 1)
    return values // by


def mod(values, by):
    if by & (by - 1) == 0:
        return values & (by - 1)
    return values % by


def dot(a, b):
    return jnp.dot(a, b, preferred_element_type=f32)


def dot_t(a, b):
    return lax.dot_general(a, b, (((1,), (1,)), ((), ())), preferred_element_type=f32)


def normed(values, gain):
    widened = values.astype(f32)
    spread = jnp.mean(widened * widened, axis=-1, keepdims=True)
    return (widened * lax.rsqrt(spread + norm_eps) * gain).astype(bf16)


def params(mib):
    return pltpu.CompilerParams(vmem_limit_bytes=mib * 2**20)


def started(*copies):
    for copy in copies:
        copy.start()
    return copies


def cost(flops, read, exps=0):
    return pl.CostEstimate(flops=int(flops), bytes_accessed=int(read), transcendentals=int(exps))


def exchange(blocks, groups=None):
    return lax.all_to_all(
        blocks, "dom", split_axis=0, concat_axis=0, tiled=True, axis_index_groups=groups
    )


def slab(values, i, late, tall):
    return values[late * tall : (late + 1) * tall, i * LANES : (i + 1) * LANES]


def ask_kernel(*refs):
    sources, out_ref, held, sems = refs[:6], refs[6], refs[7:13], refs[13]
    copies = started(
        *[
            pltpu.make_async_copy(source, ref, sems.at[i])
            for i, (source, ref) in enumerate(zip(sources, held))
        ]
    )
    w_ref, latent_ref, gain_ref, slot_ref, count_ref, need_ref = held
    rows = latent_ref.shape[0]
    width = w_ref.shape[1]
    entries = need_ref.shape[1]
    edges = slot_ref.shape[1]
    peers = out_ref.shape[0]
    both = 2 * entries // peers
    tall = rows // 2
    for copy in copies[1:]:
        copy.wait()
    rows_normed = normed(latent_ref[...], gain_ref[...])
    live = iota((edges, rows), 0) < count_ref[...]
    slots = slot_ref[...].astype(f32).T.astype(jnp.int32)
    slots = jnp.where(live, slots, entries) - entries // 2
    slots = slots.astype(f32).astype(bf16)
    tile = jnp.zeros((tall, LANES), f32)
    for g in range(edges // tall):
        to = iota((rows, LANES), 1) == iota((rows, LANES), 0) + g * rows
        tile += dot(slots, to.astype(bf16))[g * tall : (g + 1) * tall]
    row, lane = iota((tall, LANES), 0), iota((tall, LANES), 1)
    in_list = (lane >= LANES // 2) & (lane < LANES // 2 + both)
    need = need_ref[...]
    tiles = []
    for chip in range(peers // 2):
        at = chip * both
        piece = need[:, at // LANES * LANES : at // LANES * LANES + LANES].astype(f32)
        piece = pltpu.roll(jnp.broadcast_to(piece, (tall, LANES)), (LANES // 2 - at) % LANES, 1)
        high = jnp.floor(piece * (1.0 / 256.0))
        piece = jnp.where(row == 0, piece - high * 256.0, jnp.where(row == 1, high, 0.0))
        tiles.append((tile + jnp.where(in_list, piece, 0.0)).astype(bf16))
    copies[0].wait()
    queries = dot(rows_normed, w_ref[...])
    blocks = width // 2 // LANES
    slabs = [
        slab(queries, i, late, tall).astype(bf16) for i in range(2 * blocks) for late in range(2)
    ]
    for p in range(peers):
        for i in range(2 * blocks):
            out_ref[p, i] = slabs[p % 2 * 2 * blocks + i]
        out_ref[p, 2 * blocks] = tiles[p // 2]


def front_kernel(
    steps, gain_hbm, own_hbm, other_hbm, w_hbm, own_out_ref, other_out_ref,
    gain_ref, own_ref, other_ref, w_ref, sems,
):
    points = own_ref.shape[0]
    block = points // steps
    half = own_out_ref.shape[1] // 2
    core = lax.axis_index("dom") & 1
    copies = started(
        pltpu.make_async_copy(gain_hbm, gain_ref, sems.at[0]),
        *[
            pltpu.make_async_copy(
                w_hbm.at[:, pl.ds(pl.multiple_of((core + 2 * i) * half, half), half)],
                w_ref.at[:, pl.ds(i * half, half)],
                sems.at[1 + i],
            )
            for i in range(2)
        ],
        pltpu.make_async_copy(own_hbm, own_ref, sems.at[3]),
        pltpu.make_async_copy(other_hbm, other_ref, sems.at[4]),
    )
    parts = [pl.ds(i * block, block) for i in range(steps)]
    for copy in copies[:3]:
        copy.wait()
    gain = gain_ref[...]
    sides = ((own_ref, own_out_ref), (other_ref, other_out_ref))
    for copy, (rows_ref, out_ref) in zip(copies[3:], sides):
        copy.wait()
        for part in parts:
            out_ref[part, :] = dot(normed(rows_ref[part, :], gain), w_ref[...]).astype(bf16)


def stat_parts(top, total):
    top_1 = top.astype(bf16).astype(f32)
    top_2 = (top - top_1).astype(bf16).astype(f32)
    total_1 = total.astype(bf16).astype(f32)
    return top_1, top_2, top - top_1 - top_2, total_1, total - total_1


def partial_kernel(cap, rows, edges, asked_ref, *refs):
    pairs_refs, out_ref = refs[:2], refs[2]
    me = lax.axis_index("dom")
    points, both = pairs_refs[0].shape
    chips = out_ref.shape[0]
    peers = 2 * chips
    width = both // 2
    heads = HEADS // 2
    size = width // heads
    tall = rows // 2
    blocks = width // LANES
    scale = math.log2(math.e) / math.sqrt(size)
    all_nodes, all_entries = peers * rows, peers * cap
    some = LANES // (heads * rows)
    nodes, entries = some * rows, some * cap
    tiles = asked_ref[:, 2 * blocks].astype(f32)

    tile_rows = peers * tall
    pick_row = iota((all_entries, tile_rows), 1) - div(iota((all_entries, tile_rows), 0), cap) * tall
    pick = jnp.where(pick_row == 0, 1.0, jnp.where(pick_row == 1, 256.0, 0.0)).astype(bf16)
    lists = dot(pick, tiles.reshape(tile_rows, LANES).astype(bf16))
    lane = iota((all_entries, LANES), 1) - mod(iota((all_entries, LANES), 0), cap) - LANES // 2
    gathered = []
    for other, ref in enumerate(pairs_refs):
        mine = lane == ((me ^ other) & 1) * cap
        index = jnp.sum(jnp.where(mine, lists, 0.0), axis=1, keepdims=True).astype(jnp.int32)
        gathered.append(dot(one_hot(index, (all_entries, points), 1), ref[...]))

    group, across = div(iota((tall, LANES), 1), rows), LANES // rows
    slots = []
    for g in range(edges // tall):
        line = []
        for first in range(0, peers, across):
            merged = jnp.zeros((tall, LANES), f32)
            for w in range(across):
                merged = jnp.where(
                    group == w, pltpu.roll(tiles[first + w], (w - g) * rows % LANES, 1), merged
                )
            line.append(merged)
        slots.append(jnp.concatenate(line, axis=1))
    all_slots = jnp.concatenate(slots, axis=0).astype(jnp.int32) + all_entries // 2

    listed = -(-cap // 8) * 8
    biases = []
    for other in range(2):
        slots = all_slots - (me ^ other) * cap
        uses = jnp.zeros((listed, all_nodes), f32)
        for j in range(edges):
            uses += jnp.where(slots[j : j + 1] == iota((listed, all_nodes), 0), 1.0, 0.0)
        live = uses > 0.5
        biases.append(jnp.where(live, jnp.log2(jnp.where(live, uses, 1.0)), NEG))

    window = mod(div(iota((listed, LANES), 1), rows), some)
    first_nodes = iota((listed, LANES), 1) < nodes
    first_head = iota((nodes, LANES), 1) < size
    tops, totals = [], []
    for start in range(0, peers, some):
        bias = []
        for one in biases:
            at = start * rows
            one = one[:, at // LANES * LANES : at // LANES * LANES + LANES]
            one = jnp.where(first_nodes, pltpu.roll(one, -at % LANES, 1), 0.0)
            spread = nodes
            while spread < LANES:
                one += pltpu.roll(one, spread, 1)
                spread *= 2
            bias += [jnp.where(window == w, one, NEG)[:cap] for w in range(some)]
        part = slice(start * cap, start * cap + entries)
        pairs = jnp.concatenate([one[part] for one in gathered], axis=0).astype(bf16)
        queries = [
            jnp.concatenate(
                [asked_ref[start + n // 2, 2 * i + n % 2].astype(f32) for n in range(2 * some)], axis=0
            )
            for i in range(blocks)
        ]
        queries = jnp.concatenate(queries, axis=1).astype(bf16)
        head = div(iota(queries.shape, 1), size)
        queries = jnp.concatenate(
            [jnp.where(head == h, queries, jnp.zeros_like(queries)) for h in range(heads)], axis=0
        )
        scores = dot_t(pairs[:, :width], queries) * scale + jnp.concatenate(bias, axis=0)
        top = jnp.max(scores, axis=0, keepdims=True)
        raised = jnp.exp2(scores - top)
        tops.append(top)
        totals.append(jnp.sum(raised, axis=0, keepdims=True))
        mixed = dot(raised.T.astype(bf16), pairs[:, width:])
        for i in range(blocks):
            block = mixed[:, i * LANES : (i + 1) * LANES]
            h = i * (LANES // size)
            block = jnp.where(
                first_head, block[h * nodes : (h + 1) * nodes], block[(h + 1) * nodes : (h + 2) * nodes]
            )
            for n in range(2 * some):
                place = n // 2 * 2 * blocks + 2 * i + n % 2
                out_ref[start // some, place] = slab(block, 0, n, tall).astype(bf16)

    row_lane = iota((tall, LANES), 1)
    for first in range(0, len(tops), 8):
        parts = stat_parts(
            jnp.concatenate(tops[first : first + 8], axis=0),
            jnp.concatenate(totals[first : first + 8], axis=0),
        )
        rest = jnp.zeros((LANES - 8 * len(parts), LANES), f32)
        columns = jnp.concatenate([*parts, rest], axis=0).T
        for g in range(8):
            tile = jnp.zeros((tall, LANES), f32)
            for w in range(some):
                for h in range(heads):
                    for late in range(2):
                        at = h * nodes + w * rows + late * tall
                        to = w * heads + h
                        here = (mod(row_lane, 8) == to) & (div(row_lane, LANES // 2) == late)
                        move = late * (LANES // 2) + to - g
                        piece = pltpu.roll(columns[at : at + tall], move % LANES, 1)
                        tile = jnp.where(here, piece, tile)
            out_ref[first + g, some * 2 * blocks] = tile.astype(bf16)


def merge_kernel(parts_ref, out_ref):
    heads, half = HEADS // 2, out_ref.shape[1]
    size, blocks = half // heads, half // LANES
    windows = (parts_ref.shape[1] - 1) // (2 * blocks)
    tile = parts_ref[:, windows * 2 * blocks].astype(f32)

    def moved(columns):
        return pltpu.roll(tile, LANES - columns, 2)

    top = tile + moved(8) + moved(16)
    factor = jnp.exp2(top - jnp.max(top, axis=0, keepdims=True))
    factor = factor / jnp.sum((moved(24) + moved(32)) * factor, axis=0, keepdims=True)
    head = div(iota(tile.shape, 2), size)
    nodes = []
    for w in range(windows):
        for late in range(2):
            line = []
            for i in range(blocks):
                wide = jnp.zeros(tile.shape, f32)
                for h in range(LANES // size):
                    at = late * (LANES // 2) + w * heads + i * (LANES // size) + h
                    wide = jnp.where(head == h, factor[..., at : at + 1], wide)
                part = parts_ref[:, w * 2 * blocks + 2 * i + late].astype(f32)
                line.append(jnp.sum(part * wide, axis=0))
            nodes.append(jnp.concatenate(line, axis=1))
    out_ref[...] = jnp.concatenate(nodes, axis=0).astype(bf16)


def combine_kernel(
    mixed_ref, other_mixed_ref, latent_ref, other_latent_ref, gain_ref, w_o_ref, w_kv_ref,
    latent_out_ref, out_ref,
):
    rows = latent_ref.shape[0]
    core = lax.axis_index("dom") & 1

    def in_order(own_ref, other_ref, axis):
        own, other = own_ref[...], other_ref[...]
        both = [jnp.where(core == 0, own, other), jnp.where(core == 0, other, own)]
        return jnp.concatenate(both, axis=axis)

    update = dot(in_order(mixed_ref, other_mixed_ref, 1), w_o_ref[...])
    latent_in = in_order(latent_ref, other_latent_ref, 0)
    latent_out = (latent_in.astype(f32) + update).astype(bf16)
    latent_out_ref[...] = jnp.where(core == 0, latent_out[:rows], latent_out[rows:])
    latent_rows = normed(latent_out, gain_ref[...])
    pairs = dot(latent_rows, w_kv_ref[...]).astype(bf16)
    for k in range(out_ref.shape[0]):
        out_ref[k] = pairs


def middle_kernel(
    steps, peers, rows, gain_ref, need_ref, slot_ref, x_hbm, w_hbm, w_kv_hbm,
    query_ref, node_ref, w_kv_ref, x_ref, w_ref, sems,
):
    copies = started(
        pltpu.make_async_copy(w_hbm, w_ref, sems.at[0]),
        pltpu.make_async_copy(x_hbm, x_ref, sems.at[1]),
    )
    half = w_kv_ref.shape[1] // 2
    core = lax.axis_index("dom") & 1
    later = started(
        *[
            pltpu.make_async_copy(
                w_kv_hbm.at[:, pl.ds(pl.multiple_of((core + 2 * i) * half, half), half)],
                w_kv_ref.at[:, pl.ds(i * half, half)],
                sems.at[2 + i],
            )
            for i in range(2)
        ]
    )
    points = x_ref.shape[0]
    block = points // steps
    high_count = need_ref.shape[0]
    cap = high_count * LANES // peers
    need = need_ref[...].astype(f32).astype(bf16)
    for j in range(slot_ref.shape[0]):
        slots = slot_ref[j : j + 1, :]
        row_of = (div(slots, LANES) == iota((high_count, points), 0)).astype(bf16)
        listed = lax.dot_general(need, row_of, (((0,), (0,)), ((), ())), preferred_element_type=f32)
        own = mod(slots, LANES) == iota((LANES, points), 0)
        found = jnp.sum(jnp.where(own, listed, 0.0), axis=0, keepdims=True).astype(jnp.int32)
        node_ref[j : j + 1, :] = div(slots, cap) * rows + found
    for copy in copies:
        copy.wait()
    for i in range(steps):
        part = pl.ds(i * block, block)
        queries = dot(normed(x_ref[part, :], gain_ref[...]), w_ref[...])
        query_ref[:, part] = queries.T.astype(bf16)
    for copy in later:
        copy.wait()


def attend_half(pairs, queries, nodes):
    half, points = queries.shape
    edges = nodes.shape[0]
    heads = HEADS // 2
    size = half // heads
    picks = [one_hot(nodes[j : j + 1], (pairs.shape[1], points), 0) for j in range(edges)]
    scores, values = [], []
    for j in range(edges):
        chosen = dot(pairs, picks[j])
        products = (chosen[:half] * queries.astype(f32)).reshape(heads, size, points)
        scores.append(jnp.sum(products, axis=1) * (1.0 / math.sqrt(size)))
        values.append(chosen[half:].reshape(heads, size, points))
    highest = functools.reduce(jnp.maximum, scores)
    raised = [jnp.exp(score - highest) for score in scores]
    inverse = 1.0 / sum(raised)
    mixed = jnp.zeros((heads, size, points), f32)
    for j in range(edges):
        weight = (raised[j] * inverse).astype(bf16).astype(f32).reshape(heads, 1, points)
        mixed += values[j] * weight
    return mixed.reshape(half, points).T.astype(bf16)


def half_of(ref, first, half):
    return ref.at[pl.ds(pl.multiple_of(first, half), half)]


def own_kernel(steps, pairs_ref, node_ref, query_ref, out_ref):
    points, half = out_ref.shape
    block = points // steps
    core = lax.axis_index("dom") & 1
    queries = half_of(query_ref, core * half, half)
    pairs = pairs_ref[...].T
    for i in range(steps):
        part = pl.ds(i * block, block)
        out_ref[part, :] = attend_half(pairs, queries[:, part], node_ref[:, part])


def other_kernel(
    steps, pairs_ref, own_ref, node_ref, query_ref, x_ref, w_ref, latent_ref,
    out_hbm, latent_hbm, out_ref, sems,
):
    latent_copy = pltpu.make_async_copy(latent_ref, latent_hbm, sems.at[steps])
    latent_copy.start()
    points, half = own_ref.shape
    block = points // steps
    core = lax.axis_index("dom") & 1
    queries = half_of(query_ref, (1 - core) * half, half)
    pairs = pairs_ref[...].T
    sends = []
    parts = [pl.ds(i * block, block) for i in range(steps)]

    def attended(part):
        return attend_half(pairs, queries[:, part], node_ref[:, part])

    mixed = attended(parts[0])
    for i, part in enumerate(parts):
        following = attended(parts[i + 1]) if i + 1 < steps else None
        own = own_ref[part, :]
        both = [jnp.where(core == 0, own, mixed), jnp.where(core == 0, mixed, own)]
        update = dot(jnp.concatenate(both, axis=1), w_ref[...])
        out_ref[part, :] = (x_ref[part, :].astype(f32) + update).astype(bf16)
        sends += started(pltpu.make_async_copy(out_ref.at[part], out_hbm.at[part], sems.at[i]))
        mixed = following
    for send in sends:
        send.wait()
    latent_copy.wait()


def in_hbm(array):
    return pltpu.with_memory_space_constraint(array, pltpu.HBM)


def in_vmem(array):
    return pltpu.with_memory_space_constraint(array, pltpu.VMEM)


def on_device(
    grid,
    latent_in,
    grid_gain,
    node_gain,
    dec_gain,
    w_q_enc,
    w_kv_enc,
    w_o_enc,
    w_q_dec,
    w_kv_dec,
    w_o_dec,
    enc_need,
    enc_slot,
    enc_count,
    dec_need,
    dec_slot,
):
    peers = lax.axis_size("dom")
    points, depth = grid.shape
    rows = latent_in.shape[0]
    width = w_q_enc.shape[1]
    nodes = peers * rows
    entries = enc_need.shape[1]
    edges = enc_slot.shape[0]
    cap = entries // peers
    half = width // 2
    sent = (peers, 2 * (half // LANES) + 1, rows // 2, LANES)
    swap = [(i, i ^ 1) for i in range(peers)]
    vmem = pl.BlockSpec(memory_space=pltpu.VMEM)
    hbm = pl.BlockSpec(memory_space=pltpu.HBM)

    other_grid = lax.ppermute(grid, "dom", swap)
    other_latent = lax.ppermute(latent_in, "dom", swap)
    ask_inputs = (
        w_q_enc,
        latent_in,
        node_gain.reshape(1, -1),
        enc_slot.T,
        enc_count.reshape(1, -1),
        enc_need,
    )
    asked = pl.pallas_call(
        ask_kernel,
        in_specs=[hbm] * len(ask_inputs),
        out_specs=vmem,
        out_shape=pltpu.VMEM(sent, bf16),
        scratch_shapes=[pltpu.VMEM(one.shape, one.dtype) for one in ask_inputs]
        + [pltpu.SemaphoreType.DMA((len(ask_inputs),))],
        compiler_params=params(62),
        cost_estimate=cost(2 * rows * depth * width, 2 * depth * width),
        name="ask",
    )(*map(in_hbm, ask_inputs))
    asked = exchange(asked)

    block = math.gcd(points, 256)
    steps = points // block
    pairs = pl.pallas_call(
        functools.partial(front_kernel, steps),
        in_specs=[hbm] * 4,
        out_specs=[vmem] * 2,
        out_shape=[pltpu.VMEM((points, width), bf16)] * 2,
        scratch_shapes=[
            pltpu.VMEM((1, depth), f32),
            pltpu.VMEM((points, depth), bf16),
            pltpu.VMEM((points, depth), bf16),
            pltpu.VMEM((depth, width), bf16),
            pltpu.SemaphoreType.DMA((5,)),
        ],
        compiler_params=params(40),
        cost_estimate=cost(4 * points * depth * width, 8 * points * depth),
        name="front",
    )(*map(in_hbm, (grid_gain.reshape(1, -1), grid, other_grid, w_kv_enc)))

    parts = pl.pallas_call(
        functools.partial(partial_kernel, cap, rows, edges),
        in_specs=[vmem] * 3,
        out_specs=vmem,
        out_shape=pltpu.VMEM((peers // 2, 2 * sent[1] - 1, *sent[2:]), bf16),
        compiler_params=params(40),
        cost_estimate=cost(4 * entries * points * width, 4 * points * width),
        name="partial",
    )(asked, *map(in_vmem, pairs))
    parts, dec_need, dec_slot = lax.optimization_barrier((parts, dec_need, dec_slot))
    same_core = [list(range(c, peers, 2)) for c in range(2)]
    parts = exchange(parts, same_core)

    slot_total = dec_need.shape[1]
    edge_count = dec_slot.shape[0]
    queries, node_of, w_kv_half = pl.pallas_call(
        functools.partial(middle_kernel, steps, peers, rows),
        in_specs=[vmem] * 3 + [hbm] * 3,
        out_specs=[vmem] * 3,
        out_shape=[
            pltpu.VMEM((width, points), bf16),
            jax.ShapeDtypeStruct((edge_count, points), jnp.int32),
            pltpu.VMEM((depth, width), bf16),
        ],
        scratch_shapes=[
            pltpu.VMEM((points, depth), bf16),
            pltpu.VMEM((depth, width), bf16),
            pltpu.SemaphoreType.DMA((4,)),
        ],
        compiler_params=params(40),
        cost_estimate=cost(2 * points * depth * width, 8 * points * depth),
        name="middle",
    )(
        grid_gain.reshape(1, -1),
        dec_need.reshape(slot_total // LANES, LANES),
        dec_slot,
        in_hbm(grid),
        in_hbm(w_q_dec),
        in_hbm(w_kv_dec),
    )
    parts, queries, node_of = lax.optimization_barrier((parts, queries, node_of))

    mixed = pl.pallas_call(
        merge_kernel,
        in_specs=[vmem],
        out_specs=vmem,
        out_shape=jax.ShapeDtypeStruct((2 * rows, half), bf16),
        compiler_params=params(24),
        cost_estimate=cost(8 * nodes * half, 8 * nodes * half),
        name="merge",
    )(parts)
    latent_out, everyone = pl.pallas_call(
        combine_kernel,
        in_specs=[vmem] * 7,
        out_specs=[vmem] * 2,
        out_shape=[
            pltpu.VMEM((rows, depth), bf16),
            jax.ShapeDtypeStruct((peers // 2, 2 * rows, width), bf16),
        ],
        compiler_params=params(24),
        cost_estimate=cost(6 * rows * depth * width, 6 * depth * width),
        name="combine",
    )(
        mixed,
        lax.ppermute(mixed, "dom", swap),
        latent_in,
        other_latent,
        dec_gain.reshape(1, -1),
        w_o_enc,
        in_vmem(w_kv_half),
    )
    own = exchange(everyone, same_core).reshape(nodes, width)
    other = lax.ppermute(own, "dom", swap)

    queries = in_vmem(queries)
    own_mixed = pl.pallas_call(
        functools.partial(own_kernel, steps),
        in_specs=[vmem] * 3,
        out_shape=jax.ShapeDtypeStruct((points, half), bf16),
        compiler_params=params(48),
        cost_estimate=cost(4 * points * nodes * width, 8 * points * nodes),
        name="own",
    )(own, node_of, queries)
    grid_out, latent_out = pl.pallas_call(
        functools.partial(other_kernel, steps),
        in_specs=[vmem] * 7,
        out_specs=[hbm] * 2,
        out_shape=[pltpu.HBM((points, depth), bf16), pltpu.HBM((rows, depth), bf16)],
        scratch_shapes=[
            pltpu.VMEM((points, depth), bf16),
            pltpu.SemaphoreType.DMA((steps + 1,)),
        ],
        compiler_params=params(48),
        cost_estimate=cost(4 * points * depth * width, 8 * points * depth),
        name="other",
    )(other, own_mixed, node_of, queries, grid, w_o_dec, in_vmem(latent_out))
    return (latent_out, grid_out)


def solution(mesh):
    return jax.shard_map(
        on_device,
        mesh=mesh,
        in_specs=(
            P(("groups", "dom"), None),
            P(("groups", "dom"), None),
            P(),
            P(),
            P(),
            P(),
            P(),
            P(),
            P(),
            P(),
            P(),
            P("dom", None),
            P(None, "dom"),
            P("dom"),
            P("dom", None),
            P(None, "dom"),
        ),
        out_specs=(P(("groups", "dom"), None), P(("groups", "dom"), None)),
        check_vma=False,
    )
```

```python
import functools
import math

import jax
import jax.numpy as jnp
from jax import lax
from jax.experimental import pallas as pl
from jax.experimental.pallas import tpu as pltpu
from jax.sharding import PartitionSpec as P

HEADS = 8
LANES = 128
NEG = -1e30
norm_eps = 1e-06
f32 = jnp.float32
bf16 = jnp.bfloat16


def iota(shape, dim):
    return lax.broadcasted_iota(jnp.int32, shape, dim)


def one_hot(places, shape, dim):
    return (places == iota(shape, dim)).astype(bf16)


def div(values, by):
    if by & (by - 1) == 0:
        return values >> (by.bit_length() - 1)
    return values // by


def mod(values, by):
    if by & (by - 1) == 0:
        return values & (by - 1)
    return values % by


def dot(a, b):
    return jnp.dot(a, b, preferred_element_type=f32)


def dot_t(a, b):
    return lax.dot_general(a, b, (((1,), (1,)), ((), ())), preferred_element_type=f32)


def normed(values, gain):
    widened = values.astype(f32)
    spread = jnp.mean(widened * widened, axis=-1, keepdims=True)
    return (widened * lax.rsqrt(spread + norm_eps) * gain).astype(bf16)


def params(mib):
    return pltpu.CompilerParams(vmem_limit_bytes=mib * 2**20)


def started(*copies):
    for copy in copies:
        copy.start()
    return copies


def split_copy(source, target, sems, count):
    rows = target.shape[0] // count
    parts = [pl.ds(i * rows, rows) for i in range(count)]
    return [
        pltpu.make_async_copy(source.at[part], target.at[part], sems.at[i])
        for i, part in enumerate(parts)
    ]


def cost(flops, read, exps=0):
    return pl.CostEstimate(flops=int(flops), bytes_accessed=int(read), transcendentals=int(exps))


def exchange(blocks, groups=None):
    return lax.all_to_all(
        blocks, "dom", split_axis=0, concat_axis=0, tiled=True, axis_index_groups=groups
    )


def slab(values, i, late, tall):
    return values[late * tall : (late + 1) * tall, i * LANES : (i + 1) * LANES]


def ask_kernel(*refs):
    sources, out_ref, held, sems = refs[:6], refs[6], refs[7:13], refs[13]
    copies = started(
        *[
            pltpu.make_async_copy(source, ref, sems.at[i])
            for i, (source, ref) in enumerate(zip(sources, held))
        ]
    )
    w_ref, latent_ref, gain_ref, slot_ref, count_ref, need_ref = held
    rows = latent_ref.shape[0]
    width = w_ref.shape[1]
    entries = need_ref.shape[1]
    edges = slot_ref.shape[1]
    peers = out_ref.shape[0]
    both = 2 * entries // peers
    tall = rows // 2
    for copy in copies[1:]:
        copy.wait()
    rows_normed = normed(latent_ref[...], gain_ref[...])
    live = iota((edges, rows), 0) < count_ref[...]
    slots = slot_ref[...].astype(f32).T.astype(jnp.int32)
    slots = jnp.where(live, slots, entries) - entries // 2
    slots = slots.astype(f32).astype(bf16)
    tile = jnp.zeros((tall, LANES), f32)
    for g in range(edges // tall):
        to = iota((rows, LANES), 1) == iota((rows, LANES), 0) + g * rows
        tile += dot(slots, to.astype(bf16))[g * tall : (g + 1) * tall]
    row, lane = iota((tall, LANES), 0), iota((tall, LANES), 1)
    in_list = (lane >= LANES // 2) & (lane < LANES // 2 + both)
    need = need_ref[...]
    tiles = []
    for chip in range(peers // 2):
        at = chip * both
        piece = need[:, at // LANES * LANES : at // LANES * LANES + LANES].astype(f32)
        piece = pltpu.roll(jnp.broadcast_to(piece, (tall, LANES)), (LANES // 2 - at) % LANES, 1)
        high = jnp.floor(piece * (1.0 / 256.0))
        piece = jnp.where(row == 0, piece - high * 256.0, jnp.where(row == 1, high, 0.0))
        tiles.append((tile + jnp.where(in_list, piece, 0.0)).astype(bf16))
    copies[0].wait()
    queries = dot(rows_normed, w_ref[...])
    blocks = width // 2 // LANES
    slabs = [
        slab(queries, i, late, tall).astype(bf16) for i in range(2 * blocks) for late in range(2)
    ]
    for p in range(peers):
        for i in range(2 * blocks):
            out_ref[p, i] = slabs[p % 2 * 2 * blocks + i]
        out_ref[p, 2 * blocks] = tiles[p // 2]


def front_kernel(
    steps, gain_hbm, own_hbm, other_hbm, w_hbm, own_out_ref, other_out_ref,
    gain_ref, own_ref, other_ref, w_ref, sems,
):
    points = own_ref.shape[0]
    block = points // steps
    half = own_out_ref.shape[1] // 2
    core = lax.axis_index("dom") & 1
    copies = started(
        pltpu.make_async_copy(gain_hbm, gain_ref, sems.at[0]),
        *[
            pltpu.make_async_copy(
                w_hbm.at[:, pl.ds(pl.multiple_of((core + 2 * i) * half, half), half)],
                w_ref.at[:, pl.ds(i * half, half)],
                sems.at[1 + i],
            )
            for i in range(2)
        ],
        pltpu.make_async_copy(own_hbm, own_ref, sems.at[3]),
        pltpu.make_async_copy(other_hbm, other_ref, sems.at[4]),
    )
    parts = [pl.ds(i * block, block) for i in range(steps)]
    for copy in copies[:3]:
        copy.wait()
    gain = gain_ref[...]
    sides = ((own_ref, own_out_ref), (other_ref, other_out_ref))
    for copy, (rows_ref, out_ref) in zip(copies[3:], sides):
        copy.wait()
        for part in parts:
            out_ref[part, :] = dot(normed(rows_ref[part, :], gain), w_ref[...]).astype(bf16)


def stat_parts(top, total):
    top_1 = top.astype(bf16).astype(f32)
    top_2 = (top - top_1).astype(bf16).astype(f32)
    total_1 = total.astype(bf16).astype(f32)
    return top_1, top_2, top - top_1 - top_2, total_1, total - total_1


def partial_kernel(cap, rows, edges, asked_ref, *refs):
    pairs_refs, out_ref = refs[:2], refs[2]
    me = lax.axis_index("dom")
    points, both = pairs_refs[0].shape
    chips = out_ref.shape[0]
    peers = 2 * chips
    width = both // 2
    heads = HEADS // 2
    size = width // heads
    tall = rows // 2
    blocks = width // LANES
    scale = math.log2(math.e) / math.sqrt(size)
    all_nodes, all_entries = peers * rows, peers * cap
    some = LANES // (heads * rows)
    nodes, entries = some * rows, some * cap
    tiles = asked_ref[:, 2 * blocks].astype(f32)

    tile_rows = peers * tall
    pick_row = iota((all_entries, tile_rows), 1) - div(iota((all_entries, tile_rows), 0), cap) * tall
    pick = jnp.where(pick_row == 0, 1.0, jnp.where(pick_row == 1, 256.0, 0.0)).astype(bf16)
    lists = dot(pick, tiles.reshape(tile_rows, LANES).astype(bf16))
    lane = iota((all_entries, LANES), 1) - mod(iota((all_entries, LANES), 0), cap) - LANES // 2
    gathered = []
    for other, ref in enumerate(pairs_refs):
        mine = lane == ((me ^ other) & 1) * cap
        index = jnp.sum(jnp.where(mine, lists, 0.0), axis=1, keepdims=True).astype(jnp.int32)
        gathered.append(dot(one_hot(index, (all_entries, points), 1), ref[...]))

    group, across = div(iota((tall, LANES), 1), rows), LANES // rows
    slots = []
    for g in range(edges // tall):
        line = []
        for first in range(0, peers, across):
            merged = jnp.zeros((tall, LANES), f32)
            for w in range(across):
                merged = jnp.where(
                    group == w, pltpu.roll(tiles[first + w], (w - g) * rows % LANES, 1), merged
                )
            line.append(merged)
        slots.append(jnp.concatenate(line, axis=1))
    all_slots = jnp.concatenate(slots, axis=0).astype(jnp.int32) + all_entries // 2

    listed = -(-cap // 8) * 8
    biases = []
    for other in range(2):
        slots = all_slots - (me ^ other) * cap
        uses = jnp.zeros((listed, all_nodes), f32)
        for j in range(edges):
            uses += jnp.where(slots[j : j + 1] == iota((listed, all_nodes), 0), 1.0, 0.0)
        live = uses > 0.5
        biases.append(jnp.where(live, jnp.log2(jnp.where(live, uses, 1.0)), NEG))

    window = mod(div(iota((listed, LANES), 1), rows), some)
    first_nodes = iota((listed, LANES), 1) < nodes
    first_head = iota((nodes, LANES), 1) < size
    tops, totals = [], []
    for start in range(0, peers, some):
        bias = []
        for one in biases:
            at = start * rows
            one = one[:, at // LANES * LANES : at // LANES * LANES + LANES]
            one = jnp.where(first_nodes, pltpu.roll(one, -at % LANES, 1), 0.0)
            spread = nodes
            while spread < LANES:
                one += pltpu.roll(one, spread, 1)
                spread *= 2
            bias += [jnp.where(window == w, one, NEG)[:cap] for w in range(some)]
        part = slice(start * cap, start * cap + entries)
        pairs = jnp.concatenate([one[part] for one in gathered], axis=0).astype(bf16)
        queries = [
            jnp.concatenate(
                [asked_ref[start + n // 2, 2 * i + n % 2].astype(f32) for n in range(2 * some)], axis=0
            )
            for i in range(blocks)
        ]
        queries = jnp.concatenate(queries, axis=1).astype(bf16)
        head = div(iota(queries.shape, 1), size)
        queries = jnp.concatenate(
            [jnp.where(head == h, queries, jnp.zeros_like(queries)) for h in range(heads)], axis=0
        )
        scores = dot_t(pairs[:, :width], queries) * scale + jnp.concatenate(bias, axis=0)
        top = jnp.max(scores, axis=0, keepdims=True)
        raised = jnp.exp2(scores - top)
        tops.append(top)
        totals.append(jnp.sum(raised, axis=0, keepdims=True))
        mixed = dot(raised.T.astype(bf16), pairs[:, width:])
        for i in range(blocks):
            block = mixed[:, i * LANES : (i + 1) * LANES]
            h = i * (LANES // size)
            block = jnp.where(
                first_head, block[h * nodes : (h + 1) * nodes], block[(h + 1) * nodes : (h + 2) * nodes]
            )
            for n in range(2 * some):
                place = n // 2 * 2 * blocks + 2 * i + n % 2
                out_ref[start // some, place] = slab(block, 0, n, tall).astype(bf16)

    row_lane = iota((tall, LANES), 1)
    for first in range(0, len(tops), 8):
        parts = stat_parts(
            jnp.concatenate(tops[first : first + 8], axis=0),
            jnp.concatenate(totals[first : first + 8], axis=0),
        )
        rest = jnp.zeros((LANES - 8 * len(parts), LANES), f32)
        columns = jnp.concatenate([*parts, rest], axis=0).T
        for g in range(8):
            tile = jnp.zeros((tall, LANES), f32)
            for w in range(some):
                for h in range(heads):
                    for late in range(2):
                        at = h * nodes + w * rows + late * tall
                        to = w * heads + h
                        here = (mod(row_lane, 8) == to) & (div(row_lane, LANES // 2) == late)
                        move = late * (LANES // 2) + to - g
                        piece = pltpu.roll(columns[at : at + tall], move % LANES, 1)
                        tile = jnp.where(here, piece, tile)
            out_ref[first + g, some * 2 * blocks] = tile.astype(bf16)


def merge_kernel(parts_ref, out_ref):
    heads, half = HEADS // 2, out_ref.shape[1]
    size, blocks = half // heads, half // LANES
    windows = (parts_ref.shape[1] - 1) // (2 * blocks)
    tile = parts_ref[:, windows * 2 * blocks].astype(f32)

    def moved(columns):
        return pltpu.roll(tile, LANES - columns, 2)

    top = tile + moved(8) + moved(16)
    factor = jnp.exp2(top - jnp.max(top, axis=0, keepdims=True))
    factor = factor / jnp.sum((moved(24) + moved(32)) * factor, axis=0, keepdims=True)
    head = div(iota(tile.shape, 2), size)
    nodes = []
    for w in range(windows):
        for late in range(2):
            line = []
            for i in range(blocks):
                wide = jnp.zeros(tile.shape, f32)
                for h in range(LANES // size):
                    at = late * (LANES // 2) + w * heads + i * (LANES // size) + h
                    wide = jnp.where(head == h, factor[..., at : at + 1], wide)
                part = parts_ref[:, w * 2 * blocks + 2 * i + late].astype(f32)
                line.append(jnp.sum(part * wide, axis=0))
            nodes.append(jnp.concatenate(line, axis=1))
    out_ref[...] = jnp.concatenate(nodes, axis=0).astype(bf16)


def combine_kernel(
    mixed_ref, other_mixed_ref, latent_ref, other_latent_ref, gain_ref, w_o_ref, w_kv_ref,
    latent_out_ref, out_ref,
):
    rows = latent_ref.shape[0]
    core = lax.axis_index("dom") & 1

    def in_order(own_ref, other_ref, axis):
        own, other = own_ref[...], other_ref[...]
        both = [jnp.where(core == 0, own, other), jnp.where(core == 0, other, own)]
        return jnp.concatenate(both, axis=axis)

    update = dot(in_order(mixed_ref, other_mixed_ref, 1), w_o_ref[...])
    latent_in = in_order(latent_ref, other_latent_ref, 0)
    latent_out = (latent_in.astype(f32) + update).astype(bf16)
    latent_out_ref[...] = jnp.where(core == 0, latent_out[:rows], latent_out[rows:])
    latent_rows = normed(latent_out, gain_ref[...])
    pairs = dot(latent_rows, w_kv_ref[...]).astype(bf16)
    for k in range(out_ref.shape[0]):
        out_ref[k] = pairs


def middle_kernel(
    steps, peers, rows, gain_ref, need_ref, slot_ref, x_hbm, w_hbm, w_kv_hbm,
    query_ref, node_ref, w_kv_ref, x_ref, w_ref, sems,
):
    copies = started(
        pltpu.make_async_copy(w_hbm, w_ref, sems.at[0]),
        *split_copy(x_hbm, x_ref, sems.at[pl.ds(4, 2)], 2),
    )
    half = w_kv_ref.shape[1] // 2
    core = lax.axis_index("dom") & 1
    later = started(
        *[
            pltpu.make_async_copy(
                w_kv_hbm.at[:, pl.ds(pl.multiple_of((core + 2 * i) * half, half), half)],
                w_kv_ref.at[:, pl.ds(i * half, half)],
                sems.at[2 + i],
            )
            for i in range(2)
        ]
    )
    points = x_ref.shape[0]
    block = points // steps
    high_count = need_ref.shape[0]
    cap = high_count * LANES // peers
    need = need_ref[...].astype(f32).astype(bf16)
    for j in range(slot_ref.shape[0]):
        slots = slot_ref[j : j + 1, :]
        row_of = (div(slots, LANES) == iota((high_count, points), 0)).astype(bf16)
        listed = lax.dot_general(need, row_of, (((0,), (0,)), ((), ())), preferred_element_type=f32)
        own = mod(slots, LANES) == iota((LANES, points), 0)
        found = jnp.sum(jnp.where(own, listed, 0.0), axis=0, keepdims=True).astype(jnp.int32)
        node_ref[j : j + 1, :] = div(slots, cap) * rows + found
    copies[0].wait()
    for i in range(steps):
        if i * 2 % steps == 0:
            copies[1 + i * 2 // steps].wait()
        part = pl.ds(i * block, block)
        queries = dot(normed(x_ref[part, :], gain_ref[...]), w_ref[...])
        query_ref[:, part] = queries.T.astype(bf16)
    for copy in later:
        copy.wait()


def attend_half(pairs, queries, nodes):
    half, points = queries.shape
    edges = nodes.shape[0]
    heads = HEADS // 2
    size = half // heads
    picks = [one_hot(nodes[j : j + 1], (pairs.shape[1], points), 0) for j in range(edges)]
    scores, values = [], []
    for j in range(edges):
        chosen = dot(pairs, picks[j])
        products = (chosen[:half] * queries.astype(f32)).reshape(heads, size, points)
        scores.append(jnp.sum(products, axis=1) * (1.0 / math.sqrt(size)))
        values.append(chosen[half:].reshape(heads, size, points))
    highest = functools.reduce(jnp.maximum, scores)
    raised = [jnp.exp(score - highest) for score in scores]
    inverse = 1.0 / sum(raised)
    mixed = jnp.zeros((heads, size, points), f32)
    for j in range(edges):
        weight = (raised[j] * inverse).astype(bf16).astype(f32).reshape(heads, 1, points)
        mixed += values[j] * weight
    return mixed.reshape(half, points).T.astype(bf16)


def half_of(ref, first, half):
    return ref.at[pl.ds(pl.multiple_of(first, half), half)]


def own_kernel(steps, pairs_ref, node_ref, query_ref, out_ref):
    points, half = out_ref.shape
    block = points // steps
    core = lax.axis_index("dom") & 1
    queries = half_of(query_ref, core * half, half)
    pairs = pairs_ref[...].T
    for i in range(steps):
        part = pl.ds(i * block, block)
        out_ref[part, :] = attend_half(pairs, queries[:, part], node_ref[:, part])


def other_kernel(
    steps, pairs_ref, own_ref, node_ref, query_ref, x_ref, w_ref, latent_ref,
    out_hbm, latent_hbm, out_ref, sems,
):
    latent_copy = pltpu.make_async_copy(latent_ref, latent_hbm, sems.at[steps])
    latent_copy.start()
    points, half = own_ref.shape
    block = points // steps
    core = lax.axis_index("dom") & 1
    queries = half_of(query_ref, (1 - core) * half, half)
    pairs = pairs_ref[...].T
    sends = []
    parts = [pl.ds(i * block, block) for i in range(steps)]

    def attended(part):
        return attend_half(pairs, queries[:, part], node_ref[:, part])

    mixed = attended(parts[0])
    for i, part in enumerate(parts):
        following = attended(parts[i + 1]) if i + 1 < steps else None
        own = own_ref[part, :]
        both = [jnp.where(core == 0, own, mixed), jnp.where(core == 0, mixed, own)]
        update = dot(jnp.concatenate(both, axis=1), w_ref[...])
        out_ref[part, :] = (x_ref[part, :].astype(f32) + update).astype(bf16)
        sends += started(pltpu.make_async_copy(out_ref.at[part], out_hbm.at[part], sems.at[i]))
        mixed = following
    for send in sends:
        send.wait()
    latent_copy.wait()


def in_hbm(array):
    return pltpu.with_memory_space_constraint(array, pltpu.HBM)


def in_vmem(array):
    return pltpu.with_memory_space_constraint(array, pltpu.VMEM)


def on_device(
    grid,
    latent_in,
    grid_gain,
    node_gain,
    dec_gain,
    w_q_enc,
    w_kv_enc,
    w_o_enc,
    w_q_dec,
    w_kv_dec,
    w_o_dec,
    enc_need,
    enc_slot,
    enc_count,
    dec_need,
    dec_slot,
):
    peers = lax.axis_size("dom")
    points, depth = grid.shape
    rows = latent_in.shape[0]
    width = w_q_enc.shape[1]
    nodes = peers * rows
    entries = enc_need.shape[1]
    edges = enc_slot.shape[0]
    cap = entries // peers
    half = width // 2
    sent = (peers, 2 * (half // LANES) + 1, rows // 2, LANES)
    swap = [(i, i ^ 1) for i in range(peers)]
    vmem = pl.BlockSpec(memory_space=pltpu.VMEM)
    hbm = pl.BlockSpec(memory_space=pltpu.HBM)

    other_grid = lax.ppermute(grid, "dom", swap)
    other_latent = lax.ppermute(latent_in, "dom", swap)
    ask_inputs = (
        w_q_enc,
        latent_in,
        node_gain.reshape(1, -1),
        enc_slot.T,
        enc_count.reshape(1, -1),
        enc_need,
    )
    asked = pl.pallas_call(
        ask_kernel,
        in_specs=[hbm] * len(ask_inputs),
        out_specs=vmem,
        out_shape=pltpu.VMEM(sent, bf16),
        scratch_shapes=[pltpu.VMEM(one.shape, one.dtype) for one in ask_inputs]
        + [pltpu.SemaphoreType.DMA((len(ask_inputs),))],
        compiler_params=params(62),
        cost_estimate=cost(2 * rows * depth * width, 2 * depth * width),
        name="ask",
    )(*map(in_hbm, ask_inputs))
    asked = exchange(asked)

    block = math.gcd(points, 256)
    steps = points // block
    pairs = pl.pallas_call(
        functools.partial(front_kernel, steps),
        in_specs=[hbm] * 4,
        out_specs=[vmem] * 2,
        out_shape=[pltpu.VMEM((points, width), bf16)] * 2,
        scratch_shapes=[
            pltpu.VMEM((1, depth), f32),
            pltpu.VMEM((points, depth), bf16),
            pltpu.VMEM((points, depth), bf16),
            pltpu.VMEM((depth, width), bf16),
            pltpu.SemaphoreType.DMA((5,)),
        ],
        compiler_params=params(40),
        cost_estimate=cost(4 * points * depth * width, 8 * points * depth),
        name="front",
    )(*map(in_hbm, (grid_gain.reshape(1, -1), grid, other_grid, w_kv_enc)))

    parts = pl.pallas_call(
        functools.partial(partial_kernel, cap, rows, edges),
        in_specs=[vmem] * 3,
        out_specs=vmem,
        out_shape=pltpu.VMEM((peers // 2, 2 * sent[1] - 1, *sent[2:]), bf16),
        compiler_params=params(40),
        cost_estimate=cost(4 * entries * points * width, 4 * points * width),
        name="partial",
    )(asked, *map(in_vmem, pairs))
    parts, dec_need, dec_slot = lax.optimization_barrier((parts, dec_need, dec_slot))
    same_core = [list(range(c, peers, 2)) for c in range(2)]
    parts = exchange(parts, same_core)

    slot_total = dec_need.shape[1]
    edge_count = dec_slot.shape[0]
    queries, node_of, w_kv_half = pl.pallas_call(
        functools.partial(middle_kernel, steps, peers, rows),
        in_specs=[vmem] * 3 + [hbm] * 3,
        out_specs=[vmem] * 3,
        out_shape=[
            pltpu.VMEM((width, points), bf16),
            jax.ShapeDtypeStruct((edge_count, points), jnp.int32),
            pltpu.VMEM((depth, width), bf16),
        ],
        scratch_shapes=[
            pltpu.VMEM((points, depth), bf16),
            pltpu.VMEM((depth, width), bf16),
            pltpu.SemaphoreType.DMA((6,)),
        ],
        compiler_params=params(40),
        cost_estimate=cost(2 * points * depth * width, 8 * points * depth),
        name="middle",
    )(
        grid_gain.reshape(1, -1),
        dec_need.reshape(slot_total // LANES, LANES),
        dec_slot,
        in_hbm(grid),
        in_hbm(w_q_dec),
        in_hbm(w_kv_dec),
    )
    parts, queries, node_of = lax.optimization_barrier((parts, queries, node_of))

    mixed = pl.pallas_call(
        merge_kernel,
        in_specs=[vmem],
        out_specs=vmem,
        out_shape=jax.ShapeDtypeStruct((2 * rows, half), bf16),
        compiler_params=params(24),
        cost_estimate=cost(8 * nodes * half, 8 * nodes * half),
        name="merge",
    )(parts)
    latent_out, everyone = pl.pallas_call(
        combine_kernel,
        in_specs=[vmem] * 7,
        out_specs=[vmem] * 2,
        out_shape=[
            pltpu.VMEM((rows, depth), bf16),
            jax.ShapeDtypeStruct((peers // 2, 2 * rows, width), bf16),
        ],
        compiler_params=params(24),
        cost_estimate=cost(6 * rows * depth * width, 6 * depth * width),
        name="combine",
    )(
        mixed,
        lax.ppermute(mixed, "dom", swap),
        latent_in,
        other_latent,
        dec_gain.reshape(1, -1),
        w_o_enc,
        in_vmem(w_kv_half),
    )
    own = exchange(everyone, same_core).reshape(nodes, width)
    other = lax.ppermute(own, "dom", swap)

    queries = in_vmem(queries)
    own_mixed = pl.pallas_call(
        functools.partial(own_kernel, steps),
        in_specs=[vmem] * 3,
        out_shape=jax.ShapeDtypeStruct((points, half), bf16),
        compiler_params=params(48),
        cost_estimate=cost(4 * points * nodes * width, 8 * points * nodes),
        name="own",
    )(own, node_of, queries)
    grid_out, latent_out = pl.pallas_call(
        functools.partial(other_kernel, steps),
        in_specs=[vmem] * 7,
        out_specs=[hbm] * 2,
        out_shape=[pltpu.HBM((points, depth), bf16), pltpu.HBM((rows, depth), bf16)],
        scratch_shapes=[
            pltpu.VMEM((points, depth), bf16),
            pltpu.SemaphoreType.DMA((steps + 1,)),
        ],
        compiler_params=params(48),
        cost_estimate=cost(4 * points * depth * width, 8 * points * depth),
        name="other",
    )(other, own_mixed, node_of, queries, grid, w_o_dec, in_vmem(latent_out))
    return (latent_out, grid_out)


def solution(mesh):
    return jax.shard_map(
        on_device,
        mesh=mesh,
        in_specs=(
            P(("groups", "dom"), None),
            P(("groups", "dom"), None),
            P(),
            P(),
            P(),
            P(),
            P(),
            P(),
            P(),
            P(),
            P(),
            P("dom", None),
            P(None, "dom"),
            P("dom"),
            P("dom", None),
            P(None, "dom"),
        ),
        out_specs=(P(("groups", "dom"), None), P(("groups", "dom"), None)),
        check_vma=False,
    )
```

```python
import functools
import math

import jax
import jax.numpy as jnp
from jax import lax
from jax.experimental import pallas as pl
from jax.experimental.pallas import tpu as pltpu
from jax.sharding import PartitionSpec as P

HEADS = 8
LANES = 128
NEG = -1e30
norm_eps = 1e-06
f32 = jnp.float32
bf16 = jnp.bfloat16


def iota(shape, dim):
    return lax.broadcasted_iota(jnp.int32, shape, dim)


def one_hot(places, shape, dim):
    return (places == iota(shape, dim)).astype(bf16)


def div(values, by):
    if by & (by - 1) == 0:
        return values >> (by.bit_length() - 1)
    return values // by


def mod(values, by):
    if by & (by - 1) == 0:
        return values & (by - 1)
    return values % by


def dot(a, b):
    return jnp.dot(a, b, preferred_element_type=f32)


def dot_t(a, b):
    return lax.dot_general(a, b, (((1,), (1,)), ((), ())), preferred_element_type=f32)


def normed(values, gain):
    widened = values.astype(f32)
    spread = jnp.mean(widened * widened, axis=-1, keepdims=True)
    return (widened * lax.rsqrt(spread + norm_eps) * gain).astype(bf16)


def params(mib):
    return pltpu.CompilerParams(vmem_limit_bytes=mib * 2**20)


def started(*copies):
    for copy in copies:
        copy.start()
    return copies


def split_copy(source, target, sems, count):
    rows = target.shape[0] // count
    parts = [pl.ds(i * rows, rows) for i in range(count)]
    return [
        pltpu.make_async_copy(source.at[part], target.at[part], sems.at[i])
        for i, part in enumerate(parts)
    ]


def cost(flops, read, exps=0):
    return pl.CostEstimate(flops=int(flops), bytes_accessed=int(read), transcendentals=int(exps))


def exchange(blocks, groups=None):
    return lax.all_to_all(
        blocks, "dom", split_axis=0, concat_axis=0, tiled=True, axis_index_groups=groups
    )


def slab(values, i, late, tall):
    return values[late * tall : (late + 1) * tall, i * LANES : (i + 1) * LANES]


def ask_kernel(*refs):
    sources, out_ref, held, sems = refs[:6], refs[6], refs[7:13], refs[13]
    copies = started(
        *[
            pltpu.make_async_copy(source, ref, sems.at[i])
            for i, (source, ref) in enumerate(zip(sources, held))
        ]
    )
    w_ref, latent_ref, gain_ref, slot_ref, count_ref, need_ref = held
    rows = latent_ref.shape[0]
    width = w_ref.shape[1]
    entries = need_ref.shape[1]
    edges = slot_ref.shape[1]
    peers = out_ref.shape[0]
    both = 2 * entries // peers
    tall = rows // 2
    for copy in copies[1:]:
        copy.wait()
    rows_normed = normed(latent_ref[...], gain_ref[...])
    live = iota((edges, rows), 0) < count_ref[...]
    slots = slot_ref[...].astype(f32).T.astype(jnp.int32)
    slots = jnp.where(live, slots, entries) - entries // 2
    slots = slots.astype(f32).astype(bf16)
    tile = jnp.zeros((tall, LANES), f32)
    for g in range(edges // tall):
        to = iota((rows, LANES), 1) == iota((rows, LANES), 0) + g * rows
        tile += dot(slots, to.astype(bf16))[g * tall : (g + 1) * tall]
    row, lane = iota((tall, LANES), 0), iota((tall, LANES), 1)
    in_list = (lane >= LANES // 2) & (lane < LANES // 2 + both)
    need = need_ref[...]
    tiles = []
    for chip in range(peers // 2):
        at = chip * both
        piece = need[:, at // LANES * LANES : at // LANES * LANES + LANES].astype(f32)
        piece = pltpu.roll(jnp.broadcast_to(piece, (tall, LANES)), (LANES // 2 - at) % LANES, 1)
        high = jnp.floor(piece * (1.0 / 256.0))
        piece = jnp.where(row == 0, piece - high * 256.0, jnp.where(row == 1, high, 0.0))
        tiles.append((tile + jnp.where(in_list, piece, 0.0)).astype(bf16))
    copies[0].wait()
    queries = dot(rows_normed, w_ref[...])
    blocks = width // 2 // LANES
    slabs = [
        slab(queries, i, late, tall).astype(bf16) for i in range(2 * blocks) for late in range(2)
    ]
    for p in range(peers):
        for i in range(2 * blocks):
            out_ref[p, i] = slabs[p % 2 * 2 * blocks + i]
        out_ref[p, 2 * blocks] = tiles[p // 2]


def front_kernel(
    steps, gain_hbm, own_hbm, other_hbm, w_hbm, own_out_ref, other_out_ref,
    gain_ref, own_ref, other_ref, w_ref, sems,
):
    points = own_ref.shape[0]
    block = points // steps
    half = own_out_ref.shape[1] // 2
    core = lax.axis_index("dom") & 1
    copies = started(
        pltpu.make_async_copy(gain_hbm, gain_ref, sems.at[0]),
        *[
            pltpu.make_async_copy(
                w_hbm.at[:, pl.ds(pl.multiple_of((core + 2 * i) * half, half), half)],
                w_ref.at[:, pl.ds(i * half, half)],
                sems.at[1 + i],
            )
            for i in range(2)
        ],
        pltpu.make_async_copy(own_hbm, own_ref, sems.at[3]),
        pltpu.make_async_copy(other_hbm, other_ref, sems.at[4]),
    )
    parts = [pl.ds(i * block, block) for i in range(steps)]
    for copy in copies[:3]:
        copy.wait()
    gain = gain_ref[...]
    sides = ((own_ref, own_out_ref), (other_ref, other_out_ref))
    for copy, (rows_ref, out_ref) in zip(copies[3:], sides):
        copy.wait()
        for part in parts:
            out_ref[part, :] = dot(normed(rows_ref[part, :], gain), w_ref[...]).astype(bf16)


def stat_parts(top, total):
    top_1 = top.astype(bf16).astype(f32)
    top_2 = (top - top_1).astype(bf16).astype(f32)
    total_1 = total.astype(bf16).astype(f32)
    return top_1, top_2, top - top_1 - top_2, total_1, total - total_1


def partial_kernel(cap, rows, edges, asked_ref, *refs):
    pairs_refs, out_ref = refs[:2], refs[2]
    me = lax.axis_index("dom")
    points, both = pairs_refs[0].shape
    chips = out_ref.shape[0]
    peers = 2 * chips
    width = both // 2
    heads = HEADS // 2
    size = width // heads
    tall = rows // 2
    blocks = width // LANES
    scale = math.log2(math.e) / math.sqrt(size)
    all_nodes, all_entries = peers * rows, peers * cap
    some = LANES // (heads * rows)
    nodes, entries = some * rows, some * cap
    tiles = asked_ref[:, 2 * blocks].astype(f32)

    tile_rows = peers * tall
    pick_row = iota((all_entries, tile_rows), 1) - div(iota((all_entries, tile_rows), 0), cap) * tall
    pick = jnp.where(pick_row == 0, 1.0, jnp.where(pick_row == 1, 256.0, 0.0)).astype(bf16)
    lists = dot(pick, tiles.reshape(tile_rows, LANES).astype(bf16))
    lane = iota((all_entries, LANES), 1) - mod(iota((all_entries, LANES), 0), cap) - LANES // 2
    gathered = []
    for other, ref in enumerate(pairs_refs):
        mine = lane == ((me ^ other) & 1) * cap
        index = jnp.sum(jnp.where(mine, lists, 0.0), axis=1, keepdims=True).astype(jnp.int32)
        gathered.append(dot(one_hot(index, (all_entries, points), 1), ref[...]))

    group, across = div(iota((tall, LANES), 1), rows), LANES // rows
    slots = []
    for g in range(edges // tall):
        line = []
        for first in range(0, peers, across):
            merged = jnp.zeros((tall, LANES), f32)
            for w in range(across):
                merged = jnp.where(
                    group == w, pltpu.roll(tiles[first + w], (w - g) * rows % LANES, 1), merged
                )
            line.append(merged)
        slots.append(jnp.concatenate(line, axis=1))
    all_slots = jnp.concatenate(slots, axis=0).astype(jnp.int32) + all_entries // 2

    listed = -(-cap // 8) * 8
    biases = []
    for other in range(2):
        slots = all_slots - (me ^ other) * cap
        uses = jnp.zeros((listed, all_nodes), f32)
        for j in range(edges):
            uses += jnp.where(slots[j : j + 1] == iota((listed, all_nodes), 0), 1.0, 0.0)
        live = uses > 0.5
        biases.append(jnp.where(live, jnp.log2(jnp.where(live, uses, 1.0)), NEG))

    window = mod(div(iota((listed, LANES), 1), rows), some)
    first_nodes = iota((listed, LANES), 1) < nodes
    first_head = iota((nodes, LANES), 1) < size
    tops, totals = [], []
    for start in range(0, peers, some):
        bias = []
        for one in biases:
            at = start * rows
            one = one[:, at // LANES * LANES : at // LANES * LANES + LANES]
            one = jnp.where(first_nodes, pltpu.roll(one, -at % LANES, 1), 0.0)
            spread = nodes
            while spread < LANES:
                one += pltpu.roll(one, spread, 1)
                spread *= 2
            bias += [jnp.where(window == w, one, NEG)[:cap] for w in range(some)]
        part = slice(start * cap, start * cap + entries)
        pairs = jnp.concatenate([one[part] for one in gathered], axis=0).astype(bf16)
        queries = [
            jnp.concatenate(
                [asked_ref[start + n // 2, 2 * i + n % 2].astype(f32) for n in range(2 * some)], axis=0
            )
            for i in range(blocks)
        ]
        queries = jnp.concatenate(queries, axis=1).astype(bf16)
        head = div(iota(queries.shape, 1), size)
        queries = jnp.concatenate(
            [jnp.where(head == h, queries, jnp.zeros_like(queries)) for h in range(heads)], axis=0
        )
        scores = dot_t(pairs[:, :width], queries) * scale + jnp.concatenate(bias, axis=0)
        top = jnp.max(scores, axis=0, keepdims=True)
        raised = jnp.exp2(scores - top)
        tops.append(top)
        totals.append(jnp.sum(raised, axis=0, keepdims=True))
        mixed = dot(raised.T.astype(bf16), pairs[:, width:])
        for i in range(blocks):
            block = mixed[:, i * LANES : (i + 1) * LANES]
            h = i * (LANES // size)
            block = jnp.where(
                first_head, block[h * nodes : (h + 1) * nodes], block[(h + 1) * nodes : (h + 2) * nodes]
            )
            for n in range(2 * some):
                place = n // 2 * 2 * blocks + 2 * i + n % 2
                out_ref[start // some, place] = slab(block, 0, n, tall).astype(bf16)

    row_lane = iota((tall, LANES), 1)
    for first in range(0, len(tops), 8):
        parts = stat_parts(
            jnp.concatenate(tops[first : first + 8], axis=0),
            jnp.concatenate(totals[first : first + 8], axis=0),
        )
        rest = jnp.zeros((LANES - 8 * len(parts), LANES), f32)
        columns = jnp.concatenate([*parts, rest], axis=0).T
        for g in range(8):
            tile = jnp.zeros((tall, LANES), f32)
            for w in range(some):
                for h in range(heads):
                    for late in range(2):
                        at = h * nodes + w * rows + late * tall
                        to = w * heads + h
                        here = (mod(row_lane, 8) == to) & (div(row_lane, LANES // 2) == late)
                        move = late * (LANES // 2) + to - g
                        piece = pltpu.roll(columns[at : at + tall], move % LANES, 1)
                        tile = jnp.where(here, piece, tile)
            out_ref[first + g, some * 2 * blocks] = tile.astype(bf16)


def merge_kernel(parts_ref, out_ref):
    heads, half = HEADS // 2, out_ref.shape[1]
    size, blocks = half // heads, half // LANES
    windows = (parts_ref.shape[1] - 1) // (2 * blocks)
    tile = parts_ref[:, windows * 2 * blocks].astype(f32)

    def moved(columns):
        return pltpu.roll(tile, LANES - columns, 2)

    top = tile + moved(8) + moved(16)
    factor = jnp.exp2(top - jnp.max(top, axis=0, keepdims=True))
    factor = factor / jnp.sum((moved(24) + moved(32)) * factor, axis=0, keepdims=True)
    head = div(iota(tile.shape, 2), size)
    nodes = []
    for w in range(windows):
        for late in range(2):
            line = []
            for i in range(blocks):
                wide = jnp.zeros(tile.shape, f32)
                for h in range(LANES // size):
                    at = late * (LANES // 2) + w * heads + i * (LANES // size) + h
                    wide = jnp.where(head == h, factor[..., at : at + 1], wide)
                part = parts_ref[:, w * 2 * blocks + 2 * i + late].astype(f32)
                line.append(jnp.sum(part * wide, axis=0))
            nodes.append(jnp.concatenate(line, axis=1))
    out_ref[...] = jnp.concatenate(nodes, axis=0).astype(bf16)


def combine_kernel(
    mixed_ref, other_mixed_ref, latent_ref, other_latent_ref, gain_ref, w_o_ref, w_kv_ref,
    latent_out_ref, out_ref,
):
    rows = latent_ref.shape[0]
    core = lax.axis_index("dom") & 1

    def in_order(own_ref, other_ref, axis):
        own, other = own_ref[...], other_ref[...]
        both = [jnp.where(core == 0, own, other), jnp.where(core == 0, other, own)]
        return jnp.concatenate(both, axis=axis)

    update = dot(in_order(mixed_ref, other_mixed_ref, 1), w_o_ref[...])
    latent_in = in_order(latent_ref, other_latent_ref, 0)
    latent_out = (latent_in.astype(f32) + update).astype(bf16)
    latent_out_ref[...] = jnp.where(core == 0, latent_out[:rows], latent_out[rows:])
    latent_rows = normed(latent_out, gain_ref[...])
    pairs = dot(latent_rows, w_kv_ref[...]).astype(bf16)
    for k in range(out_ref.shape[0]):
        out_ref[k] = pairs


def middle_kernel(
    steps, peers, rows, gain_ref, need_ref, slot_ref, x_hbm, w_hbm, w_kv_hbm,
    query_ref, node_ref, w_kv_ref, x_ref, w_ref, sems,
):
    copies = started(
        pltpu.make_async_copy(w_hbm, w_ref, sems.at[0]),
        *split_copy(x_hbm, x_ref, sems.at[pl.ds(4, 2)], 2),
    )
    half = w_kv_ref.shape[1] // 2
    core = lax.axis_index("dom") & 1
    later = started(
        *[
            pltpu.make_async_copy(
                w_kv_hbm.at[:, pl.ds(pl.multiple_of((core + 2 * i) * half, half), half)],
                w_kv_ref.at[:, pl.ds(i * half, half)],
                sems.at[2 + i],
            )
            for i in range(2)
        ]
    )
    points = x_ref.shape[0]
    block = points // steps
    high_count = need_ref.shape[0]
    cap = high_count * LANES // peers
    need = need_ref[...].astype(f32).astype(bf16)
    for j in range(slot_ref.shape[0]):
        slots = slot_ref[j : j + 1, :]
        row_of = (div(slots, LANES) == iota((high_count, points), 0)).astype(bf16)
        listed = lax.dot_general(need, row_of, (((0,), (0,)), ((), ())), preferred_element_type=f32)
        own = mod(slots, LANES) == iota((LANES, points), 0)
        found = jnp.sum(jnp.where(own, listed, 0.0), axis=0, keepdims=True).astype(jnp.int32)
        node_ref[j : j + 1, :] = div(slots, cap) * rows + found
    copies[0].wait()
    for i in range(steps):
        if i * 2 % steps == 0:
            copies[1 + i * 2 // steps].wait()
        part = pl.ds(i * block, block)
        queries = dot(normed(x_ref[part, :], gain_ref[...]), w_ref[...])
        query_ref[:, part] = queries.T.astype(bf16)
    for copy in later:
        copy.wait()


def attend_half(pairs, queries, nodes):
    half, points = queries.shape
    edges = nodes.shape[0]
    heads = HEADS // 2
    size = half // heads
    picks = [one_hot(nodes[j : j + 1], (pairs.shape[1], points), 0) for j in range(edges)]
    scores, values = [], []
    for j in range(edges):
        chosen = dot(pairs, picks[j])
        products = (chosen[:half] * queries.astype(f32)).reshape(heads, size, points)
        scores.append(jnp.sum(products, axis=1) * (1.0 / math.sqrt(size)))
        values.append(chosen[half:].reshape(heads, size, points))
    highest = functools.reduce(jnp.maximum, scores)
    raised = [jnp.exp(score - highest) for score in scores]
    inverse = 1.0 / sum(raised)
    mixed = jnp.zeros((heads, size, points), f32)
    for j in range(edges):
        weight = (raised[j] * inverse).astype(bf16).astype(f32).reshape(heads, 1, points)
        mixed += values[j] * weight
    return mixed.reshape(half, points).T.astype(bf16)


def half_of(ref, first, half):
    return ref.at[pl.ds(pl.multiple_of(first, half), half)]


def own_kernel(steps, pairs_ref, node_ref, query_ref, out_ref):
    points, half = out_ref.shape
    block = points // steps
    core = lax.axis_index("dom") & 1
    queries = half_of(query_ref, core * half, half)
    pairs = pairs_ref[...].T
    for i in range(steps):
        part = pl.ds(i * block, block)
        out_ref[part, :] = attend_half(pairs, queries[:, part], node_ref[:, part])


def other_kernel(
    steps, pairs_ref, own_ref, node_ref, query_ref, x_ref, w_ref, latent_ref,
    out_hbm, latent_hbm, out_ref, sems,
):
    latent_copy = pltpu.make_async_copy(latent_ref, latent_hbm, sems.at[steps])
    latent_copy.start()
    points, half = own_ref.shape
    block = points // steps
    core = lax.axis_index("dom") & 1
    queries = half_of(query_ref, (1 - core) * half, half)
    pairs = pairs_ref[...].T
    sends = []
    parts = [pl.ds(i * block, block) for i in range(steps)]

    def attended(part):
        return attend_half(pairs, queries[:, part], node_ref[:, part])

    mixed = attended(parts[0])
    for i, part in enumerate(parts):
        following = attended(parts[i + 1]) if i + 1 < steps else None
        own = own_ref[part, :]
        both = [jnp.where(core == 0, own, mixed), jnp.where(core == 0, mixed, own)]
        update = dot(jnp.concatenate(both, axis=1), w_ref[...])
        out_ref[part, :] = (x_ref[part, :].astype(f32) + update).astype(bf16)
        sends += started(pltpu.make_async_copy(out_ref.at[part], out_hbm.at[part], sems.at[i]))
        mixed = following
    for send in sends:
        send.wait()
    latent_copy.wait()


def in_hbm(array):
    return pltpu.with_memory_space_constraint(array, pltpu.HBM)


def in_vmem(array):
    return pltpu.with_memory_space_constraint(array, pltpu.VMEM)


def on_device(
    grid,
    latent_in,
    grid_gain,
    node_gain,
    dec_gain,
    w_q_enc,
    w_kv_enc,
    w_o_enc,
    w_q_dec,
    w_kv_dec,
    w_o_dec,
    enc_need,
    enc_slot,
    enc_count,
    dec_need,
    dec_slot,
):
    peers = lax.axis_size("dom")
    points, depth = grid.shape
    rows = latent_in.shape[0]
    width = w_q_enc.shape[1]
    nodes = peers * rows
    entries = enc_need.shape[1]
    edges = enc_slot.shape[0]
    cap = entries // peers
    half = width // 2
    sent = (peers, 2 * (half // LANES) + 1, rows // 2, LANES)
    swap = [(i, i ^ 1) for i in range(peers)]
    vmem = pl.BlockSpec(memory_space=pltpu.VMEM)
    hbm = pl.BlockSpec(memory_space=pltpu.HBM)

    other_grid = lax.ppermute(grid, "dom", swap)
    other_latent = lax.ppermute(latent_in, "dom", swap)
    ask_inputs = (
        w_q_enc,
        latent_in,
        node_gain.reshape(1, -1),
        enc_slot.T,
        enc_count.reshape(1, -1),
        enc_need,
    )
    asked = pl.pallas_call(
        ask_kernel,
        in_specs=[hbm] * len(ask_inputs),
        out_specs=vmem,
        out_shape=pltpu.VMEM(sent, bf16),
        scratch_shapes=[pltpu.VMEM(one.shape, one.dtype) for one in ask_inputs]
        + [pltpu.SemaphoreType.DMA((len(ask_inputs),))],
        compiler_params=params(62),
        cost_estimate=cost(2 * rows * depth * width, 2 * depth * width),
        name="ask",
    )(*map(in_hbm, ask_inputs))
    asked = exchange(asked)

    block = math.gcd(points, 256)
    steps = points // block
    pairs = pl.pallas_call(
        functools.partial(front_kernel, steps),
        in_specs=[hbm] * 4,
        out_specs=[vmem] * 2,
        out_shape=[pltpu.VMEM((points, width), bf16)] * 2,
        scratch_shapes=[
            pltpu.VMEM((1, depth), f32),
            pltpu.VMEM((points, depth), bf16),
            pltpu.VMEM((points, depth), bf16),
            pltpu.VMEM((depth, width), bf16),
            pltpu.SemaphoreType.DMA((5,)),
        ],
        compiler_params=params(40),
        cost_estimate=cost(4 * points * depth * width, 8 * points * depth),
        name="front",
    )(*map(in_hbm, (grid_gain.reshape(1, -1), grid, other_grid, w_kv_enc)))

    parts = pl.pallas_call(
        functools.partial(partial_kernel, cap, rows, edges),
        in_specs=[vmem] * 3,
        out_specs=vmem,
        out_shape=pltpu.VMEM((peers // 2, 2 * sent[1] - 1, *sent[2:]), bf16),
        compiler_params=params(40),
        cost_estimate=cost(4 * entries * points * width, 4 * points * width),
        name="partial",
    )(asked, *map(in_vmem, pairs))
    parts, dec_need, dec_slot = lax.optimization_barrier((parts, dec_need, dec_slot))
    same_core = [list(range(c, peers, 2)) for c in range(2)]
    parts = exchange(parts, same_core)

    slot_total = dec_need.shape[1]
    edge_count = dec_slot.shape[0]
    queries, node_of, w_kv_half = pl.pallas_call(
        functools.partial(middle_kernel, steps, peers, rows),
        in_specs=[vmem] * 3 + [hbm] * 3,
        out_specs=[vmem] * 3,
        out_shape=[
            pltpu.VMEM((width, points), bf16),
            jax.ShapeDtypeStruct((edge_count, points), jnp.int32),
            pltpu.VMEM((depth, width), bf16),
        ],
        scratch_shapes=[
            pltpu.VMEM((points, depth), bf16),
            pltpu.VMEM((depth, width), bf16),
            pltpu.SemaphoreType.DMA((6,)),
        ],
        compiler_params=params(40),
        cost_estimate=cost(2 * points * depth * width, 8 * points * depth),
        name="middle",
    )(
        grid_gain.reshape(1, -1),
        dec_need.reshape(slot_total // LANES, LANES),
        dec_slot,
        in_hbm(grid),
        in_hbm(w_q_dec),
        in_hbm(w_kv_dec),
    )
    parts, queries, node_of = lax.optimization_barrier((parts, queries, node_of))

    mixed = pl.pallas_call(
        merge_kernel,
        in_specs=[vmem],
        out_specs=vmem,
        out_shape=jax.ShapeDtypeStruct((2 * rows, half), bf16),
        compiler_params=params(24),
        cost_estimate=cost(8 * nodes * half, 8 * nodes * half),
        name="merge",
    )(parts)
    latent_out, everyone = pl.pallas_call(
        combine_kernel,
        in_specs=[vmem] * 7,
        out_specs=[vmem] * 2,
        out_shape=[
            pltpu.VMEM((rows, depth), bf16),
            jax.ShapeDtypeStruct((peers // 2, 2 * rows, width), bf16),
        ],
        compiler_params=params(24),
        cost_estimate=cost(6 * rows * depth * width, 6 * depth * width),
        name="combine",
    )(
        mixed,
        lax.ppermute(mixed, "dom", swap),
        latent_in,
        other_latent,
        dec_gain.reshape(1, -1),
        w_o_enc,
        in_vmem(w_kv_half),
    )
    own = exchange(everyone, same_core).reshape(nodes, width)
    other = lax.ppermute(own, "dom", swap)

    queries = in_vmem(queries)
    own_mixed = pl.pallas_call(
        functools.partial(own_kernel, 2 * steps),
        in_specs=[vmem] * 3,
        out_shape=jax.ShapeDtypeStruct((points, half), bf16),
        compiler_params=params(48),
        cost_estimate=cost(4 * points * nodes * width, 8 * points * nodes),
        name="own",
    )(own, node_of, queries)
    grid_out, latent_out = pl.pallas_call(
        functools.partial(other_kernel, steps),
        in_specs=[vmem] * 7,
        out_specs=[hbm] * 2,
        out_shape=[pltpu.HBM((points, depth), bf16), pltpu.HBM((rows, depth), bf16)],
        scratch_shapes=[
            pltpu.VMEM((points, depth), bf16),
            pltpu.SemaphoreType.DMA((steps + 1,)),
        ],
        compiler_params=params(48),
        cost_estimate=cost(4 * points * depth * width, 8 * points * depth),
        name="other",
    )(other, own_mixed, node_of, queries, grid, w_o_dec, in_vmem(latent_out))
    return (latent_out, grid_out)


def solution(mesh):
    return jax.shard_map(
        on_device,
        mesh=mesh,
        in_specs=(
            P(("groups", "dom"), None),
            P(("groups", "dom"), None),
            P(),
            P(),
            P(),
            P(),
            P(),
            P(),
            P(),
            P(),
            P(),
            P("dom", None),
            P(None, "dom"),
            P("dom"),
            P("dom", None),
            P(None, "dom"),
        ),
        out_specs=(P(("groups", "dom"), None), P(("groups", "dom"), None)),
        check_vma=False,
    )
```
